32 devices in a mesh: dp: 16 (over z, y, core), space: 2 (over x).
Axes of the slice: x: 2, y: 2, z: 4, core: 2. Of those that a mesh axis runs over, the one named last changes fastest.
Arguments:
- occupancy: int32 [16, 5, 32, 128], P('dp', None, 'space'), may hold values from 0 to 8191
- state_labels: int32 [16, 2, 8], P('dp', 'space'), may hold values 0 or 1
- lift_weight: bfloat16 [13, 32], replicated, may hold values from -1.75 to 1.75
- temporal_weight: bfloat16 [3, 3, 5, 32, 64], replicated, may hold values from -0.21875 to 0.21875
- middle_weight: bfloat16 [3, 3, 64, 128], replicated, may hold values from -0.375 to 0.375
- deeper_weight: bfloat16 [3, 3, 128, 256], replicated, may hold values from -0.25 to 0.25
- deepest_weight: bfloat16 [3, 3, 256, 512], replicated, may hold values from -0.1875 to 0.1875
- head_weight: bfloat16 [512], replicated, may hold values from -0.25 to 0.25
Outputs:
- temporal_grad: float32 [3, 3, 5, 32, 64], replicated
- middle_grad: float32 [3, 3, 64, 128], replicated
- deeper_grad: float32 [3, 3, 128, 256], replicated
- deepest_grad: float32 [3, 3, 256, 512], replicated
- head_grad: float32 [512], replicated
The draws below stay inside these ranges and needn't reach their ends.
All inputs are finite; a program needn't handle non-finite values. No bound on the sum of `state_labels` on one device may be relied on, other than what follows from the above.
Results may differ from the reference program's by a relative error of at most 0.015.
Values may be sent and summed in bfloat16 or wider, within the bound.
No kernel may reach another device: no remote copies, remote signals or barrier semaphores. Data moves between devices by JAX's collectives and lax.ppermute only.
A program may use at most 64 MiB of HBM per device.

```python
import jax
import jax.numpy as jnp
from jax import lax

HEIGHTS = 13
CH_LIFT = 32
CH_ONE = 64
CH_TWO = 128
CH_THREE = 256
CH_FOUR = 512
FRAMES = 5
COLS = 128
BATCH = 16
HEIGHT_CELLS = 32


def plant(drawn, rng, least, largest):
    index_at = [jax.random.randint(jax.random.fold_in(rng, axis), (), 0, length) for axis, length in enumerate(drawn.shape)]
    longest = drawn.shape.index(max(drawn.shape))
    neighbour = index_at[:longest] + [(index_at[longest] + 1) % drawn.shape[longest]] + index_at[longest + 1:]
    return drawn.at[tuple(index_at)].set(least).at[tuple(neighbour)].set(largest)


def bell_draw(stream_key, extent, spread, bound, held_as=jnp.bfloat16):
    array = spread * jax.random.normal(stream_key, extent, jnp.float32)
    return jnp.clip(array, min=-bound, max=bound).astype(held_as)


def setup_inputs(seed: int = 0) -> dict:
    key_list = jax.random.split(jax.random.key(seed), 9)
    occupancy = plant(jax.random.randint(key_list[0], (BATCH, FRAMES, HEIGHT_CELLS, COLS), 0, 2 ** HEIGHTS), jax.random.fold_in(key_list[0], 1), 0, (2 ** HEIGHTS) - 1).astype(jnp.int32)
    state_labels = plant((jax.random.randint(key_list[1], (BATCH, HEIGHT_CELLS // 16, COLS // 16), 0, 2) < 1).astype(jnp.int32), jax.random.fold_in(key_list[1], 1), 0, 1)
    lift_weight = bell_draw(key_list[2], (HEIGHTS, CH_LIFT), HEIGHTS ** -0.5, 1.75)
    temporal_weight = bell_draw(key_list[3], (3, 3, FRAMES, CH_LIFT, CH_ONE), (9 * FRAMES * CH_LIFT // 2) ** -0.5, 0.21875)
    middle_weight = bell_draw(key_list[4], (3, 3, CH_ONE, CH_TWO), (9 * CH_ONE // 2) ** -0.5, 0.375)
    deeper_weight = bell_draw(key_list[5], (3, 3, CH_TWO, CH_THREE), (9 * CH_TWO // 2) ** -0.5, 0.25)
    deepest_weight = bell_draw(key_list[6], (3, 3, CH_THREE, CH_FOUR), (9 * CH_THREE // 2) ** -0.5, 0.1875)
    head_weight = bell_draw(key_list[7], (CH_FOUR,), CH_FOUR ** -0.5, 0.25)
    return {"occupancy": occupancy, "state_labels": state_labels, "lift_weight": lift_weight, "temporal_weight": temporal_weight, "middle_weight": middle_weight, "deeper_weight": deeper_weight, "deepest_weight": deepest_weight, "head_weight": head_weight}


def tap_view(padded, row_tap, col_tap, out_rows, out_cols):
    leading = padded.shape[:-2]
    anchor = (0,) * len(leading) + (row_tap, col_tap)
    bounds = tuple(leading) + (row_tap + 2 * out_rows - 1, col_tap + 2 * out_cols - 1)
    strides = (1,) * len(leading) + (2, 2)
    return lax.slice(padded, anchor, bounds, strides)

def pad_field(feature_map):
    return jnp.pad(feature_map, ((0, 0), (1, 0), (1, 0)))

def conv_layer(feature_map, weight):
    padded = pad_field(feature_map)
    out_rows = feature_map.shape[1] // 2
    out_cols = feature_map.shape[2] // 2
    accumulated = jnp.zeros((weight.shape[3], out_rows, out_cols), jnp.float32)
    for row_tap in range(3):
        for col_tap in range(3):
            cells = tap_view(padded, row_tap, col_tap, out_rows, out_cols).astype(jnp.float32)
            accumulated = accumulated + jnp.einsum('crw,co->orw', cells, weight[row_tap, col_tap].astype(jnp.float32))
    gate = jax.nn.sigmoid(accumulated)
    slope = gate * (1.0 + accumulated * (1.0 - gate))
    return ((accumulated * gate).astype(jnp.bfloat16), slope, padded)

def weight_grad(padded, delta):
    out_rows = delta.shape[1]
    out_cols = delta.shape[2]
    rows_list = []
    for row_tap in range(3):
        cols_list = []
        for col_tap in range(3):
            cells = tap_view(padded, row_tap, col_tap, out_rows, out_cols).astype(jnp.float32)
            cols_list.append(jnp.einsum('crw,orw->co', cells, delta.astype(jnp.float32)))
        rows_list.append(jnp.stack(cols_list))
    return jnp.stack(rows_list)

def input_grad(delta, weight):
    out_rows = delta.shape[1]
    out_cols = delta.shape[2]
    accumulated = jnp.zeros((weight.shape[2], 2 * out_rows + 1, 2 * out_cols + 1), jnp.float32)
    for row_tap in range(3):
        for col_tap in range(3):
            contribution = jnp.einsum('orw,co->crw', delta.astype(jnp.float32), weight[row_tap, col_tap].astype(jnp.float32))
            zero_value = jnp.zeros((), contribution.dtype)
            accumulated = accumulated + lax.pad(contribution, zero_value, ((0, 0, 0), (row_tap, 2 - row_tap, 1), (col_tap, 2 - col_tap, 1)))
    return accumulated[:, 1:, 1:]

def sample_grads(occupancy_sample, labels, lift_weight, temporal_weight, middle_weight, deeper_weight, deepest_weight, head_weight):
    shifts = jnp.arange(HEIGHTS, dtype=jnp.int32)
    height_bits = jnp.bitwise_and(jnp.right_shift(occupancy_sample[:, None], shifts[None, :, None, None]), 1).astype(jnp.float32)
    lifted = jnp.einsum('tcrw,ck->tkrw', height_bits, lift_weight.astype(jnp.float32))
    lifted = jnp.maximum(lifted, 0.0).astype(jnp.bfloat16)
    lifted = lifted.reshape(FRAMES * CH_LIFT, lifted.shape[2], lifted.shape[3])
    first_kernel = temporal_weight.reshape(3, 3, FRAMES * CH_LIFT, CH_ONE)
    first_map, first_slope, lifted_padded = conv_layer(lifted, first_kernel)
    second_map, second_slope, first_padded = conv_layer(first_map, middle_weight)
    third_map, third_slope, second_padded = conv_layer(second_map, deeper_weight)
    fourth_map, fourth_slope, third_padded = conv_layer(third_map, deepest_weight)
    head_float = head_weight.astype(jnp.float32)
    fourth_float = fourth_map.astype(jnp.float32)
    logits = jnp.einsum('orw,o->rw', fourth_float, head_float)
    logit_grad = (jax.nn.sigmoid(logits) - labels.astype(jnp.float32)) / BATCH
    head_grad = jnp.einsum('orw,rw->o', fourth_float, logit_grad)
    fourth_delta = (logit_grad[None] * head_float[:, None, None] * fourth_slope).astype(jnp.bfloat16)
    deepest_grad = weight_grad(third_padded, fourth_delta)
    third_delta = (input_grad(fourth_delta, deepest_weight) * third_slope).astype(jnp.bfloat16)
    deeper_grad = weight_grad(second_padded, third_delta)
    second_delta = (input_grad(third_delta, deeper_weight) * second_slope).astype(jnp.bfloat16)
    middle_grad = weight_grad(first_padded, second_delta)
    first_delta = (input_grad(second_delta, middle_weight) * first_slope).astype(jnp.bfloat16)
    temporal_grad = weight_grad(lifted_padded, first_delta).reshape(3, 3, FRAMES, CH_LIFT, CH_ONE)
    return (temporal_grad, middle_grad, deeper_grad, deepest_grad, head_grad)

def reference(occupancy, state_labels, lift_weight, temporal_weight, middle_weight, deeper_weight, deepest_weight, head_weight):
    initial = (jnp.zeros(temporal_weight.shape, jnp.float32), jnp.zeros(middle_weight.shape, jnp.float32), jnp.zeros(deeper_weight.shape, jnp.float32), jnp.zeros(deepest_weight.shape, jnp.float32), jnp.zeros(head_weight.shape, jnp.float32))

    def accumulate(running, sample):
        gradients = sample_grads(sample[0], sample[1], lift_weight, temporal_weight, middle_weight, deeper_weight, deepest_weight, head_weight)
        return (jax.tree.map(lambda left, right: left + right, running, gradients), None)
    summed, _ = lax.scan(accumulate, initial, (occupancy, state_labels))
    return (summed[0], summed[1], summed[2], summed[3], summed[4])
```

```python
import functools

import jax
import jax.numpy as jnp
from jax import lax
from jax.experimental import pallas as pl
from jax.experimental.pallas import tpu as pltpu
from jax.sharding import PartitionSpec as P

BLOCK = 8
UP_ROWS = 3
DOWN_ROWS = 5
MIB = 1 << 20


def f32_dot(left, right, contract):
    return lax.dot_general(
        left, right, ((contract[0], contract[1]), ((), ())), preferred_element_type=jnp.float32
    )


def dot_nn(left, right):
    return f32_dot(left, right, ((1,), (0,)))


def dot_nt(left, right):
    return f32_dot(left, right, ((1,), (1,)))


def dot_tn(left, right):
    return f32_dot(left, right, ((0,), (0,)))


def rounded(value):
    return value.astype(jnp.bfloat16).astype(jnp.float32)


def silu_and_slope(pre):
    gate = jax.nn.sigmoid(pre)
    return rounded(pre * gate), gate * (1.0 + pre * (1.0 - gate))


def shift_block(value, step):
    shape = value.shape
    flat = value.reshape(-1, shape[-1])
    moved = pltpu.roll(flat, step % flat.shape[0], 0)
    index = lax.broadcasted_iota(jnp.int32, flat.shape, 0) % BLOCK
    edge = 0 if step > 0 else BLOCK - 1
    return jnp.where(index == edge, 0.0, moved).reshape(shape)


def fill_map(ref, value, offset):
    n, rows, phases, _, channels = value.shape
    split = value.reshape(n, rows, phases // 2, 2, BLOCK, channels)
    for row in range(rows):
        pair, parity = divmod(row + offset, 2)
        ref[:, pair, parity, pl.ds(0, phases // 2), 1] = split[:, row, :, 0]
        ref[:, pair, parity, pl.ds(1, phases // 2), 0] = split[:, row, :, 1]
        ref[:, pair, parity, 0, 0] = shift_block(split[:, row, phases // 2 - 1, 1], 1)


def map_tap(ref, row_tap, col_tap, out_rows, out_phases):
    cells = ref[
        :,
        pl.ds(row_tap // 2, out_rows),
        row_tap % 2,
        pl.ds(col_tap // 2, out_phases),
        col_tap % 2,
    ]
    return cells.reshape(-1, cells.shape[-1]).astype(jnp.bfloat16)


def fill_delta(ref, value):
    rows, phases = value.shape[1:3]
    ref[:, pl.ds(0, rows), pl.ds(0, phases)] = value
    ref[:, pl.ds(0, rows), phases] = shift_block(value[:, :, 0], -1)


def delta_parts(ref, weight_ref, row_parity, col_parity, rows, phases):
    taps = (((1, 0),), ((2, 0), (0, 1)))
    total = None
    for row_tap, row_step in taps[row_parity]:
        for col_tap, col_step in taps[col_parity]:
            cells = ref[:, pl.ds(row_step, rows), pl.ds(col_step, phases)]
            lead = cells.shape[:-1]
            flat = cells.reshape(-1, cells.shape[-1]).astype(jnp.bfloat16)
            part = dot_nt(flat, weight_ref[3 * row_tap + col_tap])
            total = part if total is None else total + part
    return total.reshape(*lead, total.shape[-1])


def early_kernel(
    up_ref,
    own_ref,
    down_ref,
    lift_ref,
    first_w_ref,
    second_w_ref,
    label_ref,
    send_ref,
    lifted_ref,
    first_ref,
    first_slope_ref,
    second_slope_ref,
    bits_ref,
):
    frames, band, cols = own_ref.shape
    phases = cols // BLOCK
    rows = UP_ROWS + band + DOWN_ROWS
    first_rows = (rows - 2) // 2
    second_rows = (first_rows - 1) // 2
    height = lax.broadcasted_iota(jnp.int32, (16, cols), 0)
    bits_ref[...] = jnp.zeros(bits_ref.shape, jnp.bfloat16)
    for row in range(rows):
        for frame in range(frames):
            if row < UP_ROWS:
                line = up_ref[frame, pl.ds(row, 1)]
            elif row < UP_ROWS + band:
                line = own_ref[frame, pl.ds(row - UP_ROWS, 1)]
            else:
                line = down_ref[frame, pl.ds(row - UP_ROWS - band, 1)]
            bit = jnp.bitwise_and(jnp.right_shift(jnp.broadcast_to(line, height.shape), height), 1)
            bits_ref[pl.ds(row * 128 + frame * 16, 16)] = bit.astype(jnp.float32).astype(
                jnp.bfloat16
            )
    place = lax.broadcasted_iota(jnp.int32, (cols, cols), 0)
    column = lax.broadcasted_iota(jnp.int32, (cols, cols), 1)
    order = jnp.where(column == (place % BLOCK) * phases + place // BLOCK, 1.0, 0.0)
    spread = dot_nt(order.astype(jnp.bfloat16), bits_ref[...]).astype(jnp.bfloat16)
    stacked = jnp.concatenate(
        [spread[:, row * 128 : row * 128 + 128] for row in range(rows)], axis=0
    )
    lifted = rounded(jnp.maximum(dot_nn(stacked, lift_ref[...]), 0.0))
    fill_map(lifted_ref, lifted.reshape(1, rows, phases, BLOCK, lifted.shape[-1]), 0)

    phases //= 2
    pre = None
    for tap in range(9):
        cells = map_tap(lifted_ref, tap // 3, tap % 3, first_rows, phases)
        part = dot_nn(cells, first_w_ref[tap])
        pre = part if pre is None else pre + part
    value, slope = silu_and_slope(pre)
    shape = (1, first_rows, phases, BLOCK, value.shape[-1])
    fill_map(first_ref, value.reshape(shape), 0)
    first_slope_ref[...] = slope.reshape(shape)[:, 1 : 1 + band // 2]

    phases //= 2
    pre = None
    for tap in range(9):
        cells = map_tap(first_ref, tap // 3, tap % 3, second_rows, phases)
        part = dot_nn(cells, second_w_ref[tap])
        pre = part if pre is None else pre + part
    value, slope = silu_and_slope(pre)
    second_slope_ref[...] = slope.reshape(1, second_rows, phases, BLOCK, slope.shape[-1])
    sent = band // 4 * phases * BLOCK
    send_ref[pl.ds(0, sent)] = value[:sent].astype(jnp.bfloat16)
    send_ref[pl.ds(sent, 16)] = label_ref[...]


def deep_kernel(
    batch,
    bands,
    got_ref,
    third_w_ref,
    fourth_w_ref,
    fourth_wt_ref,
    head_ref,
    third_delta_ref,
    third_taps_ref,
    fourth_taps_ref,
    fourth_flat_ref,
    head_grad_ref,
    second_ref,
    third_ref,
    third_slope_ref,
    fourth_delta_ref,
):
    samples = got_ref.shape[0] // bands
    channels = got_ref.shape[2]
    rows, phases = 4 * bands, 4
    cells = got_ref.shape[1] - 16
    second_ref[:, 0, 0] = jnp.zeros(second_ref.shape[:1] + second_ref.shape[3:], jnp.float32)
    second = got_ref[:, pl.ds(0, cells)].astype(jnp.float32)
    fill_map(second_ref, second.reshape(samples, rows, phases, BLOCK, channels), 1)
    labels = got_ref[:, pl.ds(cells, 16)].astype(jnp.float32)[:, :BLOCK].reshape(-1, channels)

    rows, phases = rows // 2, phases // 2
    for tap in range(9):
        third_taps_ref[:, pl.ds(tap * channels, channels)] = map_tap(
            second_ref, tap // 3, tap % 3, rows, phases
        )
    value, slope = silu_and_slope(dot_nn(third_taps_ref[...], third_w_ref[...]))
    channels = value.shape[-1]
    third_ref[:, 0, 0] = jnp.zeros(third_ref.shape[:1] + third_ref.shape[3:], jnp.float32)
    fill_map(third_ref, value.reshape(samples, rows, phases, BLOCK, channels), 1)
    third_slope_ref[...] = slope.reshape(third_slope_ref.shape)

    rows, phases = rows // 2, phases // 2
    for tap in range(9):
        fourth_taps_ref[:, pl.ds(tap * channels, channels)] = map_tap(
            third_ref, tap // 3, tap % 3, rows, phases
        )
    value, slope = silu_and_slope(dot_nn(fourth_taps_ref[...], fourth_w_ref[...]))
    head = head_ref[...]
    logits = jnp.sum(value * head, axis=1, keepdims=True)
    logit_grad = (jax.nn.sigmoid(logits) - labels[:, :1]) / batch

    @pl.when(pl.program_id(0) == 0)
    def _():
        head_grad_ref[...] = jnp.zeros(head_grad_ref.shape, jnp.float32)

    head_grad_ref[...] += jnp.sum(value * logit_grad, axis=0, keepdims=True)
    delta = rounded(logit_grad * head * slope)
    fourth_flat_ref[...] = delta.astype(jnp.bfloat16)
    fourth_delta_ref[:, rows] = jnp.zeros(
        fourth_delta_ref.shape[:1] + fourth_delta_ref.shape[2:], jnp.float32
    )
    fill_delta(fourth_delta_ref, delta.reshape(samples, rows, phases, BLOCK, delta.shape[-1]))
    for row_parity in range(2):
        for col_parity in range(2):
            part = delta_parts(
                fourth_delta_ref, fourth_wt_ref, row_parity, col_parity, rows, phases
            )
            part = rounded(part * third_slope_ref[:, :, row_parity, :, col_parity])
            for row in range(rows):
                third_delta_ref[:, 2 * row + row_parity, col_parity] = part[:, row, 0]
    third_delta_ref[:, 2 * rows] = jnp.zeros(
        third_delta_ref.shape[:1] + third_delta_ref.shape[2:], jnp.float32
    )


def late_kernel(
    place_ref,
    third_delta_ref,
    third_wt_ref,
    second_wt_ref,
    lifted_ref,
    first_ref,
    first_slope_ref,
    second_slope_ref,
    out_ref,
    third_ref,
    second_ref,
    first_delta_ref,
):
    row_from = 2 * place_ref[1]
    fill_delta(third_ref, third_delta_ref[:, pl.ds(row_from, 3)])
    band_rows, phases = 4, 2
    for row_parity in range(2):
        rows = 3 - row_parity
        for col_parity in range(2):
            part = delta_parts(third_ref, third_wt_ref, row_parity, col_parity, rows, phases)
            for row in range(rows):
                for phase in range(phases):
                    at = (slice(None), 2 * row + row_parity, 2 * phase + col_parity)
                    second_ref[at] = rounded(part[:, row, phase] * second_slope_ref[at])
    phases = 4
    second_ref[:, :, phases] = shift_block(second_ref[:, :, 0], -1)
    for row_parity in range(2):
        for col_parity in range(2):
            part = delta_parts(
                second_ref, second_wt_ref, row_parity, col_parity, band_rows, phases
            )
            for row in range(band_rows):
                for phase in range(phases):
                    at = (slice(None), 2 * row + row_parity, 2 * phase + col_parity)
                    first_delta_ref[at] = rounded(part[:, row, phase] * first_slope_ref[at])
    delta = second_ref[:, pl.ds(0, band_rows), pl.ds(0, phases)]
    delta = delta.reshape(-1, delta.shape[-1]).astype(jnp.bfloat16)
    depth = first_ref.shape[-1]
    base = 9 * lifted_ref.shape[-1] // 2
    for tap in range(9):
        cells = map_tap(first_ref, tap // 3, tap % 3, band_rows, phases)
        out_ref[pl.ds(base + tap * depth, depth)] = dot_tn(cells, delta)
    delta = first_delta_ref[...]
    delta = delta.reshape(-1, delta.shape[-1]).astype(jnp.bfloat16)
    parts = []
    for tap in range(9):
        cells = map_tap(lifted_ref, 2 + tap // 3, tap % 3, 2 * band_rows, 2 * phases)
        parts.append(dot_tn(cells, delta))
    whole = jnp.concatenate(parts, axis=0)
    out_ref[pl.ds(0, base)] = jnp.concatenate([whole[:base], whole[base:]], axis=1)


def grads_kernel(third_taps_ref, third_delta_ref, fourth_taps_ref, fourth_flat_ref, out3, out4):
    @pl.when(pl.program_id(1) == 0)
    def _():
        out3[...] = jnp.zeros(out3.shape, jnp.float32)
        out4[...] = jnp.zeros(out4.shape, jnp.float32)

    out4[...] += dot_tn(fourth_taps_ref[...], fourth_flat_ref[...])
    delta = third_delta_ref[:, pl.ds(0, third_delta_ref.shape[1] - 1)]
    delta = delta.reshape(-1, delta.shape[-1]).astype(jnp.bfloat16)
    out3[...] += dot_tn(third_taps_ref[...], delta)


def cost(flops, size):
    return pl.CostEstimate(flops=flops, bytes_accessed=size, transcendentals=0)


def step(shift):
    devices = range(lax.axis_size("space"))
    return [(i, i + shift) for i in devices if i + shift in devices]


def local(
    occupancy,
    state_labels,
    lift_weight,
    temporal_weight,
    middle_weight,
    deeper_weight,
    deepest_weight,
    head_weight,
):
    bands = lax.axis_size("space")
    samples = lax.axis_size("dp")
    _, frames, band, cols = occupancy.shape
    heights, lift_width = lift_weight.shape
    lift_all = frames * lift_width
    one, two = middle_weight.shape[2:]
    three, four = deepest_weight.shape[2:]
    f32 = jnp.float32

    own = occupancy[0]
    up = lax.ppermute(own[:, band - UP_ROWS :], "space", step(1))
    down = lax.ppermute(own[:, :DOWN_ROWS], "space", step(-1))
    label = jnp.zeros((16, two), jnp.bfloat16)
    label = label.at[:BLOCK].set(
        jnp.broadcast_to(state_labels.reshape(BLOCK, 1), (BLOCK, two)).astype(jnp.bfloat16)
    )
    lift = jnp.pad(lift_weight, ((0, 16 - heights), (0, 0)))
    lift = jnp.einsum("ab,ck->acbk", jnp.eye(frames, dtype=lift.dtype), lift)
    lift = jnp.pad(lift.reshape(frames * 16, lift_all), ((0, 128 - frames * 16), (0, 0)))
    first_w = temporal_weight.reshape(9, lift_all, one)
    second_w = middle_weight.reshape(9, one, two)
    third_w = deeper_weight.reshape(9, two, three)
    fourth_w = deepest_weight.reshape(9, three, four)
    head = head_weight.astype(f32).reshape(1, four)

    rows = UP_ROWS + band + DOWN_ROWS
    first_rows = (rows - 2) // 2
    second_rows = (first_rows - 1) // 2
    vmem = pl.BlockSpec(memory_space=pltpu.VMEM)
    sent = band // 4 * 4 * BLOCK + 16
    payload, lifted, first, first_slope, second_slope = pl.pallas_call(
        early_kernel,
        out_shape=(
            jax.ShapeDtypeStruct((sent, two), jnp.bfloat16),
            jax.ShapeDtypeStruct((1, rows // 2, 2, cols // 16 + 1, 2, BLOCK, lift_all), f32),
            jax.ShapeDtypeStruct((1, first_rows // 2 + 1, 2, cols // 32 + 1, 2, BLOCK, one), f32),
            jax.ShapeDtypeStruct((1, band // 2, cols // 16, BLOCK, one), f32),
            jax.ShapeDtypeStruct((1, second_rows, cols // 32, BLOCK, two), f32),
        ),
        in_specs=[vmem] * 7,
        out_specs=(vmem,) * 5,
        scratch_shapes=[pltpu.VMEM((rows * 128, cols), jnp.bfloat16)],
        compiler_params=pltpu.CompilerParams(vmem_limit_bytes=32 * MIB),
        cost_estimate=cost(200_000_000, 4_000_000),
        name="early",
    )(up, own, down, lift, first_w, second_w, label)

    gathered = lax.all_gather(payload, ("dp", "space"), axis=0, tiled=False)

    chunk = max(1, min(samples, 32 // bands))
    steps = samples // chunk
    third_cells = 2 * bands * 2 * BLOCK
    fourth_cells = bands * BLOCK
    full = lambda *shape: pl.BlockSpec(shape, lambda i: (0,) * len(shape))
    third_delta, third_taps, fourth_taps, fourth_flat, head_grad = pl.pallas_call(
        functools.partial(deep_kernel, samples, bands),
        grid=(steps,),
        out_shape=(
            jax.ShapeDtypeStruct((samples, 2 * bands + 1, 2, BLOCK, three), f32),
            jax.ShapeDtypeStruct((samples * third_cells, 9 * two), jnp.bfloat16),
            jax.ShapeDtypeStruct((samples * fourth_cells, 9 * three), jnp.bfloat16),
            jax.ShapeDtypeStruct((samples * fourth_cells, four), jnp.bfloat16),
            jax.ShapeDtypeStruct((1, four), f32),
        ),
        in_specs=[
            pl.BlockSpec((chunk * bands, sent, two), lambda i: (i, 0, 0)),
            full(9 * two, three),
            full(9 * three, four),
            full(9, three, four),
            full(1, four),
        ],
        out_specs=(
            pl.BlockSpec((chunk, 2 * bands + 1, 2, BLOCK, three), lambda i: (i, 0, 0, 0, 0)),
            pl.BlockSpec((chunk * third_cells, 9 * two), lambda i: (i, 0)),
            pl.BlockSpec((chunk * fourth_cells, 9 * three), lambda i: (i, 0)),
            pl.BlockSpec((chunk * fourth_cells, four), lambda i: (i, 0)),
            full(1, four),
        ),
        scratch_shapes=[
            pltpu.VMEM((chunk, 2 * bands + 1, 2, 3, 2, BLOCK, two), f32),
            pltpu.VMEM((chunk, bands + 1, 2, 2, 2, BLOCK, three), f32),
            pltpu.VMEM((chunk, bands, 2, 1, 2, BLOCK, three), f32),
            pltpu.VMEM((chunk, bands + 1, 2, BLOCK, four), f32),
        ],
        compiler_params=pltpu.CompilerParams(vmem_limit_bytes=56 * MIB),
        cost_estimate=cost(2_000_000_000, 12_000_000),
        name="deep",
    )(gathered, third_w.reshape(9 * two, three), fourth_w.reshape(9 * three, four), fourth_w, head)

    place = jnp.stack([lax.axis_index("dp"), lax.axis_index("space")]).astype(jnp.int32)
    whole = lambda *shape: pl.BlockSpec(shape, lambda i, place: (0,) * len(shape))
    half = 9 * lift_all // 2
    partial = pl.pallas_call(
        late_kernel,
        grid_spec=pltpu.PrefetchScalarGridSpec(
            num_scalar_prefetch=1,
            grid=(1,),
            in_specs=[
                pl.BlockSpec(
                    (1, 2 * bands + 1, 2, BLOCK, three), lambda i, place: (place[0], 0, 0, 0, 0)
                ),
                whole(*third_w.shape),
                whole(*second_w.shape),
                whole(*lifted.shape),
                whole(*first.shape),
                whole(*first_slope.shape),
                whole(*second_slope.shape),
            ],
            out_specs=whole(half + 9 * one, two),
            scratch_shapes=[
                pltpu.VMEM((1, 3, 3, BLOCK, three), f32),
                pltpu.VMEM((1, 5, 5, BLOCK, two), f32),
                pltpu.VMEM((1, band // 2, cols // 16, BLOCK, one), f32),
            ],
        ),
        out_shape=jax.ShapeDtypeStruct((half + 9 * one, two), f32),
        compiler_params=pltpu.CompilerParams(vmem_limit_bytes=32 * MIB),
        cost_estimate=cost(200_000_000, 6_000_000),
        name="late",
    )(place, third_delta, third_w, second_w, lifted, first, first_slope, second_slope)

    summed = lax.psum(partial, ("dp", "space"))

    deeper_grad, deepest_grad = pl.pallas_call(
        grads_kernel,
        grid=(9, steps),
        out_shape=(
            jax.ShapeDtypeStruct((9 * two, three), f32),
            jax.ShapeDtypeStruct((9 * three, four), f32),
        ),
        in_specs=[
            pl.BlockSpec((chunk * third_cells, two), lambda t, i: (i, t)),
            pl.BlockSpec((chunk, 2 * bands + 1, 2, BLOCK, three), lambda t, i: (i, 0, 0, 0, 0)),
            pl.BlockSpec((chunk * fourth_cells, three), lambda t, i: (i, t)),
            pl.BlockSpec((chunk * fourth_cells, four), lambda t, i: (i, 0)),
        ],
        out_specs=(
            pl.BlockSpec((two, three), lambda t, i: (t, 0)),
            pl.BlockSpec((three, four), lambda t, i: (t, 0)),
        ),
        compiler_params=pltpu.CompilerParams(vmem_limit_bytes=32 * MIB),
        cost_estimate=cost(1_300_000_000, 10_000_000),
        name="grads",
    )(third_taps, third_delta, fourth_taps, fourth_flat)

    temporal = jnp.concatenate([summed[:half, :one], summed[:half, one:]], axis=0)
    return (
        temporal.reshape(temporal_weight.shape),
        summed[half:].reshape(middle_weight.shape),
        deeper_grad.reshape(deeper_weight.shape),
        deepest_grad.reshape(deepest_weight.shape),
        head_grad.reshape(four),
    )


def solution(mesh):
    return jax.shard_map(
        local,
        mesh=mesh,
        in_specs=(
            P("dp", None, "space", None),
            P("dp", "space", None),
            P(),
            P(),
            P(),
            P(),
            P(),
            P(),
        ),
        out_specs=(P(), P(), P(), P(), P()),
        check_vma=False,
    )
```

```python
import functools

import jax
import jax.numpy as jnp
from jax import lax
from jax.experimental import pallas as pl
from jax.experimental.pallas import tpu as pltpu
from jax.sharding import PartitionSpec as P

BLOCK = 8
MIB = 1 << 20


def f32_dot(left, right, contract):
    return lax.dot_general(
        left, right, ((contract[0], contract[1]), ((), ())), preferred_element_type=jnp.float32
    )


def dot_nn(left, right):
    return f32_dot(left, right, ((1,), (0,)))


def dot_nt(left, right):
    return f32_dot(left, right, ((1,), (1,)))


def dot_tn(left, right):
    return f32_dot(left, right, ((0,), (0,)))


def rounded(value):
    return value.astype(jnp.bfloat16).astype(jnp.float32)


def silu_and_slope(pre):
    gate = jax.nn.sigmoid(pre)
    return rounded(pre * gate), gate * (1.0 + pre * (1.0 - gate))


def zero_row(ref):
    ref[:, 0, 0] = jnp.zeros(ref.shape[:1] + ref.shape[3:], ref.dtype)


def last_row_zero(ref):
    ref[:, ref.shape[1] - 1] = jnp.zeros(ref.shape[:1] + ref.shape[2:], ref.dtype)


def shift_block(value, step):
    shape = value.shape
    flat = value.reshape(-1, shape[-1])
    moved = pltpu.roll(flat, step % flat.shape[0], 0)
    index = lax.broadcasted_iota(jnp.int32, flat.shape, 0) % BLOCK
    edge = 0 if step > 0 else BLOCK - 1
    return jnp.where(index == edge, 0.0, moved).reshape(shape)


def fill_map(ref, value, offset):
    n, rows, phases, _, channels = value.shape
    split = value.reshape(n, rows, phases // 2, 2, BLOCK, channels)
    for row in range(rows):
        pair, parity = divmod(row + offset, 2)
        ref[:, pair, parity, pl.ds(0, phases // 2), 1] = split[:, row, :, 0]
        ref[:, pair, parity, pl.ds(1, phases // 2), 0] = split[:, row, :, 1]
        ref[:, pair, parity, 0, 0] = shift_block(split[:, row, phases // 2 - 1, 1], 1)


def map_tap(ref, row_tap, col_tap, out_rows, out_phases):
    cells = ref[
        :,
        pl.ds(row_tap // 2, out_rows),
        row_tap % 2,
        pl.ds(col_tap // 2, out_phases),
        col_tap % 2,
    ]
    return cells.reshape(-1, cells.shape[-1]).astype(jnp.bfloat16)


def fill_delta(ref, value):
    rows, phases = value.shape[1:3]
    ref[:, pl.ds(0, rows), pl.ds(0, phases)] = value
    ref[:, pl.ds(0, rows), phases] = shift_block(value[:, :, 0], -1)


def delta_parts(ref, weight_ref, row_parity, col_parity, rows, phases):
    taps = (((1, 0),), ((2, 0), (0, 1)))
    total = None
    for row_tap, row_step in taps[row_parity]:
        for col_tap, col_step in taps[col_parity]:
            cells = ref[:, pl.ds(row_step, rows), pl.ds(col_step, phases)]
            lead = cells.shape[:-1]
            flat = cells.reshape(-1, cells.shape[-1]).astype(jnp.bfloat16)
            part = dot_nt(flat, weight_ref[3 * row_tap + col_tap])
            total = part if total is None else total + part
    return total.reshape(*lead, total.shape[-1])


def early_kernel(
    frames,
    slot_ref,
    got_ref,
    lift_ref,
    first_w_ref,
    second_w_ref,
    send_ref,
    even_ref,
    odd_ref,
    first_ref,
    first_slope_ref,
    second_slope_ref,
    bits_ref,
):
    bands, lines, cols = got_ref.shape
    band = (lines - BLOCK) // frames
    phases = cols // BLOCK
    row_cells = cols // 2
    height = lax.broadcasted_iota(jnp.int32, (16, cols), 0)
    place = lax.broadcasted_iota(jnp.int32, (cols, cols), 0)
    column = lax.broadcasted_iota(jnp.int32, (cols, cols), 1)
    order = jnp.where(column == (place % BLOCK) * phases + place // BLOCK, 1.0, 0.0)
    order = order.astype(jnp.bfloat16)
    sent = (band // 4) * bands * (phases // 4) * BLOCK
    lane16 = lax.broadcasted_iota(jnp.int32, (16, send_ref.shape[1]), 1)
    bits_ref[...] = jnp.zeros(bits_ref.shape, jnp.bfloat16)
    odd_ref[pl.ds(0, row_cells)] = jnp.zeros((row_cells, odd_ref.shape[1]), jnp.bfloat16)
    for index in range(bands):
        slot = slot_ref[index]
        for row in range(band):
            for frame in range(frames):
                line = jnp.broadcast_to(got_ref[slot, pl.ds(frame * band + row, 1)], height.shape)
                bit = jnp.bitwise_and(jnp.right_shift(line, height), 1)
                bits_ref[pl.ds(row * 128 + frame * 16, 16)] = bit.astype(jnp.float32).astype(
                    jnp.bfloat16
                )
        line = jnp.broadcast_to(got_ref[slot, pl.ds(frames * band, 1)], height.shape)
        bits_ref[pl.ds(frames * 16, 16)] = line.astype(jnp.float32).astype(jnp.bfloat16)
        spread = dot_nt(order, bits_ref[...])
        label = jnp.where(lane16 == index, spread[:16, frames * 16 : frames * 16 + 1], 0.0)
        labels = label if index == 0 else labels + label
        spread = spread.astype(jnp.bfloat16)
        stacked = jnp.concatenate(
            [spread[:, row * 128 : row * 128 + 128] for row in range(band)], axis=0
        )
        lifted = jnp.maximum(dot_nn(stacked, lift_ref[...]), 0.0)
        lifted = lifted.reshape(band // 2, 2, phases // 2, 2, BLOCK, lifted.shape[-1])
        for parity, ref in ((0, even_ref), (1, odd_ref)):
            here = lifted[:, parity, :, 0]
            right = lifted[:, parity, :, 1]
            left = jnp.concatenate([shift_block(right[:, -1], 1)[:, None], right[:, :-1]], axis=1)
            taps = [part.reshape(-1, part.shape[-1]) for part in (left, here, right)]
            lane = lax.broadcasted_iota(jnp.int32, (taps[0].shape[0], 128), 1)
            tail = jnp.where(lane < 32, taps[0][:, 128:], taps[1][:, 128:])
            tail = jnp.where(lane < 64, tail, taps[2][:, 128:])
            cells = jnp.concatenate([part[:, :128] for part in taps] + [tail], axis=1)
            at = (index * (band // 2) + parity) * row_cells
            ref[pl.ds(at, cells.shape[0])] = cells.astype(jnp.bfloat16)

    send_ref[pl.ds(sent, 16)] = labels.astype(jnp.bfloat16)
    rows, phases = bands * band // 2, phases // 2
    cells = rows * row_cells
    pre = dot_nn(odd_ref[pl.ds(0, cells)], first_w_ref[0])
    pre += dot_nn(even_ref[...], first_w_ref[1])
    pre += dot_nn(odd_ref[pl.ds(row_cells, cells)], first_w_ref[2])
    value, slope = silu_and_slope(pre)
    shape = (1, rows, phases, BLOCK, value.shape[-1])
    zero_row(first_ref)
    fill_map(first_ref, value.reshape(shape), 1)
    first_slope_ref[...] = slope.reshape(shape)

    rows, phases = rows // 2, phases // 2
    pre = None
    for tap in range(9):
        cells = map_tap(first_ref, tap // 3, tap % 3, rows, phases)
        part = dot_nn(cells, second_w_ref[tap])
        pre = part if pre is None else pre + part
    value, slope = silu_and_slope(pre)
    second_slope_ref[...] = slope.reshape(second_slope_ref.shape)
    send_ref[pl.ds(0, value.shape[0])] = value.astype(jnp.bfloat16)


def deep_kernel(
    batch,
    bands,
    slot_ref,
    got_ref,
    third_w_ref,
    fourth_w_ref,
    fourth_wt_ref,
    head_ref,
    third_delta_ref,
    fourth_taps_ref,
    fourth_flat_ref,
    head_grad_ref,
    third_grad_ref,
    second_ref,
    third_taps_ref,
    third_ref,
    third_slope_ref,
    fourth_delta_ref,
):
    samples = second_ref.shape[0]
    channels = got_ref.shape[2]
    rows, phases = 4 * bands, 4
    cells = rows * phases * BLOCK
    zero_row(second_ref)
    labels = []
    for sample in range(samples):
        slot = slot_ref[pl.program_id(0) * samples + sample]
        second = got_ref[slot, pl.ds(0, cells)].astype(jnp.float32)
        fill_map(
            second_ref.at[pl.ds(sample, 1)],
            second.reshape(1, rows, phases, BLOCK, channels),
            1,
        )
        label = got_ref[slot, pl.ds(cells, 16)].astype(jnp.float32)
        labels += [label[:BLOCK, index : index + 1] for index in range(bands)]
    labels = jnp.concatenate(labels, axis=0)

    rows, phases = rows // 2, phases // 2
    for tap in range(9):
        third_taps_ref[:, pl.ds(tap * channels, channels)] = map_tap(
            second_ref, tap // 3, tap % 3, rows, phases
        )
    value, slope = silu_and_slope(dot_nn(third_taps_ref[...], third_w_ref[...]))
    channels = value.shape[-1]
    zero_row(third_ref)
    fill_map(third_ref, value.reshape(samples, rows, phases, BLOCK, channels), 1)
    third_slope_ref[...] = slope.reshape(third_slope_ref.shape)

    rows, phases = rows // 2, phases // 2
    for tap in range(9):
        fourth_taps_ref[:, pl.ds(tap * channels, channels)] = map_tap(
            third_ref, tap // 3, tap % 3, rows, phases
        )
    value, slope = silu_and_slope(dot_nn(fourth_taps_ref[...], fourth_w_ref[...]))
    head = head_ref[...]
    logits = jnp.sum(value * head, axis=1, keepdims=True)
    logit_grad = (jax.nn.sigmoid(logits) - labels) / batch

    @pl.when(pl.program_id(0) == 0)
    def _():
        head_grad_ref[...] = jnp.zeros(head_grad_ref.shape, jnp.float32)
        third_grad_ref[...] = jnp.zeros(third_grad_ref.shape, jnp.float32)

    head_grad_ref[...] += jnp.sum(value * logit_grad, axis=0, keepdims=True)
    delta = rounded(logit_grad * head * slope)
    fourth_flat_ref[...] = delta.astype(jnp.bfloat16)
    last_row_zero(fourth_delta_ref)
    fill_delta(fourth_delta_ref, delta.reshape(samples, rows, phases, BLOCK, delta.shape[-1]))
    for row_parity in range(2):
        for col_parity in range(2):
            part = delta_parts(
                fourth_delta_ref, fourth_wt_ref, row_parity, col_parity, rows, phases
            )
            part = rounded(part * third_slope_ref[:, :, row_parity, :, col_parity])
            for row in range(rows):
                third_delta_ref[:, 2 * row + row_parity, col_parity] = part[:, row, 0]
    last_row_zero(third_delta_ref)
    delta = third_delta_ref[:, pl.ds(0, 2 * rows)]
    delta = delta.reshape(-1, delta.shape[-1]).astype(jnp.bfloat16)
    third_grad_ref[...] += dot_tn(third_taps_ref[...], delta)


def late_kernel(
    place_ref,
    third_delta_ref,
    third_wt_ref,
    second_wt_ref,
    even_ref,
    odd_ref,
    first_ref,
    first_slope_ref,
    second_slope_ref,
    out_ref,
    third_ref,
    second_ref,
    first_delta_ref,
):
    rows, phases = third_delta_ref.shape[1] - 1, third_delta_ref.shape[2]
    fill_delta(third_ref, third_delta_ref[...])
    last_row_zero(second_ref)
    for row_parity in range(2):
        for col_parity in range(2):
            part = delta_parts(third_ref, third_wt_ref, row_parity, col_parity, rows, phases)
            for row in range(rows):
                for phase in range(phases):
                    at = (slice(None), 2 * row + row_parity, 2 * phase + col_parity)
                    second_ref[at] = rounded(part[:, row, phase] * second_slope_ref[at])
    rows, phases = 2 * rows, 2 * phases
    second_ref[:, :, phases] = shift_block(second_ref[:, :, 0], -1)
    for row_parity in range(2):
        for col_parity in range(2):
            part = delta_parts(second_ref, second_wt_ref, row_parity, col_parity, rows, phases)
            for row in range(rows):
                for phase in range(phases):
                    at = (slice(None), 2 * row + row_parity, 2 * phase + col_parity)
                    first_delta_ref[at] = rounded(part[:, row, phase] * first_slope_ref[at])
    delta = second_ref[:, pl.ds(0, rows), pl.ds(0, phases)]
    delta = delta.reshape(-1, delta.shape[-1]).astype(jnp.bfloat16)
    depth = first_ref.shape[-1]
    base = out_ref.shape[0] - 9 * depth
    for tap in range(9):
        cells = map_tap(first_ref, tap // 3, tap % 3, rows, phases)
        out_ref[pl.ds(base + tap * depth, depth)] = dot_tn(cells, delta)
    delta = first_delta_ref[...]
    delta = delta.reshape(-1, delta.shape[-1]).astype(jnp.bfloat16)
    cells = delta.shape[0]
    row_cells = cells // (2 * rows)
    taps = (odd_ref[pl.ds(0, cells)], even_ref[...], odd_ref[pl.ds(row_cells, cells)])
    for tap in range(3):
        part = dot_tn(delta, taps[tap])
        for piece in range(part.shape[1] // 128):
            at = (tap * (part.shape[1] // 128) + piece) * depth
            out_ref[pl.ds(at, depth)] = part[:, piece * 128 : piece * 128 + 128]


def grads_kernel(fourth_taps_ref, fourth_flat_ref, out_ref):
    @pl.when(pl.program_id(1) == 0)
    def _():
        out_ref[...] = jnp.zeros(out_ref.shape, jnp.float32)

    out_ref[...] += dot_tn(fourth_taps_ref[...], fourth_flat_ref[...])


def finish_kernel(got_ref, temporal_ref, middle_ref):
    depth = temporal_ref.shape[2]
    base = 12 * depth
    middle_ref[...] = got_ref[pl.ds(base, middle_ref.shape[0])].astype(jnp.float32)
    for tap in range(3):
        parts = [
            got_ref[pl.ds((4 * tap + piece) * depth, depth)].astype(jnp.float32).T
            for piece in range(4)
        ]
        for col_tap in range(3):
            rest = temporal_ref.shape[1] - 128
            temporal_ref[3 * tap + col_tap, pl.ds(0, 128)] = parts[col_tap]
            temporal_ref[3 * tap + col_tap, pl.ds(128, rest)] = parts[3][
                col_tap * rest : col_tap * rest + rest
            ]


def cost(flops, size):
    return pl.CostEstimate(flops=flops, bytes_accessed=size, transcendentals=0)


def doubled(value, axis, bits):
    order = [0]
    for bit in bits:
        route = [(i, i ^ bit) for i in range(lax.axis_size(axis))]
        value = jnp.concatenate([value, lax.ppermute(value, axis, route)], axis=0)
        order = order + [m ^ bit for m in order]
    return value, order


def slots(axis, order):
    place = [order.index(i) for i in range(len(order))]
    table = jnp.asarray([[place[i ^ me] for i in range(len(order))] for me in range(len(order))])
    return lax.dynamic_index_in_dim(table.astype(jnp.int32), lax.axis_index(axis), 0, False)


def bits_of(size, descending):
    bits = [1 << k for k in range(size.bit_length() - 1)]
    return bits[::-1] if descending else bits


def summed_over_dp(partial, samples):
    rows, lanes = partial.shape
    share = -(-rows // (8 * samples)) * 8
    sent = jnp.pad(partial.astype(jnp.bfloat16), ((0, share * samples - rows), (0, 0)))
    sent = sent.reshape(samples, share, lanes)
    got = lax.all_to_all(sent, "dp", 0, 0)
    total = jnp.sum(got.astype(jnp.float32), axis=0).astype(jnp.bfloat16)
    sent = jnp.broadcast_to(total[None], got.shape)
    got = lax.all_to_all(sent, "dp", 0, 0)
    return got.reshape(samples * share, lanes)


def local(
    occupancy,
    state_labels,
    lift_weight,
    temporal_weight,
    middle_weight,
    deeper_weight,
    deepest_weight,
    head_weight,
):
    bands = lax.axis_size("space")
    samples = lax.axis_size("dp")
    _, frames, band, cols = occupancy.shape
    heights, lift_width = lift_weight.shape
    lift_all = frames * lift_width
    one, two = middle_weight.shape[2:]
    three, four = deepest_weight.shape[2:]
    f32 = jnp.float32
    phases = cols // BLOCK

    zero = jnp.zeros((), jnp.int32)
    label = lax.pad(state_labels[0], zero, ((0, BLOCK - 1, 0), (0, phases - 1, phases - 1)))
    lines = jnp.concatenate([occupancy.reshape(frames * band, cols), label], axis=0)
    lines, order = doubled(lines[None], "space", bits_of(bands, False))
    band_slots = slots("space", order)
    rest = lift_all - 128
    lift = jnp.pad(lift_weight, ((0, 16 - heights), (0, 0)))
    lift = jnp.einsum("ab,ck->acbk", jnp.eye(frames, dtype=lift.dtype), lift)
    lift = lift.reshape(frames * 16, lift_all)
    lift = jnp.concatenate([lift] + [lift[:, 128:]] * 2, axis=1)
    lift = jnp.pad(lift, ((0, 128 - frames * 16), (0, 128 - 3 * rest)))
    first_w = temporal_weight.reshape(3, 3, lift_all, one)
    first_w = jnp.concatenate(
        [
            first_w[:, :, :128].reshape(3, 384, one),
            first_w[:, :, 128:].reshape(3, 3 * rest, one),
            jnp.zeros((3, 128 - 3 * rest, one), first_w.dtype),
        ],
        axis=1,
    )
    second_w = middle_weight.reshape(9, one, two)
    third_w = deeper_weight.reshape(9, two, three)
    fourth_w = deepest_weight.reshape(9, three, four)
    head = head_weight.astype(f32).reshape(1, four)

    rows = bands * band
    vmem = pl.BlockSpec(memory_space=pltpu.VMEM)
    smem = pl.BlockSpec(memory_space=pltpu.SMEM)
    sent = rows // 4 * phases // 4 * BLOCK + 16
    payload, even, odd, first, first_slope, second_slope = pl.pallas_call(
        functools.partial(early_kernel, frames),
        out_shape=(
            jax.ShapeDtypeStruct((sent, two), jnp.bfloat16),
            jax.ShapeDtypeStruct((rows // 2 * cols // 2, 512), jnp.bfloat16),
            jax.ShapeDtypeStruct(((rows // 2 + 1) * cols // 2, 512), jnp.bfloat16),
            jax.ShapeDtypeStruct((1, rows // 4 + 1, 2, phases // 4 + 1, 2, BLOCK, one), f32),
            jax.ShapeDtypeStruct((1, rows // 2, phases // 2, BLOCK, one), f32),
            jax.ShapeDtypeStruct((1, rows // 4, phases // 4, BLOCK, two), f32),
        ),
        in_specs=[smem] + [vmem] * 4,
        out_specs=(vmem,) * 6,
        scratch_shapes=[pltpu.VMEM((band * 128, cols), jnp.bfloat16)],
        compiler_params=pltpu.CompilerParams(vmem_limit_bytes=56 * MIB),
        cost_estimate=cost(200_000_000, 4_000_000),
        name="early",
    )(band_slots, lines, lift, first_w, second_w)

    gathered, order = doubled(payload[None], "dp", bits_of(samples, True))
    sample_slots = slots("dp", order)

    chunk = max(1, min(samples, 32 // bands))
    steps = samples // chunk
    third_cells = 2 * bands * 2 * BLOCK
    fourth_cells = bands * BLOCK
    full = lambda *shape: pl.BlockSpec(shape, lambda i, slot: (0,) * len(shape))
    third_delta, fourth_taps, fourth_flat, head_grad, deeper_grad = pl.pallas_call(
        functools.partial(deep_kernel, samples, bands),
        grid_spec=pltpu.PrefetchScalarGridSpec(
            num_scalar_prefetch=1,
            grid=(steps,),
            in_specs=[
                full(samples, sent, two),
                full(9 * two, three),
                full(9 * three, four),
                full(9, three, four),
                full(1, four),
            ],
            out_specs=(
                pl.BlockSpec(
                    (chunk, 2 * bands + 1, 2, BLOCK, three), lambda i, slot: (i, 0, 0, 0, 0)
                ),
                pl.BlockSpec((chunk * fourth_cells, 9 * three), lambda i, slot: (i, 0)),
                pl.BlockSpec((chunk * fourth_cells, four), lambda i, slot: (i, 0)),
                full(1, four),
                full(9 * two, three),
            ),
            scratch_shapes=[
                pltpu.VMEM((chunk, 2 * bands + 1, 2, 3, 2, BLOCK, two), f32),
                pltpu.VMEM((chunk * third_cells, 9 * two), jnp.bfloat16),
                pltpu.VMEM((chunk, bands + 1, 2, 2, 2, BLOCK, three), f32),
                pltpu.VMEM((chunk, bands, 2, 1, 2, BLOCK, three), f32),
                pltpu.VMEM((chunk, bands + 1, 2, BLOCK, four), f32),
            ],
        ),
        out_shape=(
            jax.ShapeDtypeStruct((samples, 2 * bands + 1, 2, BLOCK, three), f32),
            jax.ShapeDtypeStruct((samples * fourth_cells, 9 * three), jnp.bfloat16),
            jax.ShapeDtypeStruct((samples * fourth_cells, four), jnp.bfloat16),
            jax.ShapeDtypeStruct((1, four), f32),
            jax.ShapeDtypeStruct((9 * two, three), f32),
        ),
        compiler_params=pltpu.CompilerParams(vmem_limit_bytes=56 * MIB),
        cost_estimate=cost(2_000_000_000, 12_000_000),
        name="deep",
    )(
        sample_slots,
        gathered,
        third_w.reshape(9 * two, three),
        fourth_w.reshape(9 * three, four),
        fourth_w,
        head,
    )

    place = lax.axis_index("dp").astype(jnp.int32).reshape(1)
    whole = lambda *shape: pl.BlockSpec(shape, lambda i, place: (0,) * len(shape))
    partial = pl.pallas_call(
        late_kernel,
        grid_spec=pltpu.PrefetchScalarGridSpec(
            num_scalar_prefetch=1,
            grid=(1,),
            in_specs=[
                pl.BlockSpec(
                    (1, 2 * bands + 1, 2, BLOCK, three), lambda i, place: (place[0], 0, 0, 0, 0)
                ),
                whole(*third_w.shape),
                whole(*second_w.shape),
                whole(*even.shape),
                whole(*odd.shape),
                whole(*first.shape),
                whole(*first_slope.shape),
                whole(*second_slope.shape),
            ],
            out_specs=whole(21 * one, two),
            scratch_shapes=[
                pltpu.VMEM((1, 2 * bands + 1, 3, BLOCK, three), f32),
                pltpu.VMEM((1, 4 * bands + 1, 5, BLOCK, two), f32),
                pltpu.VMEM(first_slope.shape, f32),
            ],
        ),
        out_shape=jax.ShapeDtypeStruct((21 * one, two), f32),
        compiler_params=pltpu.CompilerParams(vmem_limit_bytes=60 * MIB),
        cost_estimate=cost(200_000_000, 6_000_000),
        name="late",
    )(place, third_delta, third_w, second_w, even, odd, first, first_slope, second_slope)

    summed = summed_over_dp(partial, samples)

    deepest_grad = pl.pallas_call(
        grads_kernel,
        grid=(9, steps),
        out_shape=jax.ShapeDtypeStruct((9 * three, four), f32),
        in_specs=[
            pl.BlockSpec((chunk * fourth_cells, three), lambda t, i: (i, t)),
            pl.BlockSpec((chunk * fourth_cells, four), lambda t, i: (i, 0)),
        ],
        out_specs=pl.BlockSpec((three, four), lambda t, i: (t, 0)),
        compiler_params=pltpu.CompilerParams(vmem_limit_bytes=32 * MIB),
        cost_estimate=cost(600_000_000, 6_000_000),
        name="grads",
    )(fourth_taps, fourth_flat)
    temporal_grad, middle_grad = pl.pallas_call(
        finish_kernel,
        out_shape=(
            jax.ShapeDtypeStruct((9, lift_all, one), f32),
            jax.ShapeDtypeStruct((9 * one, two), f32),
        ),
        in_specs=[vmem],
        out_specs=(vmem, vmem),
        cost_estimate=cost(1_000_000, 1_500_000),
        name="finish",
    )(summed)
    return (
        temporal_grad.reshape(temporal_weight.shape),
        middle_grad.reshape(middle_weight.shape),
        deeper_grad.reshape(deeper_weight.shape),
        deepest_grad.reshape(deepest_weight.shape),
        head_grad.reshape(four),
    )


def solution(mesh):
    return jax.shard_map(
        local,
        mesh=mesh,
        in_specs=(
            P("dp", None, "space", None),
            P("dp", "space", None),
            P(),
            P(),
            P(),
            P(),
            P(),
            P(),
        ),
        out_specs=(P(), P(), P(), P(), P()),
        check_vma=False,
    )
```

```python
import functools

import jax
import jax.numpy as jnp
from jax import lax
from jax.experimental import pallas as pl
from jax.experimental.pallas import tpu as pltpu
from jax.sharding import PartitionSpec as P

BLOCK = 8
MIB = 1 << 20


def f32_dot(left, right, contract):
    return lax.dot_general(
        left, right, ((contract[0], contract[1]), ((), ())), preferred_element_type=jnp.float32
    )


def dot_nn(left, right):
    return f32_dot(left, right, ((1,), (0,)))


def dot_nt(left, right):
    return f32_dot(left, right, ((1,), (1,)))


def dot_tn(left, right):
    return f32_dot(left, right, ((0,), (0,)))


def rounded(value):
    return value.astype(jnp.bfloat16).astype(jnp.float32)


def silu_and_slope(pre):
    gate = jax.nn.sigmoid(pre)
    return rounded(pre * gate), gate * (1.0 + pre * (1.0 - gate))


def zero_row(ref):
    ref[:, 0, 0] = jnp.zeros(ref.shape[:1] + ref.shape[3:], ref.dtype)


def last_row_zero(ref):
    ref[:, ref.shape[1] - 1] = jnp.zeros(ref.shape[:1] + ref.shape[2:], ref.dtype)


def shift_block(value, step):
    shape = value.shape
    flat = value.reshape(-1, shape[-1])
    moved = pltpu.roll(flat, step % flat.shape[0], 0)
    index = lax.broadcasted_iota(jnp.int32, flat.shape, 0) % BLOCK
    edge = 0 if step > 0 else BLOCK - 1
    return jnp.where(index == edge, 0.0, moved).reshape(shape)


def fill_map(ref, value, offset):
    n, rows, phases, _, channels = value.shape
    split = value.reshape(n, rows, phases // 2, 2, BLOCK, channels)
    for row in range(rows):
        pair, parity = divmod(row + offset, 2)
        ref[:, pair, parity, pl.ds(0, phases // 2), 1] = split[:, row, :, 0]
        ref[:, pair, parity, pl.ds(1, phases // 2), 0] = split[:, row, :, 1]
        ref[:, pair, parity, 0, 0] = shift_block(split[:, row, phases // 2 - 1, 1], 1)


def map_tap(ref, row_tap, col_tap, out_rows, out_phases):
    cells = ref[
        :,
        pl.ds(row_tap // 2, out_rows),
        row_tap % 2,
        pl.ds(col_tap // 2, out_phases),
        col_tap % 2,
    ]
    return cells.reshape(-1, cells.shape[-1]).astype(jnp.bfloat16)


def fill_delta(ref, value):
    rows, phases = value.shape[1:3]
    ref[:, pl.ds(0, rows), pl.ds(0, phases)] = value
    ref[:, pl.ds(0, rows), phases] = shift_block(value[:, :, 0], -1)


def delta_parts(ref, weight_ref, row_parity, col_parity, rows, phases):
    taps = (((1, 0),), ((2, 0), (0, 1)))
    total = None
    for row_tap, row_step in taps[row_parity]:
        for col_tap, col_step in taps[col_parity]:
            cells = ref[:, pl.ds(row_step, rows), pl.ds(col_step, phases)]
            lead = cells.shape[:-1]
            flat = cells.reshape(-1, cells.shape[-1]).astype(jnp.bfloat16)
            part = dot_nn(flat, weight_ref[3 * row_tap + col_tap])
            total = part if total is None else total + part
    return total.reshape(*lead, total.shape[-1])


def early_kernel(frames, pieces, *refs):
    got_refs = refs[:pieces]
    label_refs = refs[pieces : 2 * pieces]
    (
        lift_ref,
        first_w_ref,
        second_w_ref,
        send_ref,
        even_ref,
        odd_ref,
        first_ref,
        first_slope_ref,
        second_slope_ref,
        bits_ref,
        lift_all_ref,
        first_all_ref,
    ) = refs[2 * pieces :]
    me = lax.axis_index("space")
    bands = 1 << (pieces - 1)
    _, _, band, cols = got_refs[0].shape
    phases = cols // BLOCK
    row_cells = cols // 2
    heights, width = lift_ref.shape
    rest = first_w_ref.shape[1] - 128

    tall = jnp.concatenate(
        [lift_ref[...].astype(jnp.float32), jnp.zeros((16 - heights, width), jnp.float32)], axis=0
    )
    tall = jnp.concatenate([tall] * (256 // width), axis=1)
    tall = jnp.concatenate([tall] * 8, axis=0)
    frame_of_row = lax.broadcasted_iota(jnp.int32, tall.shape, 0) // 16
    lane = lax.broadcasted_iota(jnp.int32, tall.shape, 1)
    frame_of_lane = jnp.minimum(lane // width, frames - 1)
    keep = (frame_of_row == frame_of_lane) & (lane < 128 + 3 * rest)
    lift_all_ref[...] = jnp.where(keep, tall, 0.0).astype(jnp.bfloat16)
    first_all_ref[...] = jnp.zeros(first_all_ref.shape, jnp.bfloat16)
    for tap in range(9):
        row_tap, col_tap = divmod(tap, 3)
        first_all_ref[row_tap, pl.ds(col_tap * 128, 128)] = first_w_ref[tap, pl.ds(0, 128)]
        first_all_ref[row_tap, pl.ds(384 + col_tap * rest, rest)] = first_w_ref[
            tap, pl.ds(128, rest)
        ]

    height = lax.broadcasted_iota(jnp.int32, (16, cols), 0)
    place = lax.broadcasted_iota(jnp.int32, (cols, cols), 0)
    column = lax.broadcasted_iota(jnp.int32, (cols, cols), 1)
    order = jnp.where(column == (place % BLOCK) * phases + place // BLOCK, 1.0, 0.0)
    order = order.astype(jnp.bfloat16)
    sent = (band // 4) * bands * (phases // 4) * BLOCK
    label_lane = lax.broadcasted_iota(jnp.int32, (16, send_ref.shape[1]), 1)
    label_row = lax.broadcasted_iota(jnp.int32, (16, BLOCK), 0)
    label_column = lax.broadcasted_iota(jnp.int32, (16, BLOCK), 1)
    labels = jnp.zeros((16, send_ref.shape[1]), jnp.float32)
    bits_ref[...] = jnp.zeros(bits_ref.shape, jnp.bfloat16)
    odd_ref[pl.ds(0, row_cells)] = jnp.zeros((row_cells, odd_ref.shape[1]), jnp.bfloat16)
    for slot in range(bands):
        index = me ^ slot
        piece = slot.bit_length()
        inner = slot - (1 << (piece - 1)) if slot else 0
        got_ref, label_ref = got_refs[piece], label_refs[piece]
        for row in range(band):
            for frame in range(frames):
                line = jnp.broadcast_to(got_ref[inner, frame, pl.ds(row, 1)], height.shape)
                bit = jnp.bitwise_and(jnp.right_shift(line, height), 1)
                bits_ref[pl.ds(row * 128 + frame * 16, 16)] = bit.astype(jnp.float32).astype(
                    jnp.bfloat16
                )
        label = jnp.broadcast_to(label_ref[inner].astype(jnp.float32), label_row.shape)
        label = jnp.sum(
            jnp.where(label_row == label_column, label, 0.0), axis=1, keepdims=True
        )
        labels += jnp.where(label_lane == index, label, 0.0)
        spread = dot_nt(order, bits_ref[...]).astype(jnp.bfloat16)
        stacked = jnp.concatenate(
            [spread[:, row * 128 : row * 128 + 128] for row in range(band)], axis=0
        )
        lifted = jnp.maximum(dot_nn(stacked, lift_all_ref[...]), 0.0)
        lifted = lifted.reshape(band // 2, 2, phases // 2, 2, BLOCK, lifted.shape[-1])
        for parity, ref in ((0, even_ref), (1, odd_ref)):
            here = lifted[:, parity, :, 0]
            right = lifted[:, parity, :, 1]
            left = jnp.concatenate([shift_block(right[:, -1], 1)[:, None], right[:, :-1]], axis=1)
            taps = [part.reshape(-1, part.shape[-1]) for part in (left, here, right)]
            lane = lax.broadcasted_iota(jnp.int32, (taps[0].shape[0], 128), 1)
            tail = jnp.where(lane < rest, taps[0][:, 128:], taps[1][:, 128:])
            tail = jnp.where(lane < 2 * rest, tail, taps[2][:, 128:])
            cells = jnp.concatenate([part[:, :128] for part in taps] + [tail], axis=1)
            at = pl.multiple_of((index * (band // 2) + parity) * row_cells, row_cells)
            ref[pl.ds(at, cells.shape[0])] = cells.astype(jnp.bfloat16)

    send_ref[pl.ds(sent, 16)] = labels.astype(jnp.bfloat16)
    rows, phases = bands * band // 2, phases // 2
    cells = rows * row_cells
    pre = dot_nn(odd_ref[pl.ds(0, cells)], first_all_ref[0])
    pre += dot_nn(even_ref[...], first_all_ref[1])
    pre += dot_nn(odd_ref[pl.ds(row_cells, cells)], first_all_ref[2])
    value, slope = silu_and_slope(pre)
    shape = (1, rows, phases, BLOCK, value.shape[-1])
    zero_row(first_ref)
    fill_map(first_ref, value.reshape(shape), 1)
    first_slope_ref[...] = slope.reshape(shape)

    rows, phases = rows // 2, phases // 2
    pre = None
    for tap in range(9):
        cells = map_tap(first_ref, tap // 3, tap % 3, rows, phases)
        part = dot_nn(cells, second_w_ref[tap])
        pre = part if pre is None else pre + part
    value, slope = silu_and_slope(pre)
    second_slope_ref[...] = slope.reshape(second_slope_ref.shape)
    send_ref[pl.ds(0, value.shape[0])] = value.astype(jnp.bfloat16)


def transpose_kernel(second_w_ref, third_w_ref, fourth_w_ref, second_ref, third_ref, fourth_ref):
    for tap in range(9):
        second_ref[tap] = second_w_ref[tap].T
        third_ref[tap] = third_w_ref[tap].T
        fourth_ref[tap] = fourth_w_ref[tap].T


def take_samples(near_ref, far_ref, second_ref, label_ref, bands):
    half = near_ref.shape[0]
    width = half.bit_length()
    chunk, channels = second_ref.shape[0], second_ref.shape[-1]
    rows, phases = 4 * bands, 4
    cells = rows * phases * BLOCK
    me = lax.axis_index("dp")
    for slot in range(2 * half):
        reverse = sum(((slot >> k) & 1) << (width - 1 - k) for k in range(width))
        sample = me ^ reverse
        ref = near_ref if slot < half else far_ref

        def take(ref=ref, inner=slot % half, place=sample % chunk):
            second = ref[inner, pl.ds(0, cells)].astype(jnp.float32)
            fill_map(
                second_ref.at[pl.ds(place, 1)],
                second.reshape(1, rows, phases, BLOCK, channels),
                1,
            )
            if label_ref is not None:
                label = ref[inner, pl.ds(cells, 16)].astype(jnp.float32)[:BLOCK]
                for index in range(bands):
                    label_ref[place, index] = jnp.broadcast_to(
                        label[:, index : index + 1], label.shape
                    )

        if chunk == 2 * half:
            take()
        else:
            pl.when(sample // chunk == pl.program_id(0))(take)


def third_taps(second_ref, taps_ref, rows, phases):
    channels = second_ref.shape[-1]
    for tap in range(9):
        taps_ref[:, pl.ds(tap * channels, channels)] = map_tap(
            second_ref, tap // 3, tap % 3, rows, phases
        )


def deep_kernel(
    batch,
    bands,
    near_ref,
    far_ref,
    third_w_ref,
    fourth_w_ref,
    fourth_wt_ref,
    head_ref,
    third_delta_ref,
    fourth_taps_ref,
    fourth_flat_ref,
    head_grad_ref,
    second_ref,
    label_ref,
    third_taps_ref,
    third_ref,
    third_slope_ref,
    fourth_delta_ref,
):
    samples = second_ref.shape[0]
    zero_row(second_ref)
    take_samples(near_ref, far_ref, second_ref, label_ref, bands)
    labels = label_ref[...].reshape(-1, label_ref.shape[-1])[:, :1]

    rows, phases = 2 * bands, 2
    third_taps(second_ref, third_taps_ref, rows, phases)
    value, slope = silu_and_slope(dot_nn(third_taps_ref[...], third_w_ref[...]))
    channels = value.shape[-1]
    zero_row(third_ref)
    fill_map(third_ref, value.reshape(samples, rows, phases, BLOCK, channels), 1)
    third_slope_ref[...] = slope.reshape(third_slope_ref.shape)

    rows, phases = rows // 2, phases // 2
    for tap in range(9):
        fourth_taps_ref[:, pl.ds(tap * channels, channels)] = map_tap(
            third_ref, tap // 3, tap % 3, rows, phases
        )
    value, slope = silu_and_slope(dot_nn(fourth_taps_ref[...], fourth_w_ref[...]))
    head = head_ref[...].astype(jnp.float32)
    logits = jnp.sum(value * head, axis=1, keepdims=True)
    logit_grad = (jax.nn.sigmoid(logits) - labels) / batch

    @pl.when(pl.program_id(0) == 0)
    def _():
        head_grad_ref[...] = jnp.zeros(head_grad_ref.shape, jnp.float32)

    head_grad_ref[...] += jnp.sum(value * logit_grad, axis=0, keepdims=True)
    delta = rounded(logit_grad * head * slope)
    fourth_flat_ref[...] = delta.astype(jnp.bfloat16)
    last_row_zero(fourth_delta_ref)
    fill_delta(fourth_delta_ref, delta.reshape(samples, rows, phases, BLOCK, delta.shape[-1]))
    for row_parity in range(2):
        for col_parity in range(2):
            part = delta_parts(
                fourth_delta_ref, fourth_wt_ref, row_parity, col_parity, rows, phases
            )
            part = rounded(part * third_slope_ref[:, :, row_parity, :, col_parity])
            for row in range(rows):
                third_delta_ref[:, 2 * row + row_parity, col_parity] = part[:, row, 0]
    last_row_zero(third_delta_ref)


def late_kernel(
    third_delta_ref,
    third_wt_ref,
    second_wt_ref,
    even_ref,
    odd_ref,
    first_ref,
    first_slope_ref,
    second_slope_ref,
    out_ref,
    third_ref,
    second_ref,
    first_delta_ref,
):
    sample = lax.axis_index("dp")
    rows, phases = third_delta_ref.shape[1] - 1, third_delta_ref.shape[2]
    fill_delta(third_ref, third_delta_ref[pl.ds(sample, 1)])
    last_row_zero(second_ref)
    for row_parity in range(2):
        for col_parity in range(2):
            part = delta_parts(third_ref, third_wt_ref, row_parity, col_parity, rows, phases)
            for row in range(rows):
                for phase in range(phases):
                    at = (slice(None), 2 * row + row_parity, 2 * phase + col_parity)
                    second_ref[at] = rounded(part[:, row, phase] * second_slope_ref[at])
    rows, phases = 2 * rows, 2 * phases

    @pl.when(lax.axis_index("space") != 0)
    def _():
        delta = second_ref[:, pl.ds(0, rows), pl.ds(0, phases)]
        delta = delta.reshape(-1, delta.shape[-1]).astype(jnp.bfloat16)
        depth = first_ref.shape[-1]
        for tap in range(9):
            cells = map_tap(first_ref, tap // 3, tap % 3, rows, phases)
            out_ref[pl.ds(tap * depth, depth)] = dot_tn(cells, delta).astype(jnp.bfloat16)
        left = out_ref.shape[0] - 9 * depth
        out_ref[pl.ds(9 * depth, left)] = jnp.zeros((left, out_ref.shape[1]), jnp.bfloat16)

    @pl.when(lax.axis_index("space") == 0)
    def _():
        second_ref[:, :, phases] = shift_block(second_ref[:, :, 0], -1)
        for row_parity in range(2):
            for col_parity in range(2):
                part = delta_parts(
                    second_ref, second_wt_ref, row_parity, col_parity, rows, phases
                )
                for row in range(rows):
                    for phase in range(phases):
                        at = (slice(None), 2 * row + row_parity, 2 * phase + col_parity)
                        first_delta_ref[at] = rounded(part[:, row, phase] * first_slope_ref[at])
        delta = first_delta_ref[...]
        delta = delta.reshape(-1, delta.shape[-1]).astype(jnp.bfloat16)
        cells, depth = delta.shape
        row_cells = cells // (2 * rows)
        taps = (odd_ref[pl.ds(0, cells)], even_ref[...], odd_ref[pl.ds(row_cells, cells)])
        for tap in range(3):
            part = dot_tn(delta, taps[tap]).astype(jnp.bfloat16)
            for piece in range(4):
                out_ref[pl.ds((4 * tap + piece) * depth, depth)] = part[
                    :, piece * 128 : piece * 128 + 128
                ]


def third_grad_kernel(
    bands, near_ref, far_ref, delta_ref, out_ref, second_ref, third_taps_ref
):
    zero_row(second_ref)
    take_samples(near_ref, far_ref, second_ref, None, bands)
    third_taps(second_ref, third_taps_ref, 2 * bands, 2)
    delta = delta_ref[:, pl.ds(0, 2 * bands)]
    delta = delta.reshape(-1, delta.shape[-1]).astype(jnp.bfloat16)

    @pl.when(pl.program_id(0) == 0)
    def _():
        out_ref[...] = jnp.zeros(out_ref.shape, jnp.float32)

    out_ref[...] += dot_tn(third_taps_ref[...], delta)


def fourth_grad_kernel(fourth_taps_ref, fourth_flat_ref, out_ref):
    @pl.when(pl.program_id(1) == 0)
    def _():
        out_ref[...] = jnp.zeros(out_ref.shape, jnp.float32)

    out_ref[...] += dot_tn(fourth_taps_ref[...], fourth_flat_ref[...])


def sum_kernel(got_ref, out_ref):
    total = got_ref[0].astype(jnp.float32)
    for index in range(1, got_ref.shape[0]):
        total += got_ref[index].astype(jnp.float32)
    total = total.astype(jnp.bfloat16)
    for index in range(out_ref.shape[0]):
        out_ref[index] = total


def finish_kernel(got_ref, temporal_ref, middle_ref, flat_ref):
    samples, _, share, lanes = got_ref.shape
    depth = temporal_ref.shape[2]
    for sample in range(samples):
        flat_ref[pl.ds(sample * share, share)] = got_ref[sample, 0].astype(jnp.float32)
        rows = min(share, middle_ref.shape[0] - sample * share)
        if rows > 0:
            middle_ref[pl.ds(sample * share, rows)] = got_ref[sample, 1].astype(jnp.float32)[:rows]
    rest = temporal_ref.shape[1] - 128
    for tap in range(3):
        parts = [flat_ref[pl.ds((4 * tap + piece) * depth, depth)].T for piece in range(4)]
        for col_tap in range(3):
            temporal_ref[3 * tap + col_tap, pl.ds(0, 128)] = parts[col_tap]
            temporal_ref[3 * tap + col_tap, pl.ds(128, rest)] = parts[3][
                col_tap * rest : col_tap * rest + rest
            ]


def cost(flops, size):
    return pl.CostEstimate(flops=flops, bytes_accessed=size, transcendentals=0)


def swapped(value, axis, bit):
    return lax.ppermute(value, axis, [(i, i ^ bit) for i in range(lax.axis_size(axis))])


def band_pieces(value, bands):
    pieces = [value]
    bit = 1
    while bit < bands:
        whole = pieces[0] if bit == 1 else jnp.concatenate(pieces, axis=0)
        pieces.append(swapped(whole, "space", bit))
        bit *= 2
    return pieces


def gathered_halves(value, samples):
    half = samples // 2
    near = jnp.zeros((half,) + value.shape[1:], value.dtype)
    near = lax.dynamic_update_slice(near, value, (0, 0, 0))
    count = 1
    while count < half:
        part = swapped(near[:count], "dp", half // count)
        near = lax.dynamic_update_slice(near, part, (count, 0, 0))
        count *= 2
    return near, swapped(near, "dp", 1)


def local(
    occupancy,
    state_labels,
    lift_weight,
    temporal_weight,
    middle_weight,
    deeper_weight,
    deepest_weight,
    head_weight,
):
    bands = lax.axis_size("space")
    samples = lax.axis_size("dp")
    _, frames, band, cols = occupancy.shape
    lift_all = frames * lift_weight.shape[1]
    one, two = middle_weight.shape[2:]
    three, four = deepest_weight.shape[2:]
    f32, bf16 = jnp.float32, jnp.bfloat16
    shaped = jax.ShapeDtypeStruct
    phases = cols // BLOCK
    rows = bands * band
    small = samples * bands <= 32
    vmem = pl.BlockSpec(memory_space=pltpu.VMEM)

    def grant(size):
        return pltpu.CompilerParams(vmem_limit_bytes=(size if small else 60) * MIB)

    lines = band_pieces(occupancy, bands)
    labels = band_pieces(state_labels, bands)
    first_w = temporal_weight.reshape(9, lift_all, one)
    second_w = middle_weight.reshape(9, one, two)
    third_w = deeper_weight.reshape(9, two, three)
    fourth_w = deepest_weight.reshape(9, three, four)
    head = head_weight.reshape(1, four)

    sent = rows // 4 * phases // 4 * BLOCK + 16
    payload, even, odd, first, first_slope, second_slope = pl.pallas_call(
        functools.partial(early_kernel, frames, len(lines)),
        out_shape=(
            shaped((sent, two), bf16),
            shaped((rows // 2 * cols // 2, 512), bf16),
            shaped(((rows // 2 + 1) * cols // 2, 512), bf16),
            shaped((1, rows // 4 + 1, 2, phases // 4 + 1, 2, BLOCK, one), f32),
            shaped((1, rows // 2, phases // 2, BLOCK, one), f32),
            shaped((1, rows // 4, phases // 4, BLOCK, two), f32),
        ),
        in_specs=[vmem] * (2 * len(lines) + 3),
        out_specs=(vmem,) * 6,
        scratch_shapes=[
            pltpu.VMEM((band * 128, cols), bf16),
            pltpu.VMEM((128, 256), bf16),
            pltpu.VMEM((3, 512, one), bf16),
        ],
        compiler_params=grant(24),
        cost_estimate=cost(200_000_000, 4_000_000),
        name="early",
    )(*lines, *labels, lift_weight, first_w, second_w)

    near, far = gathered_halves(payload[None], samples)

    second_wt, third_wt, fourth_wt = pl.pallas_call(
        transpose_kernel,
        out_shape=(
            shaped((9, two, one), bf16),
            shaped((9, three, two), bf16),
            shaped((9, four, three), bf16),
        ),
        in_specs=[vmem] * 3,
        out_specs=(vmem,) * 3,
        compiler_params=grant(16),
        cost_estimate=cost(10_000_000, 6_000_000),
        name="transpose",
    )(second_w, third_w, fourth_w)

    chunk = max(1, min(samples, 32 // bands))
    steps = samples // chunk
    third_cells = 2 * bands * 2 * BLOCK
    fourth_cells = bands * BLOCK
    full = lambda *shape: pl.BlockSpec(shape, lambda i: (0,) * len(shape))
    delta_block = pl.BlockSpec(
        (chunk, 2 * bands + 1, 2, BLOCK, three), lambda i: (i, 0, 0, 0, 0)
    )
    second_scratch = pltpu.VMEM((chunk, 2 * bands + 1, 2, 3, 2, BLOCK, two), f32)
    third_taps_scratch = pltpu.VMEM((chunk * third_cells, 9 * two), bf16)
    third_delta, fourth_taps, fourth_flat, head_grad = pl.pallas_call(
        functools.partial(deep_kernel, samples, bands),
        grid=(steps,),
        out_shape=(
            shaped((samples, 2 * bands + 1, 2, BLOCK, three), f32),
            shaped((samples * fourth_cells, 9 * three), bf16),
            shaped((samples * fourth_cells, four), bf16),
            shaped((1, four), f32),
        ),
        in_specs=[
            full(*near.shape),
            full(*far.shape),
            full(9 * two, three),
            full(9 * three, four),
            full(9, four, three),
            full(1, four),
        ],
        out_specs=(
            delta_block,
            pl.BlockSpec((chunk * fourth_cells, 9 * three), lambda i: (i, 0)),
            pl.BlockSpec((chunk * fourth_cells, four), lambda i: (i, 0)),
            full(1, four),
        ),
        scratch_shapes=[
            second_scratch,
            pltpu.VMEM((chunk, bands, BLOCK, two), f32),
            third_taps_scratch,
            pltpu.VMEM((chunk, bands + 1, 2, 2, 2, BLOCK, three), f32),
            pltpu.VMEM((chunk, bands, 2, 1, 2, BLOCK, three), f32),
            pltpu.VMEM((chunk, bands + 1, 2, BLOCK, four), f32),
        ],
        compiler_params=grant(40),
        cost_estimate=cost(1_300_000_000, 12_000_000),
        name="deep",
    )(
        near,
        far,
        third_w.reshape(9 * two, three),
        fourth_w.reshape(9 * three, four),
        fourth_wt,
        head,
    )

    share = 12 * one // samples
    partial = pl.pallas_call(
        late_kernel,
        out_shape=shaped((12 * one, two), bf16),
        in_specs=[vmem] * 8,
        out_specs=vmem,
        scratch_shapes=[
            pltpu.VMEM((1, 2 * bands + 1, 3, BLOCK, three), f32),
            pltpu.VMEM((1, 4 * bands + 1, 5, BLOCK, two), f32),
            pltpu.VMEM(first_slope.shape, f32),
        ],
        compiler_params=grant(24),
        cost_estimate=cost(200_000_000, 6_000_000),
        name="late",
    )(third_delta, third_wt, second_wt, even, odd, first, first_slope, second_slope)

    got = lax.all_to_all(partial.reshape(samples, share, two), "dp", 0, 0)
    total = pl.pallas_call(
        sum_kernel,
        out_shape=shaped((samples * bands, share, two), bf16),
        in_specs=[vmem],
        out_specs=vmem,
        cost_estimate=cost(100_000, 600_000),
        name="sum",
    )(got)
    got = lax.all_to_all(total, ("dp", "space"), 0, 0)

    deeper_grad = pl.pallas_call(
        functools.partial(third_grad_kernel, bands),
        grid=(steps,),
        out_shape=shaped((9 * two, three), f32),
        in_specs=[full(*near.shape), full(*far.shape), delta_block],
        out_specs=full(9 * two, three),
        scratch_shapes=[second_scratch, third_taps_scratch],
        compiler_params=grant(24),
        cost_estimate=cost(600_000_000, 6_000_000),
        name="third_grad",
    )(near, far, third_delta)
    deepest_grad = pl.pallas_call(
        fourth_grad_kernel,
        grid=(9, steps),
        out_shape=shaped((9 * three, four), f32),
        in_specs=[
            pl.BlockSpec((chunk * fourth_cells, three), lambda t, i: (i, t)),
            pl.BlockSpec((chunk * fourth_cells, four), lambda t, i: (i, 0)),
        ],
        out_specs=pl.BlockSpec((three, four), lambda t, i: (t, 0)),
        compiler_params=grant(16),
        cost_estimate=cost(600_000_000, 6_000_000),
        name="fourth_grad",
    )(fourth_taps, fourth_flat)
    temporal_grad, middle_grad = pl.pallas_call(
        finish_kernel,
        out_shape=(shaped((9, lift_all, one), f32), shaped((9 * one, two), f32)),
        in_specs=[vmem],
        out_specs=(vmem, vmem),
        scratch_shapes=[pltpu.VMEM((12 * one, two), f32)],
        compiler_params=grant(16),
        cost_estimate=cost(1_000_000, 1_500_000),
        name="finish",
    )(got.reshape(samples, bands, share, two))
    return (
        temporal_grad.reshape(temporal_weight.shape),
        middle_grad.reshape(middle_weight.shape),
        deeper_grad.reshape(deeper_weight.shape),
        deepest_grad.reshape(deepest_weight.shape),
        head_grad.reshape(four),
    )


def solution(mesh):
    return jax.shard_map(
        local,
        mesh=mesh,
        in_specs=(
            P("dp", None, "space", None),
            P("dp", "space", None),
            P(),
            P(),
            P(),
            P(),
            P(),
            P(),
        ),
        out_specs=(P(), P(), P(), P(), P()),
        check_vma=False,
    )
```

```python
import functools

import jax
import jax.numpy as jnp
from jax import lax
from jax.experimental import pallas as pl
from jax.experimental.pallas import tpu as pltpu
from jax.sharding import PartitionSpec as P

BLOCK = 8
MIB = 1 << 20


def f32_dot(left, right, contract):
    return lax.dot_general(
        left, right, ((contract[0], contract[1]), ((), ())), preferred_element_type=jnp.float32
    )


def dot_nn(left, right):
    return f32_dot(left, right, ((1,), (0,)))


def dot_nt(left, right):
    return f32_dot(left, right, ((1,), (1,)))


def dot_tn(left, right):
    return f32_dot(left, right, ((0,), (0,)))


def rounded(value):
    return value.astype(jnp.bfloat16).astype(jnp.float32)


def silu_and_slope(pre):
    gate = jax.nn.sigmoid(pre)
    return rounded(pre * gate), gate * (1.0 + pre * (1.0 - gate))


def zero_row(ref):
    ref[:, 0, 0] = jnp.zeros(ref.shape[:1] + ref.shape[3:], ref.dtype)


def last_row_zero(ref):
    ref[:, ref.shape[1] - 1] = jnp.zeros(ref.shape[:1] + ref.shape[2:], ref.dtype)


def shift_block(value, step):
    shape = value.shape
    flat = value.reshape(-1, shape[-1])
    moved = pltpu.roll(flat, step % flat.shape[0], 0)
    index = lax.broadcasted_iota(jnp.int32, flat.shape, 0) % BLOCK
    edge = 0 if step > 0 else BLOCK - 1
    return jnp.where(index == edge, 0.0, moved).reshape(shape)


def fill_map(ref, value, offset):
    n, rows, phases, _, channels = value.shape
    split = value.reshape(n, rows, phases // 2, 2, BLOCK, channels)
    for row in range(rows):
        pair, parity = divmod(row + offset, 2)
        ref[:, pair, parity, pl.ds(0, phases // 2), 1] = split[:, row, :, 0]
        ref[:, pair, parity, pl.ds(1, phases // 2), 0] = split[:, row, :, 1]
        ref[:, pair, parity, 0, 0] = shift_block(split[:, row, phases // 2 - 1, 1], 1)


def map_tap(ref, row_tap, col_tap, out_rows, out_phases):
    cells = ref[
        :,
        pl.ds(row_tap // 2, out_rows),
        row_tap % 2,
        pl.ds(col_tap // 2, out_phases),
        col_tap % 2,
    ]
    return cells.reshape(-1, cells.shape[-1]).astype(jnp.bfloat16)


def fill_delta(ref, value):
    rows, phases = value.shape[1:3]
    ref[:, pl.ds(0, rows), pl.ds(0, phases)] = value
    ref[:, pl.ds(0, rows), phases] = shift_block(value[:, :, 0], -1)


def delta_parts(ref, weight_ref, row_parity, col_parity, rows, phases):
    taps = (((1, 0),), ((2, 0), (0, 1)))
    total = None
    for row_tap, row_step in taps[row_parity]:
        for col_tap, col_step in taps[col_parity]:
            cells = ref[:, pl.ds(row_step, rows), pl.ds(col_step, phases)]
            lead = cells.shape[:-1]
            flat = cells.reshape(-1, cells.shape[-1]).astype(jnp.bfloat16)
            part = dot_nn(flat, weight_ref[3 * row_tap + col_tap])
            total = part if total is None else total + part
    return total.reshape(*lead, total.shape[-1])


def column_order(cols):
    place = lax.broadcasted_iota(jnp.int32, (cols, cols), 0)
    column = lax.broadcasted_iota(jnp.int32, (cols, cols), 1)
    source = (place % BLOCK) * (cols // BLOCK) + place // BLOCK
    return jnp.where(column == source, 1.0, 0.0).astype(jnp.bfloat16)


def band_cells(got_ref, inner, index, order, lift_ref, bits_ref, even_ref, odd_ref, rest):
    _, frames, band, cols = got_ref.shape
    phases, row_cells = cols // BLOCK, cols // 2
    height = lax.broadcasted_iota(jnp.int32, (16, cols), 0)
    for row in range(band):
        for frame in range(frames):
            line = jnp.broadcast_to(got_ref[inner, frame, pl.ds(row, 1)], height.shape)
            bit = jnp.bitwise_and(jnp.right_shift(line, height), 1)
            bits_ref[pl.ds(row * 128 + frame * 16, 16)] = bit.astype(jnp.float32).astype(
                jnp.bfloat16
            )
    spread = dot_nt(order, bits_ref[...]).astype(jnp.bfloat16)
    stacked = jnp.concatenate(
        [spread[:, row * 128 : row * 128 + 128] for row in range(band)], axis=0
    )
    lifted = jnp.maximum(dot_nn(stacked, lift_ref[...]), 0.0)
    lifted = lifted.reshape(band // 2, 2, phases // 2, 2, BLOCK, lifted.shape[-1])
    for parity, ref in ((0, even_ref), (1, odd_ref)):
        here = lifted[:, parity, :, 0]
        right = lifted[:, parity, :, 1]
        left = jnp.concatenate([shift_block(right[:, -1], 1)[:, None], right[:, :-1]], axis=1)
        taps = [part.reshape(-1, part.shape[-1]) for part in (left, here, right)]
        lane = lax.broadcasted_iota(jnp.int32, (taps[0].shape[0], 128), 1)
        tail = jnp.where(lane < rest, taps[0][:, 128:], taps[1][:, 128:])
        tail = jnp.where(lane < 2 * rest, tail, taps[2][:, 128:])
        cells = jnp.concatenate([part[:, :128] for part in taps] + [tail], axis=1)
        if index is None:
            ref[...] = cells.astype(jnp.bfloat16)
        else:
            at = pl.multiple_of((index * (band // 2) + parity) * row_cells, row_cells)
            ref[pl.ds(at, cells.shape[0])] = cells.astype(jnp.bfloat16)


def band_label(label_ref, inner, index, shape):
    lane = lax.broadcasted_iota(jnp.int32, shape, 1)
    row = lax.broadcasted_iota(jnp.int32, (shape[0], BLOCK), 0)
    column = lax.broadcasted_iota(jnp.int32, (shape[0], BLOCK), 1)
    label = jnp.broadcast_to(label_ref[inner].astype(jnp.float32), row.shape)
    label = jnp.sum(jnp.where(row == column, label, 0.0), axis=1, keepdims=True)
    return jnp.where(lane == index, label, 0.0)


def own_kernel(
    got_hbm,
    label_hbm,
    lift_hbm,
    first_w_hbm,
    second_w_hbm,
    even_ref,
    odd_ref,
    labels_ref,
    lift_all_ref,
    first_all_ref,
    second_w_ref,
    got_ref,
    label_ref,
    lift_ref,
    first_w_ref,
    bits_ref,
    sems,
):
    pairs = (
        (got_hbm, got_ref),
        (lift_hbm, lift_ref),
        (label_hbm, label_ref),
        (first_w_hbm, first_w_ref),
        (second_w_hbm, second_w_ref),
    )
    copies = [
        pltpu.make_async_copy(source, target, sems.at[k])
        for k, (source, target) in enumerate(pairs)
    ]
    for copy in copies:
        copy.start()
    me = lax.axis_index("space")
    _, frames, _, cols = got_ref.shape
    heights, width = lift_ref.shape
    rest = first_w_ref.shape[1] - 128
    bits_ref[...] = jnp.zeros(bits_ref.shape, jnp.bfloat16)
    first_all_ref[...] = jnp.zeros(first_all_ref.shape, jnp.bfloat16)
    order = column_order(cols)
    copies[1].wait()
    tall = jnp.concatenate(
        [lift_ref[...].astype(jnp.float32), jnp.zeros((16 - heights, width), jnp.float32)], axis=0
    )
    tall = jnp.concatenate([tall] * (256 // width), axis=1)
    tall = jnp.concatenate([tall] * 8, axis=0)
    frame_of_row = lax.broadcasted_iota(jnp.int32, tall.shape, 0) // 16
    lane = lax.broadcasted_iota(jnp.int32, tall.shape, 1)
    frame_of_lane = jnp.minimum(lane // width, frames - 1)
    keep = (frame_of_row == frame_of_lane) & (lane < 128 + 3 * rest)
    lift_all_ref[...] = jnp.where(keep, tall, 0.0).astype(jnp.bfloat16)
    copies[0].wait()
    band_cells(got_ref, 0, None, order, lift_all_ref, bits_ref, even_ref, odd_ref, rest)
    copies[2].wait()
    labels_ref[...] = band_label(label_ref, 0, me, labels_ref.shape)
    copies[3].wait()
    for tap in range(9):
        row_tap, col_tap = divmod(tap, 3)
        first_all_ref[row_tap, pl.ds(col_tap * 128, 128)] = first_w_ref[tap, pl.ds(0, 128)]
        first_all_ref[row_tap, pl.ds(384 + col_tap * rest, rest)] = first_w_ref[
            tap, pl.ds(128, rest)
        ]
    copies[4].wait()


def early_kernel(pieces, rest, *refs):
    got_refs = refs[:pieces]
    label_refs = refs[pieces : 2 * pieces]
    (
        labels_ref,
        lift_all_ref,
        first_all_ref,
        second_w_ref,
        own_even_ref,
        own_odd_ref,
        even_ref,
        odd_ref,
        send_ref,
        first_ref,
        first_slope_ref,
        second_slope_ref,
        bits_ref,
    ) = refs[2 * pieces :]
    me = lax.axis_index("space")
    bands = 1 << pieces
    _, _, band, cols = got_refs[0].shape
    phases, row_cells = cols // BLOCK, cols // 2
    order = column_order(cols)
    labels = labels_ref[...]
    cells = own_even_ref.shape[0]
    at = pl.multiple_of(me * cells, cells)
    even_ref[pl.ds(at, cells)] = own_even_ref[...]
    odd_ref[pl.ds(pl.multiple_of(at + row_cells, row_cells), cells)] = own_odd_ref[...]
    odd_ref[pl.ds(0, row_cells)] = jnp.zeros((row_cells, odd_ref.shape[1]), jnp.bfloat16)
    bits_ref[...] = jnp.zeros(bits_ref.shape, jnp.bfloat16)
    for slot in range(1, bands):
        piece = slot.bit_length() - 1
        inner = slot - (1 << piece)
        band_cells(
            got_refs[piece],
            inner,
            me ^ slot,
            order,
            lift_all_ref,
            bits_ref,
            even_ref,
            odd_ref,
            rest,
        )
        labels += band_label(label_refs[piece], inner, me ^ slot, labels.shape)

    rows, phases = bands * band // 2, phases // 2
    cells = rows * row_cells
    pre = dot_nn(odd_ref[pl.ds(0, cells)], first_all_ref[0])
    pre += dot_nn(even_ref[...], first_all_ref[1])
    pre += dot_nn(odd_ref[pl.ds(row_cells, cells)], first_all_ref[2])
    value, slope = silu_and_slope(pre)
    shape = (1, rows, phases, BLOCK, value.shape[-1])
    zero_row(first_ref)
    fill_map(first_ref, value.reshape(shape), 1)
    first_slope_ref[...] = slope.reshape(shape)

    rows, phases = rows // 2, phases // 2
    pre = None
    for tap in range(9):
        cells = map_tap(first_ref, tap // 3, tap % 3, rows, phases)
        part = dot_nn(cells, second_w_ref[tap])
        pre = part if pre is None else pre + part
    value, slope = silu_and_slope(pre)
    second_slope_ref[...] = slope.reshape(second_slope_ref.shape)
    sent = value.shape[0]
    send_ref[pl.ds(0, sent)] = value.astype(jnp.bfloat16)
    send_ref[pl.ds(sent, 16)] = labels.astype(jnp.bfloat16)


def transpose_kernel(second_w_ref, third_w_ref, fourth_w_ref, second_ref, third_ref, fourth_ref):
    for tap in range(9):
        second_ref[tap] = second_w_ref[tap].T
        third_ref[tap] = third_w_ref[tap].T
        fourth_ref[tap] = fourth_w_ref[tap].T


def take_samples(near_ref, far_ref, second_ref, label_ref, bands):
    half = near_ref.shape[0]
    width = half.bit_length()
    chunk, channels = second_ref.shape[0], second_ref.shape[-1]
    rows, phases = 4 * bands, 4
    cells = rows * phases * BLOCK
    me = lax.axis_index("dp")
    for slot in range(2 * half):
        reverse = sum(((slot >> k) & 1) << (width - 1 - k) for k in range(width))
        sample = me ^ reverse
        ref = near_ref if slot < half else far_ref

        def take(ref=ref, inner=slot % half, place=sample % chunk):
            second = ref[inner, pl.ds(0, cells)].astype(jnp.float32)
            fill_map(
                second_ref.at[pl.ds(place, 1)],
                second.reshape(1, rows, phases, BLOCK, channels),
                1,
            )
            if label_ref is not None:
                label = ref[inner, pl.ds(cells, 16)].astype(jnp.float32)[:BLOCK]
                for index in range(bands):
                    label_ref[place, index] = jnp.broadcast_to(
                        label[:, index : index + 1], label.shape
                    )

        if chunk == 2 * half:
            take()
        else:
            pl.when(sample // chunk == pl.program_id(0))(take)


def third_taps(second_ref, taps_ref, rows, phases):
    channels = second_ref.shape[-1]
    for tap in range(9):
        taps_ref[:, pl.ds(tap * channels, channels)] = map_tap(
            second_ref, tap // 3, tap % 3, rows, phases
        )


def deep_kernel(
    batch,
    bands,
    near_ref,
    far_ref,
    third_w_ref,
    fourth_w_ref,
    fourth_wt_ref,
    head_ref,
    third_flat_ref,
    fourth_taps_ref,
    fourth_flat_ref,
    head_grad_ref,
    second_ref,
    label_ref,
    third_taps_ref,
    third_ref,
    third_slope_ref,
    third_delta_ref,
    fourth_delta_ref,
):
    samples = second_ref.shape[0]
    zero_row(second_ref)
    take_samples(near_ref, far_ref, second_ref, label_ref, bands)
    labels = label_ref[...].reshape(-1, label_ref.shape[-1])[:, :1]

    rows, phases = 2 * bands, 2
    third_taps(second_ref, third_taps_ref, rows, phases)
    value, slope = silu_and_slope(dot_nn(third_taps_ref[...], third_w_ref[...]))
    channels = value.shape[-1]
    zero_row(third_ref)
    fill_map(third_ref, value.reshape(samples, rows, phases, BLOCK, channels), 1)
    third_slope_ref[...] = slope.reshape(third_slope_ref.shape)

    rows, phases = rows // 2, phases // 2
    for tap in range(9):
        fourth_taps_ref[:, pl.ds(tap * channels, channels)] = map_tap(
            third_ref, tap // 3, tap % 3, rows, phases
        )
    value, slope = silu_and_slope(dot_nn(fourth_taps_ref[...], fourth_w_ref[...]))
    head = head_ref[...].astype(jnp.float32)
    logits = jnp.sum(value * head, axis=1, keepdims=True)
    logit_grad = (jax.nn.sigmoid(logits) - labels) / batch

    @pl.when(pl.program_id(0) == 0)
    def _():
        head_grad_ref[...] = jnp.zeros(head_grad_ref.shape, jnp.float32)

    head_grad_ref[...] += jnp.sum(value * logit_grad, axis=0, keepdims=True)
    delta = rounded(logit_grad * head * slope)
    fourth_flat_ref[...] = delta.astype(jnp.bfloat16)
    last_row_zero(fourth_delta_ref)
    fill_delta(fourth_delta_ref, delta.reshape(samples, rows, phases, BLOCK, delta.shape[-1]))
    for row_parity in range(2):
        for col_parity in range(2):
            part = delta_parts(
                fourth_delta_ref, fourth_wt_ref, row_parity, col_parity, rows, phases
            )
            part = rounded(part * third_slope_ref[:, :, row_parity, :, col_parity])
            for row in range(rows):
                third_delta_ref[:, 2 * row + row_parity, col_parity] = part[:, row, 0]
    third_flat_ref[...] = (
        third_delta_ref[...].reshape(third_flat_ref.shape).astype(jnp.bfloat16)
    )


def late_kernel(
    third_delta_ref,
    third_wt_ref,
    second_wt_ref,
    even_ref,
    odd_ref,
    first_ref,
    first_slope_ref,
    second_slope_ref,
    *refs,
):
    out_refs = refs[:4]
    third_ref, second_ref, first_delta_ref, flat_ref = refs[4:]
    sample = lax.axis_index("dp")
    _, rows, cells, channels = third_delta_ref.shape
    phases = cells // BLOCK
    delta = third_delta_ref[pl.ds(sample, 1)].astype(jnp.float32)
    fill_delta(third_ref, delta.reshape(1, rows, phases, BLOCK, channels))
    last_row_zero(third_ref)
    last_row_zero(second_ref)
    for row_parity in range(2):
        for col_parity in range(2):
            part = delta_parts(third_ref, third_wt_ref, row_parity, col_parity, rows, phases)
            for row in range(rows):
                for phase in range(phases):
                    at = (slice(None), 2 * row + row_parity, 2 * phase + col_parity)
                    second_ref[at] = rounded(part[:, row, phase] * second_slope_ref[at])
    rows, phases = 2 * rows, 2 * phases
    second_ref[:, :, phases] = shift_block(second_ref[:, :, 0], -1)
    for row_parity in range(2):
        for col_parity in range(2):
            part = delta_parts(second_ref, second_wt_ref, row_parity, col_parity, rows, phases)
            for row in range(rows):
                for phase in range(phases):
                    at = (slice(None), 2 * row + row_parity, 2 * phase + col_parity)
                    first_delta_ref[at] = rounded(part[:, row, phase] * first_slope_ref[at])
    delta = second_ref[:, pl.ds(0, rows), pl.ds(0, phases)]
    delta = delta.reshape(-1, delta.shape[-1]).astype(jnp.bfloat16)
    depth = first_ref.shape[-1]
    for tap in range(9):
        cells = map_tap(first_ref, tap // 3, tap % 3, rows, phases)
        flat_ref[pl.ds((12 + tap) * depth, depth)] = dot_tn(cells, delta)
    delta = first_delta_ref[...]
    delta = delta.reshape(-1, delta.shape[-1]).astype(jnp.bfloat16)
    cells = delta.shape[0]
    row_cells = cells // (2 * rows)
    taps = (odd_ref[pl.ds(0, cells)], even_ref[...], odd_ref[pl.ds(row_cells, cells)])
    for tap in range(3):
        part = dot_tn(delta, taps[tap])
        for piece in range(4):
            flat_ref[pl.ds((4 * tap + piece) * depth, depth)] = part[
                :, piece * 128 : piece * 128 + 128
            ]
    share = out_refs[0].shape[0]
    for slot in range(4):
        at = pl.multiple_of(((sample % 4) ^ slot) * share, share)
        out_refs[slot][...] = flat_ref[pl.ds(at, share)].astype(jnp.bfloat16)


def third_grad_kernel(
    bands, near_ref, far_ref, delta_ref, out_ref, second_ref, third_taps_ref
):
    zero_row(second_ref)
    take_samples(near_ref, far_ref, second_ref, None, bands)
    third_taps(second_ref, third_taps_ref, 2 * bands, 2)
    delta = delta_ref[...].reshape(-1, delta_ref.shape[-1])

    @pl.when(pl.program_id(0) == 0)
    def _():
        out_ref[...] = jnp.zeros(out_ref.shape, jnp.float32)

    out_ref[...] += dot_tn(third_taps_ref[...], delta)


def fourth_grad_kernel(fourth_taps_ref, fourth_flat_ref, out_ref):
    @pl.when(pl.program_id(1) == 0)
    def _():
        out_ref[...] = jnp.zeros(out_ref.shape, jnp.float32)

    out_ref[...] += dot_tn(fourth_taps_ref[...], fourth_flat_ref[...])


def finish_kernel(*refs):
    got_refs = refs[:4]
    temporal_ref, middle_ref, flat_ref = refs[4:]
    me = lax.axis_index("dp") % 4
    share = got_refs[0].shape[0]
    for slot in range(4):
        at = pl.multiple_of((me ^ slot) * share, share)
        flat_ref[pl.ds(at, share)] = got_refs[slot][...].astype(jnp.float32)
    depth = temporal_ref.shape[2]
    middle_ref[...] = flat_ref[pl.ds(12 * depth, 9 * depth)]
    rest = temporal_ref.shape[1] - 128
    for tap in range(3):
        parts = [flat_ref[pl.ds((4 * tap + piece) * depth, depth)].T for piece in range(4)]
        for col_tap in range(3):
            temporal_ref[3 * tap + col_tap, pl.ds(0, 128)] = parts[col_tap]
            temporal_ref[3 * tap + col_tap, pl.ds(128, rest)] = parts[3][
                col_tap * rest : col_tap * rest + rest
            ]


def cost(flops, size):
    return pl.CostEstimate(flops=flops, bytes_accessed=size, transcendentals=0)


def swapped(value, axis, bit):
    return lax.ppermute(value, axis, [(i, i ^ bit) for i in range(lax.axis_size(axis))])


def band_pieces(value, bands):
    pieces = [value]
    bit = 1
    while bit < bands:
        whole = pieces[0] if bit == 1 else jnp.concatenate(pieces, axis=0)
        pieces.append(swapped(whole, "space", bit))
        bit *= 2
    return pieces


def gathered_halves(value, samples):
    half = samples // 2
    quarter = half // 2
    near = jnp.zeros((half,) + value.shape[1:], value.dtype)
    near = lax.dynamic_update_slice(near, value, (0, 0, 0))
    last, count, others = value, 1, []
    while count < quarter:
        part = near[:count] if count > 1 else value
        got = swapped(part, "dp", half // count)
        others.append((swapped(last, "dp", 2), quarter + (count // 2 if count > 1 else 0)))
        near = lax.dynamic_update_slice(near, got, (count, 0, 0))
        last = got
        count *= 2
    others.append((swapped(last, "dp", 2), quarter + (count // 2 if count > 1 else 0)))
    for part, at in others:
        near = lax.dynamic_update_slice(near, part, (at, 0, 0))
    return near, swapped(near, "dp", 1)


def added(*parts):
    total = parts[0].astype(jnp.float32)
    for part in parts[1:]:
        total = total + part.astype(jnp.float32)
    return total.astype(jnp.bfloat16)


def local(
    occupancy,
    state_labels,
    lift_weight,
    temporal_weight,
    middle_weight,
    deeper_weight,
    deepest_weight,
    head_weight,
):
    bands = lax.axis_size("space")
    samples = lax.axis_size("dp")
    _, frames, band, cols = occupancy.shape
    lift_all = frames * lift_weight.shape[1]
    one, two = middle_weight.shape[2:]
    three, four = deepest_weight.shape[2:]
    f32, bf16 = jnp.float32, jnp.bfloat16
    shaped = jax.ShapeDtypeStruct
    phases = cols // BLOCK
    rows = bands * band
    small = samples * bands <= 32
    vmem = pl.BlockSpec(memory_space=pltpu.VMEM)

    def grant(size):
        return pltpu.CompilerParams(vmem_limit_bytes=(size if small else 60) * MIB)

    lines = band_pieces(occupancy, bands)
    labels = band_pieces(state_labels, bands)
    first_w = temporal_weight.reshape(9, lift_all, one)
    second_w = middle_weight.reshape(9, one, two)
    third_w = deeper_weight.reshape(9, two, three)
    fourth_w = deepest_weight.reshape(9, three, four)
    head = head_weight.reshape(1, four)

    sent = rows // 4 * phases // 4 * BLOCK + 16
    hbm = pl.BlockSpec(memory_space=pltpu.HBM)
    even_shape = shaped((rows // 2 * cols // 2, 512), bf16)
    odd_shape = shaped(((rows // 2 + 1) * cols // 2, 512), bf16)
    bits_scratch = pltpu.VMEM((band * 128, cols), bf16)
    own_cells = shaped((band // 2 * cols // 2, 512), bf16)
    own_args = [
        pltpu.with_memory_space_constraint(value, pltpu.HBM)
        for value in (occupancy, state_labels, lift_weight, first_w, second_w)
    ]
    own_even, own_odd, own_labels, lift_all_w, first_all, second_w2 = pl.pallas_call(
        own_kernel,
        out_shape=(
            own_cells,
            own_cells,
            shaped((16, two), f32),
            shaped((128, 256), bf16),
            shaped((3, 512, one), bf16),
            shaped(second_w.shape, bf16),
        ),
        in_specs=[hbm] * 5,
        out_specs=(vmem,) * 6,
        scratch_shapes=[
            pltpu.VMEM(occupancy.shape, occupancy.dtype),
            pltpu.VMEM(state_labels.shape, state_labels.dtype),
            pltpu.VMEM(lift_weight.shape, bf16),
            pltpu.VMEM(first_w.shape, bf16),
            bits_scratch,
            pltpu.SemaphoreType.DMA((5,)),
        ],
        compiler_params=grant(16),
        cost_estimate=cost(100_000_000, 4_000_000),
        name="own_band",
    )(*own_args)
    pieces = len(lines) - 1
    even, odd, payload, first, first_slope, second_slope = pl.pallas_call(
        functools.partial(early_kernel, pieces, lift_all - 128),
        out_shape=(
            even_shape,
            odd_shape,
            shaped((sent, two), bf16),
            shaped((1, rows // 4 + 1, 2, phases // 4 + 1, 2, BLOCK, one), f32),
            shaped((1, rows // 2, phases // 2, BLOCK, one), f32),
            shaped((1, rows // 4, phases // 4, BLOCK, two), f32),
        ),
        in_specs=[vmem] * (2 * pieces + 6),
        out_specs=(vmem,) * 6,
        scratch_shapes=[bits_scratch],
        compiler_params=grant(24),
        cost_estimate=cost(150_000_000, 4_000_000),
        name="early",
    )(*lines[1:], *labels[1:], own_labels, lift_all_w, first_all, second_w2, own_even, own_odd)

    near, far = gathered_halves(payload[None], samples)

    second_wt, third_wt, fourth_wt = pl.pallas_call(
        transpose_kernel,
        out_shape=(
            shaped((9, two, one), bf16),
            shaped((9, three, two), bf16),
            shaped((9, four, three), bf16),
        ),
        in_specs=[vmem] * 3,
        out_specs=(vmem,) * 3,
        compiler_params=grant(16),
        cost_estimate=cost(10_000_000, 6_000_000),
        name="transpose",
    )(second_w, third_w, fourth_w)

    chunk = max(1, min(samples, 32 // bands))
    steps = samples // chunk
    third_cells = 2 * bands * 2 * BLOCK
    fourth_cells = bands * BLOCK
    full = lambda *shape: pl.BlockSpec(shape, lambda i: (0,) * len(shape))
    delta_block = pl.BlockSpec(
        (chunk, 2 * bands, 2 * BLOCK, three), lambda i: (i, 0, 0, 0)
    )
    second_scratch = pltpu.VMEM((chunk, 2 * bands + 1, 2, 3, 2, BLOCK, two), f32)
    third_taps_scratch = pltpu.VMEM((chunk * third_cells, 9 * two), bf16)
    third_delta, fourth_taps, fourth_flat, head_grad = pl.pallas_call(
        functools.partial(deep_kernel, samples, bands),
        grid=(steps,),
        out_shape=(
            shaped((samples, 2 * bands, 2 * BLOCK, three), bf16),
            shaped((samples * fourth_cells, 9 * three), bf16),
            shaped((samples * fourth_cells, four), bf16),
            shaped((1, four), f32),
        ),
        in_specs=[
            full(*near.shape),
            full(*far.shape),
            full(9 * two, three),
            full(9 * three, four),
            full(9, four, three),
            full(1, four),
        ],
        out_specs=(
            delta_block,
            pl.BlockSpec((chunk * fourth_cells, 9 * three), lambda i: (i, 0)),
            pl.BlockSpec((chunk * fourth_cells, four), lambda i: (i, 0)),
            full(1, four),
        ),
        scratch_shapes=[
            second_scratch,
            pltpu.VMEM((chunk, bands, BLOCK, two), f32),
            third_taps_scratch,
            pltpu.VMEM((chunk, bands + 1, 2, 2, 2, BLOCK, three), f32),
            pltpu.VMEM((chunk, bands, 2, 1, 2, BLOCK, three), f32),
            pltpu.VMEM((chunk, 2 * bands, 2, BLOCK, three), f32),
            pltpu.VMEM((chunk, bands + 1, 2, BLOCK, four), f32),
        ],
        compiler_params=grant(40),
        cost_estimate=cost(1_300_000_000, 12_000_000),
        name="deep",
    )(
        near,
        far,
        third_w.reshape(9 * two, three),
        fourth_w.reshape(9 * three, four),
        fourth_wt,
        head,
    )

    share = 21 * one // 4
    quarters = pl.pallas_call(
        late_kernel,
        out_shape=(shaped((share, two), bf16),) * 4,
        in_specs=[vmem] * 8,
        out_specs=(vmem,) * 4,
        scratch_shapes=[
            pltpu.VMEM((1, 2 * bands + 1, 3, BLOCK, three), f32),
            pltpu.VMEM((1, 4 * bands + 1, 5, BLOCK, two), f32),
            pltpu.VMEM(first_slope.shape, f32),
            pltpu.VMEM((21 * one, two), f32),
        ],
        compiler_params=grant(24),
        cost_estimate=cost(200_000_000, 6_000_000),
        name="late",
    )(third_delta, third_wt, second_wt, even, odd, first, first_slope, second_slope)

    mine, near3, far3, delta3 = lax.optimization_barrier((quarters[0], near, far, third_delta))
    got = [swapped(quarters[slot], "dp", slot) for slot in (1, 2, 3)]
    deeper_grad = pl.pallas_call(
        functools.partial(third_grad_kernel, bands),
        grid=(steps,),
        out_shape=shaped((9 * two, three), f32),
        in_specs=[full(*near.shape), full(*far.shape), delta_block],
        out_specs=full(9 * two, three),
        scratch_shapes=[second_scratch, third_taps_scratch],
        compiler_params=grant(24),
        cost_estimate=cost(600_000_000, 6_000_000),
        name="third_grad",
    )(near3, far3, delta3)
    got[2], deeper_grad = lax.optimization_barrier((got[2], deeper_grad))
    total = added(mine, *got)
    bit = 4
    while 2 * bit < samples:
        total = added(total, swapped(total, "dp", bit))
        bit *= 2
    total, fourth_taps, fourth_flat = lax.optimization_barrier((total, fourth_taps, fourth_flat))
    other = swapped(total, "dp", bit) if bit < samples else jnp.zeros_like(total)
    deepest_grad = pl.pallas_call(
        fourth_grad_kernel,
        grid=(3, steps),
        out_shape=shaped((9 * three, four), f32),
        in_specs=[
            pl.BlockSpec((chunk * fourth_cells, 3 * three), lambda t, i: (i, t)),
            pl.BlockSpec((chunk * fourth_cells, four), lambda t, i: (i, 0)),
        ],
        out_specs=pl.BlockSpec((3 * three, four), lambda t, i: (t, 0)),
        compiler_params=grant(16),
        cost_estimate=cost(600_000_000, 6_000_000),
        name="fourth_grad",
    )(fourth_taps, fourth_flat)
    other, deepest_grad = lax.optimization_barrier((other, deepest_grad))
    total = added(total, other)
    beside = swapped(total, "dp", 2)
    core = swapped(total, "dp", 1)
    across = swapped(beside, "dp", 1)
    temporal_grad, middle_grad = pl.pallas_call(
        finish_kernel,
        out_shape=(shaped((9, lift_all, one), f32), shaped((9 * one, two), f32)),
        in_specs=[vmem] * 4,
        out_specs=(vmem, vmem),
        scratch_shapes=[pltpu.VMEM((21 * one, two), f32)],
        compiler_params=grant(16),
        cost_estimate=cost(1_000_000, 1_500_000),
        name="finish",
    )(total, core, beside, across)
    return (
        temporal_grad.reshape(temporal_weight.shape),
        middle_grad.reshape(middle_weight.shape),
        deeper_grad.reshape(deeper_weight.shape),
        deepest_grad.reshape(deepest_weight.shape),
        head_grad.reshape(four),
    )


def solution(mesh):
    return jax.shard_map(
        local,
        mesh=mesh,
        in_specs=(
            P("dp", None, "space", None),
            P("dp", "space", None),
            P(),
            P(),
            P(),
            P(),
            P(),
            P(),
        ),
        out_specs=(P(), P(), P(), P(), P()),
        check_vma=False,
    )
```

```python
import functools

import jax
import jax.numpy as jnp
from jax import lax
from jax.experimental import pallas as pl
from jax.experimental.pallas import tpu as pltpu
from jax.sharding import PartitionSpec as P

BLOCK = 8
MIB = 1 << 20


def f32_dot(left, right, contract):
    return lax.dot_general(
        left, right, ((contract[0], contract[1]), ((), ())), preferred_element_type=jnp.float32
    )


def dot_nn(left, right):
    return f32_dot(left, right, ((1,), (0,)))


def dot_nt(left, right):
    return f32_dot(left, right, ((1,), (1,)))


def dot_tn(left, right):
    return f32_dot(left, right, ((0,), (0,)))


def rounded(value):
    return value.astype(jnp.bfloat16).astype(jnp.float32)


def silu_and_slope(pre):
    gate = jax.nn.sigmoid(pre)
    return rounded(pre * gate), gate * (1.0 + pre * (1.0 - gate))


def zero_row(ref):
    ref[:, 0, 0] = jnp.zeros(ref.shape[:1] + ref.shape[3:], ref.dtype)


def last_row_zero(ref):
    ref[:, ref.shape[1] - 1] = jnp.zeros(ref.shape[:1] + ref.shape[2:], ref.dtype)


def shift_block(value, step):
    shape = value.shape
    flat = value.reshape(-1, shape[-1])
    moved = pltpu.roll(flat, step % flat.shape[0], 0)
    index = lax.broadcasted_iota(jnp.int32, flat.shape, 0) % BLOCK
    edge = 0 if step > 0 else BLOCK - 1
    return jnp.where(index == edge, 0.0, moved).reshape(shape)


def fill_map(ref, value, offset):
    n, rows, phases, _, channels = value.shape
    split = value.reshape(n, rows, phases // 2, 2, BLOCK, channels)
    for row in range(rows):
        pair, parity = divmod(row + offset, 2)
        ref[:, pair, parity, pl.ds(0, phases // 2), 1] = split[:, row, :, 0]
        ref[:, pair, parity, pl.ds(1, phases // 2), 0] = split[:, row, :, 1]
        ref[:, pair, parity, 0, 0] = shift_block(split[:, row, phases // 2 - 1, 1], 1)


def map_tap(ref, row_tap, col_tap, out_rows, out_phases):
    cells = ref[
        :,
        pl.ds(row_tap // 2, out_rows),
        row_tap % 2,
        pl.ds(col_tap // 2, out_phases),
        col_tap % 2,
    ]
    return cells.reshape(-1, cells.shape[-1]).astype(jnp.bfloat16)


def fill_delta(ref, value):
    rows, phases = value.shape[1:3]
    ref[:, pl.ds(0, rows), pl.ds(0, phases)] = value
    ref[:, pl.ds(0, rows), phases] = shift_block(value[:, :, 0], -1)


def delta_parts(ref, weight_ref, row_parity, col_parity, rows, phases):
    taps = (((1, 0),), ((2, 0), (0, 1)))
    total = None
    for row_tap, row_step in taps[row_parity]:
        for col_tap, col_step in taps[col_parity]:
            cells = ref[:, pl.ds(row_step, rows), pl.ds(col_step, phases)]
            lead = cells.shape[:-1]
            flat = cells.reshape(-1, cells.shape[-1]).astype(jnp.bfloat16)
            part = dot_nn(flat, weight_ref[3 * row_tap + col_tap])
            total = part if total is None else total + part
    return total.reshape(*lead, total.shape[-1])


def column_order(cols):
    place = lax.broadcasted_iota(jnp.int32, (cols, cols), 0)
    column = lax.broadcasted_iota(jnp.int32, (cols, cols), 1)
    source = (place % BLOCK) * (cols // BLOCK) + place // BLOCK
    return jnp.where(column == source, 1.0, 0.0).astype(jnp.bfloat16)


def band_cells(got_ref, inner, index, order, lift_ref, bits_ref, even_ref, odd_ref, rest):
    _, frames, band, cols = got_ref.shape
    phases, row_cells = cols // BLOCK, cols // 2
    height = lax.broadcasted_iota(jnp.int32, (16, cols), 0)
    for row in range(band):
        for frame in range(frames):
            line = jnp.broadcast_to(got_ref[inner, frame, pl.ds(row, 1)], height.shape)
            bit = jnp.bitwise_and(jnp.right_shift(line, height), 1)
            bits_ref[pl.ds(row * 128 + frame * 16, 16)] = bit.astype(jnp.float32).astype(
                jnp.bfloat16
            )
    spread = dot_nt(order, bits_ref[...]).astype(jnp.bfloat16)
    stacked = jnp.concatenate(
        [spread[:, row * 128 : row * 128 + 128] for row in range(band)], axis=0
    )
    lifted = jnp.maximum(dot_nn(stacked, lift_ref[...]), 0.0)
    lifted = lifted.reshape(band // 2, 2, phases // 2, 2, BLOCK, lifted.shape[-1])
    for parity, ref in ((0, even_ref), (1, odd_ref)):
        here = lifted[:, parity, :, 0]
        right = lifted[:, parity, :, 1]
        left = jnp.concatenate([shift_block(right[:, -1], 1)[:, None], right[:, :-1]], axis=1)
        taps = [part.reshape(-1, part.shape[-1]) for part in (left, here, right)]
        lane = lax.broadcasted_iota(jnp.int32, (taps[0].shape[0], 128), 1)
        tail = jnp.where(lane < rest, taps[0][:, 128:], taps[1][:, 128:])
        tail = jnp.where(lane < 2 * rest, tail, taps[2][:, 128:])
        cells = jnp.concatenate([part[:, :128] for part in taps] + [tail], axis=1)
        if index is None:
            ref[...] = cells.astype(jnp.bfloat16)
        else:
            at = pl.multiple_of((index * (band // 2) + parity) * row_cells, row_cells)
            ref[pl.ds(at, cells.shape[0])] = cells.astype(jnp.bfloat16)


def band_label(label_ref, inner, index, shape):
    lane = lax.broadcasted_iota(jnp.int32, shape, 1)
    row = lax.broadcasted_iota(jnp.int32, (shape[0], BLOCK), 0)
    column = lax.broadcasted_iota(jnp.int32, (shape[0], BLOCK), 1)
    label = jnp.broadcast_to(label_ref[inner].astype(jnp.float32), row.shape)
    label = jnp.sum(jnp.where(row == column, label, 0.0), axis=1, keepdims=True)
    return jnp.where(lane == index, label, 0.0)


def own_kernel(
    got_hbm,
    label_hbm,
    lift_hbm,
    first_w_hbm,
    second_w_hbm,
    third_w_hbm,
    fourth_w_hbm,
    even_ref,
    odd_ref,
    labels_ref,
    lift_all_ref,
    first_all_ref,
    second_w_ref,
    third_w_ref,
    fourth_w_ref,
    second_wt_ref,
    third_wt_ref,
    fourth_wt_ref,
    label_ref,
    got_ref,
    lift_ref,
    first_w_ref,
    bits_ref,
    sems,
):
    pairs = (
        (got_hbm, got_ref),
        (lift_hbm, lift_ref),
        (label_hbm, label_ref),
        (first_w_hbm, first_w_ref),
        (second_w_hbm, second_w_ref),
        (third_w_hbm, third_w_ref),
        (fourth_w_hbm, fourth_w_ref),
    )
    copies = [
        pltpu.make_async_copy(source, target, sems.at[k])
        for k, (source, target) in enumerate(pairs)
    ]
    for copy in copies:
        copy.start()
    me = lax.axis_index("space")
    _, frames, _, cols = got_ref.shape
    heights, width = lift_ref.shape
    rest = first_w_ref.shape[1] - 128
    bits_ref[...] = jnp.zeros(bits_ref.shape, jnp.bfloat16)
    first_all_ref[...] = jnp.zeros(first_all_ref.shape, jnp.bfloat16)
    order = column_order(cols)
    copies[1].wait()
    tall = jnp.concatenate(
        [lift_ref[...].astype(jnp.float32), jnp.zeros((16 - heights, width), jnp.float32)], axis=0
    )
    tall = jnp.concatenate([tall] * (256 // width), axis=1)
    tall = jnp.concatenate([tall] * 8, axis=0)
    frame_of_row = lax.broadcasted_iota(jnp.int32, tall.shape, 0) // 16
    lane = lax.broadcasted_iota(jnp.int32, tall.shape, 1)
    frame_of_lane = jnp.minimum(lane // width, frames - 1)
    keep = (frame_of_row == frame_of_lane) & (lane < 128 + 3 * rest)
    lift_all_ref[...] = jnp.where(keep, tall, 0.0).astype(jnp.bfloat16)
    copies[0].wait()
    band_cells(got_ref, 0, None, order, lift_all_ref, bits_ref, even_ref, odd_ref, rest)
    copies[2].wait()
    labels_ref[...] = band_label(label_ref, 0, me, labels_ref.shape)
    copies[3].wait()
    for tap in range(9):
        row_tap, col_tap = divmod(tap, 3)
        first_all_ref[row_tap, pl.ds(col_tap * 128, 128)] = first_w_ref[tap, pl.ds(0, 128)]
        first_all_ref[row_tap, pl.ds(384 + col_tap * rest, rest)] = first_w_ref[
            tap, pl.ds(128, rest)
        ]
    pairs = ((second_w_ref, second_wt_ref), (third_w_ref, third_wt_ref))
    pairs += ((fourth_w_ref, fourth_wt_ref),)
    for k, (source, target) in enumerate(pairs):
        copies[4 + k].wait()
        for tap in range(9):
            target[tap] = source[tap].T


def early_kernel(pieces, rest, *refs):
    got_refs = refs[:pieces]
    label_refs = refs[pieces : 2 * pieces]
    (
        labels_ref,
        lift_all_ref,
        first_all_ref,
        second_w_ref,
        own_even_ref,
        own_odd_ref,
        even_ref,
        odd_ref,
        send_ref,
        first_ref,
        first_slope_ref,
        second_slope_ref,
        bits_ref,
    ) = refs[2 * pieces :]
    me = lax.axis_index("space")
    bands = 1 << pieces
    _, _, band, cols = got_refs[0].shape
    phases, row_cells = cols // BLOCK, cols // 2
    order = column_order(cols)
    labels = labels_ref[...]
    cells = own_even_ref.shape[0]
    at = pl.multiple_of(me * cells, cells)
    even_ref[pl.ds(at, cells)] = own_even_ref[...]
    odd_ref[pl.ds(pl.multiple_of(at + row_cells, row_cells), cells)] = own_odd_ref[...]
    odd_ref[pl.ds(0, row_cells)] = jnp.zeros((row_cells, odd_ref.shape[1]), jnp.bfloat16)
    bits_ref[...] = jnp.zeros(bits_ref.shape, jnp.bfloat16)
    for slot in range(1, bands):
        piece = slot.bit_length() - 1
        inner = slot - (1 << piece)
        band_cells(
            got_refs[piece],
            inner,
            me ^ slot,
            order,
            lift_all_ref,
            bits_ref,
            even_ref,
            odd_ref,
            rest,
        )
        labels += band_label(label_refs[piece], inner, me ^ slot, labels.shape)

    rows, phases = bands * band // 2, phases // 2
    cells = rows * row_cells
    pre = dot_nn(odd_ref[pl.ds(0, cells)], first_all_ref[0])
    pre += dot_nn(even_ref[...], first_all_ref[1])
    pre += dot_nn(odd_ref[pl.ds(row_cells, cells)], first_all_ref[2])
    value, slope = silu_and_slope(pre)
    shape = (1, rows, phases, BLOCK, value.shape[-1])
    zero_row(first_ref)
    fill_map(first_ref, value.reshape(shape), 1)
    first_slope_ref[...] = slope.reshape(shape)

    rows, phases = rows // 2, phases // 2
    pre = None
    for tap in range(9):
        cells = map_tap(first_ref, tap // 3, tap % 3, rows, phases)
        part = dot_nn(cells, second_w_ref[tap])
        pre = part if pre is None else pre + part
    value, slope = silu_and_slope(pre)
    second_slope_ref[...] = slope.reshape(second_slope_ref.shape)
    sent = value.shape[0]
    send_ref[pl.ds(0, sent)] = value.astype(jnp.bfloat16)
    send_ref[pl.ds(sent, 16)] = labels.astype(jnp.bfloat16)


def take_samples(near_ref, far_ref, second_ref, label_ref, bands):
    half = near_ref.shape[0]
    width = half.bit_length()
    chunk = second_ref.shape[0]
    me = lax.axis_index("dp")
    for slot in range(2 * half):
        reverse = sum(((slot >> k) & 1) << (width - 1 - k) for k in range(width))
        sample = me ^ reverse
        ref = near_ref if slot < half else far_ref

        def take(ref=ref, inner=slot % half, place=sample % chunk):
            put_sample(ref, inner, second_ref, label_ref, place, bands)

        if chunk == 2 * half:
            take()
        else:
            pl.when(sample // chunk == pl.program_id(0))(take)


def third_taps(second_ref, taps_ref, rows, phases):
    channels = second_ref.shape[-1]
    for tap in range(9):
        taps_ref[:, pl.ds(tap * channels, channels)] = map_tap(
            second_ref, tap // 3, tap % 3, rows, phases
        )


def put_sample(ref, inner, second_ref, label_ref, place, bands):
    rows, phases = 4 * bands, 4
    cells = rows * phases * BLOCK
    second = ref[inner, pl.ds(0, cells)].astype(jnp.float32)
    fill_map(
        second_ref.at[pl.ds(place, 1)],
        second.reshape(1, rows, phases, BLOCK, second.shape[-1]),
        1,
    )
    if label_ref is not None:
        label = ref[inner, pl.ds(cells, 16)].astype(jnp.float32)[:BLOCK]
        for index in range(bands):
            label_ref[place, index] = jnp.broadcast_to(label[:, index : index + 1], label.shape)


def deep_layers(
    batch,
    bands,
    third_w_ref,
    fourth_w_ref,
    fourth_wt_ref,
    head_ref,
    fourth_taps_ref,
    second_ref,
    label_ref,
    third_taps_ref,
    third_ref,
    third_slope_ref,
    third_delta_ref,
    fourth_delta_ref,
):
    samples = second_ref.shape[0]
    rows, phases = 2 * bands, 2
    third_taps(second_ref, third_taps_ref, rows, phases)
    value, slope = silu_and_slope(dot_nn(third_taps_ref[...], third_w_ref[...]))
    channels = value.shape[-1]
    zero_row(third_ref)
    fill_map(third_ref, value.reshape(samples, rows, phases, BLOCK, channels), 1)
    third_slope_ref[...] = slope.reshape(third_slope_ref.shape)

    rows, phases = rows // 2, phases // 2
    for tap in range(9):
        fourth_taps_ref[:, pl.ds(tap * channels, channels)] = map_tap(
            third_ref, tap // 3, tap % 3, rows, phases
        )
    value, slope = silu_and_slope(dot_nn(fourth_taps_ref[...], fourth_w_ref[...]))
    head = head_ref[...].astype(jnp.float32)
    labels = label_ref[...].reshape(-1, label_ref.shape[-1])[:, :1]
    logits = jnp.sum(value * head, axis=1, keepdims=True)
    logit_grad = (jax.nn.sigmoid(logits) - labels) / batch
    delta = rounded(logit_grad * head * slope)
    last_row_zero(fourth_delta_ref)
    fill_delta(fourth_delta_ref, delta.reshape(samples, rows, phases, BLOCK, delta.shape[-1]))
    for row_parity in range(2):
        for col_parity in range(2):
            part = delta_parts(
                fourth_delta_ref, fourth_wt_ref, row_parity, col_parity, rows, phases
            )
            part = rounded(part * third_slope_ref[:, :, row_parity, :, col_parity])
            for row in range(rows):
                third_delta_ref[:, 2 * row + row_parity, col_parity] = part[:, row, 0]
    return value, logit_grad, delta


def deep_kernel(
    batch,
    bands,
    near_ref,
    far_ref,
    third_w_ref,
    fourth_w_ref,
    fourth_wt_ref,
    head_ref,
    fourth_taps_ref,
    fourth_flat_ref,
    head_grad_ref,
    third_grad_ref,
    second_ref,
    label_ref,
    third_taps_ref,
    third_ref,
    third_slope_ref,
    third_delta_ref,
    fourth_delta_ref,
):
    zero_row(second_ref)
    take_samples(near_ref, far_ref, second_ref, label_ref, bands)
    value, logit_grad, delta = deep_layers(
        batch,
        bands,
        third_w_ref,
        fourth_w_ref,
        fourth_wt_ref,
        head_ref,
        fourth_taps_ref,
        second_ref,
        label_ref,
        third_taps_ref,
        third_ref,
        third_slope_ref,
        third_delta_ref,
        fourth_delta_ref,
    )

    @pl.when(pl.program_id(0) == 0)
    def _():
        head_grad_ref[...] = jnp.zeros(head_grad_ref.shape, jnp.float32)
        third_grad_ref[...] = jnp.zeros(third_grad_ref.shape, jnp.float32)

    head_grad_ref[...] += jnp.sum(value * logit_grad, axis=0, keepdims=True)
    fourth_flat_ref[...] = delta.astype(jnp.bfloat16)
    delta = third_delta_ref[...]
    delta = delta.reshape(-1, delta.shape[-1]).astype(jnp.bfloat16)
    third_grad_ref[...] += dot_tn(third_taps_ref[...], delta)


def local_kernel(
    batch,
    bands,
    payload_ref,
    third_w_ref,
    fourth_w_ref,
    fourth_wt_ref,
    head_ref,
    third_wt_ref,
    second_wt_ref,
    even_ref,
    odd_ref,
    first_ref,
    first_slope_ref,
    second_slope_ref,
    *refs,
):
    out_refs = refs[:4]
    third_ref, second_ref, first_delta_ref, flat_ref, second_map_ref, label_ref = refs[4:10]
    fourth_taps_ref = refs[10]
    third_delta_ref = refs[14]
    zero_row(second_map_ref)
    put_sample(payload_ref, 0, second_map_ref, label_ref, 0, bands)
    deep_layers(
        batch,
        bands,
        third_w_ref,
        fourth_w_ref,
        fourth_wt_ref,
        head_ref,
        fourth_taps_ref,
        second_map_ref,
        label_ref,
        *refs[11:16],
    )
    sample = lax.axis_index("dp")
    _, rows, phases, _, _ = third_delta_ref.shape
    fill_delta(third_ref, third_delta_ref[...])
    last_row_zero(third_ref)
    last_row_zero(second_ref)
    for row_parity in range(2):
        for col_parity in range(2):
            part = delta_parts(third_ref, third_wt_ref, row_parity, col_parity, rows, phases)
            for row in range(rows):
                for phase in range(phases):
                    at = (slice(None), 2 * row + row_parity, 2 * phase + col_parity)
                    second_ref[at] = rounded(part[:, row, phase] * second_slope_ref[at])
    rows, phases = 2 * rows, 2 * phases
    second_ref[:, :, phases] = shift_block(second_ref[:, :, 0], -1)
    for row_parity in range(2):
        for col_parity in range(2):
            part = delta_parts(second_ref, second_wt_ref, row_parity, col_parity, rows, phases)
            for row in range(rows):
                for phase in range(phases):
                    at = (slice(None), 2 * row + row_parity, 2 * phase + col_parity)
                    first_delta_ref[at] = rounded(part[:, row, phase] * first_slope_ref[at])
    delta = second_ref[:, pl.ds(0, rows), pl.ds(0, phases)]
    delta = delta.reshape(-1, delta.shape[-1]).astype(jnp.bfloat16)
    depth = first_ref.shape[-1]
    for tap in range(9):
        cells = map_tap(first_ref, tap // 3, tap % 3, rows, phases)
        flat_ref[pl.ds((12 + tap) * depth, depth)] = dot_tn(cells, delta)
    delta = first_delta_ref[...]
    delta = delta.reshape(-1, delta.shape[-1]).astype(jnp.bfloat16)
    cells = delta.shape[0]
    row_cells = cells // (2 * rows)
    taps = (odd_ref[pl.ds(0, cells)], even_ref[...], odd_ref[pl.ds(row_cells, cells)])
    for tap in range(3):
        part = dot_tn(delta, taps[tap])
        for piece in range(4):
            flat_ref[pl.ds((4 * tap + piece) * depth, depth)] = part[
                :, piece * 128 : piece * 128 + 128
            ]
    share = out_refs[0].shape[0]
    for slot in range(4):
        at = pl.multiple_of(((sample % 4) ^ slot) * share, share)
        out_refs[slot][...] = flat_ref[pl.ds(at, share)].astype(jnp.bfloat16)


def fourth_grad_kernel(fourth_taps_ref, fourth_flat_ref, out_ref):
    @pl.when(pl.program_id(1) == 0)
    def _():
        out_ref[...] = jnp.zeros(out_ref.shape, jnp.float32)

    out_ref[...] += dot_tn(fourth_taps_ref[...], fourth_flat_ref[...])


def finish_kernel(*refs):
    got_refs = refs[:4]
    temporal_ref, middle_ref, flat_ref = refs[4:]
    me = lax.axis_index("dp") % 4
    share = got_refs[0].shape[0]
    for slot in range(4):
        at = pl.multiple_of((me ^ slot) * share, share)
        flat_ref[pl.ds(at, share)] = got_refs[slot][...].astype(jnp.float32)
    depth = temporal_ref.shape[2]
    middle_ref[...] = flat_ref[pl.ds(12 * depth, 9 * depth)]
    rest = temporal_ref.shape[1] - 128
    for tap in range(3):
        parts = [flat_ref[pl.ds((4 * tap + piece) * depth, depth)].T for piece in range(4)]
        for col_tap in range(3):
            temporal_ref[3 * tap + col_tap, pl.ds(0, 128)] = parts[col_tap]
            temporal_ref[3 * tap + col_tap, pl.ds(128, rest)] = parts[3][
                col_tap * rest : col_tap * rest + rest
            ]


def cost(flops, size):
    return pl.CostEstimate(flops=flops, bytes_accessed=size, transcendentals=0)


def swapped(value, axis, bit):
    return lax.ppermute(value, axis, [(i, i ^ bit) for i in range(lax.axis_size(axis))])


def band_pieces(value, bands):
    pieces = [value]
    bit = 1
    while bit < bands:
        whole = pieces[0] if bit == 1 else jnp.concatenate(pieces, axis=0)
        pieces.append(swapped(whole, "space", bit))
        bit *= 2
    return pieces


def put(buffer, part, at):
    return lax.dynamic_update_slice(buffer, part, (at,) + (0,) * (buffer.ndim - 1))


def gather_and_sum(payload, local_quarters, samples):
    tie = lax.optimization_barrier
    half, quarter = samples // 2, samples // 4
    near = put(jnp.zeros((half,) + payload.shape[1:], payload.dtype), payload, 0)
    last, last_at, count, bit = payload, 0, 1, 4
    quarters, total = None, None
    while count < quarter:
        got = swapped(near[:count] if count > 1 else payload, "dp", half // count)
        beside = swapped(last, "dp", 2)
        if quarters is None:
            quarters = local_quarters()
            got, *quarters = tie((got, *quarters))
        elif total is None:
            parts = [swapped(quarters[slot], "dp", slot) for slot in (1, 2, 3)]
            got, *parts = tie((got, *parts))
            total = added(quarters[0], *parts)
        else:
            got, other = tie((got, swapped(total, "dp", bit)))
            total = added(total, other)
            bit *= 2
        near = put(near, beside, quarter + last_at)
        near = put(near, got, count)
        last, last_at = got, count
        count *= 2
    far = jnp.zeros_like(near)
    early = swapped(near[: quarter + last_at], "dp", 1)
    beside = swapped(last, "dp", 2)
    if quarters is None:
        quarters = local_quarters()
    if total is None:
        total = added(
            quarters[0], *[swapped(quarters[slot], "dp", slot) for slot in (1, 2, 3)]
        )
    elif bit < samples:
        beside, other = tie((beside, swapped(total, "dp", bit)))
        total = added(total, other)
        bit *= 2
    near = put(near, beside, quarter + last_at)
    far = put(far, early, 0)
    far = put(far, swapped(beside, "dp", 1), quarter + last_at)
    return near, far, total, bit


def added(*parts):
    total = parts[0].astype(jnp.float32)
    for part in parts[1:]:
        total = total + part.astype(jnp.float32)
    return total.astype(jnp.bfloat16)


def local(
    occupancy,
    state_labels,
    lift_weight,
    temporal_weight,
    middle_weight,
    deeper_weight,
    deepest_weight,
    head_weight,
):
    bands = lax.axis_size("space")
    samples = lax.axis_size("dp")
    _, frames, band, cols = occupancy.shape
    lift_all = frames * lift_weight.shape[1]
    one, two = middle_weight.shape[2:]
    three, four = deepest_weight.shape[2:]
    f32, bf16 = jnp.float32, jnp.bfloat16
    shaped = jax.ShapeDtypeStruct
    phases = cols // BLOCK
    rows = bands * band
    small = samples * bands <= 32
    vmem = pl.BlockSpec(memory_space=pltpu.VMEM)

    def grant(size):
        return pltpu.CompilerParams(vmem_limit_bytes=(size if small else 60) * MIB)

    lines = band_pieces(occupancy, bands)
    first_w = temporal_weight.reshape(9, lift_all, one)
    second_w = middle_weight.reshape(9, one, two)
    third_w = deeper_weight.reshape(9, two, three)
    fourth_w = deepest_weight.reshape(9, three, four)
    head = head_weight.reshape(1, four)

    sent = rows // 4 * phases // 4 * BLOCK + 16
    hbm = pl.BlockSpec(memory_space=pltpu.HBM)
    even_shape = shaped((rows // 2 * cols // 2, 512), bf16)
    odd_shape = shaped(((rows // 2 + 1) * cols // 2, 512), bf16)
    bits_scratch = pltpu.VMEM((band * 128, cols), bf16)
    own_cells = shaped((band // 2 * cols // 2, 512), bf16)
    own_args = [
        pltpu.with_memory_space_constraint(value, pltpu.HBM)
        for value in (
            occupancy,
            state_labels,
            lift_weight,
            first_w,
            second_w,
            third_w,
            fourth_w,
        )
    ]
    (
        own_even,
        own_odd,
        own_labels,
        lift_all_w,
        first_all,
        second_w2,
        third_w2,
        fourth_w2,
        second_wt,
        third_wt,
        fourth_wt,
        labels,
    ) = pl.pallas_call(
        own_kernel,
        out_shape=(
            own_cells,
            own_cells,
            shaped((16, two), f32),
            shaped((128, 256), bf16),
            shaped((3, 512, one), bf16),
            shaped(second_w.shape, bf16),
            shaped(third_w.shape, bf16),
            shaped(fourth_w.shape, bf16),
            shaped((9, two, one), bf16),
            shaped((9, three, two), bf16),
            shaped((9, four, three), bf16),
            shaped(state_labels.shape, state_labels.dtype),
        ),
        in_specs=[hbm] * 7,
        out_specs=(vmem,) * 12,
        scratch_shapes=[
            pltpu.VMEM(occupancy.shape, occupancy.dtype),
            pltpu.VMEM(lift_weight.shape, bf16),
            pltpu.VMEM(first_w.shape, bf16),
            bits_scratch,
            pltpu.SemaphoreType.DMA((7,)),
        ],
        compiler_params=grant(24),
        cost_estimate=cost(100_000_000, 10_000_000),
        name="own_band",
    )(*own_args)
    labels = band_pieces(labels, bands)
    pieces = len(lines) - 1
    even, odd, payload, first, first_slope, second_slope = pl.pallas_call(
        functools.partial(early_kernel, pieces, lift_all - 128),
        out_shape=(
            even_shape,
            odd_shape,
            shaped((sent, two), bf16),
            shaped((1, rows // 4 + 1, 2, phases // 4 + 1, 2, BLOCK, one), f32),
            shaped((1, rows // 2, phases // 2, BLOCK, one), f32),
            shaped((1, rows // 4, phases // 4, BLOCK, two), f32),
        ),
        in_specs=[vmem] * (2 * pieces + 6),
        out_specs=(vmem,) * 6,
        scratch_shapes=[bits_scratch],
        compiler_params=grant(24),
        cost_estimate=cost(150_000_000, 4_000_000),
        name="early",
    )(*lines[1:], *labels[1:], own_labels, lift_all_w, first_all, second_w2, own_even, own_odd)

    payload = payload[None]
    deep_weights = (
        third_w2.reshape(9 * two, three),
        fourth_w2.reshape(9 * three, four),
        fourth_wt,
        head,
    )

    third_cells = 2 * bands * 2 * BLOCK
    fourth_cells = bands * BLOCK

    def second_scratch(count):
        return pltpu.VMEM((count, 2 * bands + 1, 2, 3, 2, BLOCK, two), f32)

    def third_taps_scratch(count):
        return pltpu.VMEM((count * third_cells, 9 * two), bf16)

    def deep_scratch(count):
        return [
            third_taps_scratch(count),
            pltpu.VMEM((count, bands + 1, 2, 2, 2, BLOCK, three), f32),
            pltpu.VMEM((count, bands, 2, 1, 2, BLOCK, three), f32),
            pltpu.VMEM((count, 2 * bands, 2, BLOCK, three), f32),
            pltpu.VMEM((count, bands + 1, 2, BLOCK, four), f32),
        ]

    share = 21 * one // 4
    local_call = pl.pallas_call(
        functools.partial(local_kernel, samples, bands),
        out_shape=(shaped((share, two), bf16),) * 4,
        in_specs=[vmem] * 12,
        out_specs=(vmem,) * 4,
        scratch_shapes=[
            pltpu.VMEM((1, 2 * bands + 1, 3, BLOCK, three), f32),
            pltpu.VMEM((1, 4 * bands + 1, 5, BLOCK, two), f32),
            pltpu.VMEM(first_slope.shape, f32),
            pltpu.VMEM((21 * one, two), f32),
            second_scratch(1),
            pltpu.VMEM((1, bands, BLOCK, two), f32),
            pltpu.VMEM((fourth_cells, 9 * three), bf16),
        ]
        + deep_scratch(1),
        compiler_params=grant(24),
        cost_estimate=cost(300_000_000, 9_000_000),
        name="local",
    )
    maps = (third_wt, second_wt, even, odd, first, first_slope, second_slope)
    near, far, total, bit = gather_and_sum(
        payload, lambda: local_call(payload, *deep_weights, *maps), samples
    )

    chunk = max(1, min(samples, 32 // bands))
    steps = samples // chunk
    full = lambda *shape: pl.BlockSpec(shape, lambda i: (0,) * len(shape))
    fourth_taps, fourth_flat, head_grad, deeper_grad = pl.pallas_call(
        functools.partial(deep_kernel, samples, bands),
        grid=(steps,),
        out_shape=(
            shaped((samples * fourth_cells, 9 * three), bf16),
            shaped((samples * fourth_cells, four), bf16),
            shaped((1, four), f32),
            shaped((9 * two, three), f32),
        ),
        in_specs=[
            full(*near.shape),
            full(*far.shape),
            full(9 * two, three),
            full(9 * three, four),
            full(9, four, three),
            full(1, four),
        ],
        out_specs=(
            pl.BlockSpec((chunk * fourth_cells, 9 * three), lambda i: (i, 0)),
            pl.BlockSpec((chunk * fourth_cells, four), lambda i: (i, 0)),
            full(1, four),
            full(9 * two, three),
        ),
        scratch_shapes=[second_scratch(chunk), pltpu.VMEM((chunk, bands, BLOCK, two), f32)]
        + deep_scratch(chunk),
        compiler_params=grant(40),
        cost_estimate=cost(1_300_000_000, 12_000_000),
        name="deep",
    )(near, far, *deep_weights)

    if bit < samples:
        other, fourth_flat = lax.optimization_barrier((swapped(total, "dp", bit), fourth_flat))
        total = added(total, other)
    beside = swapped(total, "dp", 2)
    core = swapped(total, "dp", 1)
    deepest_grad = pl.pallas_call(
        fourth_grad_kernel,
        grid=(3, steps),
        out_shape=shaped((9 * three, four), f32),
        in_specs=[
            pl.BlockSpec((chunk * fourth_cells, 3 * three), lambda t, i: (i, t)),
            pl.BlockSpec((chunk * fourth_cells, four), lambda t, i: (i, 0)),
        ],
        out_specs=pl.BlockSpec((3 * three, four), lambda t, i: (t, 0)),
        compiler_params=grant(16),
        cost_estimate=cost(600_000_000, 6_000_000),
        name="fourth_grad",
    )(fourth_taps, fourth_flat)
    beside, deepest_grad = lax.optimization_barrier((beside, deepest_grad))
    across = swapped(beside, "dp", 1)
    temporal_grad, middle_grad = pl.pallas_call(
        finish_kernel,
        out_shape=(shaped((9, lift_all, one), f32), shaped((9 * one, two), f32)),
        in_specs=[vmem] * 4,
        out_specs=(vmem, vmem),
        scratch_shapes=[pltpu.VMEM((21 * one, two), f32)],
        compiler_params=grant(16),
        cost_estimate=cost(1_000_000, 1_500_000),
        name="finish",
    )(total, core, beside, across)
    return (
        temporal_grad.reshape(temporal_weight.shape),
        middle_grad.reshape(middle_weight.shape),
        deeper_grad.reshape(deeper_weight.shape),
        deepest_grad.reshape(deepest_weight.shape),
        head_grad.reshape(four),
    )


def solution(mesh):
    return jax.shard_map(
        local,
        mesh=mesh,
        in_specs=(
            P("dp", None, "space", None),
            P("dp", "space", None),
            P(),
            P(),
            P(),
            P(),
            P(),
            P(),
        ),
        out_specs=(P(), P(), P(), P(), P()),
        check_vma=False,
    )
```

```python
import functools

import jax
import jax.numpy as jnp
from jax import lax
from jax.experimental import pallas as pl
from jax.experimental.pallas import tpu as pltpu
from jax.sharding import PartitionSpec as P

BLOCK = 8
MIB = 1 << 20


def f32_dot(left, right, contract):
    return lax.dot_general(
        left, right, ((contract[0], contract[1]), ((), ())), preferred_element_type=jnp.float32
    )


def dot_nn(left, right):
    return f32_dot(left, right, ((1,), (0,)))


def dot_nt(left, right):
    return f32_dot(left, right, ((1,), (1,)))


def dot_tn(left, right):
    return f32_dot(left, right, ((0,), (0,)))


def rounded(value):
    return value.astype(jnp.bfloat16).astype(jnp.float32)


def silu_and_slope(pre):
    gate = jax.nn.sigmoid(pre)
    return rounded(pre * gate), gate * (1.0 + pre * (1.0 - gate))


def zero_row(ref):
    ref[:, 0, 0] = jnp.zeros(ref.shape[:1] + ref.shape[3:], ref.dtype)


def last_row_zero(ref):
    ref[:, ref.shape[1] - 1] = jnp.zeros(ref.shape[:1] + ref.shape[2:], ref.dtype)


def shift_block(value, step):
    shape = value.shape
    flat = value.reshape(-1, shape[-1])
    moved = pltpu.roll(flat, step % flat.shape[0], 0)
    index = lax.broadcasted_iota(jnp.int32, flat.shape, 0) % BLOCK
    edge = 0 if step > 0 else BLOCK - 1
    return jnp.where(index == edge, 0.0, moved).reshape(shape)


def fill_map(ref, value, offset):
    n, rows, phases, _, channels = value.shape
    split = value.reshape(n, rows, phases // 2, 2, BLOCK, channels)
    for row in range(rows):
        pair, parity = divmod(row + offset, 2)
        ref[:, pair, parity, pl.ds(0, phases // 2), 1] = split[:, row, :, 0]
        ref[:, pair, parity, pl.ds(1, phases // 2), 0] = split[:, row, :, 1]
        ref[:, pair, parity, 0, 0] = shift_block(split[:, row, phases // 2 - 1, 1], 1)


def map_tap(ref, row_tap, col_tap, out_rows, out_phases):
    cells = ref[
        :,
        pl.ds(row_tap // 2, out_rows),
        row_tap % 2,
        pl.ds(col_tap // 2, out_phases),
        col_tap % 2,
    ]
    return cells.reshape(-1, cells.shape[-1]).astype(jnp.bfloat16)


def fill_delta(ref, value):
    rows, phases = value.shape[1:3]
    ref[:, pl.ds(0, rows), pl.ds(0, phases)] = value
    ref[:, pl.ds(0, rows), phases] = shift_block(value[:, :, 0], -1)


def delta_parts(ref, weight_ref, row_parity, col_parity, rows, phases):
    taps = (((1, 0),), ((2, 0), (0, 1)))
    total = None
    for row_tap, row_step in taps[row_parity]:
        for col_tap, col_step in taps[col_parity]:
            cells = ref[:, pl.ds(row_step, rows), pl.ds(col_step, phases)]
            lead = cells.shape[:-1]
            flat = cells.reshape(-1, cells.shape[-1]).astype(jnp.bfloat16)
            part = dot_nn(flat, weight_ref[3 * row_tap + col_tap])
            total = part if total is None else total + part
    return total.reshape(*lead, total.shape[-1])


def column_order(cols):
    place = lax.broadcasted_iota(jnp.int32, (cols, cols), 0)
    column = lax.broadcasted_iota(jnp.int32, (cols, cols), 1)
    source = (place % BLOCK) * (cols // BLOCK) + place // BLOCK
    return jnp.where(column == source, 1.0, 0.0).astype(jnp.bfloat16)


def band_cells(got_ref, inner, index, order, lift_ref, bits_ref, even_ref, odd_ref, rest):
    _, frames, band, cols = got_ref.shape
    phases, row_cells = cols // BLOCK, cols // 2
    height = lax.broadcasted_iota(jnp.int32, (16, cols), 0)
    for row in range(band):
        for frame in range(frames):
            line = jnp.broadcast_to(got_ref[inner, frame, pl.ds(row, 1)], height.shape)
            bit = jnp.bitwise_and(jnp.right_shift(line, height), 1)
            bits_ref[pl.ds(row * 128 + frame * 16, 16)] = bit.astype(jnp.float32).astype(
                jnp.bfloat16
            )
    spread = dot_nt(order, bits_ref[...]).astype(jnp.bfloat16)
    stacked = jnp.concatenate(
        [spread[:, row * 128 : row * 128 + 128] for row in range(band)], axis=0
    )
    lifted = jnp.maximum(dot_nn(stacked, lift_ref[...]), 0.0)
    lifted = lifted.reshape(band // 2, 2, phases // 2, 2, BLOCK, lifted.shape[-1])
    for parity, ref in ((0, even_ref), (1, odd_ref)):
        here = lifted[:, parity, :, 0]
        right = lifted[:, parity, :, 1]
        left = jnp.concatenate([shift_block(right[:, -1], 1)[:, None], right[:, :-1]], axis=1)
        taps = [part.reshape(-1, part.shape[-1]) for part in (left, here, right)]
        lane = lax.broadcasted_iota(jnp.int32, (taps[0].shape[0], 128), 1)
        tail = jnp.where(lane < rest, taps[0][:, 128:], taps[1][:, 128:])
        tail = jnp.where(lane < 2 * rest, tail, taps[2][:, 128:])
        cells = jnp.concatenate([part[:, :128] for part in taps] + [tail], axis=1)
        if index is None:
            ref[...] = cells.astype(jnp.bfloat16)
        else:
            at = pl.multiple_of((index * (band // 2) + parity) * row_cells, row_cells)
            ref[pl.ds(at, cells.shape[0])] = cells.astype(jnp.bfloat16)


def band_label(label_ref, inner, index, shape):
    lane = lax.broadcasted_iota(jnp.int32, shape, 1)
    row = lax.broadcasted_iota(jnp.int32, (shape[0], BLOCK), 0)
    column = lax.broadcasted_iota(jnp.int32, (shape[0], BLOCK), 1)
    label = jnp.broadcast_to(label_ref[inner].astype(jnp.float32), row.shape)
    label = jnp.sum(jnp.where(row == column, label, 0.0), axis=1, keepdims=True)
    return jnp.where(lane == index, label, 0.0)


def own_kernel(
    got_hbm,
    label_hbm,
    lift_hbm,
    first_w_hbm,
    second_w_hbm,
    third_w_hbm,
    fourth_w_hbm,
    even_ref,
    odd_ref,
    labels_ref,
    lift_all_ref,
    first_all_ref,
    second_w_ref,
    third_w_ref,
    fourth_w_ref,
    got_ref,
    label_ref,
    lift_ref,
    first_w_ref,
    bits_ref,
    sems,
):
    pairs = (
        (got_hbm, got_ref),
        (lift_hbm, lift_ref),
        (label_hbm, label_ref),
        (first_w_hbm, first_w_ref),
        (second_w_hbm, second_w_ref),
        (third_w_hbm, third_w_ref),
        (fourth_w_hbm, fourth_w_ref),
    )
    copies = [
        pltpu.make_async_copy(source, target, sems.at[k])
        for k, (source, target) in enumerate(pairs)
    ]
    for copy in copies:
        copy.start()
    me = lax.axis_index("space")
    _, frames, _, cols = got_ref.shape
    heights, width = lift_ref.shape
    rest = first_w_ref.shape[1] - 128
    bits_ref[...] = jnp.zeros(bits_ref.shape, jnp.bfloat16)
    first_all_ref[...] = jnp.zeros(first_all_ref.shape, jnp.bfloat16)
    order = column_order(cols)
    copies[1].wait()
    tall = jnp.concatenate(
        [lift_ref[...].astype(jnp.float32), jnp.zeros((16 - heights, width), jnp.float32)], axis=0
    )
    tall = jnp.concatenate([tall] * (256 // width), axis=1)
    tall = jnp.concatenate([tall] * 8, axis=0)
    frame_of_row = lax.broadcasted_iota(jnp.int32, tall.shape, 0) // 16
    lane = lax.broadcasted_iota(jnp.int32, tall.shape, 1)
    frame_of_lane = jnp.minimum(lane // width, frames - 1)
    keep = (frame_of_row == frame_of_lane) & (lane < 128 + 3 * rest)
    lift_all_ref[...] = jnp.where(keep, tall, 0.0).astype(jnp.bfloat16)
    copies[0].wait()
    band_cells(got_ref, 0, None, order, lift_all_ref, bits_ref, even_ref, odd_ref, rest)
    copies[2].wait()
    labels_ref[...] = band_label(label_ref, 0, me, labels_ref.shape).astype(jnp.bfloat16)
    copies[3].wait()
    for tap in range(9):
        row_tap, col_tap = divmod(tap, 3)
        first_all_ref[row_tap, pl.ds(col_tap * 128, 128)] = first_w_ref[tap, pl.ds(0, 128)]
        first_all_ref[row_tap, pl.ds(384 + col_tap * rest, rest)] = first_w_ref[
            tap, pl.ds(128, rest)
        ]
    for copy in copies[4:]:
        copy.wait()


def early_kernel(pieces, rest, *refs):
    got_refs = refs[:pieces]
    (
        lift_all_ref,
        first_all_ref,
        second_w_ref,
        own_even_ref,
        own_odd_ref,
        even_ref,
        odd_ref,
        send_ref,
        first_ref,
        first_slope_ref,
        second_slope_ref,
        bits_ref,
    ) = refs[pieces:]
    me = lax.axis_index("space")
    bands = 1 << pieces
    _, _, band, cols = got_refs[0].shape
    phases, row_cells = cols // BLOCK, cols // 2
    order = column_order(cols)
    cells = own_even_ref.shape[0]
    at = pl.multiple_of(me * cells, cells)
    even_ref[pl.ds(at, cells)] = own_even_ref[...]
    odd_ref[pl.ds(pl.multiple_of(at + row_cells, row_cells), cells)] = own_odd_ref[...]
    odd_ref[pl.ds(0, row_cells)] = jnp.zeros((row_cells, odd_ref.shape[1]), jnp.bfloat16)
    bits_ref[...] = jnp.zeros(bits_ref.shape, jnp.bfloat16)
    for slot in range(1, bands):
        piece = slot.bit_length() - 1
        inner = slot - (1 << piece)
        band_cells(
            got_refs[piece],
            inner,
            me ^ slot,
            order,
            lift_all_ref,
            bits_ref,
            even_ref,
            odd_ref,
            rest,
        )

    rows, phases = bands * band // 2, phases // 2
    cells = rows * row_cells
    pre = dot_nn(odd_ref[pl.ds(0, cells)], first_all_ref[0])
    pre += dot_nn(even_ref[...], first_all_ref[1])
    pre += dot_nn(odd_ref[pl.ds(row_cells, cells)], first_all_ref[2])
    value, slope = silu_and_slope(pre)
    shape = (1, rows, phases, BLOCK, value.shape[-1])
    zero_row(first_ref)
    fill_map(first_ref, value.reshape(shape), 1)
    first_slope_ref[...] = slope.reshape(shape)

    rows, phases = rows // 2, phases // 2
    pre = None
    for tap in range(9):
        cells = map_tap(first_ref, tap // 3, tap % 3, rows, phases)
        part = dot_nn(cells, second_w_ref[tap])
        pre = part if pre is None else pre + part
    value, slope = silu_and_slope(pre)
    second_slope_ref[...] = slope.reshape(second_slope_ref.shape)
    sent = value.shape[0]
    send_ref[pl.ds(0, sent)] = value.astype(jnp.bfloat16)
    send_ref[pl.ds(sent, 16)] = jnp.zeros((16, send_ref.shape[1]), jnp.bfloat16)


def transpose_kernel(weight_ref, out_ref):
    for tap in range(weight_ref.shape[0]):
        out_ref[tap] = weight_ref[tap].T


def take_samples(slot_refs, second_ref, label_ref, bands):
    count = sum(ref.shape[0] for ref in slot_refs)
    width = count.bit_length() - 1
    chunk = second_ref.shape[0]
    me = lax.axis_index("dp")
    where = [(ref, inner) for ref in slot_refs for inner in range(ref.shape[0])]
    for slot in range(count):
        reverse = sum(((slot >> k) & 1) << (width - 1 - k) for k in range(width))
        sample = me ^ reverse
        ref, inner = where[slot]

        def take(ref=ref, inner=inner, place=sample % chunk):
            put_sample(ref, inner, second_ref, label_ref, place, bands)

        if chunk == count:
            take()
        else:
            pl.when(sample // chunk == pl.program_id(0))(take)


def third_taps(second_ref, taps_ref, rows, phases):
    channels = second_ref.shape[-1]
    for tap in range(9):
        taps_ref[:, pl.ds(tap * channels, channels)] = map_tap(
            second_ref, tap // 3, tap % 3, rows, phases
        )


def delta_columns(ref, weight_ref, row_parity, col_parity, rows, phases):
    taps = (((1, 0),), ((2, 0), (0, 1)))
    total = None
    for row_tap, row_step in taps[row_parity]:
        for col_tap, col_step in taps[col_parity]:
            cells = ref[:, pl.ds(row_step, rows), pl.ds(col_step, phases)]
            lead = cells.shape[:-1]
            columns = cells.reshape(-1, cells.shape[-1]).T.astype(jnp.bfloat16)
            part = dot_nn(weight_ref[3 * row_tap + col_tap], columns)
            total = part if total is None else total + part
    return total.T.reshape(*lead, total.shape[0])


def put_sample(ref, inner, second_ref, label_ref, place, bands):
    rows, phases = 4 * bands, 4
    cells = rows * phases * BLOCK
    second = ref[inner, pl.ds(0, cells)].astype(jnp.float32)
    fill_map(
        second_ref.at[pl.ds(place, 1)],
        second.reshape(1, rows, phases, BLOCK, second.shape[-1]),
        1,
    )
    if label_ref is not None:
        label = ref[inner, pl.ds(cells, 16)].astype(jnp.float32)[:BLOCK]
        for index in range(bands):
            label_ref[place, index] = jnp.broadcast_to(label[:, index : index + 1], label.shape)


def deep_layers(
    batch,
    bands,
    third_w_ref,
    fourth_w_ref,
    fourth_parts,
    head_ref,
    fourth_taps_ref,
    second_ref,
    label_ref,
    third_taps_ref,
    third_ref,
    third_slope_ref,
    third_delta_ref,
    fourth_delta_ref,
):
    samples = second_ref.shape[0]
    rows, phases = 2 * bands, 2
    third_taps(second_ref, third_taps_ref, rows, phases)
    weight = third_w_ref[...].reshape(third_taps_ref.shape[1], -1)
    value, slope = silu_and_slope(dot_nn(third_taps_ref[...], weight))
    channels = value.shape[-1]
    zero_row(third_ref)
    fill_map(third_ref, value.reshape(samples, rows, phases, BLOCK, channels), 1)
    third_slope_ref[...] = slope.reshape(third_slope_ref.shape)

    rows, phases = rows // 2, phases // 2
    for tap in range(9):
        fourth_taps_ref[:, pl.ds(tap * channels, channels)] = map_tap(
            third_ref, tap // 3, tap % 3, rows, phases
        )
    weight = fourth_w_ref[...].reshape(fourth_taps_ref.shape[1], -1)
    value, slope = silu_and_slope(dot_nn(fourth_taps_ref[...], weight))
    head = head_ref[...].astype(jnp.float32)
    labels = label_ref[...].reshape(-1, label_ref.shape[-1])[:, :1]
    logits = jnp.sum(value * head, axis=1, keepdims=True)
    logit_grad = (jax.nn.sigmoid(logits) - labels) / batch
    delta = rounded(logit_grad * head * slope)
    last_row_zero(fourth_delta_ref)
    fill_delta(fourth_delta_ref, delta.reshape(samples, rows, phases, BLOCK, delta.shape[-1]))
    for row_parity in range(2):
        for col_parity in range(2):
            part = fourth_parts(fourth_delta_ref, row_parity, col_parity, rows, phases)
            part = rounded(part * third_slope_ref[:, :, row_parity, :, col_parity])
            for row in range(rows):
                third_delta_ref[:, 2 * row + row_parity, col_parity] = part[:, row, 0]
    return value, logit_grad, delta


def deep_kernel(
    batch,
    bands,
    stored,
    near_ref,
    far_ref,
    last_ref,
    third_w_ref,
    fourth_w_ref,
    fourth_wt_ref,
    head_ref,
    fourth_taps_ref,
    fourth_flat_ref,
    head_grad_ref,
    *refs,
):
    if stored:
        third_taps_ref, third_flat_ref, second_ref, label_ref = refs[:4]
    else:
        third_grad_ref, second_ref, label_ref, third_taps_ref = refs[:4]
    third_ref, third_slope_ref, third_delta_ref, fourth_delta_ref = refs[4:]
    zero_row(second_ref)
    take_samples((near_ref, far_ref, last_ref), second_ref, label_ref, bands)
    value, logit_grad, delta = deep_layers(
        batch,
        bands,
        third_w_ref,
        fourth_w_ref,
        lambda ref, *where: delta_parts(ref, fourth_wt_ref, *where),
        head_ref,
        fourth_taps_ref,
        second_ref,
        label_ref,
        third_taps_ref,
        third_ref,
        third_slope_ref,
        third_delta_ref,
        fourth_delta_ref,
    )

    @pl.when(pl.program_id(0) == 0)
    def _():
        head_grad_ref[...] = jnp.zeros(head_grad_ref.shape, jnp.float32)

    head_grad_ref[...] += jnp.sum(value * logit_grad, axis=0, keepdims=True)
    fourth_flat_ref[...] = delta.astype(jnp.bfloat16)
    delta = third_delta_ref[...]
    delta = delta.reshape(-1, delta.shape[-1]).astype(jnp.bfloat16)
    if stored:
        third_flat_ref[...] = delta
    else:
        third_grad_kernel(third_taps_ref, delta, third_grad_ref)


def local_kernel(
    batch,
    bands,
    payload_ref,
    third_w_ref,
    fourth_w_ref,
    head_ref,
    second_w_ref,
    even_ref,
    odd_ref,
    first_ref,
    first_slope_ref,
    second_slope_ref,
    *refs,
):
    keep_ref, pass_ref = refs[:2]
    third_ref, second_ref, first_delta_ref, flat_ref, second_map_ref, label_ref = refs[2:8]
    fourth_taps_ref = refs[8]
    third_delta_ref = refs[12]
    zero_row(second_map_ref)
    put_sample(payload_ref, 0, second_map_ref, label_ref, 0, bands)
    deep_layers(
        batch,
        bands,
        third_w_ref,
        fourth_w_ref,
        lambda ref, *where: delta_columns(ref, fourth_w_ref, *where),
        head_ref,
        fourth_taps_ref,
        second_map_ref,
        label_ref,
        *refs[9:14],
    )
    sample = lax.axis_index("dp")
    _, rows, phases, _, _ = third_delta_ref.shape
    fill_delta(third_ref, third_delta_ref[...])
    last_row_zero(third_ref)
    last_row_zero(second_ref)
    for row_parity in range(2):
        for col_parity in range(2):
            part = delta_columns(third_ref, third_w_ref, row_parity, col_parity, rows, phases)
            for row in range(rows):
                for phase in range(phases):
                    at = (slice(None), 2 * row + row_parity, 2 * phase + col_parity)
                    second_ref[at] = rounded(part[:, row, phase] * second_slope_ref[at])
    rows, phases = 2 * rows, 2 * phases
    second_ref[:, :, phases] = shift_block(second_ref[:, :, 0], -1)
    for row_parity in range(2):
        for col_parity in range(2):
            part = delta_columns(second_ref, second_w_ref, row_parity, col_parity, rows, phases)
            for row in range(rows):
                for phase in range(phases):
                    at = (slice(None), 2 * row + row_parity, 2 * phase + col_parity)
                    first_delta_ref[at] = rounded(part[:, row, phase] * first_slope_ref[at])
    delta = second_ref[:, pl.ds(0, rows), pl.ds(0, phases)]
    delta = delta.reshape(-1, delta.shape[-1]).astype(jnp.bfloat16)
    depth = first_ref.shape[-1]
    for tap in range(9):
        cells = map_tap(first_ref, tap // 3, tap % 3, rows, phases)
        flat_ref[pl.ds((12 + tap) * depth, depth)] = dot_tn(cells, delta)
    delta = first_delta_ref[...]
    delta = delta.reshape(-1, delta.shape[-1]).astype(jnp.bfloat16)
    cells = delta.shape[0]
    row_cells = cells // (2 * rows)
    taps = (odd_ref[pl.ds(0, cells)], even_ref[...], odd_ref[pl.ds(row_cells, cells)])
    for tap in range(3):
        part = dot_tn(delta, taps[tap])
        for piece in range(4):
            flat_ref[pl.ds((4 * tap + piece) * depth, depth)] = part[
                :, piece * 128 : piece * 128 + 128
            ]
    share = keep_ref.shape[1]
    for slot in range(4):
        at = pl.multiple_of(((sample % 4) ^ slot) * share, share)
        ref = pass_ref if slot % 2 else keep_ref
        ref[slot // 2] = flat_ref[pl.ds(at, share)].astype(jnp.bfloat16)


def third_grad_kernel(taps_ref, delta_ref, out_ref):
    @pl.when(pl.program_id(0) == 0)
    def _():
        out_ref[...] = jnp.zeros(out_ref.shape, jnp.float32)

    out_ref[...] += dot_tn(delta_ref[...], taps_ref[...]).T


def fourth_grad_kernel(fourth_taps_ref, fourth_flat_ref, out_ref):
    @pl.when(pl.program_id(1) == 0)
    def _():
        out_ref[...] = jnp.zeros(out_ref.shape, jnp.float32)

    out_ref[...] += dot_tn(fourth_taps_ref[...], fourth_flat_ref[...])


def finish_kernel(*refs):
    got_refs = refs[:4]
    temporal_ref, middle_ref, flat_ref = refs[4:]
    me = lax.axis_index("dp") % 4
    share = got_refs[0].shape[0]
    for slot in range(4):
        at = pl.multiple_of((me ^ slot) * share, share)
        flat_ref[pl.ds(at, share)] = got_refs[slot][...].astype(jnp.float32)
    depth = temporal_ref.shape[2]
    middle_ref[...] = flat_ref[pl.ds(12 * depth, 9 * depth)]
    rest = temporal_ref.shape[1] - 128
    for tap in range(3):
        parts = [flat_ref[pl.ds((4 * tap + piece) * depth, depth)].T for piece in range(4)]
        for col_tap in range(3):
            temporal_ref[3 * tap + col_tap, pl.ds(0, 128)] = parts[col_tap]
            temporal_ref[3 * tap + col_tap, pl.ds(128, rest)] = parts[3][
                col_tap * rest : col_tap * rest + rest
            ]


def cost(flops, size):
    return pl.CostEstimate(flops=flops, bytes_accessed=size, transcendentals=0)


def swapped(value, axis, bit):
    return lax.ppermute(value, axis, [(i, i ^ bit) for i in range(lax.axis_size(axis))])


def band_pieces(value, bands):
    pieces = [value]
    bit = 1
    while bit < bands:
        whole = pieces[0] if bit == 1 else jnp.concatenate(pieces, axis=0)
        pieces.append(swapped(whole, "space", bit))
        bit *= 2
    return pieces


def put(buffer, part, at):
    return lax.dynamic_update_slice(buffer, part, (at,) + (0,) * (buffer.ndim - 1))


def after(value, *others):
    return lax.optimization_barrier((value, *others))[0]


def gather_and_sum(payload, local_sums, transposed, samples):
    half, quarter = samples // 2, samples // 4
    near = put(jnp.zeros((half,) + payload.shape[1:], payload.dtype), payload, 0)
    got = swapped(payload, "dp", quarter * 2) if quarter > 1 else None
    keep, passed = local_sums()
    core = swapped(passed, "dp", 1)
    count, beside_count = 1, 0
    while count < quarter:
        near = put(near, after(got, keep), count)
        count *= 2
        if count < quarter:
            part = near[beside_count:count]
            got = swapped(near[:count], "dp", half // count)
            beside = swapped(part, "dp", 2)
            near = put(near, beside, quarter + beside_count)
            beside_count = count
    weights = transposed(after(keep, core))
    mine, theirs = added(keep[0], core[0]), added(keep[1], core[1])
    theirs = after(theirs, weights)
    total = added(mine, swapped(theirs, "dp", 2))
    beside = swapped(after(near[beside_count:quarter], theirs), "dp", 2)
    early = swapped(near[: quarter + beside_count], "dp", 1)
    bit = 4
    while 2 * bit < samples:
        other = swapped(total, "dp", bit)
        beside = after(beside, total)
        total = added(total, other)
        bit *= 2
    near = put(near, beside, quarter + beside_count)
    last = swapped(beside, "dp", 1)
    return near, early, last, total, bit, weights


def added(*parts):
    total = parts[0].astype(jnp.float32)
    for part in parts[1:]:
        total = total + part.astype(jnp.float32)
    return total.astype(jnp.bfloat16)


def local(
    occupancy,
    state_labels,
    lift_weight,
    temporal_weight,
    middle_weight,
    deeper_weight,
    deepest_weight,
    head_weight,
):
    bands = lax.axis_size("space")
    samples = lax.axis_size("dp")
    _, frames, band, cols = occupancy.shape
    lift_all = frames * lift_weight.shape[1]
    one, two = middle_weight.shape[2:]
    three, four = deepest_weight.shape[2:]
    f32, bf16 = jnp.float32, jnp.bfloat16
    shaped = jax.ShapeDtypeStruct
    phases = cols // BLOCK
    rows = bands * band
    small = samples * bands <= 32
    vmem = pl.BlockSpec(memory_space=pltpu.VMEM)

    def grant(size):
        return pltpu.CompilerParams(vmem_limit_bytes=(size if small else 60) * MIB)

    lines = band_pieces(occupancy, bands)
    first_w = temporal_weight.reshape(9, lift_all, one)
    second_w = middle_weight.reshape(9, one, two)
    third_w = deeper_weight.reshape(9, two, three)
    fourth_w = deepest_weight.reshape(9, three, four)
    head = head_weight.reshape(1, four)

    sent = rows // 4 * phases // 4 * BLOCK + 16
    hbm = pl.BlockSpec(memory_space=pltpu.HBM)
    even_shape = shaped((rows // 2 * cols // 2, 512), bf16)
    odd_shape = shaped(((rows // 2 + 1) * cols // 2, 512), bf16)
    bits_scratch = pltpu.VMEM((band * 128, cols), bf16)
    own_cells = shaped((band // 2 * cols // 2, 512), bf16)
    own_args = [
        pltpu.with_memory_space_constraint(value, pltpu.HBM)
        for value in (
            occupancy,
            state_labels,
            lift_weight,
            first_w,
            second_w,
            third_w,
            fourth_w,
        )
    ]
    (
        own_even,
        own_odd,
        own_labels,
        lift_all_w,
        first_all,
        second_w2,
        third_w2,
        fourth_w2,
    ) = pl.pallas_call(
        own_kernel,
        out_shape=(
            own_cells,
            own_cells,
            shaped((16, two), bf16),
            shaped((128, 256), bf16),
            shaped((3, 512, one), bf16),
            shaped(second_w.shape, bf16),
            shaped(third_w.shape, bf16),
            shaped(fourth_w.shape, bf16),
        ),
        in_specs=[hbm] * 7,
        out_specs=(vmem,) * 8,
        scratch_shapes=[
            pltpu.VMEM(occupancy.shape, occupancy.dtype),
            pltpu.VMEM(state_labels.shape, state_labels.dtype),
            pltpu.VMEM(lift_weight.shape, bf16),
            pltpu.VMEM(first_w.shape, bf16),
            bits_scratch,
            pltpu.SemaphoreType.DMA((7,)),
        ],
        compiler_params=grant(24),
        cost_estimate=cost(100_000_000, 10_000_000),
        name="own_band",
    )(*own_args)
    pieces = len(lines) - 1
    even, odd, payload, first, first_slope, second_slope = pl.pallas_call(
        functools.partial(early_kernel, pieces, lift_all - 128),
        out_shape=(
            even_shape,
            odd_shape,
            shaped((sent, two), bf16),
            shaped((1, rows // 4 + 1, 2, phases // 4 + 1, 2, BLOCK, one), f32),
            shaped((1, rows // 2, phases // 2, BLOCK, one), f32),
            shaped((1, rows // 4, phases // 4, BLOCK, two), f32),
        ),
        in_specs=[vmem] * (pieces + 5),
        out_specs=(vmem,) * 6,
        scratch_shapes=[bits_scratch],
        compiler_params=grant(24),
        cost_estimate=cost(150_000_000, 4_000_000),
        name="early",
    )(*lines[1:], lift_all_w, first_all, second_w2, own_even, own_odd)

    labels, bit = own_labels, 1
    while bit < bands:
        labels = labels + swapped(labels, "space", bit)
        bit *= 2
    payload = put(payload, labels, sent - 16)[None]
    deep_weights = (third_w2, fourth_w2)

    third_cells = 2 * bands * 2 * BLOCK
    fourth_cells = bands * BLOCK

    def second_scratch(count):
        return pltpu.VMEM((count, 2 * bands + 1, 2, 3, 2, BLOCK, two), f32)

    def third_taps_scratch(count):
        return pltpu.VMEM((count * third_cells, 9 * two), bf16)

    def deep_scratch(count):
        return [
            third_taps_scratch(count),
            pltpu.VMEM((count, bands + 1, 2, 2, 2, BLOCK, three), f32),
            pltpu.VMEM((count, bands, 2, 1, 2, BLOCK, three), f32),
            pltpu.VMEM((count, 2 * bands, 2, BLOCK, three), f32),
            pltpu.VMEM((count, bands + 1, 2, BLOCK, four), f32),
        ]

    share = 21 * one // 4
    local_call = pl.pallas_call(
        functools.partial(local_kernel, samples, bands),
        out_shape=(shaped((2, share, two), bf16),) * 2,
        in_specs=[vmem] * 10,
        out_specs=(vmem,) * 2,
        scratch_shapes=[
            pltpu.VMEM((1, 2 * bands + 1, 3, BLOCK, three), f32),
            pltpu.VMEM((1, 4 * bands + 1, 5, BLOCK, two), f32),
            pltpu.VMEM(first_slope.shape, f32),
            pltpu.VMEM((21 * one, two), f32),
            second_scratch(1),
            pltpu.VMEM((1, bands, BLOCK, two), f32),
            pltpu.VMEM((fourth_cells, 9 * three), bf16),
        ]
        + deep_scratch(1),
        compiler_params=grant(24),
        cost_estimate=cost(300_000_000, 9_000_000),
        name="local",
    )
    maps = (head, second_w2, even, odd, first, first_slope, second_slope)
    transpose_call = pl.pallas_call(
        transpose_kernel,
        out_shape=shaped((9, four, three), bf16),
        in_specs=[vmem],
        out_specs=vmem,
        compiler_params=grant(16),
        cost_estimate=cost(10_000_000, 5_000_000),
        name="transpose",
    )

    near, far, last, total, bit, fourth_wt = gather_and_sum(
        payload,
        lambda: local_call(payload, *deep_weights, *maps),
        lambda keep: transpose_call(after(fourth_w2, keep)),
        samples,
    )
    near = after(near, total)

    chunk = max(1, min(samples, 32 // bands))
    steps = samples // chunk
    full = lambda *shape: pl.BlockSpec(shape, lambda i: (0,) * len(shape))
    rows_block = pl.BlockSpec((chunk * third_cells, 9 * two), lambda i: (i, 0))
    flat_block = pl.BlockSpec((chunk * third_cells, three), lambda i: (i, 0))
    grad_shape = shaped((9 * two, three), f32)
    if small:
        third_shapes = (
            shaped((samples * third_cells, 9 * two), bf16),
            shaped((samples * third_cells, three), bf16),
        )
        third_blocks = (rows_block, flat_block)
    else:
        third_shapes, third_blocks = (grad_shape,), (full(9 * two, three),)
    fourth_taps, fourth_flat, head_grad, *thirds = pl.pallas_call(
        functools.partial(deep_kernel, samples, bands, small),
        grid=(steps,),
        out_shape=(
            shaped((samples * fourth_cells, 9 * three), bf16),
            shaped((samples * fourth_cells, four), bf16),
            shaped((1, four), f32),
            *third_shapes,
        ),
        in_specs=[
            full(*near.shape),
            full(*far.shape),
            full(*last.shape),
            full(9, two, three),
            full(9, three, four),
            full(9, four, three),
            full(1, four),
        ],
        out_specs=(
            pl.BlockSpec((chunk * fourth_cells, 9 * three), lambda i: (i, 0)),
            pl.BlockSpec((chunk * fourth_cells, four), lambda i: (i, 0)),
            full(1, four),
            *third_blocks,
        ),
        scratch_shapes=[second_scratch(chunk), pltpu.VMEM((chunk, bands, BLOCK, two), f32)]
        + deep_scratch(chunk)[1 if small else 0 :],
        compiler_params=grant(40),
        cost_estimate=cost(1_300_000_000, 12_000_000),
        name="deep",
    )(near, far, last, *deep_weights, fourth_wt, head)

    if bit < samples:
        other, fourth_flat = lax.optimization_barrier((swapped(total, "dp", bit), fourth_flat))
        total = added(total, other)
    beside = swapped(total, "dp", 2)
    core = swapped(total, "dp", 1)
    deepest_grad = pl.pallas_call(
        fourth_grad_kernel,
        grid=(3, steps),
        out_shape=shaped((9 * three, four), f32),
        in_specs=[
            pl.BlockSpec((chunk * fourth_cells, 3 * three), lambda t, i: (i, t)),
            pl.BlockSpec((chunk * fourth_cells, four), lambda t, i: (i, 0)),
        ],
        out_specs=pl.BlockSpec((3 * three, four), lambda t, i: (t, 0)),
        compiler_params=grant(16),
        cost_estimate=cost(600_000_000, 6_000_000),
        name="fourth_grad",
    )(fourth_taps, fourth_flat)
    beside, deepest_grad = lax.optimization_barrier((beside, deepest_grad))
    across = swapped(beside, "dp", 1)
    if small:
        deeper_grad = pl.pallas_call(
            third_grad_kernel,
            grid=(steps,),
            out_shape=grad_shape,
            in_specs=[rows_block, flat_block],
            out_specs=full(9 * two, three),
            compiler_params=grant(24),
            cost_estimate=cost(600_000_000, 4_000_000),
            name="third_grad",
        )(*thirds)
    else:
        deeper_grad = thirds[0]
    across, deeper_grad = lax.optimization_barrier((across, deeper_grad))
    temporal_grad, middle_grad = pl.pallas_call(
        finish_kernel,
        out_shape=(shaped((9, lift_all, one), f32), shaped((9 * one, two), f32)),
        in_specs=[vmem] * 4,
        out_specs=(vmem, vmem),
        scratch_shapes=[pltpu.VMEM((21 * one, two), f32)],
        compiler_params=grant(16),
        cost_estimate=cost(1_000_000, 1_500_000),
        name="finish",
    )(total, core, beside, across)
    return (
        temporal_grad.reshape(temporal_weight.shape),
        middle_grad.reshape(middle_weight.shape),
        deeper_grad.reshape(deeper_weight.shape),
        deepest_grad.reshape(deepest_weight.shape),
        head_grad.reshape(four),
    )


def solution(mesh):
    return jax.shard_map(
        local,
        mesh=mesh,
        in_specs=(
            P("dp", None, "space", None),
            P("dp", "space", None),
            P(),
            P(),
            P(),
            P(),
            P(),
            P(),
        ),
        out_specs=(P(), P(), P(), P(), P()),
        check_vma=False,
    )
```

```python
import functools

import jax
import jax.numpy as jnp
from jax import lax
from jax.experimental import pallas as pl
from jax.experimental.pallas import tpu as pltpu
from jax.sharding import PartitionSpec as P

BLOCK = 8
MIB = 1 << 20


def f32_dot(left, right, contract):
    return lax.dot_general(
        left, right, ((contract[0], contract[1]), ((), ())), preferred_element_type=jnp.float32
    )


def dot_nn(left, right):
    return f32_dot(left, right, ((1,), (0,)))


def dot_nt(left, right):
    return f32_dot(left, right, ((1,), (1,)))


def dot_tn(left, right):
    return f32_dot(left, right, ((0,), (0,)))


def rounded(value):
    return value.astype(jnp.bfloat16).astype(jnp.float32)


def silu_and_slope(pre):
    gate = jax.nn.sigmoid(pre)
    return rounded(pre * gate), gate * (1.0 + pre * (1.0 - gate))


def zero_row(ref):
    ref[:, 0, 0] = jnp.zeros(ref.shape[:1] + ref.shape[3:], ref.dtype)


def last_row_zero(ref):
    ref[:, ref.shape[1] - 1] = jnp.zeros(ref.shape[:1] + ref.shape[2:], ref.dtype)


def shift_block(value, step):
    shape = value.shape
    flat = value.reshape(-1, shape[-1])
    moved = pltpu.roll(flat, step % flat.shape[0], 0)
    index = lax.broadcasted_iota(jnp.int32, flat.shape, 0) % BLOCK
    edge = 0 if step > 0 else BLOCK - 1
    return jnp.where(index == edge, 0.0, moved).reshape(shape)


def fill_map(ref, value, offset):
    n, rows, phases, _, channels = value.shape
    split = value.reshape(n, rows, phases // 2, 2, BLOCK, channels)
    for row in range(rows):
        pair, parity = divmod(row + offset, 2)
        ref[:, pair, parity, pl.ds(0, phases // 2), 1] = split[:, row, :, 0]
        ref[:, pair, parity, pl.ds(1, phases // 2), 0] = split[:, row, :, 1]
        ref[:, pair, parity, 0, 0] = shift_block(split[:, row, phases // 2 - 1, 1], 1)


def map_tap(ref, row_tap, col_tap, out_rows, out_phases):
    cells = ref[
        :,
        pl.ds(row_tap // 2, out_rows),
        row_tap % 2,
        pl.ds(col_tap // 2, out_phases),
        col_tap % 2,
    ]
    return cells.reshape(-1, cells.shape[-1]).astype(jnp.bfloat16)


def fill_delta(ref, value):
    rows, phases = value.shape[1:3]
    ref[:, pl.ds(0, rows), pl.ds(0, phases)] = value
    ref[:, pl.ds(0, rows), phases] = shift_block(value[:, :, 0], -1)


def delta_parts(ref, weight_ref, row_parity, col_parity, rows, phases):
    taps = (((1, 0),), ((2, 0), (0, 1)))
    total = None
    for row_tap, row_step in taps[row_parity]:
        for col_tap, col_step in taps[col_parity]:
            cells = ref[:, pl.ds(row_step, rows), pl.ds(col_step, phases)]
            lead = cells.shape[:-1]
            flat = cells.reshape(-1, cells.shape[-1]).astype(jnp.bfloat16)
            part = dot_nn(flat, weight_ref[3 * row_tap + col_tap])
            total = part if total is None else total + part
    return total.reshape(*lead, total.shape[-1])


def column_order(cols):
    place = lax.broadcasted_iota(jnp.int32, (cols, cols), 0)
    column = lax.broadcasted_iota(jnp.int32, (cols, cols), 1)
    source = (place % BLOCK) * (cols // BLOCK) + place // BLOCK
    return jnp.where(column == source, 1.0, 0.0).astype(jnp.bfloat16)


def band_cells(got_ref, inner, index, order, lift_ref, bits_ref, even_ref, odd_ref, rest):
    _, frames, band, cols = got_ref.shape
    phases, row_cells = cols // BLOCK, cols // 2
    height = lax.broadcasted_iota(jnp.int32, (16, cols), 0)
    for row in range(band):
        for frame in range(frames):
            line = jnp.broadcast_to(got_ref[inner, frame, pl.ds(row, 1)], height.shape)
            bit = jnp.bitwise_and(jnp.right_shift(line, height), 1)
            bits_ref[pl.ds(row * 128 + frame * 16, 16)] = bit.astype(jnp.float32).astype(
                jnp.bfloat16
            )
    spread = dot_nt(order, bits_ref[...]).astype(jnp.bfloat16)
    stacked = jnp.concatenate(
        [spread[:, row * 128 : row * 128 + 128] for row in range(band)], axis=0
    )
    lifted = jnp.maximum(dot_nn(stacked, lift_ref[...]), 0.0)
    lifted = lifted.reshape(band // 2, 2, phases // 2, 2, BLOCK, lifted.shape[-1])
    for parity, ref in ((0, even_ref), (1, odd_ref)):
        here = lifted[:, parity, :, 0]
        right = lifted[:, parity, :, 1]
        left = jnp.concatenate([shift_block(right[:, -1], 1)[:, None], right[:, :-1]], axis=1)
        taps = [part.reshape(-1, part.shape[-1]) for part in (left, here, right)]
        lane = lax.broadcasted_iota(jnp.int32, (taps[0].shape[0], 128), 1)
        tail = jnp.where(lane < rest, taps[0][:, 128:], taps[1][:, 128:])
        tail = jnp.where(lane < 2 * rest, tail, taps[2][:, 128:])
        cells = jnp.concatenate([part[:, :128] for part in taps] + [tail], axis=1)
        if index is None:
            ref[...] = cells.astype(jnp.bfloat16)
        else:
            at = pl.multiple_of((index * (band // 2) + parity) * row_cells, row_cells)
            ref[pl.ds(at, cells.shape[0])] = cells.astype(jnp.bfloat16)


def band_label(label_ref, inner, index, shape):
    lane = lax.broadcasted_iota(jnp.int32, shape, 1)
    row = lax.broadcasted_iota(jnp.int32, (shape[0], BLOCK), 0)
    column = lax.broadcasted_iota(jnp.int32, (shape[0], BLOCK), 1)
    label = jnp.broadcast_to(label_ref[inner].astype(jnp.float32), row.shape)
    label = jnp.sum(jnp.where(row == column, label, 0.0), axis=1, keepdims=True)
    return jnp.where(lane == index, label, 0.0)


def own_kernel(
    got_hbm,
    label_hbm,
    lift_hbm,
    first_w_hbm,
    second_w_hbm,
    third_w_hbm,
    fourth_w_hbm,
    even_ref,
    odd_ref,
    labels_ref,
    lift_all_ref,
    first_all_ref,
    second_w_ref,
    third_w_ref,
    fourth_w_ref,
    got_ref,
    label_ref,
    lift_ref,
    first_w_ref,
    bits_ref,
    sems,
):
    pairs = (
        (got_hbm, got_ref),
        (lift_hbm, lift_ref),
        (label_hbm, label_ref),
        (first_w_hbm, first_w_ref),
        (second_w_hbm, second_w_ref),
        (third_w_hbm, third_w_ref),
        (fourth_w_hbm, fourth_w_ref),
    )
    copies = [
        pltpu.make_async_copy(source, target, sems.at[k])
        for k, (source, target) in enumerate(pairs)
    ]
    for copy in copies:
        copy.start()
    me = lax.axis_index("space")
    _, frames, _, cols = got_ref.shape
    heights, width = lift_ref.shape
    rest = first_w_ref.shape[1] - 128
    bits_ref[...] = jnp.zeros(bits_ref.shape, jnp.bfloat16)
    first_all_ref[...] = jnp.zeros(first_all_ref.shape, jnp.bfloat16)
    order = column_order(cols)
    copies[1].wait()
    tall = jnp.concatenate(
        [lift_ref[...].astype(jnp.float32), jnp.zeros((16 - heights, width), jnp.float32)], axis=0
    )
    tall = jnp.concatenate([tall] * (256 // width), axis=1)
    tall = jnp.concatenate([tall] * 8, axis=0)
    frame_of_row = lax.broadcasted_iota(jnp.int32, tall.shape, 0) // 16
    lane = lax.broadcasted_iota(jnp.int32, tall.shape, 1)
    frame_of_lane = jnp.minimum(lane // width, frames - 1)
    keep = (frame_of_row == frame_of_lane) & (lane < 128 + 3 * rest)
    lift_all_ref[...] = jnp.where(keep, tall, 0.0).astype(jnp.bfloat16)
    copies[0].wait()
    band_cells(got_ref, 0, None, order, lift_all_ref, bits_ref, even_ref, odd_ref, rest)
    copies[2].wait()
    labels_ref[...] = band_label(label_ref, 0, me, labels_ref.shape).astype(jnp.bfloat16)
    copies[3].wait()
    for tap in range(9):
        row_tap, col_tap = divmod(tap, 3)
        first_all_ref[row_tap, pl.ds(col_tap * 128, 128)] = first_w_ref[tap, pl.ds(0, 128)]
        first_all_ref[row_tap, pl.ds(384 + col_tap * rest, rest)] = first_w_ref[
            tap, pl.ds(128, rest)
        ]
    for copy in copies[4:]:
        copy.wait()


def early_kernel(pieces, rest, *refs):
    got_refs = refs[:pieces]
    (
        lift_all_ref,
        first_all_ref,
        second_w_ref,
        own_even_ref,
        own_odd_ref,
        even_ref,
        odd_ref,
        send_ref,
        first_ref,
        first_slope_ref,
        second_slope_ref,
        bits_ref,
    ) = refs[pieces:]
    me = lax.axis_index("space")
    bands = 1 << pieces
    _, _, band, cols = got_refs[0].shape
    phases, row_cells = cols // BLOCK, cols // 2
    order = column_order(cols)
    cells = own_even_ref.shape[0]
    at = pl.multiple_of(me * cells, cells)
    even_ref[pl.ds(at, cells)] = own_even_ref[...]
    odd_ref[pl.ds(pl.multiple_of(at + row_cells, row_cells), cells)] = own_odd_ref[...]
    odd_ref[pl.ds(0, row_cells)] = jnp.zeros((row_cells, odd_ref.shape[1]), jnp.bfloat16)
    bits_ref[...] = jnp.zeros(bits_ref.shape, jnp.bfloat16)
    for slot in range(1, bands):
        piece = slot.bit_length() - 1
        inner = slot - (1 << piece)
        band_cells(
            got_refs[piece],
            inner,
            me ^ slot,
            order,
            lift_all_ref,
            bits_ref,
            even_ref,
            odd_ref,
            rest,
        )

    rows, phases = bands * band // 2, phases // 2
    cells = rows * row_cells
    pre = dot_nn(odd_ref[pl.ds(0, cells)], first_all_ref[0])
    pre += dot_nn(even_ref[...], first_all_ref[1])
    pre += dot_nn(odd_ref[pl.ds(row_cells, cells)], first_all_ref[2])
    value, slope = silu_and_slope(pre)
    shape = (1, rows, phases, BLOCK, value.shape[-1])
    zero_row(first_ref)
    fill_map(first_ref, value.reshape(shape), 1)
    first_slope_ref[...] = slope.reshape(shape)

    rows, phases = rows // 2, phases // 2
    pre = None
    for tap in range(9):
        cells = map_tap(first_ref, tap // 3, tap % 3, rows, phases)
        part = dot_nn(cells, second_w_ref[tap])
        pre = part if pre is None else pre + part
    value, slope = silu_and_slope(pre)
    second_slope_ref[...] = slope.reshape(second_slope_ref.shape)
    sent = value.shape[0]
    send_ref[pl.ds(0, sent)] = value.astype(jnp.bfloat16)
    send_ref[pl.ds(sent, 16)] = jnp.zeros((16, send_ref.shape[1]), jnp.bfloat16)


def transpose_kernel(weight_ref, out_ref):
    for tap in range(weight_ref.shape[0]):
        out_ref[tap] = weight_ref[tap].T


def take_samples(slot_refs, second_ref, label_ref, bands):
    count = sum(ref.shape[0] for ref in slot_refs)
    width = count.bit_length() - 1
    chunk = second_ref.shape[0]
    me = lax.axis_index("dp")
    where = [(ref, inner) for ref in slot_refs for inner in range(ref.shape[0])]
    for slot in range(count):
        reverse = sum(((slot >> k) & 1) << (width - 1 - k) for k in range(width))
        sample = me ^ reverse
        ref, inner = where[slot]

        def take(ref=ref, inner=inner, place=sample % chunk):
            put_sample(ref, inner, second_ref, label_ref, place, bands)

        if chunk == count:
            take()
        else:
            pl.when(sample // chunk == pl.program_id(0))(take)


def third_taps(second_ref, taps_ref, rows, phases):
    channels = second_ref.shape[-1]
    for tap in range(9):
        taps_ref[:, pl.ds(tap * channels, channels)] = map_tap(
            second_ref, tap // 3, tap % 3, rows, phases
        )


def delta_columns(ref, weight_ref, row_parity, col_parity, rows, phases):
    taps = (((1, 0),), ((2, 0), (0, 1)))
    total = None
    for row_tap, row_step in taps[row_parity]:
        for col_tap, col_step in taps[col_parity]:
            cells = ref[:, pl.ds(row_step, rows), pl.ds(col_step, phases)]
            lead = cells.shape[:-1]
            columns = cells.reshape(-1, cells.shape[-1]).T.astype(jnp.bfloat16)
            part = dot_nn(weight_ref[3 * row_tap + col_tap], columns)
            total = part if total is None else total + part
    return total.T.reshape(*lead, total.shape[0])


def put_sample(ref, inner, second_ref, label_ref, place, bands):
    rows, phases = 4 * bands, 4
    cells = rows * phases * BLOCK
    second = ref[inner, pl.ds(0, cells)].astype(jnp.float32)
    fill_map(
        second_ref.at[pl.ds(place, 1)],
        second.reshape(1, rows, phases, BLOCK, second.shape[-1]),
        1,
    )
    if label_ref is not None:
        label = ref[inner, pl.ds(cells, 16)].astype(jnp.float32)[:BLOCK]
        for index in range(bands):
            label_ref[place, index] = jnp.broadcast_to(label[:, index : index + 1], label.shape)


def deep_layers(
    batch,
    bands,
    third_w_ref,
    fourth_w_ref,
    fourth_parts,
    head_ref,
    fourth_taps_ref,
    second_ref,
    label_ref,
    third_taps_ref,
    third_ref,
    third_slope_ref,
    third_delta_ref,
    fourth_delta_ref,
):
    samples = second_ref.shape[0]
    rows, phases = 2 * bands, 2
    third_taps(second_ref, third_taps_ref, rows, phases)
    weight = third_w_ref[...].reshape(third_taps_ref.shape[1], -1)
    value, slope = silu_and_slope(dot_nn(third_taps_ref[...], weight))
    channels = value.shape[-1]
    zero_row(third_ref)
    fill_map(third_ref, value.reshape(samples, rows, phases, BLOCK, channels), 1)
    third_slope_ref[...] = slope.reshape(third_slope_ref.shape)

    rows, phases = rows // 2, phases // 2
    for tap in range(9):
        fourth_taps_ref[:, pl.ds(tap * channels, channels)] = map_tap(
            third_ref, tap // 3, tap % 3, rows, phases
        )
    weight = fourth_w_ref[...].reshape(fourth_taps_ref.shape[1], -1)
    value, slope = silu_and_slope(dot_nn(fourth_taps_ref[...], weight))
    head = head_ref[...].astype(jnp.float32)
    labels = label_ref[...].reshape(-1, label_ref.shape[-1])[:, :1]
    logits = jnp.sum(value * head, axis=1, keepdims=True)
    logit_grad = (jax.nn.sigmoid(logits) - labels) / batch
    delta = rounded(logit_grad * head * slope)
    last_row_zero(fourth_delta_ref)
    fill_delta(fourth_delta_ref, delta.reshape(samples, rows, phases, BLOCK, delta.shape[-1]))
    for row_parity in range(2):
        for col_parity in range(2):
            part = fourth_parts(fourth_delta_ref, row_parity, col_parity, rows, phases)
            part = rounded(part * third_slope_ref[:, :, row_parity, :, col_parity])
            for row in range(rows):
                third_delta_ref[:, 2 * row + row_parity, col_parity] = part[:, row, 0]
    return value, logit_grad, delta


def deep_kernel(
    batch,
    bands,
    stored,
    near_ref,
    far_ref,
    last_ref,
    third_w_ref,
    fourth_w_ref,
    fourth_wt_ref,
    head_ref,
    fourth_taps_ref,
    fourth_flat_ref,
    head_grad_ref,
    *refs,
):
    if stored:
        third_taps_ref, third_flat_ref, second_ref, label_ref = refs[:4]
    else:
        third_grad_ref, second_ref, label_ref, third_taps_ref = refs[:4]
    third_ref, third_slope_ref, third_delta_ref, fourth_delta_ref = refs[4:]
    zero_row(second_ref)
    take_samples((near_ref, far_ref, last_ref), second_ref, label_ref, bands)
    value, logit_grad, delta = deep_layers(
        batch,
        bands,
        third_w_ref,
        fourth_w_ref,
        lambda ref, *where: delta_parts(ref, fourth_wt_ref, *where),
        head_ref,
        fourth_taps_ref,
        second_ref,
        label_ref,
        third_taps_ref,
        third_ref,
        third_slope_ref,
        third_delta_ref,
        fourth_delta_ref,
    )

    head_grad = jnp.sum(value * logit_grad, axis=0, keepdims=True)
    add_to(head_grad_ref, head_grad, stored)
    fourth_flat_ref[...] = delta.astype(jnp.bfloat16)
    delta = third_delta_ref[...]
    delta = delta.reshape(-1, delta.shape[-1]).astype(jnp.bfloat16)
    if stored:
        third_flat_ref[...] = delta
    else:
        third_grad_kernel(third_taps_ref, delta, third_grad_ref, False)


def local_kernel(
    batch,
    bands,
    payload_ref,
    third_w_ref,
    fourth_w_ref,
    head_ref,
    second_w_ref,
    even_ref,
    odd_ref,
    first_ref,
    first_slope_ref,
    second_slope_ref,
    *refs,
):
    keep_ref, pass_ref = refs[:2]
    third_ref, second_ref, first_delta_ref, flat_ref, second_map_ref, label_ref = refs[2:8]
    fourth_taps_ref = refs[8]
    third_delta_ref = refs[12]
    zero_row(second_map_ref)
    put_sample(payload_ref, 0, second_map_ref, label_ref, 0, bands)
    deep_layers(
        batch,
        bands,
        third_w_ref,
        fourth_w_ref,
        lambda ref, *where: delta_columns(ref, fourth_w_ref, *where),
        head_ref,
        fourth_taps_ref,
        second_map_ref,
        label_ref,
        *refs[9:14],
    )
    sample = lax.axis_index("dp")
    _, rows, phases, _, _ = third_delta_ref.shape
    fill_delta(third_ref, third_delta_ref[...])
    last_row_zero(third_ref)
    last_row_zero(second_ref)
    for row_parity in range(2):
        for col_parity in range(2):
            part = delta_columns(third_ref, third_w_ref, row_parity, col_parity, rows, phases)
            for row in range(rows):
                for phase in range(phases):
                    at = (slice(None), 2 * row + row_parity, 2 * phase + col_parity)
                    second_ref[at] = rounded(part[:, row, phase] * second_slope_ref[at])
    rows, phases = 2 * rows, 2 * phases
    second_ref[:, :, phases] = shift_block(second_ref[:, :, 0], -1)
    for row_parity in range(2):
        for col_parity in range(2):
            part = delta_columns(second_ref, second_w_ref, row_parity, col_parity, rows, phases)
            for row in range(rows):
                for phase in range(phases):
                    at = (slice(None), 2 * row + row_parity, 2 * phase + col_parity)
                    first_delta_ref[at] = rounded(part[:, row, phase] * first_slope_ref[at])
    delta = second_ref[:, pl.ds(0, rows), pl.ds(0, phases)]
    delta = delta.reshape(-1, delta.shape[-1]).astype(jnp.bfloat16)
    depth = first_ref.shape[-1]
    for tap in range(9):
        cells = map_tap(first_ref, tap // 3, tap % 3, rows, phases)
        flat_ref[pl.ds((12 + tap) * depth, depth)] = dot_tn(cells, delta)
    delta = first_delta_ref[...]
    delta = delta.reshape(-1, delta.shape[-1]).astype(jnp.bfloat16)
    cells = delta.shape[0]
    row_cells = cells // (2 * rows)
    taps = (odd_ref[pl.ds(0, cells)], even_ref[...], odd_ref[pl.ds(row_cells, cells)])
    for tap in range(3):
        part = dot_tn(delta, taps[tap])
        for piece in range(4):
            flat_ref[pl.ds((4 * tap + piece) * depth, depth)] = part[
                :, piece * 128 : piece * 128 + 128
            ]
    share = keep_ref.shape[1]
    for slot in range(4):
        at = pl.multiple_of(((sample % 4) ^ slot) * share, share)
        ref = pass_ref if slot % 2 else keep_ref
        ref[slot // 2] = flat_ref[pl.ds(at, share)].astype(jnp.bfloat16)


def add_to(ref, value, alone):
    if alone:
        ref[...] = value
    else:
        first = pl.program_id(0) == 0
        ref[...] = jnp.where(first, 0.0, ref[...]) + value


def third_grad_kernel(taps_ref, delta_ref, out_ref, alone=True):
    add_to(out_ref, dot_tn(delta_ref[...], taps_ref[...]).T, alone)


def fourth_grad_alone_kernel(fourth_taps_ref, fourth_flat_ref, out_hbm, grad_ref, sems):
    depth = grad_ref.shape[1]
    copies = []
    for tap in range(9):
        grad_ref[tap] = dot_tn(
            fourth_taps_ref[:, pl.ds(tap * depth, depth)], fourth_flat_ref[...]
        )
        copy = pltpu.make_async_copy(grad_ref.at[tap], out_hbm.at[tap], sems.at[tap])
        copy.start()
        copies.append(copy)
    for copy in copies:
        copy.wait()


def fourth_grad_kernel(fourth_taps_ref, fourth_flat_ref, out_ref):
    @pl.when(pl.program_id(1) == 0)
    def _():
        out_ref[...] = jnp.zeros(out_ref.shape, jnp.float32)

    out_ref[...] += dot_tn(fourth_taps_ref[...], fourth_flat_ref[...])


def finish_kernel(*refs):
    got_refs = refs[:4]
    temporal_ref, middle_ref, flat_ref = refs[4:]
    me = lax.axis_index("dp") % 4
    share = got_refs[0].shape[0]
    for slot in range(4):
        at = pl.multiple_of((me ^ slot) * share, share)
        flat_ref[pl.ds(at, share)] = got_refs[slot][...].astype(jnp.float32)
    depth = temporal_ref.shape[2]
    middle_ref[...] = flat_ref[pl.ds(12 * depth, 9 * depth)]
    rest = temporal_ref.shape[1] - 128
    for tap in range(3):
        parts = [flat_ref[pl.ds((4 * tap + piece) * depth, depth)].T for piece in range(4)]
        for col_tap in range(3):
            temporal_ref[3 * tap + col_tap, pl.ds(0, 128)] = parts[col_tap]
            temporal_ref[3 * tap + col_tap, pl.ds(128, rest)] = parts[3][
                col_tap * rest : col_tap * rest + rest
            ]


def cost(flops, size):
    return pl.CostEstimate(flops=flops, bytes_accessed=size, transcendentals=0)


def swapped(value, axis, bit):
    return lax.ppermute(value, axis, [(i, i ^ bit) for i in range(lax.axis_size(axis))])


def band_pieces(value, bands):
    pieces = [value]
    bit = 1
    while bit < bands:
        whole = pieces[0] if bit == 1 else jnp.concatenate(pieces, axis=0)
        pieces.append(swapped(whole, "space", bit))
        bit *= 2
    return pieces


def put(buffer, part, at):
    return lax.dynamic_update_slice(buffer, part, (at,) + (0,) * (buffer.ndim - 1))


def after(value, *others):
    return lax.optimization_barrier((value, *others))[0]


def gather_and_sum(payload, local_sums, transposed, samples):
    half, quarter = samples // 2, samples // 4
    near = put(jnp.zeros((half,) + payload.shape[1:], payload.dtype), payload, 0)
    got = swapped(payload, "dp", quarter * 2) if quarter > 1 else None
    keep, passed = local_sums()
    core = swapped(passed, "dp", 1)
    mine, theirs = added(keep[0], core[0]), added(keep[1], core[1])
    mine_beside = swapped(theirs, "dp", 2)
    weights = transposed(theirs)
    count, beside_count = 1, 0
    while count < quarter:
        near = put(near, after(got, keep), count)
        count *= 2
        if count < quarter:
            part = near[beside_count:count]
            got = swapped(near[:count], "dp", half // count)
            beside = swapped(after(part, theirs), "dp", 2)
            near = put(near, beside, quarter + beside_count)
            beside_count = count
    total = added(mine, after(mine_beside, weights))
    beside = swapped(after(near[beside_count:quarter], theirs), "dp", 2)
    early = swapped(near[: quarter + beside_count], "dp", 1)
    bit = 4
    while 2 * bit < samples:
        other = swapped(total, "dp", bit)
        beside = after(beside, total)
        total = added(total, other)
        bit *= 2
    near = put(near, beside, quarter + beside_count)
    last = swapped(beside, "dp", 1)
    return near, early, last, total, bit, weights


def added(*parts):
    total = parts[0].astype(jnp.float32)
    for part in parts[1:]:
        total = total + part.astype(jnp.float32)
    return total.astype(jnp.bfloat16)


def local(
    occupancy,
    state_labels,
    lift_weight,
    temporal_weight,
    middle_weight,
    deeper_weight,
    deepest_weight,
    head_weight,
):
    bands = lax.axis_size("space")
    samples = lax.axis_size("dp")
    _, frames, band, cols = occupancy.shape
    lift_all = frames * lift_weight.shape[1]
    one, two = middle_weight.shape[2:]
    three, four = deepest_weight.shape[2:]
    f32, bf16 = jnp.float32, jnp.bfloat16
    shaped = jax.ShapeDtypeStruct
    phases = cols // BLOCK
    rows = bands * band
    small = samples * bands <= 32
    vmem = pl.BlockSpec(memory_space=pltpu.VMEM)

    def grant(size):
        return pltpu.CompilerParams(vmem_limit_bytes=(size if small else 60) * MIB)

    lines = band_pieces(occupancy, bands)
    first_w = temporal_weight.reshape(9, lift_all, one)
    second_w = middle_weight.reshape(9, one, two)
    third_w = deeper_weight.reshape(9, two, three)
    fourth_w = deepest_weight.reshape(9, three, four)
    head = head_weight.reshape(1, four)

    sent = rows // 4 * phases // 4 * BLOCK + 16
    hbm = pl.BlockSpec(memory_space=pltpu.HBM)
    even_shape = shaped((rows // 2 * cols // 2, 512), bf16)
    odd_shape = shaped(((rows // 2 + 1) * cols // 2, 512), bf16)
    bits_scratch = pltpu.VMEM((band * 128, cols), bf16)
    own_cells = shaped((band // 2 * cols // 2, 512), bf16)
    own_args = [
        pltpu.with_memory_space_constraint(value, pltpu.HBM)
        for value in (
            occupancy,
            state_labels,
            lift_weight,
            first_w,
            second_w,
            third_w,
            fourth_w,
        )
    ]
    (
        own_even,
        own_odd,
        own_labels,
        lift_all_w,
        first_all,
        second_w2,
        third_w2,
        fourth_w2,
    ) = pl.pallas_call(
        own_kernel,
        out_shape=(
            own_cells,
            own_cells,
            shaped((16, two), bf16),
            shaped((128, 256), bf16),
            shaped((3, 512, one), bf16),
            shaped(second_w.shape, bf16),
            shaped(third_w.shape, bf16),
            shaped(fourth_w.shape, bf16),
        ),
        in_specs=[hbm] * 7,
        out_specs=(vmem,) * 8,
        scratch_shapes=[
            pltpu.VMEM(occupancy.shape, occupancy.dtype),
            pltpu.VMEM(state_labels.shape, state_labels.dtype),
            pltpu.VMEM(lift_weight.shape, bf16),
            pltpu.VMEM(first_w.shape, bf16),
            bits_scratch,
            pltpu.SemaphoreType.DMA((7,)),
        ],
        compiler_params=grant(24),
        cost_estimate=cost(100_000_000, 10_000_000),
        name="own_band",
    )(*own_args)
    pieces = len(lines) - 1
    even, odd, payload, first, first_slope, second_slope = pl.pallas_call(
        functools.partial(early_kernel, pieces, lift_all - 128),
        out_shape=(
            even_shape,
            odd_shape,
            shaped((sent, two), bf16),
            shaped((1, rows // 4 + 1, 2, phases // 4 + 1, 2, BLOCK, one), f32),
            shaped((1, rows // 2, phases // 2, BLOCK, one), f32),
            shaped((1, rows // 4, phases // 4, BLOCK, two), f32),
        ),
        in_specs=[vmem] * (pieces + 5),
        out_specs=(vmem,) * 6,
        scratch_shapes=[bits_scratch],
        compiler_params=grant(24),
        cost_estimate=cost(150_000_000, 4_000_000),
        name="early",
    )(*lines[1:], lift_all_w, first_all, second_w2, own_even, own_odd)

    labels, bit = own_labels, 1
    while bit < bands:
        labels = labels + swapped(labels, "space", bit)
        bit *= 2
    payload = put(payload, labels, sent - 16)[None]
    deep_weights = (third_w2, fourth_w2)

    third_cells = 2 * bands * 2 * BLOCK
    fourth_cells = bands * BLOCK

    def second_scratch(count):
        return pltpu.VMEM((count, 2 * bands + 1, 2, 3, 2, BLOCK, two), f32)

    def third_taps_scratch(count):
        return pltpu.VMEM((count * third_cells, 9 * two), bf16)

    def deep_scratch(count):
        return [
            third_taps_scratch(count),
            pltpu.VMEM((count, bands + 1, 2, 2, 2, BLOCK, three), f32),
            pltpu.VMEM((count, bands, 2, 1, 2, BLOCK, three), f32),
            pltpu.VMEM((count, 2 * bands, 2, BLOCK, three), f32),
            pltpu.VMEM((count, bands + 1, 2, BLOCK, four), f32),
        ]

    share = 21 * one // 4
    local_call = pl.pallas_call(
        functools.partial(local_kernel, samples, bands),
        out_shape=(shaped((2, share, two), bf16),) * 2,
        in_specs=[vmem] * 10,
        out_specs=(vmem,) * 2,
        scratch_shapes=[
            pltpu.VMEM((1, 2 * bands + 1, 3, BLOCK, three), f32),
            pltpu.VMEM((1, 4 * bands + 1, 5, BLOCK, two), f32),
            pltpu.VMEM(first_slope.shape, f32),
            pltpu.VMEM((21 * one, two), f32),
            second_scratch(1),
            pltpu.VMEM((1, bands, BLOCK, two), f32),
            pltpu.VMEM((fourth_cells, 9 * three), bf16),
        ]
        + deep_scratch(1),
        compiler_params=grant(24),
        cost_estimate=cost(300_000_000, 9_000_000),
        name="local",
    )
    maps = (head, second_w2, even, odd, first, first_slope, second_slope)
    transpose_call = pl.pallas_call(
        transpose_kernel,
        out_shape=shaped((9, four, three), bf16),
        in_specs=[vmem],
        out_specs=vmem,
        compiler_params=grant(16),
        cost_estimate=cost(10_000_000, 5_000_000),
        name="transpose",
    )

    near, far, last, total, bit, fourth_wt = gather_and_sum(
        payload,
        lambda: local_call(payload, *deep_weights, *maps),
        lambda keep: transpose_call(after(fourth_w2, keep)),
        samples,
    )
    near = after(near, total)

    chunk = max(1, min(samples, 32 // bands))
    steps = samples // chunk
    full = lambda *shape: pl.BlockSpec(shape, lambda i: (0,) * len(shape))
    grad_shape = shaped((9 * two, three), f32)
    third_shapes = (grad_shape,)
    if small:
        third_shapes = (
            shaped((samples * third_cells, 9 * two), bf16),
            shaped((samples * third_cells, three), bf16),
        )
    fourth_taps, fourth_flat, head_grad, *thirds = pl.pallas_call(
        functools.partial(deep_kernel, samples, bands, small),
        **({} if small else {"grid": (steps,)}),
        out_shape=(
            shaped((samples * fourth_cells, 9 * three), bf16),
            shaped((samples * fourth_cells, four), bf16),
            shaped((1, four), f32),
            *third_shapes,
        ),
        in_specs=[vmem] * 7 if small else [
            full(*value.shape) for value in (near, far, last, *deep_weights, fourth_wt, head)
        ],
        out_specs=(vmem,) * 5 if small else (
            pl.BlockSpec((chunk * fourth_cells, 9 * three), lambda i: (i, 0)),
            pl.BlockSpec((chunk * fourth_cells, four), lambda i: (i, 0)),
            full(1, four),
            full(9 * two, three),
        ),
        scratch_shapes=[second_scratch(chunk), pltpu.VMEM((chunk, bands, BLOCK, two), f32)]
        + deep_scratch(chunk)[1 if small else 0 :],
        compiler_params=grant(40),
        cost_estimate=cost(1_300_000_000, 12_000_000),
        name="deep",
    )(near, far, last, *deep_weights, fourth_wt, head)

    if bit < samples:
        other, fourth_flat = lax.optimization_barrier((swapped(total, "dp", bit), fourth_flat))
        total = added(total, other)
    beside = swapped(total, "dp", 2)
    core = swapped(total, "dp", 1)
    if small:
        deepest_grad = pl.pallas_call(
            fourth_grad_alone_kernel,
            out_shape=shaped((9, three, four), f32),
            in_specs=[vmem] * 2,
            out_specs=pl.BlockSpec(memory_space=pl.ANY),
            scratch_shapes=[
                pltpu.VMEM((9, three, four), f32),
                pltpu.SemaphoreType.DMA((9,)),
            ],
            compiler_params=grant(16),
            cost_estimate=cost(600_000_000, 6_000_000),
            name="fourth_grad",
        )(fourth_taps, fourth_flat)
    else:
        deepest_grad = pl.pallas_call(
            fourth_grad_kernel,
            grid=(3, steps),
            out_shape=shaped((9 * three, four), f32),
            in_specs=[
                pl.BlockSpec((chunk * fourth_cells, 3 * three), lambda t, i: (i, t)),
                pl.BlockSpec((chunk * fourth_cells, four), lambda t, i: (i, 0)),
            ],
            out_specs=pl.BlockSpec((3 * three, four), lambda t, i: (t, 0)),
            compiler_params=grant(16),
            cost_estimate=cost(600_000_000, 6_000_000),
            name="fourth_grad",
        )(fourth_taps, fourth_flat)
    beside, deepest_grad = lax.optimization_barrier((beside, deepest_grad))
    across = swapped(beside, "dp", 1)
    if small:
        deeper_grad = pl.pallas_call(
            third_grad_kernel,
            out_shape=grad_shape,
            in_specs=[vmem] * 2,
            out_specs=vmem,
            compiler_params=grant(24),
            cost_estimate=cost(600_000_000, 4_000_000),
            name="third_grad",
        )(*thirds)
    else:
        deeper_grad = thirds[0]
    across, deeper_grad = lax.optimization_barrier((across, deeper_grad))
    temporal_grad, middle_grad = pl.pallas_call(
        finish_kernel,
        out_shape=(shaped((9, lift_all, one), f32), shaped((9 * one, two), f32)),
        in_specs=[vmem] * 4,
        out_specs=(vmem, vmem),
        scratch_shapes=[pltpu.VMEM((21 * one, two), f32)],
        compiler_params=grant(16),
        cost_estimate=cost(1_000_000, 1_500_000),
        name="finish",
    )(total, core, beside, across)
    return (
        temporal_grad.reshape(temporal_weight.shape),
        middle_grad.reshape(middle_weight.shape),
        deeper_grad.reshape(deeper_weight.shape),
        deepest_grad.reshape(deepest_weight.shape),
        head_grad.reshape(four),
    )


def solution(mesh):
    return jax.shard_map(
        local,
        mesh=mesh,
        in_specs=(
            P("dp", None, "space", None),
            P("dp", "space", None),
            P(),
            P(),
            P(),
            P(),
            P(),
            P(),
        ),
        out_specs=(P(), P(), P(), P(), P()),
        check_vma=False,
    )
```

```python
import functools

import jax
import jax.numpy as jnp
from jax import lax
from jax.experimental import pallas as pl
from jax.experimental.pallas import tpu as pltpu
from jax.sharding import PartitionSpec as P

BLOCK = 8
LABEL_BIT = 13
MIB = 1 << 20


def f32_dot(left, right, contract):
    return lax.dot_general(
        left, right, ((contract[0], contract[1]), ((), ())), preferred_element_type=jnp.float32
    )


def dot_nn(left, right):
    return f32_dot(left, right, ((1,), (0,)))


def dot_nt(left, right):
    return f32_dot(left, right, ((1,), (1,)))


def dot_tn(left, right):
    return f32_dot(left, right, ((0,), (0,)))


def rounded(value):
    return value.astype(jnp.bfloat16).astype(jnp.float32)


def sigmoid(value):
    below = 1.0 + jnp.exp(jnp.minimum(-value, 80.0))
    guess = pl.reciprocal(below, approx=True)
    return guess * (2.0 - below * guess)


def silu_and_slope(pre):
    gate = sigmoid(pre)
    value = pre * gate
    return rounded(value), gate + value * (1.0 - gate)


def zero_row(ref):
    ref[:, 0, 0] = jnp.zeros(ref.shape[:1] + ref.shape[3:], ref.dtype)


def last_row_zero(ref):
    ref[:, ref.shape[1] - 1] = jnp.zeros(ref.shape[:1] + ref.shape[2:], ref.dtype)


def shift_block(value, step):
    shape = value.shape
    flat = value.reshape(-1, shape[-1])
    moved = pltpu.roll(flat, step % flat.shape[0], 0)
    index = lax.broadcasted_iota(jnp.int32, flat.shape, 0) % BLOCK
    edge = 0 if step > 0 else BLOCK - 1
    return jnp.where(index == edge, 0.0, moved).reshape(shape)


def fill_map(ref, value, offset):
    n, rows, phases, _, channels = value.shape
    split = value.reshape(n, rows, phases // 2, 2, BLOCK, channels)
    for row in range(rows):
        pair, parity = divmod(row + offset, 2)
        ref[:, pair, parity, pl.ds(0, phases // 2), 1] = split[:, row, :, 0]
        ref[:, pair, parity, pl.ds(1, phases // 2), 0] = split[:, row, :, 1]
        ref[:, pair, parity, 0, 0] = shift_block(split[:, row, phases // 2 - 1, 1], 1)


def map_tap(ref, row_tap, col_tap, out_rows, out_phases):
    cells = ref[
        :,
        pl.ds(row_tap // 2, out_rows),
        row_tap % 2,
        pl.ds(col_tap // 2, out_phases),
        col_tap % 2,
    ]
    return cells.reshape(-1, cells.shape[-1]).astype(jnp.bfloat16)


def fill_delta(ref, value):
    rows, phases = value.shape[1:3]
    ref[:, pl.ds(0, rows), pl.ds(0, phases)] = value
    ref[:, pl.ds(0, rows), phases] = shift_block(value[:, :, 0], -1)


def delta_parts(ref, weight_ref, row_parity, col_parity, rows, phases):
    taps = (((1, 0),), ((2, 0), (0, 1)))
    total = None
    for row_tap, row_step in taps[row_parity]:
        for col_tap, col_step in taps[col_parity]:
            cells = ref[:, pl.ds(row_step, rows), pl.ds(col_step, phases)]
            lead = cells.shape[:-1]
            flat = cells.reshape(-1, cells.shape[-1]).astype(jnp.bfloat16)
            part = dot_nn(flat, weight_ref[3 * row_tap + col_tap])
            total = part if total is None else total + part
    return total.reshape(*lead, total.shape[-1])


def column_order(cols):
    place = lax.broadcasted_iota(jnp.int32, (cols, cols), 0)
    column = lax.broadcasted_iota(jnp.int32, (cols, cols), 1)
    source = (place % BLOCK) * (cols // BLOCK) + place // BLOCK
    return jnp.where(column == source, 1.0, 0.0).astype(jnp.bfloat16)


def band_cells(
    got_ref, inner, index, label_lane, order, lift_ref, bits_ref, even_ref, odd_ref, rest
):
    _, frames, band, cols = got_ref.shape
    phases, row_cells = cols // BLOCK, cols // 2
    height = lax.broadcasted_iota(jnp.int32, (16, cols), 0)
    for row in range(band):
        for frame in range(frames):
            line = jnp.broadcast_to(got_ref[inner, frame, pl.ds(row, 1)], height.shape)
            bit = jnp.bitwise_and(jnp.right_shift(line, height), 1)
            bits_ref[pl.ds(row * 128 + frame * 16, 16)] = bit.astype(jnp.float32).astype(
                jnp.bfloat16
            )
    spread = dot_nt(order, bits_ref[...]).astype(jnp.bfloat16)
    line = jnp.broadcast_to(got_ref[inner, 0, pl.ds(0, 1)], height.shape)
    line = jnp.bitwise_and(jnp.right_shift(line, LABEL_BIT), 1).astype(jnp.float32)
    lane = lax.broadcasted_iota(jnp.int32, line.shape, 1)
    row = lax.broadcasted_iota(jnp.int32, line.shape, 0)
    label = jnp.sum(jnp.where(row == lane, line, 0.0), axis=1, keepdims=True)
    label = jnp.where(lane == label_lane, label, 0.0)
    stacked = jnp.concatenate(
        [spread[:, row * 128 : row * 128 + 128] for row in range(band)], axis=0
    )
    lifted = jnp.maximum(dot_nn(stacked, lift_ref[...]), 0.0)
    lifted = lifted.reshape(band // 2, 2, phases // 2, 2, BLOCK, lifted.shape[-1])
    for parity, ref in ((0, even_ref), (1, odd_ref)):
        here = lifted[:, parity, :, 0]
        right = lifted[:, parity, :, 1]
        left = jnp.concatenate([shift_block(right[:, -1], 1)[:, None], right[:, :-1]], axis=1)
        taps = [part.reshape(-1, part.shape[-1]) for part in (left, here, right)]
        lane = lax.broadcasted_iota(jnp.int32, (taps[0].shape[0], 128), 1)
        tail = jnp.where(lane < rest, taps[0][:, 128:], taps[1][:, 128:])
        tail = jnp.where(lane < 2 * rest, tail, taps[2][:, 128:])
        cells = jnp.concatenate([part[:, :128] for part in taps] + [tail], axis=1)
        if index is None:
            ref[...] = cells.astype(jnp.bfloat16)
        else:
            at = pl.multiple_of((index * (band // 2) + parity) * row_cells, row_cells)
            ref[pl.ds(at, cells.shape[0])] = cells.astype(jnp.bfloat16)
    return label


def own_kernel(
    got_ref,
    lift_hbm,
    first_w_hbm,
    second_w_hbm,
    even_ref,
    odd_ref,
    labels_ref,
    lift_all_ref,
    first_all_ref,
    second_w_ref,
    lift_ref,
    first_w_ref,
    bits_ref,
    sems,
):
    pairs = (
        (lift_hbm, lift_ref),
        (first_w_hbm, first_w_ref),
        (second_w_hbm, second_w_ref),
    )
    copies = [
        pltpu.make_async_copy(source, target, sems.at[k])
        for k, (source, target) in enumerate(pairs)
    ]
    for copy in copies:
        copy.start()
    me = lax.axis_index("space")
    _, frames, _, cols = got_ref.shape
    heights, width = lift_ref.shape
    rest = first_w_ref.shape[1] - 128
    bits_ref[...] = jnp.zeros(bits_ref.shape, jnp.bfloat16)
    first_all_ref[...] = jnp.zeros(first_all_ref.shape, jnp.bfloat16)
    order = column_order(cols)
    copies[0].wait()
    tall = jnp.concatenate(
        [lift_ref[...].astype(jnp.float32), jnp.zeros((16 - heights, width), jnp.float32)], axis=0
    )
    tall = jnp.concatenate([tall] * (256 // width), axis=1)
    tall = jnp.concatenate([tall] * 8, axis=0)
    frame_of_row = lax.broadcasted_iota(jnp.int32, tall.shape, 0) // 16
    lane = lax.broadcasted_iota(jnp.int32, tall.shape, 1)
    frame_of_lane = jnp.minimum(lane // width, frames - 1)
    keep = (frame_of_row == frame_of_lane) & (lane < 128 + 3 * rest)
    lift_all_ref[...] = jnp.where(keep, tall, 0.0).astype(jnp.bfloat16)
    labels_ref[...] = band_cells(
        got_ref, 0, None, me, order, lift_all_ref, bits_ref, even_ref, odd_ref, rest
    )
    copies[1].wait()
    for tap in range(9):
        row_tap, col_tap = divmod(tap, 3)
        first_all_ref[row_tap, pl.ds(col_tap * 128, 128)] = first_w_ref[tap, pl.ds(0, 128)]
        first_all_ref[row_tap, pl.ds(384 + col_tap * rest, rest)] = first_w_ref[
            tap, pl.ds(128, rest)
        ]
    copies[2].wait()


def early_kernel(pieces, rest, *refs):
    got_refs = refs[:pieces]
    (
        labels_ref,
        lift_all_ref,
        first_all_ref,
        second_w_ref,
        own_even_ref,
        own_odd_ref,
        third_w_hbm,
        fourth_w_hbm,
        third_w_ref,
        fourth_w_ref,
        even_ref,
        odd_ref,
        send_ref,
        first_ref,
        first_slope_ref,
        second_slope_ref,
        bits_ref,
        sems,
    ) = refs[pieces:]
    copies = [
        pltpu.make_async_copy(third_w_hbm, third_w_ref, sems.at[0]),
        pltpu.make_async_copy(fourth_w_hbm, fourth_w_ref, sems.at[1]),
    ]
    for copy in copies:
        copy.start()
    me = lax.axis_index("space")
    bands = 1 << pieces
    _, _, band, cols = got_refs[0].shape
    phases, row_cells = cols // BLOCK, cols // 2
    order = column_order(cols)
    cells = own_even_ref.shape[0]
    at = pl.multiple_of(me * cells, cells)
    even_ref[pl.ds(at, cells)] = own_even_ref[...]
    odd_ref[pl.ds(pl.multiple_of(at + row_cells, row_cells), cells)] = own_odd_ref[...]
    odd_ref[pl.ds(0, row_cells)] = jnp.zeros((row_cells, odd_ref.shape[1]), jnp.bfloat16)
    bits_ref[...] = jnp.zeros(bits_ref.shape, jnp.bfloat16)
    labels = labels_ref[...]
    for slot in range(1, bands):
        piece = slot.bit_length() - 1
        inner = slot - (1 << piece)
        labels += band_cells(
            got_refs[piece],
            inner,
            me ^ slot,
            me ^ slot,
            order,
            lift_all_ref,
            bits_ref,
            even_ref,
            odd_ref,
            rest,
        )

    rows, phases = bands * band // 2, phases // 2
    cells = rows * row_cells
    pre = dot_nn(odd_ref[pl.ds(0, cells)], first_all_ref[0])
    pre += dot_nn(even_ref[...], first_all_ref[1])
    pre += dot_nn(odd_ref[pl.ds(row_cells, cells)], first_all_ref[2])
    value, slope = silu_and_slope(pre)
    shape = (1, rows, phases, BLOCK, value.shape[-1])
    zero_row(first_ref)
    fill_map(first_ref, value.reshape(shape), 1)
    first_slope_ref[...] = slope.reshape(shape)

    rows, phases = rows // 2, phases // 2
    pre = None
    for tap in range(9):
        cells = map_tap(first_ref, tap // 3, tap % 3, rows, phases)
        part = dot_nn(cells, second_w_ref[tap])
        pre = part if pre is None else pre + part
    value, slope = silu_and_slope(pre)
    second_slope_ref[...] = slope.reshape(second_slope_ref.shape)
    sent = value.shape[0]
    send_ref[pl.ds(0, sent)] = value.astype(jnp.bfloat16)
    send_ref[pl.ds(sent, 16)] = labels.astype(jnp.bfloat16)
    for copy in copies:
        copy.wait()


def transpose_kernel(weight_ref, out_ref):
    for tap in range(weight_ref.shape[0]):
        out_ref[tap] = weight_ref[tap].T


def take_samples(slot_refs, second_ref, label_ref, bands):
    count = sum(ref.shape[0] for ref in slot_refs)
    width = count.bit_length() - 1
    chunk = second_ref.shape[0]
    me = lax.axis_index("dp")
    where = [(ref, inner) for ref in slot_refs for inner in range(ref.shape[0])]
    for slot in range(count):
        reverse = sum(((slot >> k) & 1) << (width - 1 - k) for k in range(width))
        sample = me ^ reverse
        ref, inner = where[slot]

        def take(ref=ref, inner=inner, place=sample % chunk):
            put_sample(ref, inner, second_ref, label_ref, place, bands)

        if chunk == count:
            take()
        else:
            pl.when(sample // chunk == pl.program_id(0))(take)


def third_taps(second_ref, taps_ref, rows, phases):
    channels = second_ref.shape[-1]
    for tap in range(9):
        taps_ref[:, pl.ds(tap * channels, channels)] = map_tap(
            second_ref, tap // 3, tap % 3, rows, phases
        )


def delta_columns(ref, weight_ref, row_parity, col_parity, rows, phases):
    taps = (((1, 0),), ((2, 0), (0, 1)))
    total = None
    for row_tap, row_step in taps[row_parity]:
        for col_tap, col_step in taps[col_parity]:
            cells = ref[:, pl.ds(row_step, rows), pl.ds(col_step, phases)]
            lead = cells.shape[:-1]
            columns = cells.reshape(-1, cells.shape[-1]).T.astype(jnp.bfloat16)
            part = dot_nn(weight_ref[3 * row_tap + col_tap], columns)
            total = part if total is None else total + part
    return total.T.reshape(*lead, total.shape[0])


def put_sample(ref, inner, second_ref, label_ref, place, bands):
    rows, phases = 4 * bands, 4
    cells = rows * phases * BLOCK
    second = ref[inner, pl.ds(0, cells)].astype(jnp.float32)
    fill_map(
        second_ref.at[pl.ds(place, 1)],
        second.reshape(1, rows, phases, BLOCK, second.shape[-1]),
        1,
    )
    if label_ref is not None:
        label = ref[inner, pl.ds(cells, 16)].astype(jnp.float32)[:BLOCK]
        for index in range(bands):
            label_ref[place, index] = jnp.broadcast_to(label[:, index : index + 1], label.shape)


def deep_layers(
    batch,
    bands,
    third_w_ref,
    fourth_w_ref,
    fourth_parts,
    head_ref,
    fourth_taps_ref,
    second_ref,
    label_ref,
    third_taps_ref,
    third_ref,
    third_slope_ref,
    third_delta_ref,
    fourth_delta_ref,
):
    samples = second_ref.shape[0]
    rows, phases = 2 * bands, 2
    third_taps(second_ref, third_taps_ref, rows, phases)
    weight = third_w_ref[...].reshape(third_taps_ref.shape[1], -1)
    value, slope = silu_and_slope(dot_nn(third_taps_ref[...], weight))
    channels = value.shape[-1]
    zero_row(third_ref)
    fill_map(third_ref, value.reshape(samples, rows, phases, BLOCK, channels), 1)
    third_slope_ref[...] = slope.reshape(third_slope_ref.shape)

    rows, phases = rows // 2, phases // 2
    for tap in range(9):
        fourth_taps_ref[:, pl.ds(tap * channels, channels)] = map_tap(
            third_ref, tap // 3, tap % 3, rows, phases
        )
    weight = fourth_w_ref[...].reshape(fourth_taps_ref.shape[1], -1)
    value, slope = silu_and_slope(dot_nn(fourth_taps_ref[...], weight))
    head = head_ref[...].astype(jnp.float32)
    labels = label_ref[...].reshape(-1, label_ref.shape[-1])[:, :1]
    logits = jnp.sum(value * head, axis=1, keepdims=True)
    logit_grad = (sigmoid(logits) - labels) / batch
    delta = rounded(logit_grad * head * slope)
    last_row_zero(fourth_delta_ref)
    fill_delta(fourth_delta_ref, delta.reshape(samples, rows, phases, BLOCK, delta.shape[-1]))
    for row_parity in range(2):
        for col_parity in range(2):
            part = fourth_parts(fourth_delta_ref, row_parity, col_parity, rows, phases)
            part = rounded(part * third_slope_ref[:, :, row_parity, :, col_parity])
            for row in range(rows):
                third_delta_ref[:, 2 * row + row_parity, col_parity] = part[:, row, 0]
    return value, logit_grad, delta


def deep_kernel(
    batch,
    bands,
    stored,
    near_ref,
    far_ref,
    last_ref,
    third_w_ref,
    fourth_w_ref,
    fourth_wt_ref,
    head_ref,
    fourth_taps_ref,
    fourth_flat_ref,
    head_grad_ref,
    *refs,
):
    if stored:
        third_taps_ref, third_flat_ref, second_ref, label_ref = refs[:4]
    else:
        third_grad_ref, second_ref, label_ref, third_taps_ref = refs[:4]
    third_ref, third_slope_ref, third_delta_ref, fourth_delta_ref = refs[4:]
    zero_row(second_ref)
    take_samples((near_ref, far_ref, last_ref), second_ref, label_ref, bands)
    value, logit_grad, delta = deep_layers(
        batch,
        bands,
        third_w_ref,
        fourth_w_ref,
        lambda ref, *where: delta_parts(ref, fourth_wt_ref, *where),
        head_ref,
        fourth_taps_ref,
        second_ref,
        label_ref,
        third_taps_ref,
        third_ref,
        third_slope_ref,
        third_delta_ref,
        fourth_delta_ref,
    )

    head_grad = jnp.sum(value * logit_grad, axis=0, keepdims=True)
    add_to(head_grad_ref, head_grad, stored)
    fourth_flat_ref[...] = delta.astype(jnp.bfloat16)
    delta = third_delta_ref[...]
    delta = delta.reshape(-1, delta.shape[-1]).astype(jnp.bfloat16)
    if stored:
        third_flat_ref[...] = delta
    else:
        third_grad_kernel(third_taps_ref, delta, third_grad_ref, False)


def local_kernel(
    batch,
    bands,
    payload_ref,
    third_w_ref,
    fourth_w_ref,
    head_ref,
    second_w_ref,
    even_ref,
    odd_ref,
    first_ref,
    first_slope_ref,
    second_slope_ref,
    *refs,
):
    keep_ref, pass_ref = refs[:2]
    third_ref, second_ref, first_delta_ref, flat_ref, second_map_ref, label_ref = refs[2:8]
    fourth_taps_ref = refs[8]
    third_delta_ref = refs[12]
    zero_row(second_map_ref)
    put_sample(payload_ref, 0, second_map_ref, label_ref, 0, bands)
    deep_layers(
        batch,
        bands,
        third_w_ref,
        fourth_w_ref,
        lambda ref, *where: delta_columns(ref, fourth_w_ref, *where),
        head_ref,
        fourth_taps_ref,
        second_map_ref,
        label_ref,
        *refs[9:14],
    )
    sample = lax.axis_index("dp")
    _, rows, phases, _, _ = third_delta_ref.shape
    fill_delta(third_ref, third_delta_ref[...])
    last_row_zero(third_ref)
    last_row_zero(second_ref)
    for row_parity in range(2):
        for col_parity in range(2):
            part = delta_columns(third_ref, third_w_ref, row_parity, col_parity, rows, phases)
            for row in range(rows):
                for phase in range(phases):
                    at = (slice(None), 2 * row + row_parity, 2 * phase + col_parity)
                    second_ref[at] = rounded(part[:, row, phase] * second_slope_ref[at])
    rows, phases = 2 * rows, 2 * phases
    second_ref[:, :, phases] = shift_block(second_ref[:, :, 0], -1)
    for row_parity in range(2):
        for col_parity in range(2):
            part = delta_columns(second_ref, second_w_ref, row_parity, col_parity, rows, phases)
            for row in range(rows):
                for phase in range(phases):
                    at = (slice(None), 2 * row + row_parity, 2 * phase + col_parity)
                    first_delta_ref[at] = rounded(part[:, row, phase] * first_slope_ref[at])
    delta = second_ref[:, pl.ds(0, rows), pl.ds(0, phases)]
    delta = delta.reshape(-1, delta.shape[-1]).astype(jnp.bfloat16)
    depth = first_ref.shape[-1]
    for tap in range(9):
        cells = map_tap(first_ref, tap // 3, tap % 3, rows, phases)
        flat_ref[pl.ds((12 + tap) * depth, depth)] = dot_tn(cells, delta)
    delta = first_delta_ref[...]
    delta = delta.reshape(-1, delta.shape[-1]).astype(jnp.bfloat16)
    cells = delta.shape[0]
    row_cells = cells // (2 * rows)
    taps = (odd_ref[pl.ds(0, cells)], even_ref[...], odd_ref[pl.ds(row_cells, cells)])
    for tap in range(3):
        part = dot_tn(delta, taps[tap])
        for piece in range(4):
            flat_ref[pl.ds((4 * tap + piece) * depth, depth)] = part[
                :, piece * 128 : piece * 128 + 128
            ]
    share = keep_ref.shape[1]
    for slot in range(4):
        at = pl.multiple_of(((sample % 4) ^ slot) * share, share)
        ref = pass_ref if slot % 2 else keep_ref
        ref[slot // 2] = flat_ref[pl.ds(at, share)].astype(jnp.bfloat16)


def add_to(ref, value, alone):
    if alone:
        ref[...] = value
    else:
        first = pl.program_id(0) == 0
        ref[...] = jnp.where(first, 0.0, ref[...]) + value


def third_grad_kernel(taps_ref, delta_ref, out_ref, alone=True):
    add_to(out_ref, dot_tn(delta_ref[...], taps_ref[...]).T, alone)


def fourth_grad_alone_kernel(fourth_taps_ref, fourth_flat_ref, out_hbm, grad_ref, sems):
    depth = grad_ref.shape[1]
    copies = []
    for tap in range(9):
        grad_ref[tap] = dot_tn(
            fourth_taps_ref[:, pl.ds(tap * depth, depth)], fourth_flat_ref[...]
        )
        copy = pltpu.make_async_copy(grad_ref.at[tap], out_hbm.at[tap], sems.at[tap])
        copy.start()
        copies.append(copy)
    for copy in copies:
        copy.wait()


def fourth_grad_kernel(fourth_taps_ref, fourth_flat_ref, out_ref):
    @pl.when(pl.program_id(1) == 0)
    def _():
        out_ref[...] = jnp.zeros(out_ref.shape, jnp.float32)

    out_ref[...] += dot_tn(fourth_taps_ref[...], fourth_flat_ref[...])


def finish_kernel(*refs):
    got_refs = refs[:4]
    temporal_ref, middle_ref, flat_ref = refs[4:]
    me = lax.axis_index("dp") % 4
    share = got_refs[0].shape[0]
    for slot in range(4):
        at = pl.multiple_of((me ^ slot) * share, share)
        flat_ref[pl.ds(at, share)] = got_refs[slot][...].astype(jnp.float32)
    depth = temporal_ref.shape[2]
    middle_ref[...] = flat_ref[pl.ds(12 * depth, 9 * depth)]
    rest = temporal_ref.shape[1] - 128
    for tap in range(3):
        parts = [flat_ref[pl.ds((4 * tap + piece) * depth, depth)].T for piece in range(4)]
        for col_tap in range(3):
            temporal_ref[3 * tap + col_tap, pl.ds(0, 128)] = parts[col_tap]
            temporal_ref[3 * tap + col_tap, pl.ds(128, rest)] = parts[3][
                col_tap * rest : col_tap * rest + rest
            ]


def cost(flops, size):
    return pl.CostEstimate(flops=flops, bytes_accessed=size, transcendentals=0)


def swapped(value, axis, bit):
    return lax.ppermute(value, axis, [(i, i ^ bit) for i in range(lax.axis_size(axis))])


def band_pieces(value, bands):
    pieces = [value]
    bit = 1
    while bit < bands:
        whole = pieces[0] if bit == 1 else jnp.concatenate(pieces, axis=0)
        pieces.append(swapped(whole, "space", bit))
        bit *= 2
    return pieces


def put(buffer, part, at):
    return lax.dynamic_update_slice(buffer, part, (at,) + (0,) * (buffer.ndim - 1))


def after(value, *others):
    return lax.optimization_barrier((value, *others))[0]


def gather_and_sum(payload, local_sums, transposed, samples):
    half, quarter = samples // 2, samples // 4
    near = put(jnp.zeros((half,) + payload.shape[1:], payload.dtype), payload, 0)
    got = swapped(payload, "dp", quarter * 2) if quarter > 1 else None
    keep, passed = local_sums()
    core = swapped(passed, "dp", 1)
    mine, theirs = added(keep[0], core[0]), added(keep[1], core[1])
    mine_beside = swapped(theirs, "dp", 2)
    weights = transposed(theirs)
    count, beside_count = 1, 0
    while count < quarter:
        near = put(near, after(got, keep), count)
        count *= 2
        if count < quarter:
            part = near[beside_count:count]
            got = swapped(near[:count], "dp", half // count)
            beside = swapped(after(part, theirs), "dp", 2)
            near = put(near, beside, quarter + beside_count)
            beside_count = count
    total = added(mine, after(mine_beside, weights))
    beside = swapped(after(near[beside_count:quarter], theirs), "dp", 2)
    early = swapped(near[: quarter + beside_count], "dp", 1)
    bit = 4
    while 2 * bit < samples:
        other = swapped(total, "dp", bit)
        beside = after(beside, total)
        total = added(total, other)
        bit *= 2
    near = put(near, beside, quarter + beside_count)
    last = swapped(beside, "dp", 1)
    return near, early, last, total, bit, weights


def added(*parts):
    total = parts[0].astype(jnp.float32)
    for part in parts[1:]:
        total = total + part.astype(jnp.float32)
    return total.astype(jnp.bfloat16)


def local(
    occupancy,
    state_labels,
    lift_weight,
    temporal_weight,
    middle_weight,
    deeper_weight,
    deepest_weight,
    head_weight,
):
    bands = lax.axis_size("space")
    samples = lax.axis_size("dp")
    _, frames, band, cols = occupancy.shape
    lift_all = frames * lift_weight.shape[1]
    one, two = middle_weight.shape[2:]
    three, four = deepest_weight.shape[2:]
    f32, bf16 = jnp.float32, jnp.bfloat16
    shaped = jax.ShapeDtypeStruct
    phases = cols // BLOCK
    rows = bands * band
    small = samples * bands <= 32
    vmem = pl.BlockSpec(memory_space=pltpu.VMEM)

    def grant(size):
        return pltpu.CompilerParams(vmem_limit_bytes=(size if small else 60) * MIB)

    marks = lax.pad(
        state_labels[:, :, None, :],
        jnp.zeros((), jnp.int32),
        ((0, 0, 0), (0, frames - 1, 0), (0, band - 1, 0), (0, cols - BLOCK, 0)),
    )
    lines = band_pieces(occupancy + (marks << LABEL_BIT), bands)
    first_w = temporal_weight.reshape(9, lift_all, one)
    second_w = middle_weight.reshape(9, one, two)
    third_w = deeper_weight.reshape(9, two, three)
    fourth_w = deepest_weight.reshape(9, three, four)
    head = head_weight.reshape(1, four)

    sent = rows // 4 * phases // 4 * BLOCK + 16
    hbm = pl.BlockSpec(memory_space=pltpu.HBM)
    even_shape = shaped((rows // 2 * cols // 2, 512), bf16)
    odd_shape = shaped(((rows // 2 + 1) * cols // 2, 512), bf16)
    bits_scratch = pltpu.VMEM((band * 128, cols), bf16)
    own_cells = shaped((band // 2 * cols // 2, 512), bf16)
    own_args = [
        pltpu.with_memory_space_constraint(value, pltpu.HBM)
        for value in (
            lift_weight,
            first_w,
            second_w,
        )
    ]
    (
        own_even,
        own_odd,
        own_labels,
        lift_all_w,
        first_all,
        second_w2,
    ) = pl.pallas_call(
        own_kernel,
        out_shape=(
            own_cells,
            own_cells,
            shaped((16, two), f32),
            shaped((128, 256), bf16),
            shaped((3, 512, one), bf16),
            shaped(second_w.shape, bf16),
        ),
        in_specs=[vmem] + [hbm] * 3,
        out_specs=(vmem,) * 6,
        scratch_shapes=[
            pltpu.VMEM(lift_weight.shape, bf16),
            pltpu.VMEM(first_w.shape, bf16),
            bits_scratch,
            pltpu.SemaphoreType.DMA((3,)),
        ],
        compiler_params=grant(24),
        cost_estimate=cost(100_000_000, 10_000_000),
        name="own_band",
    )(lines[0], *own_args)
    pieces = len(lines) - 1
    third_w2, fourth_w2, even, odd, payload, first, first_slope, second_slope = pl.pallas_call(
        functools.partial(early_kernel, pieces, lift_all - 128),
        out_shape=(
            shaped(third_w.shape, bf16),
            shaped(fourth_w.shape, bf16),
            even_shape,
            odd_shape,
            shaped((sent, two), bf16),
            shaped((1, rows // 4 + 1, 2, phases // 4 + 1, 2, BLOCK, one), f32),
            shaped((1, rows // 2, phases // 2, BLOCK, one), f32),
            shaped((1, rows // 4, phases // 4, BLOCK, two), f32),
        ),
        in_specs=[vmem] * (pieces + 6) + [hbm] * 2,
        out_specs=(vmem,) * 8,
        scratch_shapes=[bits_scratch, pltpu.SemaphoreType.DMA((2,))],
        compiler_params=grant(24),
        cost_estimate=cost(150_000_000, 4_000_000),
        name="early",
    )(
        *lines[1:],
        own_labels,
        lift_all_w,
        first_all,
        second_w2,
        own_even,
        own_odd,
        pltpu.with_memory_space_constraint(third_w, pltpu.HBM),
        pltpu.with_memory_space_constraint(fourth_w, pltpu.HBM),
    )

    payload = payload[None]
    deep_weights = (third_w2, fourth_w2)

    third_cells = 2 * bands * 2 * BLOCK
    fourth_cells = bands * BLOCK

    def second_scratch(count):
        return pltpu.VMEM((count, 2 * bands + 1, 2, 3, 2, BLOCK, two), f32)

    def third_taps_scratch(count):
        return pltpu.VMEM((count * third_cells, 9 * two), bf16)

    def deep_scratch(count):
        return [
            third_taps_scratch(count),
            pltpu.VMEM((count, bands + 1, 2, 2, 2, BLOCK, three), f32),
            pltpu.VMEM((count, bands, 2, 1, 2, BLOCK, three), f32),
            pltpu.VMEM((count, 2 * bands, 2, BLOCK, three), f32),
            pltpu.VMEM((count, bands + 1, 2, BLOCK, four), f32),
        ]

    share = 21 * one // 4
    local_call = pl.pallas_call(
        functools.partial(local_kernel, samples, bands),
        out_shape=(shaped((2, share, two), bf16),) * 2,
        in_specs=[vmem] * 10,
        out_specs=(vmem,) * 2,
        scratch_shapes=[
            pltpu.VMEM((1, 2 * bands + 1, 3, BLOCK, three), f32),
            pltpu.VMEM((1, 4 * bands + 1, 5, BLOCK, two), f32),
            pltpu.VMEM(first_slope.shape, f32),
            pltpu.VMEM((21 * one, two), f32),
            second_scratch(1),
            pltpu.VMEM((1, bands, BLOCK, two), f32),
            pltpu.VMEM((fourth_cells, 9 * three), bf16),
        ]
        + deep_scratch(1),
        compiler_params=grant(24),
        cost_estimate=cost(300_000_000, 9_000_000),
        name="local",
    )
    maps = (head, second_w2, even, odd, first, first_slope, second_slope)
    transpose_call = pl.pallas_call(
        transpose_kernel,
        out_shape=shaped((9, four, three), bf16),
        in_specs=[vmem],
        out_specs=vmem,
        compiler_params=grant(16),
        cost_estimate=cost(10_000_000, 5_000_000),
        name="transpose",
    )

    near, far, last, total, bit, fourth_wt = gather_and_sum(
        payload,
        lambda: local_call(payload, *deep_weights, *maps),
        lambda keep: transpose_call(after(fourth_w2, keep)),
        samples,
    )
    near = after(near, total)

    chunk = max(1, min(samples, 32 // bands))
    steps = samples // chunk
    full = lambda *shape: pl.BlockSpec(shape, lambda i: (0,) * len(shape))
    grad_shape = shaped((9 * two, three), f32)
    third_shapes = (grad_shape,)
    if small:
        third_shapes = (
            shaped((samples * third_cells, 9 * two), bf16),
            shaped((samples * third_cells, three), bf16),
        )
    fourth_taps, fourth_flat, head_grad, *thirds = pl.pallas_call(
        functools.partial(deep_kernel, samples, bands, small),
        **({} if small else {"grid": (steps,)}),
        out_shape=(
            shaped((samples * fourth_cells, 9 * three), bf16),
            shaped((samples * fourth_cells, four), bf16),
            shaped((1, four), f32),
            *third_shapes,
        ),
        in_specs=[vmem] * 7 if small else [
            full(*value.shape) for value in (near, far, last, *deep_weights, fourth_wt, head)
        ],
        out_specs=(vmem,) * 5 if small else (
            pl.BlockSpec((chunk * fourth_cells, 9 * three), lambda i: (i, 0)),
            pl.BlockSpec((chunk * fourth_cells, four), lambda i: (i, 0)),
            full(1, four),
            full(9 * two, three),
        ),
        scratch_shapes=[second_scratch(chunk), pltpu.VMEM((chunk, bands, BLOCK, two), f32)]
        + deep_scratch(chunk)[1 if small else 0 :],
        compiler_params=grant(40),
        cost_estimate=cost(1_300_000_000, 12_000_000),
        name="deep",
    )(near, far, last, *deep_weights, fourth_wt, head)

    if bit < samples:
        other, fourth_flat = lax.optimization_barrier((swapped(total, "dp", bit), fourth_flat))
        total = added(total, other)
    beside = swapped(total, "dp", 2)
    core = swapped(total, "dp", 1)
    if small:
        deepest_grad = pl.pallas_call(
            fourth_grad_alone_kernel,
            out_shape=shaped((9, three, four), f32),
            in_specs=[vmem] * 2,
            out_specs=pl.BlockSpec(memory_space=pl.ANY),
            scratch_shapes=[
                pltpu.VMEM((9, three, four), f32),
                pltpu.SemaphoreType.DMA((9,)),
            ],
            compiler_params=grant(16),
            cost_estimate=cost(600_000_000, 6_000_000),
            name="fourth_grad",
        )(fourth_taps, fourth_flat)
    else:
        deepest_grad = pl.pallas_call(
            fourth_grad_kernel,
            grid=(3, steps),
            out_shape=shaped((9 * three, four), f32),
            in_specs=[
                pl.BlockSpec((chunk * fourth_cells, 3 * three), lambda t, i: (i, t)),
                pl.BlockSpec((chunk * fourth_cells, four), lambda t, i: (i, 0)),
            ],
            out_specs=pl.BlockSpec((3 * three, four), lambda t, i: (t, 0)),
            compiler_params=grant(16),
            cost_estimate=cost(600_000_000, 6_000_000),
            name="fourth_grad",
        )(fourth_taps, fourth_flat)
    beside, deepest_grad = lax.optimization_barrier((beside, deepest_grad))
    across = swapped(beside, "dp", 1)
    if small:
        deeper_grad = pl.pallas_call(
            third_grad_kernel,
            out_shape=grad_shape,
            in_specs=[vmem] * 2,
            out_specs=vmem,
            compiler_params=grant(24),
            cost_estimate=cost(600_000_000, 4_000_000),
            name="third_grad",
        )(*thirds)
    else:
        deeper_grad = thirds[0]
    across, deeper_grad = lax.optimization_barrier((across, deeper_grad))
    temporal_grad, middle_grad = pl.pallas_call(
        finish_kernel,
        out_shape=(shaped((9, lift_all, one), f32), shaped((9 * one, two), f32)),
        in_specs=[vmem] * 4,
        out_specs=(vmem, vmem),
        scratch_shapes=[pltpu.VMEM((21 * one, two), f32)],
        compiler_params=grant(16),
        cost_estimate=cost(1_000_000, 1_500_000),
        name="finish",
    )(total, core, beside, across)
    return (
        temporal_grad.reshape(temporal_weight.shape),
        middle_grad.reshape(middle_weight.shape),
        deeper_grad.reshape(deeper_weight.shape),
        deepest_grad.reshape(deepest_weight.shape),
        head_grad.reshape(four),
    )


def solution(mesh):
    return jax.shard_map(
        local,
        mesh=mesh,
        in_specs=(
            P("dp", None, "space", None),
            P("dp", "space", None),
            P(),
            P(),
            P(),
            P(),
            P(),
            P(),
        ),
        out_specs=(P(), P(), P(), P(), P()),
        check_vma=False,
    )
```

```python
import functools

import jax
import jax.numpy as jnp
from jax import lax
from jax.experimental import pallas as pl
from jax.experimental.pallas import tpu as pltpu
from jax.sharding import PartitionSpec as P

BLOCK = 8
MIB = 1 << 20


def f32_dot(left, right, contract):
    return lax.dot_general(
        left, right, ((contract[0], contract[1]), ((), ())), preferred_element_type=jnp.float32
    )


def dot_nn(left, right):
    return f32_dot(left, right, ((1,), (0,)))


def dot_nt(left, right):
    return f32_dot(left, right, ((1,), (1,)))


def dot_tn(left, right):
    return f32_dot(left, right, ((0,), (0,)))


def rounded(value):
    return value.astype(jnp.bfloat16).astype(jnp.float32)


def silu_and_slope(pre):
    gate = jax.nn.sigmoid(pre)
    return rounded(pre * gate), gate * (1.0 + pre * (1.0 - gate))


def zero_row(ref):
    ref[:, 0, 0] = jnp.zeros(ref.shape[:1] + ref.shape[3:], ref.dtype)


def last_row_zero(ref):
    ref[:, ref.shape[1] - 1] = jnp.zeros(ref.shape[:1] + ref.shape[2:], ref.dtype)


def shift_block(value, step):
    shape = value.shape
    flat = value.reshape(-1, shape[-1])
    moved = pltpu.roll(flat, step % flat.shape[0], 0)
    index = lax.broadcasted_iota(jnp.int32, flat.shape, 0) % BLOCK
    edge = 0 if step > 0 else BLOCK - 1
    return jnp.where(index == edge, 0.0, moved).reshape(shape)


def fill_map(ref, value, offset):
    n, rows, phases, _, channels = value.shape
    split = value.reshape(n, rows, phases // 2, 2, BLOCK, channels)
    for row in range(rows):
        pair, parity = divmod(row + offset, 2)
        ref[:, pair, parity, pl.ds(0, phases // 2), 1] = split[:, row, :, 0]
        ref[:, pair, parity, pl.ds(1, phases // 2), 0] = split[:, row, :, 1]
        ref[:, pair, parity, 0, 0] = shift_block(split[:, row, phases // 2 - 1, 1], 1)


def map_tap(ref, row_tap, col_tap, out_rows, out_phases):
    cells = ref[
        :,
        pl.ds(row_tap // 2, out_rows),
        row_tap % 2,
        pl.ds(col_tap // 2, out_phases),
        col_tap % 2,
    ]
    return cells.reshape(-1, cells.shape[-1]).astype(jnp.bfloat16)


def fill_delta(ref, value):
    rows, phases = value.shape[1:3]
    ref[:, pl.ds(0, rows), pl.ds(0, phases)] = value
    ref[:, pl.ds(0, rows), phases] = shift_block(value[:, :, 0], -1)


def delta_parts(ref, weight_ref, row_parity, col_parity, rows, phases):
    taps = (((1, 0),), ((2, 0), (0, 1)))
    total = None
    for row_tap, row_step in taps[row_parity]:
        for col_tap, col_step in taps[col_parity]:
            cells = ref[:, pl.ds(row_step, rows), pl.ds(col_step, phases)]
            lead = cells.shape[:-1]
            flat = cells.reshape(-1, cells.shape[-1]).astype(jnp.bfloat16)
            part = dot_nn(flat, weight_ref[3 * row_tap + col_tap])
            total = part if total is None else total + part
    return total.reshape(*lead, total.shape[-1])


def column_order(cols):
    place = lax.broadcasted_iota(jnp.int32, (cols, cols), 0)
    column = lax.broadcasted_iota(jnp.int32, (cols, cols), 1)
    source = (place % BLOCK) * (cols // BLOCK) + place // BLOCK
    return jnp.where(column == source, 1.0, 0.0).astype(jnp.bfloat16)


def band_cells(got_ref, inner, index, order, lift_ref, bits_ref, even_ref, odd_ref, rest):
    _, frames, band, cols = got_ref.shape
    phases, row_cells = cols // BLOCK, cols // 2
    height = lax.broadcasted_iota(jnp.int32, (16, cols), 0)
    for row in range(band):
        for frame in range(frames):
            line = jnp.broadcast_to(got_ref[inner, frame, pl.ds(row, 1)], height.shape)
            bit = jnp.bitwise_and(jnp.right_shift(line, height), 1)
            bits_ref[pl.ds(row * 128 + frame * 16, 16)] = bit.astype(jnp.float32).astype(
                jnp.bfloat16
            )
    spread = dot_nt(order, bits_ref[...]).astype(jnp.bfloat16)
    stacked = jnp.concatenate(
        [spread[:, row * 128 : row * 128 + 128] for row in range(band)], axis=0
    )
    lifted = jnp.maximum(dot_nn(stacked, lift_ref[...]), 0.0)
    lifted = lifted.reshape(band // 2, 2, phases // 2, 2, BLOCK, lifted.shape[-1])
    for parity, ref in ((0, even_ref), (1, odd_ref)):
        here = lifted[:, parity, :, 0]
        right = lifted[:, parity, :, 1]
        left = jnp.concatenate([shift_block(right[:, -1], 1)[:, None], right[:, :-1]], axis=1)
        taps = [part.reshape(-1, part.shape[-1]) for part in (left, here, right)]
        lane = lax.broadcasted_iota(jnp.int32, (taps[0].shape[0], 128), 1)
        tail = jnp.where(lane < rest, taps[0][:, 128:], taps[1][:, 128:])
        tail = jnp.where(lane < 2 * rest, tail, taps[2][:, 128:])
        cells = jnp.concatenate([part[:, :128] for part in taps] + [tail], axis=1)
        if index is None:
            ref[...] = cells.astype(jnp.bfloat16)
        else:
            at = pl.multiple_of((index * (band // 2) + parity) * row_cells, row_cells)
            ref[pl.ds(at, cells.shape[0])] = cells.astype(jnp.bfloat16)


def band_label(label_ref, inner, index, shape):
    lane = lax.broadcasted_iota(jnp.int32, shape, 1)
    row = lax.broadcasted_iota(jnp.int32, (shape[0], BLOCK), 0)
    column = lax.broadcasted_iota(jnp.int32, (shape[0], BLOCK), 1)
    label = jnp.broadcast_to(label_ref[inner].astype(jnp.float32), row.shape)
    label = jnp.sum(jnp.where(row == column, label, 0.0), axis=1, keepdims=True)
    return jnp.where(lane == index, label, 0.0)


def own_kernel(
    got_hbm,
    label_hbm,
    lift_hbm,
    first_w_hbm,
    second_w_hbm,
    third_w_hbm,
    fourth_w_hbm,
    even_ref,
    odd_ref,
    labels_ref,
    lift_all_ref,
    first_all_ref,
    second_w_ref,
    third_w_ref,
    fourth_w_ref,
    got_ref,
    label_ref,
    lift_ref,
    first_w_ref,
    bits_ref,
    sems,
):
    pairs = (
        (got_hbm, got_ref),
        (lift_hbm, lift_ref),
        (label_hbm, label_ref),
        (first_w_hbm, first_w_ref),
        (second_w_hbm, second_w_ref),
        (third_w_hbm, third_w_ref),
        (fourth_w_hbm, fourth_w_ref),
    )
    copies = [
        pltpu.make_async_copy(source, target, sems.at[k])
        for k, (source, target) in enumerate(pairs)
    ]
    for copy in copies:
        copy.start()
    me = lax.axis_index("space")
    _, frames, _, cols = got_ref.shape
    heights, width = lift_ref.shape
    rest = first_w_ref.shape[1] - 128
    bits_ref[...] = jnp.zeros(bits_ref.shape, jnp.bfloat16)
    first_all_ref[...] = jnp.zeros(first_all_ref.shape, jnp.bfloat16)
    order = column_order(cols)
    copies[1].wait()
    tall = jnp.concatenate(
        [lift_ref[...].astype(jnp.float32), jnp.zeros((16 - heights, width), jnp.float32)], axis=0
    )
    tall = jnp.concatenate([tall] * (256 // width), axis=1)
    tall = jnp.concatenate([tall] * 8, axis=0)
    frame_of_row = lax.broadcasted_iota(jnp.int32, tall.shape, 0) // 16
    lane = lax.broadcasted_iota(jnp.int32, tall.shape, 1)
    frame_of_lane = jnp.minimum(lane // width, frames - 1)
    keep = (frame_of_row == frame_of_lane) & (lane < 128 + 3 * rest)
    lift_all_ref[...] = jnp.where(keep, tall, 0.0).astype(jnp.bfloat16)
    copies[0].wait()
    band_cells(got_ref, 0, None, order, lift_all_ref, bits_ref, even_ref, odd_ref, rest)
    copies[2].wait()
    labels_ref[...] = band_label(label_ref, 0, me, labels_ref.shape).astype(jnp.bfloat16)
    copies[3].wait()
    for tap in range(9):
        row_tap, col_tap = divmod(tap, 3)
        first_all_ref[row_tap, pl.ds(col_tap * 128, 128)] = first_w_ref[tap, pl.ds(0, 128)]
        first_all_ref[row_tap, pl.ds(384 + col_tap * rest, rest)] = first_w_ref[
            tap, pl.ds(128, rest)
        ]
    for copy in copies[4:]:
        copy.wait()


def early_kernel(pieces, rest, *refs):
    got_refs = refs[:pieces]
    (
        lift_all_ref,
        first_all_ref,
        second_w_ref,
        own_even_ref,
        own_odd_ref,
        even_ref,
        odd_ref,
        send_ref,
        first_ref,
        first_slope_ref,
        second_slope_ref,
        bits_ref,
    ) = refs[pieces:]
    me = lax.axis_index("space")
    bands = 1 << pieces
    _, _, band, cols = got_refs[0].shape
    phases, row_cells = cols // BLOCK, cols // 2
    order = column_order(cols)
    cells = own_even_ref.shape[0]
    at = pl.multiple_of(me * cells, cells)
    even_ref[pl.ds(at, cells)] = own_even_ref[...]
    odd_ref[pl.ds(pl.multiple_of(at + row_cells, row_cells), cells)] = own_odd_ref[...]
    odd_ref[pl.ds(0, row_cells)] = jnp.zeros((row_cells, odd_ref.shape[1]), jnp.bfloat16)
    bits_ref[...] = jnp.zeros(bits_ref.shape, jnp.bfloat16)
    for slot in range(1, bands):
        piece = slot.bit_length() - 1
        inner = slot - (1 << piece)
        band_cells(
            got_refs[piece],
            inner,
            me ^ slot,
            order,
            lift_all_ref,
            bits_ref,
            even_ref,
            odd_ref,
            rest,
        )

    rows, phases = bands * band // 2, phases // 2
    cells = rows * row_cells
    pre = dot_nn(odd_ref[pl.ds(0, cells)], first_all_ref[0])
    pre += dot_nn(even_ref[...], first_all_ref[1])
    pre += dot_nn(odd_ref[pl.ds(row_cells, cells)], first_all_ref[2])
    value, slope = silu_and_slope(pre)
    shape = (1, rows, phases, BLOCK, value.shape[-1])
    zero_row(first_ref)
    fill_map(first_ref, value.reshape(shape), 1)
    first_slope_ref[...] = slope.reshape(shape)

    rows, phases = rows // 2, phases // 2
    pre = None
    for tap in range(9):
        cells = map_tap(first_ref, tap // 3, tap % 3, rows, phases)
        part = dot_nn(cells, second_w_ref[tap])
        pre = part if pre is None else pre + part
    value, slope = silu_and_slope(pre)
    second_slope_ref[...] = slope.reshape(second_slope_ref.shape)
    sent = value.shape[0]
    send_ref[pl.ds(0, sent)] = value.astype(jnp.bfloat16)
    send_ref[pl.ds(sent, 16)] = jnp.zeros((16, send_ref.shape[1]), jnp.bfloat16)


def transpose_kernel(weight_ref, out_ref):
    for tap in range(weight_ref.shape[0]):
        out_ref[tap] = weight_ref[tap].T


def take_samples(slot_refs, second_ref, label_ref, bands):
    count = sum(ref.shape[0] for ref in slot_refs)
    width = count.bit_length() - 1
    chunk = second_ref.shape[0]
    me = lax.axis_index("dp")
    where = [(ref, inner) for ref in slot_refs for inner in range(ref.shape[0])]
    for slot in range(count):
        reverse = sum(((slot >> k) & 1) << (width - 1 - k) for k in range(width))
        sample = me ^ reverse
        ref, inner = where[slot]

        def take(ref=ref, inner=inner, place=sample % chunk):
            put_sample(ref, inner, second_ref, label_ref, place, bands)

        if chunk == count:
            take()
        else:
            pl.when(sample // chunk == pl.program_id(0))(take)


def third_taps(second_ref, taps_ref, rows, phases):
    channels = second_ref.shape[-1]
    for tap in range(9):
        taps_ref[:, pl.ds(tap * channels, channels)] = map_tap(
            second_ref, tap // 3, tap % 3, rows, phases
        )


def delta_columns(ref, weight_ref, row_parity, col_parity, rows, phases):
    taps = (((1, 0),), ((2, 0), (0, 1)))
    total = None
    for row_tap, row_step in taps[row_parity]:
        for col_tap, col_step in taps[col_parity]:
            cells = ref[:, pl.ds(row_step, rows), pl.ds(col_step, phases)]
            lead = cells.shape[:-1]
            columns = cells.reshape(-1, cells.shape[-1]).T.astype(jnp.bfloat16)
            part = dot_nn(weight_ref[3 * row_tap + col_tap], columns)
            total = part if total is None else total + part
    return total.T.reshape(*lead, total.shape[0])


def put_label(ref, inner, label_ref, place, bands):
    cells = 4 * bands * 4 * BLOCK
    label = ref[inner, pl.ds(cells, 16)].astype(jnp.float32)[:BLOCK]
    for index in range(bands):
        label_ref[place, index] = jnp.broadcast_to(label[:, index : index + 1], label.shape)


def put_sample(ref, inner, second_ref, label_ref, place, bands):
    rows, phases = 4 * bands, 4
    cells = rows * phases * BLOCK
    second = ref[inner, pl.ds(0, cells)].astype(jnp.float32)
    fill_map(
        second_ref.at[pl.ds(place, 1)],
        second.reshape(1, rows, phases, BLOCK, second.shape[-1]),
        1,
    )
    if label_ref is not None:
        put_label(ref, inner, label_ref, place, bands)


def deep_layers(
    batch,
    bands,
    third_w_ref,
    fourth_w_ref,
    fourth_parts,
    head_ref,
    fourth_taps_ref,
    second_ref,
    label_ref,
    third_taps_ref,
    third_ref,
    third_slope_ref,
    third_delta_ref,
    fourth_delta_ref,
):
    value, slope = third_layer(second_ref, third_w_ref, third_taps_ref, bands)
    zero_row(third_ref)
    fill_map(third_ref, value, 1)
    third_slope_ref[...] = slope.reshape(third_slope_ref.shape)
    return deeper_layers(
        batch,
        bands,
        fourth_w_ref,
        fourth_parts,
        head_ref,
        fourth_taps_ref,
        label_ref,
        third_ref,
        third_slope_ref,
        third_delta_ref,
        fourth_delta_ref,
    )


def third_layer(second_ref, third_w_ref, third_taps_ref, bands):
    rows, phases = 2 * bands, 2
    third_taps(second_ref, third_taps_ref, rows, phases)
    weight = third_w_ref[...].reshape(third_taps_ref.shape[1], -1)
    value, slope = silu_and_slope(dot_nn(third_taps_ref[...], weight))
    shape = (second_ref.shape[0], rows, phases, BLOCK, value.shape[-1])
    return value.reshape(shape), slope.reshape(shape)


def deeper_layers(
    batch,
    bands,
    fourth_w_ref,
    fourth_parts,
    head_ref,
    fourth_taps_ref,
    label_ref,
    third_ref,
    third_slope_ref,
    third_delta_ref,
    fourth_delta_ref,
):
    samples, channels = third_ref.shape[0], third_ref.shape[-1]
    rows, phases = bands, 1
    for tap in range(9):
        fourth_taps_ref[:, pl.ds(tap * channels, channels)] = map_tap(
            third_ref, tap // 3, tap % 3, rows, phases
        )
    weight = fourth_w_ref[...].reshape(fourth_taps_ref.shape[1], -1)
    value, slope = silu_and_slope(dot_nn(fourth_taps_ref[...], weight))
    head = head_ref[...].astype(jnp.float32)
    labels = label_ref[...].reshape(-1, label_ref.shape[-1])[:, :1]
    logits = jnp.sum(value * head, axis=1, keepdims=True)
    logit_grad = (jax.nn.sigmoid(logits) - labels) / batch
    delta = rounded(logit_grad * head * slope)
    last_row_zero(fourth_delta_ref)
    fill_delta(fourth_delta_ref, delta.reshape(samples, rows, phases, BLOCK, delta.shape[-1]))
    for row_parity in range(2):
        for col_parity in range(2):
            part = fourth_parts(fourth_delta_ref, row_parity, col_parity, rows, phases)
            part = rounded(part * third_slope_ref[:, :, row_parity, :, col_parity])
            for row in range(rows):
                third_delta_ref[:, 2 * row + row_parity, col_parity] = part[:, row, 0]
    return value, logit_grad, delta


def near_kernel(bands, near_ref, third_w_ref, taps_ref, map_ref, slope_ref, second_ref):
    zero_row(second_ref)
    for slot in range(near_ref.shape[0]):
        put_sample(near_ref, slot, second_ref, None, slot, bands)
    value, slope = third_layer(second_ref, third_w_ref, taps_ref, bands)
    map_ref[...] = value
    slope_ref[...] = slope


def far_kernel(
    batch,
    bands,
    near_ref,
    far_ref,
    last_ref,
    near_taps_ref,
    near_map_ref,
    near_slope_ref,
    third_w_ref,
    fourth_w_ref,
    fourth_wt_ref,
    head_ref,
    fourth_taps_ref,
    fourth_flat_ref,
    head_grad_ref,
    third_taps_ref,
    third_flat_ref,
    second_ref,
    far_taps_ref,
    label_ref,
    third_ref,
    third_slope_ref,
    third_delta_ref,
    fourth_delta_ref,
):
    half, early = near_ref.shape[0], far_ref.shape[0]
    zero_row(second_ref)
    for slot in range(half):
        ref, inner = (far_ref, slot) if slot < early else (last_ref, slot - early)
        put_sample(ref, inner, second_ref, None, slot, bands)
    value, slope = third_layer(second_ref, third_w_ref, far_taps_ref, bands)
    cells = far_taps_ref.shape[0] // half
    width = half.bit_length()
    me = lax.axis_index("dp")
    zero_row(third_ref)
    for slot in range(2 * half):
        place = me ^ sum(((slot >> k) & 1) << (width - 1 - k) for k in range(width))
        inner = slot % half
        at = pl.ds(pl.multiple_of(place * cells, cells), cells)
        one = pl.ds(place, 1)
        if slot < half:
            third_taps_ref[at] = near_taps_ref[pl.ds(inner * cells, cells)]
            fill_map(third_ref.at[one], near_map_ref[pl.ds(inner, 1)], 1)
            third_slope_ref[one] = near_slope_ref[pl.ds(inner, 1)].reshape(
                (1,) + third_slope_ref.shape[1:]
            )
            put_label(near_ref, inner, label_ref, place, bands)
        else:
            third_taps_ref[at] = far_taps_ref[pl.ds(inner * cells, cells)]
            fill_map(third_ref.at[one], value[inner : inner + 1], 1)
            third_slope_ref[one] = slope[inner : inner + 1].reshape(
                (1,) + third_slope_ref.shape[1:]
            )
            ref, inner = (far_ref, inner) if inner < early else (last_ref, inner - early)
            put_label(ref, inner, label_ref, place, bands)
    value, logit_grad, delta = deeper_layers(
        batch,
        bands,
        fourth_w_ref,
        lambda ref, *where: delta_parts(ref, fourth_wt_ref, *where),
        head_ref,
        fourth_taps_ref,
        label_ref,
        third_ref,
        third_slope_ref,
        third_delta_ref,
        fourth_delta_ref,
    )
    head_grad_ref[...] = jnp.sum(value * logit_grad, axis=0, keepdims=True)
    fourth_flat_ref[...] = delta.astype(jnp.bfloat16)
    delta = third_delta_ref[...]
    third_flat_ref[...] = delta.reshape(-1, delta.shape[-1]).astype(jnp.bfloat16)


def deep_kernel(
    batch,
    bands,
    near_ref,
    far_ref,
    last_ref,
    third_w_ref,
    fourth_w_ref,
    fourth_wt_ref,
    head_ref,
    fourth_taps_ref,
    fourth_flat_ref,
    head_grad_ref,
    *refs,
):
    third_grad_ref, second_ref, label_ref, third_taps_ref = refs[:4]
    third_ref, third_slope_ref, third_delta_ref, fourth_delta_ref = refs[4:]
    zero_row(second_ref)
    take_samples((near_ref, far_ref, last_ref), second_ref, label_ref, bands)
    value, logit_grad, delta = deep_layers(
        batch,
        bands,
        third_w_ref,
        fourth_w_ref,
        lambda ref, *where: delta_parts(ref, fourth_wt_ref, *where),
        head_ref,
        fourth_taps_ref,
        second_ref,
        label_ref,
        third_taps_ref,
        third_ref,
        third_slope_ref,
        third_delta_ref,
        fourth_delta_ref,
    )

    head_grad = jnp.sum(value * logit_grad, axis=0, keepdims=True)
    add_to(head_grad_ref, head_grad)
    fourth_flat_ref[...] = delta.astype(jnp.bfloat16)
    delta = third_delta_ref[...]
    delta = delta.reshape(-1, delta.shape[-1]).astype(jnp.bfloat16)
    add_to(third_grad_ref, dot_tn(delta, third_taps_ref[...]).T)


def local_kernel(
    batch,
    bands,
    payload_ref,
    third_w_ref,
    fourth_w_ref,
    head_ref,
    second_w_ref,
    even_ref,
    odd_ref,
    first_ref,
    first_slope_ref,
    second_slope_ref,
    *refs,
):
    keep_ref, pass_ref = refs[:2]
    third_ref, second_ref, first_delta_ref, flat_ref, second_map_ref, label_ref = refs[2:8]
    fourth_taps_ref = refs[8]
    third_delta_ref = refs[12]
    zero_row(second_map_ref)
    put_sample(payload_ref, 0, second_map_ref, label_ref, 0, bands)
    deep_layers(
        batch,
        bands,
        third_w_ref,
        fourth_w_ref,
        lambda ref, *where: delta_columns(ref, fourth_w_ref, *where),
        head_ref,
        fourth_taps_ref,
        second_map_ref,
        label_ref,
        *refs[9:14],
    )
    sample = lax.axis_index("dp")
    _, rows, phases, _, _ = third_delta_ref.shape
    fill_delta(third_ref, third_delta_ref[...])
    last_row_zero(third_ref)
    last_row_zero(second_ref)
    for row_parity in range(2):
        for col_parity in range(2):
            part = delta_columns(third_ref, third_w_ref, row_parity, col_parity, rows, phases)
            for row in range(rows):
                for phase in range(phases):
                    at = (slice(None), 2 * row + row_parity, 2 * phase + col_parity)
                    second_ref[at] = rounded(part[:, row, phase] * second_slope_ref[at])
    rows, phases = 2 * rows, 2 * phases
    second_ref[:, :, phases] = shift_block(second_ref[:, :, 0], -1)
    for row_parity in range(2):
        for col_parity in range(2):
            part = delta_columns(second_ref, second_w_ref, row_parity, col_parity, rows, phases)
            for row in range(rows):
                for phase in range(phases):
                    at = (slice(None), 2 * row + row_parity, 2 * phase + col_parity)
                    first_delta_ref[at] = rounded(part[:, row, phase] * first_slope_ref[at])
    delta = second_ref[:, pl.ds(0, rows), pl.ds(0, phases)]
    delta = delta.reshape(-1, delta.shape[-1]).astype(jnp.bfloat16)
    depth = first_ref.shape[-1]
    for tap in range(9):
        cells = map_tap(first_ref, tap // 3, tap % 3, rows, phases)
        flat_ref[pl.ds((12 + tap) * depth, depth)] = dot_tn(cells, delta)
    delta = first_delta_ref[...]
    delta = delta.reshape(-1, delta.shape[-1]).astype(jnp.bfloat16)
    cells = delta.shape[0]
    row_cells = cells // (2 * rows)
    taps = (odd_ref[pl.ds(0, cells)], even_ref[...], odd_ref[pl.ds(row_cells, cells)])
    for tap in range(3):
        part = dot_tn(delta, taps[tap])
        for piece in range(4):
            flat_ref[pl.ds((4 * tap + piece) * depth, depth)] = part[
                :, piece * 128 : piece * 128 + 128
            ]
    share = keep_ref.shape[1]
    for slot in range(4):
        at = pl.multiple_of(((sample % 4) ^ slot) * share, share)
        ref = pass_ref if slot % 2 else keep_ref
        ref[slot // 2] = flat_ref[pl.ds(at, share)].astype(jnp.bfloat16)


def add_to(ref, value):
    first = pl.program_id(0) == 0
    ref[...] = jnp.where(first, 0.0, ref[...]) + value


def third_grad_kernel(taps_ref, delta_ref, out_ref):
    out_ref[...] = dot_tn(delta_ref[...], taps_ref[...]).T


def fourth_grad_alone_kernel(fourth_taps_ref, fourth_flat_ref, out_hbm, grad_ref, sems):
    depth = grad_ref.shape[1]
    copies = []
    for tap in range(9):
        grad_ref[tap] = dot_tn(
            fourth_taps_ref[:, pl.ds(tap * depth, depth)], fourth_flat_ref[...]
        )
        copy = pltpu.make_async_copy(grad_ref.at[tap], out_hbm.at[tap], sems.at[tap])
        copy.start()
        copies.append(copy)
    for copy in copies:
        copy.wait()


def fourth_grad_kernel(fourth_taps_ref, fourth_flat_ref, out_ref):
    @pl.when(pl.program_id(1) == 0)
    def _():
        out_ref[...] = jnp.zeros(out_ref.shape, jnp.float32)

    out_ref[...] += dot_tn(fourth_taps_ref[...], fourth_flat_ref[...])


def finish_kernel(*refs):
    got_refs = refs[:4]
    temporal_ref, middle_ref, flat_ref = refs[4:]
    me = lax.axis_index("dp") % 4
    share = got_refs[0].shape[0]
    for slot in range(4):
        at = pl.multiple_of((me ^ slot) * share, share)
        flat_ref[pl.ds(at, share)] = got_refs[slot][...].astype(jnp.float32)
    depth = temporal_ref.shape[2]
    middle_ref[...] = flat_ref[pl.ds(12 * depth, 9 * depth)]
    rest = temporal_ref.shape[1] - 128
    for tap in range(3):
        parts = [flat_ref[pl.ds((4 * tap + piece) * depth, depth)].T for piece in range(4)]
        for col_tap in range(3):
            temporal_ref[3 * tap + col_tap, pl.ds(0, 128)] = parts[col_tap]
            temporal_ref[3 * tap + col_tap, pl.ds(128, rest)] = parts[3][
                col_tap * rest : col_tap * rest + rest
            ]


def cost(flops, size):
    return pl.CostEstimate(flops=flops, bytes_accessed=size, transcendentals=0)


def swapped(value, axis, bit):
    return lax.ppermute(value, axis, [(i, i ^ bit) for i in range(lax.axis_size(axis))])


def band_pieces(value, bands):
    pieces = [value]
    bit = 1
    while bit < bands:
        whole = pieces[0] if bit == 1 else jnp.concatenate(pieces, axis=0)
        pieces.append(swapped(whole, "space", bit))
        bit *= 2
    return pieces


def put(buffer, part, at):
    return lax.dynamic_update_slice(buffer, part, (at,) + (0,) * (buffer.ndim - 1))


def after(value, *others):
    return lax.optimization_barrier((value, *others))[0]


def gather_and_sum(payload, local_sums, transposed, samples):
    half, quarter = samples // 2, samples // 4
    near = put(jnp.zeros((half,) + payload.shape[1:], payload.dtype), payload, 0)
    got = swapped(payload, "dp", quarter * 2) if quarter > 1 else None
    keep, passed = local_sums()
    core = swapped(passed, "dp", 1)
    mine, theirs = added(keep[0], core[0]), added(keep[1], core[1])
    mine_beside = swapped(theirs, "dp", 2)
    weights = transposed(theirs)
    count, beside_count = 1, 0
    while count < quarter:
        near = put(near, after(got, keep), count)
        count *= 2
        if count < quarter:
            part = near[beside_count:count]
            got = swapped(near[:count], "dp", half // count)
            beside = swapped(after(part, theirs), "dp", 2)
            near = put(near, beside, quarter + beside_count)
            beside_count = count
    total = added(mine, after(mine_beside, weights))
    beside = swapped(after(near[beside_count:quarter], total), "dp", 2)
    early = swapped(near[: quarter + beside_count], "dp", 1)
    bit = 4
    while 2 * bit < samples:
        total = added(total, swapped(total, "dp", bit))
        beside = after(beside, total)
        bit *= 2
    near = put(near, beside, quarter + beside_count)
    last = swapped(beside, "dp", 1)
    return near, early, last, total, bit, weights


def added(*parts):
    total = parts[0].astype(jnp.float32)
    for part in parts[1:]:
        total = total + part.astype(jnp.float32)
    return total.astype(jnp.bfloat16)


def local(
    occupancy,
    state_labels,
    lift_weight,
    temporal_weight,
    middle_weight,
    deeper_weight,
    deepest_weight,
    head_weight,
):
    bands = lax.axis_size("space")
    samples = lax.axis_size("dp")
    _, frames, band, cols = occupancy.shape
    lift_all = frames * lift_weight.shape[1]
    one, two = middle_weight.shape[2:]
    three, four = deepest_weight.shape[2:]
    f32, bf16 = jnp.float32, jnp.bfloat16
    shaped = jax.ShapeDtypeStruct
    phases = cols // BLOCK
    rows = bands * band
    small = samples * bands <= 32
    vmem = pl.BlockSpec(memory_space=pltpu.VMEM)

    def grant(size):
        return pltpu.CompilerParams(vmem_limit_bytes=(size if small else 60) * MIB)

    lines = band_pieces(occupancy, bands)
    first_w = temporal_weight.reshape(9, lift_all, one)
    second_w = middle_weight.reshape(9, one, two)
    third_w = deeper_weight.reshape(9, two, three)
    fourth_w = deepest_weight.reshape(9, three, four)
    head = head_weight.reshape(1, four)

    sent = rows // 4 * phases // 4 * BLOCK + 16
    hbm = pl.BlockSpec(memory_space=pltpu.HBM)
    even_shape = shaped((rows // 2 * cols // 2, 512), bf16)
    odd_shape = shaped(((rows // 2 + 1) * cols // 2, 512), bf16)
    bits_scratch = pltpu.VMEM((band * 128, cols), bf16)
    own_cells = shaped((band // 2 * cols // 2, 512), bf16)
    own_args = [
        pltpu.with_memory_space_constraint(value, pltpu.HBM)
        for value in (
            occupancy,
            state_labels,
            lift_weight,
            first_w,
            second_w,
            third_w,
            fourth_w,
        )
    ]
    (
        own_even,
        own_odd,
        own_labels,
        lift_all_w,
        first_all,
        second_w2,
        third_w2,
        fourth_w2,
    ) = pl.pallas_call(
        own_kernel,
        out_shape=(
            own_cells,
            own_cells,
            shaped((16, two), bf16),
            shaped((128, 256), bf16),
            shaped((3, 512, one), bf16),
            shaped(second_w.shape, bf16),
            shaped(third_w.shape, bf16),
            shaped(fourth_w.shape, bf16),
        ),
        in_specs=[hbm] * 7,
        out_specs=(vmem,) * 8,
        scratch_shapes=[
            pltpu.VMEM(occupancy.shape, occupancy.dtype),
            pltpu.VMEM(state_labels.shape, state_labels.dtype),
            pltpu.VMEM(lift_weight.shape, bf16),
            pltpu.VMEM(first_w.shape, bf16),
            bits_scratch,
            pltpu.SemaphoreType.DMA((7,)),
        ],
        compiler_params=grant(24),
        cost_estimate=cost(100_000_000, 10_000_000),
        name="own_band",
    )(*own_args)
    pieces = len(lines) - 1
    even, odd, payload, first, first_slope, second_slope = pl.pallas_call(
        functools.partial(early_kernel, pieces, lift_all - 128),
        out_shape=(
            even_shape,
            odd_shape,
            shaped((sent, two), bf16),
            shaped((1, rows // 4 + 1, 2, phases // 4 + 1, 2, BLOCK, one), f32),
            shaped((1, rows // 2, phases // 2, BLOCK, one), f32),
            shaped((1, rows // 4, phases // 4, BLOCK, two), f32),
        ),
        in_specs=[vmem] * (pieces + 5),
        out_specs=(vmem,) * 6,
        scratch_shapes=[bits_scratch],
        compiler_params=grant(24),
        cost_estimate=cost(150_000_000, 4_000_000),
        name="early",
    )(*lines[1:], lift_all_w, first_all, second_w2, own_even, own_odd)

    labels, bit = own_labels, 1
    while bit < bands:
        labels = labels + swapped(labels, "space", bit)
        bit *= 2
    payload = put(payload, labels, sent - 16)[None]
    deep_weights = (third_w2, fourth_w2)

    third_cells = 2 * bands * 2 * BLOCK
    fourth_cells = bands * BLOCK

    def second_scratch(count):
        return pltpu.VMEM((count, 2 * bands + 1, 2, 3, 2, BLOCK, two), f32)

    def third_taps_scratch(count):
        return pltpu.VMEM((count * third_cells, 9 * two), bf16)

    def deep_scratch(count):
        return [
            third_taps_scratch(count),
            pltpu.VMEM((count, bands + 1, 2, 2, 2, BLOCK, three), f32),
            pltpu.VMEM((count, bands, 2, 1, 2, BLOCK, three), f32),
            pltpu.VMEM((count, 2 * bands, 2, BLOCK, three), f32),
            pltpu.VMEM((count, bands + 1, 2, BLOCK, four), f32),
        ]

    share = 21 * one // 4
    local_call = pl.pallas_call(
        functools.partial(local_kernel, samples, bands),
        out_shape=(shaped((2, share, two), bf16),) * 2,
        in_specs=[vmem] * 10,
        out_specs=(vmem,) * 2,
        scratch_shapes=[
            pltpu.VMEM((1, 2 * bands + 1, 3, BLOCK, three), f32),
            pltpu.VMEM((1, 4 * bands + 1, 5, BLOCK, two), f32),
            pltpu.VMEM(first_slope.shape, f32),
            pltpu.VMEM((21 * one, two), f32),
            second_scratch(1),
            pltpu.VMEM((1, bands, BLOCK, two), f32),
            pltpu.VMEM((fourth_cells, 9 * three), bf16),
        ]
        + deep_scratch(1),
        compiler_params=grant(24),
        cost_estimate=cost(300_000_000, 9_000_000),
        name="local",
    )
    maps = (head, second_w2, even, odd, first, first_slope, second_slope)
    transpose_call = pl.pallas_call(
        transpose_kernel,
        out_shape=shaped((9, four, three), bf16),
        in_specs=[vmem],
        out_specs=vmem,
        compiler_params=grant(16),
        cost_estimate=cost(10_000_000, 5_000_000),
        name="transpose",
    )

    near, far, last, total, bit, fourth_wt = gather_and_sum(
        payload,
        lambda: local_call(payload, *deep_weights, *maps),
        lambda keep: transpose_call(after(fourth_w2, keep)),
        samples,
    )
    near = after(near, total)

    chunk = max(1, min(samples, 32 // bands))
    steps = samples // chunk
    full = lambda *shape: pl.BlockSpec(shape, lambda i: (0,) * len(shape))
    grad_shape = shaped((9 * two, three), f32)
    fourth_shapes = (
        shaped((samples * fourth_cells, 9 * three), bf16),
        shaped((samples * fourth_cells, four), bf16),
        shaped((1, four), f32),
    )
    label_scratch = pltpu.VMEM((chunk, bands, BLOCK, two), f32)
    deep_cost = cost(1_300_000_000, 12_000_000)
    if small:
        half = samples // 2
        half_shapes = (
            shaped((half * third_cells, 9 * two), bf16),
            shaped((half, 2 * bands, 2, BLOCK, three), f32),
            shaped((half, 2 * bands, 2, BLOCK, three), f32),
        )
        near_third = pl.pallas_call(
            functools.partial(near_kernel, bands),
            out_shape=half_shapes,
            in_specs=[vmem] * 2,
            out_specs=(vmem,) * 3,
            scratch_shapes=[second_scratch(half)],
            compiler_params=grant(24),
            cost_estimate=cost(300_000_000, 4_000_000),
            name="near",
        )(near, third_w2)
        fourth_taps, fourth_flat, head_grad, *thirds = pl.pallas_call(
            functools.partial(far_kernel, samples, bands),
            out_shape=fourth_shapes
            + (
                shaped((samples * third_cells, 9 * two), bf16),
                shaped((samples * third_cells, three), bf16),
            ),
            in_specs=[vmem] * 10,
            out_specs=(vmem,) * 5,
            scratch_shapes=[second_scratch(half), third_taps_scratch(half), label_scratch]
            + deep_scratch(chunk)[1:],
            compiler_params=grant(40),
            cost_estimate=deep_cost,
            name="deep",
        )(near, far, last, *near_third, *deep_weights, fourth_wt, head)
        deeper_grad = None
    else:
        fourth_taps, fourth_flat, head_grad, deeper_grad = pl.pallas_call(
            functools.partial(deep_kernel, samples, bands),
            grid=(steps,),
            out_shape=fourth_shapes + (grad_shape,),
            in_specs=[
                full(*value.shape) for value in (near, far, last, *deep_weights, fourth_wt, head)
            ],
            out_specs=(
                pl.BlockSpec((chunk * fourth_cells, 9 * three), lambda i: (i, 0)),
                pl.BlockSpec((chunk * fourth_cells, four), lambda i: (i, 0)),
                full(1, four),
                full(9 * two, three),
            ),
            scratch_shapes=[second_scratch(chunk), label_scratch] + deep_scratch(chunk),
            compiler_params=grant(40),
            cost_estimate=deep_cost,
            name="deep",
        )(near, far, last, *deep_weights, fourth_wt, head)

    if bit < samples:
        other, fourth_flat = lax.optimization_barrier((swapped(total, "dp", bit), fourth_flat))
        total = added(total, other)
    beside = swapped(total, "dp", 2)
    core = swapped(total, "dp", 1)
    if small:
        deepest_grad = pl.pallas_call(
            fourth_grad_alone_kernel,
            out_shape=shaped((9, three, four), f32),
            in_specs=[vmem] * 2,
            out_specs=pl.BlockSpec(memory_space=pl.ANY),
            scratch_shapes=[
                pltpu.VMEM((9, three, four), f32),
                pltpu.SemaphoreType.DMA((9,)),
            ],
            compiler_params=grant(16),
            cost_estimate=cost(600_000_000, 6_000_000),
            name="fourth_grad",
        )(fourth_taps, fourth_flat)
    else:
        deepest_grad = pl.pallas_call(
            fourth_grad_kernel,
            grid=(3, steps),
            out_shape=shaped((9 * three, four), f32),
            in_specs=[
                pl.BlockSpec((chunk * fourth_cells, 3 * three), lambda t, i: (i, t)),
                pl.BlockSpec((chunk * fourth_cells, four), lambda t, i: (i, 0)),
            ],
            out_specs=pl.BlockSpec((3 * three, four), lambda t, i: (t, 0)),
            compiler_params=grant(16),
            cost_estimate=cost(600_000_000, 6_000_000),
            name="fourth_grad",
        )(fourth_taps, fourth_flat)
    beside, deepest_grad = lax.optimization_barrier((beside, deepest_grad))
    across = swapped(beside, "dp", 1)
    if small:
        deeper_grad = pl.pallas_call(
            third_grad_kernel,
            out_shape=grad_shape,
            in_specs=[vmem] * 2,
            out_specs=vmem,
            compiler_params=grant(24),
            cost_estimate=cost(600_000_000, 4_000_000),
            name="third_grad",
        )(*thirds)
    across, deeper_grad = lax.optimization_barrier((across, deeper_grad))
    temporal_grad, middle_grad = pl.pallas_call(
        finish_kernel,
        out_shape=(shaped((9, lift_all, one), f32), shaped((9 * one, two), f32)),
        in_specs=[vmem] * 4,
        out_specs=(vmem, vmem),
        scratch_shapes=[pltpu.VMEM((21 * one, two), f32)],
        compiler_params=grant(16),
        cost_estimate=cost(1_000_000, 1_500_000),
        name="finish",
    )(total, core, beside, across)
    return (
        temporal_grad.reshape(temporal_weight.shape),
        middle_grad.reshape(middle_weight.shape),
        deeper_grad.reshape(deeper_weight.shape),
        deepest_grad.reshape(deepest_weight.shape),
        head_grad.reshape(four),
    )


def solution(mesh):
    return jax.shard_map(
        local,
        mesh=mesh,
        in_specs=(
            P("dp", None, "space", None),
            P("dp", "space", None),
            P(),
            P(),
            P(),
            P(),
            P(),
            P(),
        ),
        out_specs=(P(), P(), P(), P(), P()),
        check_vma=False,
    )
```

```python
import functools

import jax
import jax.numpy as jnp
from jax import lax
from jax.experimental import pallas as pl
from jax.experimental.pallas import tpu as pltpu
from jax.sharding import PartitionSpec as P

BLOCK = 8
MIB = 1 << 20


def f32_dot(left, right, contract):
    return lax.dot_general(
        left, right, ((contract[0], contract[1]), ((), ())), preferred_element_type=jnp.float32
    )


def dot_nn(left, right):
    return f32_dot(left, right, ((1,), (0,)))


def dot_nt(left, right):
    return f32_dot(left, right, ((1,), (1,)))


def dot_tn(left, right):
    return f32_dot(left, right, ((0,), (0,)))


def rounded(value):
    return value.astype(jnp.bfloat16).astype(jnp.float32)


def silu_and_slope(pre):
    gate = jax.nn.sigmoid(pre)
    return rounded(pre * gate), gate * (1.0 + pre * (1.0 - gate))


def zero_row(ref):
    ref[:, 0, 0] = jnp.zeros(ref.shape[:1] + ref.shape[3:], ref.dtype)


def last_row_zero(ref):
    ref[:, ref.shape[1] - 1] = jnp.zeros(ref.shape[:1] + ref.shape[2:], ref.dtype)


def shift_block(value, step):
    shape = value.shape
    flat = value.reshape(-1, shape[-1])
    moved = pltpu.roll(flat, step % flat.shape[0], 0)
    index = lax.broadcasted_iota(jnp.int32, flat.shape, 0) % BLOCK
    edge = 0 if step > 0 else BLOCK - 1
    return jnp.where(index == edge, 0.0, moved).reshape(shape)


def fill_map(ref, value, offset):
    n, rows, phases, _, channels = value.shape
    split = value.reshape(n, rows, phases // 2, 2, BLOCK, channels)
    for row in range(rows):
        pair, parity = divmod(row + offset, 2)
        ref[:, pair, parity, pl.ds(0, phases // 2), 1] = split[:, row, :, 0]
        ref[:, pair, parity, pl.ds(1, phases // 2), 0] = split[:, row, :, 1]
        ref[:, pair, parity, 0, 0] = shift_block(split[:, row, phases // 2 - 1, 1], 1)


def map_tap(ref, row_tap, col_tap, out_rows, out_phases):
    cells = ref[
        :,
        pl.ds(row_tap // 2, out_rows),
        row_tap % 2,
        pl.ds(col_tap // 2, out_phases),
        col_tap % 2,
    ]
    return cells.reshape(-1, cells.shape[-1]).astype(jnp.bfloat16)


def fill_delta(ref, value):
    rows, phases = value.shape[1:3]
    ref[:, pl.ds(0, rows), pl.ds(0, phases)] = value
    ref[:, pl.ds(0, rows), phases] = shift_block(value[:, :, 0], -1)


def delta_parts(ref, weight_ref, row_parity, col_parity, rows, phases):
    taps = (((1, 0),), ((2, 0), (0, 1)))
    total = None
    for row_tap, row_step in taps[row_parity]:
        for col_tap, col_step in taps[col_parity]:
            cells = ref[:, pl.ds(row_step, rows), pl.ds(col_step, phases)]
            lead = cells.shape[:-1]
            flat = cells.reshape(-1, cells.shape[-1]).astype(jnp.bfloat16)
            part = dot_nn(flat, weight_ref[3 * row_tap + col_tap])
            total = part if total is None else total + part
    return total.reshape(*lead, total.shape[-1])


def column_order(cols):
    place = lax.broadcasted_iota(jnp.int32, (cols, cols), 0)
    column = lax.broadcasted_iota(jnp.int32, (cols, cols), 1)
    source = (place % BLOCK) * (cols // BLOCK) + place // BLOCK
    return jnp.where(column == source, 1.0, 0.0).astype(jnp.bfloat16)


def band_cells(got_ref, inner, index, order, lift_ref, bits_ref, even_ref, odd_ref, rest):
    _, frames, band, cols = got_ref.shape
    phases, row_cells = cols // BLOCK, cols // 2
    height = lax.broadcasted_iota(jnp.int32, (16, cols), 0)
    for row in range(band):
        for frame in range(frames):
            line = jnp.broadcast_to(got_ref[inner, frame, pl.ds(row, 1)], height.shape)
            bit = jnp.bitwise_and(jnp.right_shift(line, height), 1)
            bits_ref[pl.ds(row * 128 + frame * 16, 16)] = bit.astype(jnp.float32).astype(
                jnp.bfloat16
            )
    spread = dot_nt(order, bits_ref[...]).astype(jnp.bfloat16)
    stacked = jnp.concatenate(
        [spread[:, row * 128 : row * 128 + 128] for row in range(band)], axis=0
    )
    lifted = jnp.maximum(dot_nn(stacked, lift_ref[...]), 0.0)
    lifted = lifted.reshape(band // 2, 2, phases // 2, 2, BLOCK, lifted.shape[-1])
    for parity, ref in ((0, even_ref), (1, odd_ref)):
        here = lifted[:, parity, :, 0]
        right = lifted[:, parity, :, 1]
        left = jnp.concatenate([shift_block(right[:, -1], 1)[:, None], right[:, :-1]], axis=1)
        taps = [part.reshape(-1, part.shape[-1]) for part in (left, here, right)]
        lane = lax.broadcasted_iota(jnp.int32, (taps[0].shape[0], 128), 1)
        tail = jnp.where(lane < rest, taps[0][:, 128:], taps[1][:, 128:])
        tail = jnp.where(lane < 2 * rest, tail, taps[2][:, 128:])
        cells = jnp.concatenate([part[:, :128] for part in taps] + [tail], axis=1)
        if index is None:
            ref[...] = cells.astype(jnp.bfloat16)
        else:
            at = pl.multiple_of((index * (band // 2) + parity) * row_cells, row_cells)
            ref[pl.ds(at, cells.shape[0])] = cells.astype(jnp.bfloat16)


def band_label(label_ref, inner, index, shape):
    lane = lax.broadcasted_iota(jnp.int32, shape, 1)
    row = lax.broadcasted_iota(jnp.int32, (shape[0], BLOCK), 0)
    column = lax.broadcasted_iota(jnp.int32, (shape[0], BLOCK), 1)
    label = jnp.broadcast_to(label_ref[inner].astype(jnp.float32), row.shape)
    label = jnp.sum(jnp.where(row == column, label, 0.0), axis=1, keepdims=True)
    return jnp.where(lane == index, label, 0.0)


def own_kernel(
    got_hbm,
    label_hbm,
    lift_hbm,
    first_w_hbm,
    second_w_hbm,
    third_w_hbm,
    fourth_w_hbm,
    even_ref,
    odd_ref,
    labels_ref,
    lift_all_ref,
    first_all_ref,
    second_w_ref,
    third_w_ref,
    fourth_w_ref,
    got_ref,
    label_ref,
    lift_ref,
    first_w_ref,
    bits_ref,
    sems,
):
    pairs = (
        (got_hbm, got_ref),
        (lift_hbm, lift_ref),
        (label_hbm, label_ref),
        (first_w_hbm, first_w_ref),
        (second_w_hbm, second_w_ref),
        (third_w_hbm, third_w_ref),
        (fourth_w_hbm, fourth_w_ref),
    )
    pairs = pairs[:-1] + tuple(
        (fourth_w_hbm.at[pl.ds(tap, 1)], fourth_w_ref.at[pl.ds(tap, 1)]) for tap in range(9)
    )
    copies = [
        pltpu.make_async_copy(source, target, sems.at[k])
        for k, (source, target) in enumerate(pairs)
    ]
    for copy in copies:
        copy.start()
    me = lax.axis_index("space")
    _, frames, _, cols = got_ref.shape
    heights, width = lift_ref.shape
    rest = first_w_ref.shape[1] - 128
    bits_ref[...] = jnp.zeros(bits_ref.shape, jnp.bfloat16)
    first_all_ref[...] = jnp.zeros(first_all_ref.shape, jnp.bfloat16)
    order = column_order(cols)
    copies[1].wait()
    tall = jnp.concatenate(
        [lift_ref[...].astype(jnp.float32), jnp.zeros((16 - heights, width), jnp.float32)], axis=0
    )
    tall = jnp.concatenate([tall] * (256 // width), axis=1)
    tall = jnp.concatenate([tall] * 8, axis=0)
    frame_of_row = lax.broadcasted_iota(jnp.int32, tall.shape, 0) // 16
    lane = lax.broadcasted_iota(jnp.int32, tall.shape, 1)
    frame_of_lane = jnp.minimum(lane // width, frames - 1)
    keep = (frame_of_row == frame_of_lane) & (lane < 128 + 3 * rest)
    lift_all_ref[...] = jnp.where(keep, tall, 0.0).astype(jnp.bfloat16)
    copies[0].wait()
    band_cells(got_ref, 0, None, order, lift_all_ref, bits_ref, even_ref, odd_ref, rest)
    copies[2].wait()
    labels_ref[...] = band_label(label_ref, 0, me, labels_ref.shape).astype(jnp.bfloat16)
    copies[3].wait()
    for tap in range(9):
        row_tap, col_tap = divmod(tap, 3)
        first_all_ref[row_tap, pl.ds(col_tap * 128, 128)] = first_w_ref[tap, pl.ds(0, 128)]
        first_all_ref[row_tap, pl.ds(384 + col_tap * rest, rest)] = first_w_ref[
            tap, pl.ds(128, rest)
        ]
    for copy in copies[4:]:
        copy.wait()


def early_kernel(pieces, rest, *refs):
    got_refs = refs[:pieces]
    (
        lift_all_ref,
        first_all_ref,
        second_w_ref,
        own_even_ref,
        own_odd_ref,
        even_ref,
        odd_ref,
        send_ref,
        first_ref,
        first_slope_ref,
        second_slope_ref,
        bits_ref,
    ) = refs[pieces:]
    me = lax.axis_index("space")
    bands = 1 << pieces
    _, _, band, cols = got_refs[0].shape
    phases, row_cells = cols // BLOCK, cols // 2
    order = column_order(cols)
    cells = own_even_ref.shape[0]
    at = pl.multiple_of(me * cells, cells)
    even_ref[pl.ds(at, cells)] = own_even_ref[...]
    odd_ref[pl.ds(pl.multiple_of(at + row_cells, row_cells), cells)] = own_odd_ref[...]
    odd_ref[pl.ds(0, row_cells)] = jnp.zeros((row_cells, odd_ref.shape[1]), jnp.bfloat16)
    bits_ref[...] = jnp.zeros(bits_ref.shape, jnp.bfloat16)
    for slot in range(1, bands):
        piece = slot.bit_length() - 1
        inner = slot - (1 << piece)
        band_cells(
            got_refs[piece],
            inner,
            me ^ slot,
            order,
            lift_all_ref,
            bits_ref,
            even_ref,
            odd_ref,
            rest,
        )

    rows, phases = bands * band // 2, phases // 2
    cells = rows * row_cells
    pre = dot_nn(odd_ref[pl.ds(0, cells)], first_all_ref[0])
    pre += dot_nn(even_ref[...], first_all_ref[1])
    pre += dot_nn(odd_ref[pl.ds(row_cells, cells)], first_all_ref[2])
    value, slope = silu_and_slope(pre)
    shape = (1, rows, phases, BLOCK, value.shape[-1])
    zero_row(first_ref)
    fill_map(first_ref, value.reshape(shape), 1)
    first_slope_ref[...] = slope.reshape(shape)

    rows, phases = rows // 2, phases // 2
    pre = None
    for tap in range(9):
        cells = map_tap(first_ref, tap // 3, tap % 3, rows, phases)
        part = dot_nn(cells, second_w_ref[tap])
        pre = part if pre is None else pre + part
    value, slope = silu_and_slope(pre)
    second_slope_ref[...] = slope.reshape(second_slope_ref.shape)
    sent = value.shape[0]
    send_ref[pl.ds(0, sent)] = value.astype(jnp.bfloat16)
    send_ref[pl.ds(sent, 16)] = jnp.zeros((16, send_ref.shape[1]), jnp.bfloat16)


def transpose_kernel(weight_ref, out_ref):
    for tap in range(weight_ref.shape[0]):
        out_ref[tap] = weight_ref[tap].T


def take_samples(slot_refs, second_ref, label_ref, bands):
    count = sum(ref.shape[0] for ref in slot_refs)
    width = count.bit_length() - 1
    chunk = second_ref.shape[0]
    me = lax.axis_index("dp")
    where = [(ref, inner) for ref in slot_refs for inner in range(ref.shape[0])]
    for slot in range(count):
        reverse = sum(((slot >> k) & 1) << (width - 1 - k) for k in range(width))
        sample = me ^ reverse
        ref, inner = where[slot]

        def take(ref=ref, inner=inner, place=sample % chunk):
            put_sample(ref, inner, second_ref, label_ref, place, bands)

        if chunk == count:
            take()
        else:
            pl.when(sample // chunk == pl.program_id(0))(take)


def third_taps(second_ref, taps_ref, rows, phases):
    channels = second_ref.shape[-1]
    for tap in range(9):
        taps_ref[:, pl.ds(tap * channels, channels)] = map_tap(
            second_ref, tap // 3, tap % 3, rows, phases
        )


def delta_columns(ref, rows, phases):
    columns = {}
    for row_step in range(2):
        for col_step in range(2):
            cells = ref[:, pl.ds(row_step, rows), pl.ds(col_step, phases)]
            cells = cells.reshape(-1, cells.shape[-1])
            columns[row_step, col_step] = cells.T.astype(jnp.bfloat16)
    return columns


def column_parts(columns, weight_ref, row_parity, col_parity, rows, phases):
    taps = (((1, 0),), ((2, 0), (0, 1)))
    total = None
    for row_tap, row_step in taps[row_parity]:
        for col_tap, col_step in taps[col_parity]:
            part = dot_nn(weight_ref[3 * row_tap + col_tap], columns[row_step, col_step])
            total = part if total is None else total + part
    return total.T.reshape(-1, rows, phases, BLOCK, total.shape[0])


def put_label(ref, inner, label_ref, place, bands):
    cells = 4 * bands * 4 * BLOCK
    label = ref[inner, pl.ds(cells, 16)].astype(jnp.float32)[:BLOCK]
    for index in range(bands):
        label_ref[place, index] = jnp.broadcast_to(label[:, index : index + 1], label.shape)


def put_sample(ref, inner, second_ref, label_ref, place, bands):
    rows, phases = 4 * bands, 4
    cells = rows * phases * BLOCK
    second = ref[inner, pl.ds(0, cells)].astype(jnp.float32)
    fill_map(
        second_ref.at[pl.ds(place, 1)],
        second.reshape(1, rows, phases, BLOCK, second.shape[-1]),
        1,
    )
    if label_ref is not None:
        put_label(ref, inner, label_ref, place, bands)


def deep_layers(
    batch,
    bands,
    third_w_ref,
    fourth_w_ref,
    fourth_parts,
    head_ref,
    fourth_taps_ref,
    second_ref,
    label_ref,
    third_taps_ref,
    third_ref,
    third_slope_ref,
    third_delta_ref,
    fourth_delta_ref,
):
    value, slope = third_layer(second_ref, third_w_ref, third_taps_ref, bands)
    zero_row(third_ref)
    fill_map(third_ref, value, 1)
    third_slope_ref[...] = slope.reshape(third_slope_ref.shape)
    return deeper_layers(
        batch,
        bands,
        fourth_w_ref,
        fourth_parts,
        head_ref,
        fourth_taps_ref,
        label_ref,
        third_ref,
        third_slope_ref,
        third_delta_ref,
        fourth_delta_ref,
    )


def third_layer(second_ref, third_w_ref, third_taps_ref, bands):
    rows, phases = 2 * bands, 2
    third_taps(second_ref, third_taps_ref, rows, phases)
    weight = third_w_ref[...].reshape(third_taps_ref.shape[1], -1)
    value, slope = silu_and_slope(dot_nn(third_taps_ref[...], weight))
    shape = (second_ref.shape[0], rows, phases, BLOCK, value.shape[-1])
    return value.reshape(shape), slope.reshape(shape)


def deeper_layers(
    batch,
    bands,
    fourth_w_ref,
    fourth_parts,
    head_ref,
    fourth_taps_ref,
    label_ref,
    third_ref,
    third_slope_ref,
    third_delta_ref,
    fourth_delta_ref,
):
    samples, channels = third_ref.shape[0], third_ref.shape[-1]
    rows, phases = bands, 1
    for tap in range(9):
        fourth_taps_ref[:, pl.ds(tap * channels, channels)] = map_tap(
            third_ref, tap // 3, tap % 3, rows, phases
        )
    weight = fourth_w_ref[...].reshape(fourth_taps_ref.shape[1], -1)
    value, slope = silu_and_slope(dot_nn(fourth_taps_ref[...], weight))
    head = head_ref[...].astype(jnp.float32)
    labels = label_ref[...].reshape(-1, label_ref.shape[-1])[:, :1]
    logits = jnp.sum(value * head, axis=1, keepdims=True)
    logit_grad = (jax.nn.sigmoid(logits) - labels) / batch
    delta = rounded(logit_grad * head * slope)
    last_row_zero(fourth_delta_ref)
    fill_delta(fourth_delta_ref, delta.reshape(samples, rows, phases, BLOCK, delta.shape[-1]))
    parts = fourth_parts(fourth_delta_ref, rows, phases)
    for row_parity in range(2):
        for col_parity in range(2):
            part = parts(row_parity, col_parity, rows, phases)
            part = rounded(part * third_slope_ref[:, :, row_parity, :, col_parity])
            for row in range(rows):
                third_delta_ref[:, 2 * row + row_parity, col_parity] = part[:, row, 0]
    return value, logit_grad, delta


def near_kernel(bands, near_ref, third_w_ref, taps_ref, map_ref, slope_ref, second_ref):
    zero_row(second_ref)
    for slot in range(near_ref.shape[0]):
        put_sample(near_ref, slot, second_ref, None, slot, bands)
    value, slope = third_layer(second_ref, third_w_ref, taps_ref, bands)
    map_ref[...] = value
    slope_ref[...] = slope


def far_kernel(
    batch,
    bands,
    near_ref,
    far_ref,
    last_ref,
    near_taps_ref,
    near_map_ref,
    near_slope_ref,
    third_w_ref,
    fourth_w_ref,
    fourth_wt_ref,
    head_ref,
    fourth_taps_ref,
    fourth_flat_ref,
    head_grad_ref,
    third_taps_ref,
    third_flat_ref,
    second_ref,
    far_taps_ref,
    label_ref,
    third_ref,
    third_slope_ref,
    third_delta_ref,
    fourth_delta_ref,
):
    half, early = near_ref.shape[0], far_ref.shape[0]
    zero_row(second_ref)
    for slot in range(half):
        ref, inner = (far_ref, slot) if slot < early else (last_ref, slot - early)
        put_sample(ref, inner, second_ref, None, slot, bands)
    value, slope = third_layer(second_ref, third_w_ref, far_taps_ref, bands)
    cells = far_taps_ref.shape[0] // half
    width = half.bit_length()
    me = lax.axis_index("dp")
    zero_row(third_ref)
    for slot in range(2 * half):
        place = me ^ sum(((slot >> k) & 1) << (width - 1 - k) for k in range(width))
        inner = slot % half
        at = pl.ds(pl.multiple_of(place * cells, cells), cells)
        one = pl.ds(place, 1)
        if slot < half:
            third_taps_ref[at] = near_taps_ref[pl.ds(inner * cells, cells)]
            fill_map(third_ref.at[one], near_map_ref[pl.ds(inner, 1)], 1)
            third_slope_ref[one] = near_slope_ref[pl.ds(inner, 1)].reshape(
                (1,) + third_slope_ref.shape[1:]
            )
            put_label(near_ref, inner, label_ref, place, bands)
        else:
            third_taps_ref[at] = far_taps_ref[pl.ds(inner * cells, cells)]
            fill_map(third_ref.at[one], value[inner : inner + 1], 1)
            third_slope_ref[one] = slope[inner : inner + 1].reshape(
                (1,) + third_slope_ref.shape[1:]
            )
            ref, inner = (far_ref, inner) if inner < early else (last_ref, inner - early)
            put_label(ref, inner, label_ref, place, bands)
    value, logit_grad, delta = deeper_layers(
        batch,
        bands,
        fourth_w_ref,
        lambda ref, *_: functools.partial(delta_parts, ref, fourth_wt_ref),
        head_ref,
        fourth_taps_ref,
        label_ref,
        third_ref,
        third_slope_ref,
        third_delta_ref,
        fourth_delta_ref,
    )
    head_grad_ref[...] = jnp.sum(value * logit_grad, axis=0, keepdims=True)
    fourth_flat_ref[...] = delta.astype(jnp.bfloat16)
    delta = third_delta_ref[...]
    third_flat_ref[...] = delta.reshape(-1, delta.shape[-1]).astype(jnp.bfloat16)


def deep_kernel(
    batch,
    bands,
    near_ref,
    far_ref,
    last_ref,
    third_w_ref,
    fourth_w_ref,
    fourth_wt_ref,
    head_ref,
    fourth_taps_ref,
    fourth_flat_ref,
    head_grad_ref,
    *refs,
):
    third_grad_ref, second_ref, label_ref, third_taps_ref = refs[:4]
    third_ref, third_slope_ref, third_delta_ref, fourth_delta_ref = refs[4:]
    zero_row(second_ref)
    take_samples((near_ref, far_ref, last_ref), second_ref, label_ref, bands)
    value, logit_grad, delta = deep_layers(
        batch,
        bands,
        third_w_ref,
        fourth_w_ref,
        lambda ref, *_: functools.partial(delta_parts, ref, fourth_wt_ref),
        head_ref,
        fourth_taps_ref,
        second_ref,
        label_ref,
        third_taps_ref,
        third_ref,
        third_slope_ref,
        third_delta_ref,
        fourth_delta_ref,
    )

    head_grad = jnp.sum(value * logit_grad, axis=0, keepdims=True)
    add_to(head_grad_ref, head_grad)
    fourth_flat_ref[...] = delta.astype(jnp.bfloat16)
    delta = third_delta_ref[...]
    delta = delta.reshape(-1, delta.shape[-1]).astype(jnp.bfloat16)
    add_to(third_grad_ref, dot_tn(delta, third_taps_ref[...]).T)


def local_kernel(
    batch,
    bands,
    payload_ref,
    third_w_ref,
    fourth_w_ref,
    head_ref,
    second_w_ref,
    even_ref,
    odd_ref,
    first_ref,
    first_slope_ref,
    second_slope_ref,
    *refs,
):
    keep_ref, pass_ref = refs[:2]
    third_ref, second_ref, first_delta_ref, flat_ref, second_map_ref, label_ref = refs[2:8]
    fourth_taps_ref = refs[8]
    third_delta_ref = refs[12]
    zero_row(second_map_ref)
    put_sample(payload_ref, 0, second_map_ref, label_ref, 0, bands)
    deep_layers(
        batch,
        bands,
        third_w_ref,
        fourth_w_ref,
        lambda ref, *size: functools.partial(
            column_parts, delta_columns(ref, *size), fourth_w_ref
        ),
        head_ref,
        fourth_taps_ref,
        second_map_ref,
        label_ref,
        *refs[9:14],
    )
    sample = lax.axis_index("dp")
    _, rows, phases, _, _ = third_delta_ref.shape
    fill_delta(third_ref, third_delta_ref[...])
    last_row_zero(third_ref)
    last_row_zero(second_ref)
    columns = delta_columns(third_ref, rows, phases)
    for row_parity in range(2):
        for col_parity in range(2):
            part = column_parts(columns, third_w_ref, row_parity, col_parity, rows, phases)
            for row in range(rows):
                for phase in range(phases):
                    at = (slice(None), 2 * row + row_parity, 2 * phase + col_parity)
                    second_ref[at] = rounded(part[:, row, phase] * second_slope_ref[at])
    rows, phases = 2 * rows, 2 * phases
    second_ref[:, :, phases] = shift_block(second_ref[:, :, 0], -1)
    columns = delta_columns(second_ref, rows, phases)
    for row_parity in range(2):
        for col_parity in range(2):
            part = column_parts(columns, second_w_ref, row_parity, col_parity, rows, phases)
            for row in range(rows):
                for phase in range(phases):
                    at = (slice(None), 2 * row + row_parity, 2 * phase + col_parity)
                    first_delta_ref[at] = rounded(part[:, row, phase] * first_slope_ref[at])
    delta = second_ref[:, pl.ds(0, rows), pl.ds(0, phases)]
    delta = delta.reshape(-1, delta.shape[-1]).astype(jnp.bfloat16)
    depth = first_ref.shape[-1]
    for tap in range(9):
        cells = map_tap(first_ref, tap // 3, tap % 3, rows, phases)
        flat_ref[pl.ds((12 + tap) * depth, depth)] = dot_tn(cells, delta)
    delta = first_delta_ref[...]
    delta = delta.reshape(-1, delta.shape[-1]).astype(jnp.bfloat16)
    cells = delta.shape[0]
    row_cells = cells // (2 * rows)
    taps = (odd_ref[pl.ds(0, cells)], even_ref[...], odd_ref[pl.ds(row_cells, cells)])
    for tap in range(3):
        part = dot_tn(delta, taps[tap])
        for piece in range(4):
            flat_ref[pl.ds((4 * tap + piece) * depth, depth)] = part[
                :, piece * 128 : piece * 128 + 128
            ]
    share = keep_ref.shape[1]
    for slot in range(4):
        at = pl.multiple_of(((sample % 4) ^ slot) * share, share)
        ref = pass_ref if slot % 2 else keep_ref
        ref[slot // 2] = flat_ref[pl.ds(at, share)].astype(jnp.bfloat16)


def add_to(ref, value):
    first = pl.program_id(0) == 0
    ref[...] = jnp.where(first, 0.0, ref[...]) + value


def third_grad_kernel(taps_ref, delta_ref, out_ref):
    out_ref[...] = dot_tn(delta_ref[...], taps_ref[...]).T


def fourth_grad_alone_kernel(fourth_taps_ref, fourth_flat_ref, out_hbm, grad_ref, sems):
    depth = grad_ref.shape[1]
    copies = []
    for tap in range(9):
        grad_ref[tap] = dot_tn(
            fourth_taps_ref[:, pl.ds(tap * depth, depth)], fourth_flat_ref[...]
        )
        copy = pltpu.make_async_copy(grad_ref.at[tap], out_hbm.at[tap], sems.at[tap])
        copy.start()
        copies.append(copy)
    for copy in copies:
        copy.wait()


def fourth_grad_kernel(fourth_taps_ref, fourth_flat_ref, out_ref):
    @pl.when(pl.program_id(1) == 0)
    def _():
        out_ref[...] = jnp.zeros(out_ref.shape, jnp.float32)

    out_ref[...] += dot_tn(fourth_taps_ref[...], fourth_flat_ref[...])


def finish_kernel(*refs):
    got_refs = refs[:4]
    temporal_ref, middle_ref, flat_ref = refs[4:]
    me = lax.axis_index("dp") % 4
    share = got_refs[0].shape[0]
    for slot in range(4):
        at = pl.multiple_of((me ^ slot) * share, share)
        flat_ref[pl.ds(at, share)] = got_refs[slot][...].astype(jnp.float32)
    depth = temporal_ref.shape[2]
    middle_ref[...] = flat_ref[pl.ds(12 * depth, 9 * depth)]
    rest = temporal_ref.shape[1] - 128
    for tap in range(3):
        parts = [flat_ref[pl.ds((4 * tap + piece) * depth, depth)].T for piece in range(4)]
        for col_tap in range(3):
            temporal_ref[3 * tap + col_tap, pl.ds(0, 128)] = parts[col_tap]
            temporal_ref[3 * tap + col_tap, pl.ds(128, rest)] = parts[3][
                col_tap * rest : col_tap * rest + rest
            ]


def cost(flops, size):
    return pl.CostEstimate(flops=flops, bytes_accessed=size, transcendentals=0)


def swapped(value, axis, bit):
    return lax.ppermute(value, axis, [(i, i ^ bit) for i in range(lax.axis_size(axis))])


def band_pieces(value, bands):
    pieces = [value]
    bit = 1
    while bit < bands:
        whole = pieces[0] if bit == 1 else jnp.concatenate(pieces, axis=0)
        pieces.append(swapped(whole, "space", bit))
        bit *= 2
    return pieces


def put(buffer, part, at):
    return lax.dynamic_update_slice(buffer, part, (at,) + (0,) * (buffer.ndim - 1))


def after(value, *others):
    return lax.optimization_barrier((value, *others))[0]


def gather_and_sum(payload, local_sums, transposed, samples):
    half, quarter = samples // 2, samples // 4
    near = put(jnp.zeros((half,) + payload.shape[1:], payload.dtype), payload, 0)
    got = swapped(payload, "dp", quarter * 2) if quarter > 1 else None
    keep, passed = local_sums()
    core = swapped(passed, "dp", 1)
    mine, theirs = added(keep[0], core[0]), added(keep[1], core[1])
    mine_beside = swapped(theirs, "dp", 2)
    weights = transposed(theirs)
    count, beside_count = 1, 0
    while count < quarter:
        near = put(near, after(got, keep), count)
        count *= 2
        if count < quarter:
            part = near[beside_count:count]
            got = swapped(near[:count], "dp", half // count)
            beside = swapped(after(part, theirs), "dp", 2)
            near = put(near, beside, quarter + beside_count)
            beside_count = count
    total = added(mine, after(mine_beside, weights))
    beside = swapped(after(near[beside_count:quarter], theirs), "dp", 2)
    early = swapped(near[: quarter + beside_count], "dp", 1)
    bit = 4
    while 2 * bit < samples:
        other = swapped(total, "dp", bit)
        beside = after(beside, total)
        total = added(total, after(other, beside))
        bit *= 2
    near = put(near, beside, quarter + beside_count)
    last = swapped(beside, "dp", 1)
    return near, early, last, total, bit, weights


def added(*parts):
    total = parts[0].astype(jnp.float32)
    for part in parts[1:]:
        total = total + part.astype(jnp.float32)
    return total.astype(jnp.bfloat16)


def local(
    occupancy,
    state_labels,
    lift_weight,
    temporal_weight,
    middle_weight,
    deeper_weight,
    deepest_weight,
    head_weight,
):
    bands = lax.axis_size("space")
    samples = lax.axis_size("dp")
    _, frames, band, cols = occupancy.shape
    lift_all = frames * lift_weight.shape[1]
    one, two = middle_weight.shape[2:]
    three, four = deepest_weight.shape[2:]
    f32, bf16 = jnp.float32, jnp.bfloat16
    shaped = jax.ShapeDtypeStruct
    phases = cols // BLOCK
    rows = bands * band
    small = samples * bands <= 32
    vmem = pl.BlockSpec(memory_space=pltpu.VMEM)

    def grant(size):
        return pltpu.CompilerParams(vmem_limit_bytes=(size if small else 60) * MIB)

    lines = band_pieces(occupancy, bands)
    first_w = temporal_weight.reshape(9, lift_all, one)
    second_w = middle_weight.reshape(9, one, two)
    third_w = deeper_weight.reshape(9, two, three)
    fourth_w = deepest_weight.reshape(9, three, four)
    head = head_weight.reshape(1, four)

    sent = rows // 4 * phases // 4 * BLOCK + 16
    hbm = pl.BlockSpec(memory_space=pltpu.HBM)
    even_shape = shaped((rows // 2 * cols // 2, 512), bf16)
    odd_shape = shaped(((rows // 2 + 1) * cols // 2, 512), bf16)
    bits_scratch = pltpu.VMEM((band * 128, cols), bf16)
    own_cells = shaped((band // 2 * cols // 2, 512), bf16)
    own_args = [
        pltpu.with_memory_space_constraint(value, pltpu.HBM)
        for value in (
            occupancy,
            state_labels,
            lift_weight,
            first_w,
            second_w,
            third_w,
            fourth_w,
        )
    ]
    (
        own_even,
        own_odd,
        own_labels,
        lift_all_w,
        first_all,
        second_w2,
        third_w2,
        fourth_w2,
    ) = pl.pallas_call(
        own_kernel,
        out_shape=(
            own_cells,
            own_cells,
            shaped((16, two), bf16),
            shaped((128, 256), bf16),
            shaped((3, 512, one), bf16),
            shaped(second_w.shape, bf16),
            shaped(third_w.shape, bf16),
            shaped(fourth_w.shape, bf16),
        ),
        in_specs=[hbm] * 7,
        out_specs=(vmem,) * 8,
        scratch_shapes=[
            pltpu.VMEM(occupancy.shape, occupancy.dtype),
            pltpu.VMEM(state_labels.shape, state_labels.dtype),
            pltpu.VMEM(lift_weight.shape, bf16),
            pltpu.VMEM(first_w.shape, bf16),
            bits_scratch,
            pltpu.SemaphoreType.DMA((15,)),
        ],
        compiler_params=grant(24),
        cost_estimate=cost(100_000_000, 10_000_000),
        name="own_band",
    )(*own_args)
    pieces = len(lines) - 1
    even, odd, payload, first, first_slope, second_slope = pl.pallas_call(
        functools.partial(early_kernel, pieces, lift_all - 128),
        out_shape=(
            even_shape,
            odd_shape,
            shaped((sent, two), bf16),
            shaped((1, rows // 4 + 1, 2, phases // 4 + 1, 2, BLOCK, one), f32),
            shaped((1, rows // 2, phases // 2, BLOCK, one), f32),
            shaped((1, rows // 4, phases // 4, BLOCK, two), f32),
        ),
        in_specs=[vmem] * (pieces + 5),
        out_specs=(vmem,) * 6,
        scratch_shapes=[bits_scratch],
        compiler_params=grant(24),
        cost_estimate=cost(150_000_000, 4_000_000),
        name="early",
    )(*lines[1:], lift_all_w, first_all, second_w2, own_even, own_odd)

    labels, bit = own_labels, 1
    while bit < bands:
        labels = labels + swapped(labels, "space", bit)
        bit *= 2
    payload = put(payload, labels, sent - 16)[None]
    deep_weights = (third_w2, fourth_w2)

    third_cells = 2 * bands * 2 * BLOCK
    fourth_cells = bands * BLOCK

    def second_scratch(count):
        return pltpu.VMEM((count, 2 * bands + 1, 2, 3, 2, BLOCK, two), f32)

    def third_taps_scratch(count):
        return pltpu.VMEM((count * third_cells, 9 * two), bf16)

    def deep_scratch(count):
        return [
            third_taps_scratch(count),
            pltpu.VMEM((count, bands + 1, 2, 2, 2, BLOCK, three), f32),
            pltpu.VMEM((count, bands, 2, 1, 2, BLOCK, three), f32),
            pltpu.VMEM((count, 2 * bands, 2, BLOCK, three), f32),
            pltpu.VMEM((count, bands + 1, 2, BLOCK, four), f32),
        ]

    share = 21 * one // 4
    local_call = pl.pallas_call(
        functools.partial(local_kernel, samples, bands),
        out_shape=(shaped((2, share, two), bf16),) * 2,
        in_specs=[vmem] * 10,
        out_specs=(vmem,) * 2,
        scratch_shapes=[
            pltpu.VMEM((1, 2 * bands + 1, 3, BLOCK, three), f32),
            pltpu.VMEM((1, 4 * bands + 1, 5, BLOCK, two), f32),
            pltpu.VMEM(first_slope.shape, f32),
            pltpu.VMEM((21 * one, two), f32),
            second_scratch(1),
            pltpu.VMEM((1, bands, BLOCK, two), f32),
            pltpu.VMEM((fourth_cells, 9 * three), bf16),
        ]
        + deep_scratch(1),
        compiler_params=grant(24),
        cost_estimate=cost(300_000_000, 9_000_000),
        name="local",
    )
    maps = (head, second_w2, even, odd, first, first_slope, second_slope)
    transpose_call = pl.pallas_call(
        transpose_kernel,
        out_shape=shaped((9, four, three), bf16),
        in_specs=[vmem],
        out_specs=vmem,
        compiler_params=grant(16),
        cost_estimate=cost(10_000_000, 5_000_000),
        name="transpose",
    )

    near, far, last, total, bit, fourth_wt = gather_and_sum(
        payload,
        lambda: local_call(payload, *deep_weights, *maps),
        lambda keep: transpose_call(after(fourth_w2, keep)),
        samples,
    )
    near = after(near, total)

    chunk = max(1, min(samples, 32 // bands))
    steps = samples // chunk
    full = lambda *shape: pl.BlockSpec(shape, lambda i: (0,) * len(shape))
    grad_shape = shaped((9 * two, three), f32)
    fourth_shapes = (
        shaped((samples * fourth_cells, 9 * three), bf16),
        shaped((samples * fourth_cells, four), bf16),
        shaped((1, four), f32),
    )
    label_scratch = pltpu.VMEM((chunk, bands, BLOCK, two), f32)
    deep_cost = cost(1_300_000_000, 12_000_000)
    if small:
        half = samples // 2
        half_shapes = (
            shaped((half * third_cells, 9 * two), bf16),
            shaped((half, 2 * bands, 2, BLOCK, three), f32),
            shaped((half, 2 * bands, 2, BLOCK, three), f32),
        )
        near_third = pl.pallas_call(
            functools.partial(near_kernel, bands),
            out_shape=half_shapes,
            in_specs=[vmem] * 2,
            out_specs=(vmem,) * 3,
            scratch_shapes=[second_scratch(half)],
            compiler_params=grant(24),
            cost_estimate=cost(300_000_000, 4_000_000),
            name="near",
        )(near, third_w2)
        fourth_taps, fourth_flat, head_grad, *thirds = pl.pallas_call(
            functools.partial(far_kernel, samples, bands),
            out_shape=fourth_shapes
            + (
                shaped((samples * third_cells, 9 * two), bf16),
                shaped((samples * third_cells, three), bf16),
            ),
            in_specs=[vmem] * 10,
            out_specs=(vmem,) * 5,
            scratch_shapes=[second_scratch(half), third_taps_scratch(half), label_scratch]
            + deep_scratch(chunk)[1:],
            compiler_params=grant(40),
            cost_estimate=deep_cost,
            name="deep",
        )(near, far, last, *near_third, *deep_weights, fourth_wt, head)
        deeper_grad = None
    else:
        fourth_taps, fourth_flat, head_grad, deeper_grad = pl.pallas_call(
            functools.partial(deep_kernel, samples, bands),
            grid=(steps,),
            out_shape=fourth_shapes + (grad_shape,),
            in_specs=[
                full(*value.shape) for value in (near, far, last, *deep_weights, fourth_wt, head)
            ],
            out_specs=(
                pl.BlockSpec((chunk * fourth_cells, 9 * three), lambda i: (i, 0)),
                pl.BlockSpec((chunk * fourth_cells, four), lambda i: (i, 0)),
                full(1, four),
                full(9 * two, three),
            ),
            scratch_shapes=[second_scratch(chunk), label_scratch] + deep_scratch(chunk),
            compiler_params=grant(40),
            cost_estimate=deep_cost,
            name="deep",
        )(near, far, last, *deep_weights, fourth_wt, head)

    if bit < samples:
        other, fourth_flat = lax.optimization_barrier((swapped(total, "dp", bit), fourth_flat))
        total = added(total, other)
    beside = swapped(total, "dp", 2)
    core = swapped(total, "dp", 1)
    if small:
        deepest_grad = pl.pallas_call(
            fourth_grad_alone_kernel,
            out_shape=shaped((9, three, four), f32),
            in_specs=[vmem] * 2,
            out_specs=pl.BlockSpec(memory_space=pl.ANY),
            scratch_shapes=[
                pltpu.VMEM((9, three, four), f32),
                pltpu.SemaphoreType.DMA((9,)),
            ],
            compiler_params=grant(16),
            cost_estimate=cost(600_000_000, 6_000_000),
            name="fourth_grad",
        )(fourth_taps, fourth_flat)
    else:
        deepest_grad = pl.pallas_call(
            fourth_grad_kernel,
            grid=(3, steps),
            out_shape=shaped((9 * three, four), f32),
            in_specs=[
                pl.BlockSpec((chunk * fourth_cells, 3 * three), lambda t, i: (i, t)),
                pl.BlockSpec((chunk * fourth_cells, four), lambda t, i: (i, 0)),
            ],
            out_specs=pl.BlockSpec((3 * three, four), lambda t, i: (t, 0)),
            compiler_params=grant(16),
            cost_estimate=cost(600_000_000, 6_000_000),
            name="fourth_grad",
        )(fourth_taps, fourth_flat)
    beside, deepest_grad = lax.optimization_barrier((beside, deepest_grad))
    across = swapped(beside, "dp", 1)
    if small:
        deeper_grad = pl.pallas_call(
            third_grad_kernel,
            out_shape=grad_shape,
            in_specs=[vmem] * 2,
            out_specs=vmem,
            compiler_params=grant(24),
            cost_estimate=cost(600_000_000, 4_000_000),
            name="third_grad",
        )(*thirds)
    across, deeper_grad = lax.optimization_barrier((across, deeper_grad))
    temporal_grad, middle_grad = pl.pallas_call(
        finish_kernel,
        out_shape=(shaped((9, lift_all, one), f32), shaped((9 * one, two), f32)),
        in_specs=[vmem] * 4,
        out_specs=(vmem, vmem),
        scratch_shapes=[pltpu.VMEM((21 * one, two), f32)],
        compiler_params=grant(16),
        cost_estimate=cost(1_000_000, 1_500_000),
        name="finish",
    )(total, core, beside, across)
    return (
        temporal_grad.reshape(temporal_weight.shape),
        middle_grad.reshape(middle_weight.shape),
        deeper_grad.reshape(deeper_weight.shape),
        deepest_grad.reshape(deepest_weight.shape),
        head_grad.reshape(four),
    )


def solution(mesh):
    return jax.shard_map(
        local,
        mesh=mesh,
        in_specs=(
            P("dp", None, "space", None),
            P("dp", "space", None),
            P(),
            P(),
            P(),
            P(),
            P(),
            P(),
        ),
        out_specs=(P(), P(), P(), P(), P()),
        check_vma=False,
    )
```

```python
import functools

import jax
import jax.numpy as jnp
from jax import lax
from jax.experimental import pallas as pl
from jax.experimental.pallas import tpu as pltpu
from jax.sharding import PartitionSpec as P

BLOCK = 8
MIB = 1 << 20


def f32_dot(left, right, contract):
    return lax.dot_general(
        left, right, ((contract[0], contract[1]), ((), ())), preferred_element_type=jnp.float32
    )


def dot_nn(left, right):
    return f32_dot(left, right, ((1,), (0,)))


def dot_nt(left, right):
    return f32_dot(left, right, ((1,), (1,)))


def dot_tn(left, right):
    return f32_dot(left, right, ((0,), (0,)))


def rounded(value):
    return value.astype(jnp.bfloat16).astype(jnp.float32)


def silu_and_slope(pre):
    gate = jax.nn.sigmoid(pre)
    return rounded(pre * gate), gate * (1.0 + pre * (1.0 - gate))


def zero_row(ref):
    ref[:, 0, 0] = jnp.zeros(ref.shape[:1] + ref.shape[3:], ref.dtype)


def last_row_zero(ref):
    ref[:, ref.shape[1] - 1] = jnp.zeros(ref.shape[:1] + ref.shape[2:], ref.dtype)


def shift_block(value, step):
    shape = value.shape
    flat = value.reshape(-1, shape[-1])
    moved = pltpu.roll(flat, step % flat.shape[0], 0)
    index = lax.broadcasted_iota(jnp.int32, flat.shape, 0) % BLOCK
    edge = 0 if step > 0 else BLOCK - 1
    return jnp.where(index == edge, 0.0, moved).reshape(shape)


def fill_map(ref, value, offset):
    n, rows, phases, _, channels = value.shape
    split = value.reshape(n, rows, phases // 2, 2, BLOCK, channels)
    for row in range(rows):
        pair, parity = divmod(row + offset, 2)
        ref[:, pair, parity, pl.ds(0, phases // 2), 1] = split[:, row, :, 0]
        ref[:, pair, parity, pl.ds(1, phases // 2), 0] = split[:, row, :, 1]
        ref[:, pair, parity, 0, 0] = shift_block(split[:, row, phases // 2 - 1, 1], 1)


def map_tap(ref, row_tap, col_tap, out_rows, out_phases):
    cells = ref[
        :,
        pl.ds(row_tap // 2, out_rows),
        row_tap % 2,
        pl.ds(col_tap // 2, out_phases),
        col_tap % 2,
    ]
    return cells.reshape(-1, cells.shape[-1]).astype(jnp.bfloat16)


def fill_delta(ref, value):
    rows, phases = value.shape[1:3]
    ref[:, pl.ds(0, rows), pl.ds(0, phases)] = value
    ref[:, pl.ds(0, rows), phases] = shift_block(value[:, :, 0], -1)


def delta_parts(ref, weight_ref, row_parity, col_parity, rows, phases):
    taps = (((1, 0),), ((2, 0), (0, 1)))
    total = None
    for row_tap, row_step in taps[row_parity]:
        for col_tap, col_step in taps[col_parity]:
            cells = ref[:, pl.ds(row_step, rows), pl.ds(col_step, phases)]
            lead = cells.shape[:-1]
            flat = cells.reshape(-1, cells.shape[-1]).astype(jnp.bfloat16)
            part = dot_nn(flat, weight_ref[3 * row_tap + col_tap])
            total = part if total is None else total + part
    return total.reshape(*lead, total.shape[-1])


def column_order(cols):
    place = lax.broadcasted_iota(jnp.int32, (cols, cols), 0)
    column = lax.broadcasted_iota(jnp.int32, (cols, cols), 1)
    source = (place % BLOCK) * (cols // BLOCK) + place // BLOCK
    return jnp.where(column == source, 1.0, 0.0).astype(jnp.bfloat16)


def band_cells(got_ref, inner, index, order, lift_ref, bits_ref, even_ref, odd_ref, rest):
    _, frames, band, cols = got_ref.shape
    phases, row_cells = cols // BLOCK, cols // 2
    height = lax.broadcasted_iota(jnp.int32, (16, cols), 0)
    for row in range(band):
        for frame in range(frames):
            line = jnp.broadcast_to(got_ref[inner, frame, pl.ds(row, 1)], height.shape)
            bit = jnp.bitwise_and(jnp.right_shift(line, height), 1)
            bits_ref[pl.ds(row * 128 + frame * 16, 16)] = bit.astype(jnp.float32).astype(
                jnp.bfloat16
            )
    spread = dot_nt(order, bits_ref[...]).astype(jnp.bfloat16)
    stacked = jnp.concatenate(
        [spread[:, row * 128 : row * 128 + 128] for row in range(band)], axis=0
    )
    lifted = jnp.maximum(dot_nn(stacked, lift_ref[...]), 0.0)
    lifted = lifted.reshape(band // 2, 2, phases // 2, 2, BLOCK, lifted.shape[-1])
    for parity, ref in ((0, even_ref), (1, odd_ref)):
        here = lifted[:, parity, :, 0]
        right = lifted[:, parity, :, 1]
        left = jnp.concatenate([shift_block(right[:, -1], 1)[:, None], right[:, :-1]], axis=1)
        taps = [part.reshape(-1, part.shape[-1]) for part in (left, here, right)]
        lane = lax.broadcasted_iota(jnp.int32, (taps[0].shape[0], 128), 1)
        tail = jnp.where(lane < rest, taps[0][:, 128:], taps[1][:, 128:])
        tail = jnp.where(lane < 2 * rest, tail, taps[2][:, 128:])
        cells = jnp.concatenate([part[:, :128] for part in taps] + [tail], axis=1)
        if index is None:
            ref[...] = cells.astype(jnp.bfloat16)
        else:
            at = pl.multiple_of((index * (band // 2) + parity) * row_cells, row_cells)
            ref[pl.ds(at, cells.shape[0])] = cells.astype(jnp.bfloat16)


def band_label(label_ref, inner, index, shape):
    lane = lax.broadcasted_iota(jnp.int32, shape, 1)
    row = lax.broadcasted_iota(jnp.int32, (shape[0], BLOCK), 0)
    column = lax.broadcasted_iota(jnp.int32, (shape[0], BLOCK), 1)
    label = jnp.broadcast_to(label_ref[inner].astype(jnp.float32), row.shape)
    label = jnp.sum(jnp.where(row == column, label, 0.0), axis=1, keepdims=True)
    return jnp.where(lane == index, label, 0.0)


def own_kernel(
    got_hbm,
    label_hbm,
    lift_hbm,
    first_w_hbm,
    second_w_hbm,
    third_w_hbm,
    fourth_w_hbm,
    even_ref,
    odd_ref,
    labels_ref,
    lift_all_ref,
    first_all_ref,
    second_w_ref,
    third_w_ref,
    fourth_w_ref,
    got_ref,
    label_ref,
    lift_ref,
    first_w_ref,
    bits_ref,
    sems,
):
    pairs = (
        (got_hbm, got_ref),
        (lift_hbm, lift_ref),
        (label_hbm, label_ref),
        (first_w_hbm, first_w_ref),
        (second_w_hbm, second_w_ref),
        (third_w_hbm, third_w_ref),
        (fourth_w_hbm, fourth_w_ref),
    )
    pairs = pairs[:-1] + tuple(
        (fourth_w_hbm.at[pl.ds(tap, 1)], fourth_w_ref.at[pl.ds(tap, 1)]) for tap in range(9)
    )
    copies = [
        pltpu.make_async_copy(source, target, sems.at[k])
        for k, (source, target) in enumerate(pairs)
    ]
    for copy in copies:
        copy.start()
    me = lax.axis_index("space")
    _, frames, _, cols = got_ref.shape
    heights, width = lift_ref.shape
    rest = first_w_ref.shape[1] - 128
    bits_ref[...] = jnp.zeros(bits_ref.shape, jnp.bfloat16)
    first_all_ref[...] = jnp.zeros(first_all_ref.shape, jnp.bfloat16)
    order = column_order(cols)
    copies[1].wait()
    tall = jnp.concatenate(
        [lift_ref[...].astype(jnp.float32), jnp.zeros((16 - heights, width), jnp.float32)], axis=0
    )
    tall = jnp.concatenate([tall] * (256 // width), axis=1)
    tall = jnp.concatenate([tall] * 8, axis=0)
    frame_of_row = lax.broadcasted_iota(jnp.int32, tall.shape, 0) // 16
    lane = lax.broadcasted_iota(jnp.int32, tall.shape, 1)
    frame_of_lane = jnp.minimum(lane // width, frames - 1)
    keep = (frame_of_row == frame_of_lane) & (lane < 128 + 3 * rest)
    lift_all_ref[...] = jnp.where(keep, tall, 0.0).astype(jnp.bfloat16)
    copies[0].wait()
    band_cells(got_ref, 0, None, order, lift_all_ref, bits_ref, even_ref, odd_ref, rest)
    copies[2].wait()
    labels_ref[...] = band_label(label_ref, 0, me, labels_ref.shape).astype(jnp.bfloat16)
    copies[3].wait()
    for tap in range(9):
        row_tap, col_tap = divmod(tap, 3)
        first_all_ref[row_tap, pl.ds(col_tap * 128, 128)] = first_w_ref[tap, pl.ds(0, 128)]
        first_all_ref[row_tap, pl.ds(384 + col_tap * rest, rest)] = first_w_ref[
            tap, pl.ds(128, rest)
        ]
    for copy in copies[4:]:
        copy.wait()


def early_kernel(pieces, rest, *refs):
    got_refs = refs[:pieces]
    (
        lift_all_ref,
        first_all_ref,
        second_w_ref,
        own_even_ref,
        own_odd_ref,
        even_ref,
        odd_ref,
        send_ref,
        first_ref,
        first_slope_ref,
        second_slope_ref,
        bits_ref,
    ) = refs[pieces:]
    me = lax.axis_index("space")
    bands = 1 << pieces
    _, _, band, cols = got_refs[0].shape
    phases, row_cells = cols // BLOCK, cols // 2
    order = column_order(cols)
    cells = own_even_ref.shape[0]
    at = pl.multiple_of(me * cells, cells)
    even_ref[pl.ds(at, cells)] = own_even_ref[...]
    odd_ref[pl.ds(pl.multiple_of(at + row_cells, row_cells), cells)] = own_odd_ref[...]
    odd_ref[pl.ds(0, row_cells)] = jnp.zeros((row_cells, odd_ref.shape[1]), jnp.bfloat16)
    bits_ref[...] = jnp.zeros(bits_ref.shape, jnp.bfloat16)
    for slot in range(1, bands):
        piece = slot.bit_length() - 1
        inner = slot - (1 << piece)
        band_cells(
            got_refs[piece],
            inner,
            me ^ slot,
            order,
            lift_all_ref,
            bits_ref,
            even_ref,
            odd_ref,
            rest,
        )

    rows, phases = bands * band // 2, phases // 2
    cells = rows * row_cells
    pre = dot_nn(odd_ref[pl.ds(0, cells)], first_all_ref[0])
    pre += dot_nn(even_ref[...], first_all_ref[1])
    pre += dot_nn(odd_ref[pl.ds(row_cells, cells)], first_all_ref[2])
    value, slope = silu_and_slope(pre)
    shape = (1, rows, phases, BLOCK, value.shape[-1])
    zero_row(first_ref)
    fill_map(first_ref, value.reshape(shape), 1)
    first_slope_ref[...] = slope.reshape(shape)

    rows, phases = rows // 2, phases // 2
    pre = None
    for tap in range(9):
        cells = map_tap(first_ref, tap // 3, tap % 3, rows, phases)
        part = dot_nn(cells, second_w_ref[tap])
        pre = part if pre is None else pre + part
    value, slope = silu_and_slope(pre)
    second_slope_ref[...] = slope.reshape(second_slope_ref.shape)
    sent = value.shape[0]
    send_ref[pl.ds(0, sent)] = value.astype(jnp.bfloat16)
    send_ref[pl.ds(sent, 16)] = jnp.zeros((16, send_ref.shape[1]), jnp.bfloat16)


def transpose_kernel(weight_ref, out_ref):
    for tap in range(weight_ref.shape[0]):
        out_ref[tap] = weight_ref[tap].T


def take_samples(slot_refs, second_ref, label_ref, bands):
    count = sum(ref.shape[0] for ref in slot_refs)
    width = count.bit_length() - 1
    chunk = second_ref.shape[0]
    me = lax.axis_index("dp")
    where = [(ref, inner) for ref in slot_refs for inner in range(ref.shape[0])]
    for slot in range(count):
        reverse = sum(((slot >> k) & 1) << (width - 1 - k) for k in range(width))
        sample = me ^ reverse
        ref, inner = where[slot]

        def take(ref=ref, inner=inner, place=sample % chunk):
            put_sample(ref, inner, second_ref, label_ref, place, bands)

        if chunk == count:
            take()
        else:
            pl.when(sample // chunk == pl.program_id(0))(take)


def third_taps(second_ref, taps_ref, rows, phases):
    channels = second_ref.shape[-1]
    for tap in range(9):
        taps_ref[:, pl.ds(tap * channels, channels)] = map_tap(
            second_ref, tap // 3, tap % 3, rows, phases
        )


def delta_columns(ref, rows, phases):
    columns = {}
    for row_step in range(2):
        for col_step in range(2):
            cells = ref[:, pl.ds(row_step, rows), pl.ds(col_step, phases)]
            cells = cells.reshape(-1, cells.shape[-1])
            columns[row_step, col_step] = cells.T.astype(jnp.bfloat16)
    return columns


def column_parts(columns, weight_ref, row_parity, col_parity, rows, phases):
    taps = (((1, 0),), ((2, 0), (0, 1)))
    total = None
    for row_tap, row_step in taps[row_parity]:
        for col_tap, col_step in taps[col_parity]:
            part = dot_nn(weight_ref[3 * row_tap + col_tap], columns[row_step, col_step])
            total = part if total is None else total + part
    return total.T.reshape(-1, rows, phases, BLOCK, total.shape[0])


def put_label(ref, inner, label_ref, place, bands):
    cells = 4 * bands * 4 * BLOCK
    label = ref[inner, pl.ds(cells, 16)].astype(jnp.float32)[:BLOCK]
    for index in range(bands):
        label_ref[place, index] = jnp.broadcast_to(label[:, index : index + 1], label.shape)


def put_sample(ref, inner, second_ref, label_ref, place, bands):
    rows, phases = 4 * bands, 4
    cells = rows * phases * BLOCK
    second = ref[inner, pl.ds(0, cells)].astype(jnp.float32)
    fill_map(
        second_ref.at[pl.ds(place, 1)],
        second.reshape(1, rows, phases, BLOCK, second.shape[-1]),
        1,
    )
    if label_ref is not None:
        put_label(ref, inner, label_ref, place, bands)


def deep_layers(
    batch,
    bands,
    third_w_ref,
    fourth_w_ref,
    fourth_parts,
    head_ref,
    fourth_taps_ref,
    second_ref,
    label_ref,
    third_taps_ref,
    third_ref,
    third_slope_ref,
    third_delta_ref,
    fourth_delta_ref,
):
    value, slope = third_layer(second_ref, third_w_ref, third_taps_ref, bands)
    zero_row(third_ref)
    fill_map(third_ref, value, 1)
    third_slope_ref[...] = slope.reshape(third_slope_ref.shape)
    return deeper_layers(
        batch,
        bands,
        fourth_w_ref,
        fourth_parts,
        head_ref,
        fourth_taps_ref,
        label_ref,
        third_ref,
        third_slope_ref,
        third_delta_ref,
        fourth_delta_ref,
    )


def third_layer(second_ref, third_w_ref, third_taps_ref, bands):
    rows, phases = 2 * bands, 2
    third_taps(second_ref, third_taps_ref, rows, phases)
    weight = third_w_ref[...].reshape(third_taps_ref.shape[1], -1)
    value, slope = silu_and_slope(dot_nn(third_taps_ref[...], weight))
    shape = (second_ref.shape[0], rows, phases, BLOCK, value.shape[-1])
    return value.reshape(shape), slope.reshape(shape)


def deeper_layers(
    batch,
    bands,
    fourth_w_ref,
    fourth_parts,
    head_ref,
    fourth_taps_ref,
    label_ref,
    third_ref,
    third_slope_ref,
    third_delta_ref,
    fourth_delta_ref,
):
    samples, channels = third_ref.shape[0], third_ref.shape[-1]
    rows, phases = bands, 1
    for tap in range(9):
        fourth_taps_ref[:, pl.ds(tap * channels, channels)] = map_tap(
            third_ref, tap // 3, tap % 3, rows, phases
        )
    weight = fourth_w_ref[...].reshape(fourth_taps_ref.shape[1], -1)
    value, slope = silu_and_slope(dot_nn(fourth_taps_ref[...], weight))
    head = head_ref[...].astype(jnp.float32)
    labels = label_ref[...].reshape(-1, label_ref.shape[-1])[:, :1]
    logits = jnp.sum(value * head, axis=1, keepdims=True)
    logit_grad = (jax.nn.sigmoid(logits) - labels) / batch
    delta = rounded(logit_grad * head * slope)
    last_row_zero(fourth_delta_ref)
    fill_delta(fourth_delta_ref, delta.reshape(samples, rows, phases, BLOCK, delta.shape[-1]))
    parts = fourth_parts(fourth_delta_ref, rows, phases)
    for row_parity in range(2):
        for col_parity in range(2):
            part = parts(row_parity, col_parity, rows, phases)
            part = rounded(part * third_slope_ref[:, :, row_parity, :, col_parity])
            for row in range(rows):
                third_delta_ref[:, 2 * row + row_parity, col_parity] = part[:, row, 0]
    return value, logit_grad, delta


def near_kernel(bands, near_ref, third_w_ref, taps_ref, map_ref, slope_ref, second_ref):
    zero_row(second_ref)
    for slot in range(near_ref.shape[0]):
        put_sample(near_ref, slot, second_ref, None, slot, bands)
    value, slope = third_layer(second_ref, third_w_ref, taps_ref, bands)
    map_ref[...] = value
    slope_ref[...] = slope


def far_kernel(
    batch,
    bands,
    near_ref,
    far_ref,
    last_ref,
    near_taps_ref,
    near_map_ref,
    near_slope_ref,
    third_w_ref,
    fourth_w_ref,
    fourth_wt_ref,
    head_ref,
    fourth_taps_ref,
    fourth_flat_ref,
    head_grad_ref,
    third_taps_ref,
    third_flat_ref,
    second_ref,
    far_taps_ref,
    label_ref,
    third_ref,
    third_slope_ref,
    third_delta_ref,
    fourth_delta_ref,
):
    half, early = near_ref.shape[0], far_ref.shape[0]
    zero_row(second_ref)
    for slot in range(half):
        ref, inner = (far_ref, slot) if slot < early else (last_ref, slot - early)
        put_sample(ref, inner, second_ref, None, slot, bands)
    value, slope = third_layer(second_ref, third_w_ref, far_taps_ref, bands)
    cells = far_taps_ref.shape[0] // half
    width = half.bit_length()
    me = lax.axis_index("dp")
    zero_row(third_ref)
    for slot in range(2 * half):
        place = me ^ sum(((slot >> k) & 1) << (width - 1 - k) for k in range(width))
        inner = slot % half
        at = pl.ds(pl.multiple_of(place * cells, cells), cells)
        one = pl.ds(place, 1)
        if slot < half:
            third_taps_ref[at] = near_taps_ref[pl.ds(inner * cells, cells)]
            fill_map(third_ref.at[one], near_map_ref[pl.ds(inner, 1)], 1)
            third_slope_ref[one] = near_slope_ref[pl.ds(inner, 1)].reshape(
                (1,) + third_slope_ref.shape[1:]
            )
            put_label(near_ref, inner, label_ref, place, bands)
        else:
            third_taps_ref[at] = far_taps_ref[pl.ds(inner * cells, cells)]
            fill_map(third_ref.at[one], value[inner : inner + 1], 1)
            third_slope_ref[one] = slope[inner : inner + 1].reshape(
                (1,) + third_slope_ref.shape[1:]
            )
            ref, inner = (far_ref, inner) if inner < early else (last_ref, inner - early)
            put_label(ref, inner, label_ref, place, bands)
    value, logit_grad, delta = deeper_layers(
        batch,
        bands,
        fourth_w_ref,
        lambda ref, *_: functools.partial(delta_parts, ref, fourth_wt_ref),
        head_ref,
        fourth_taps_ref,
        label_ref,
        third_ref,
        third_slope_ref,
        third_delta_ref,
        fourth_delta_ref,
    )
    head_grad_ref[...] = jnp.sum(value * logit_grad, axis=0, keepdims=True)
    fourth_flat_ref[...] = delta.astype(jnp.bfloat16)
    delta = third_delta_ref[...]
    third_flat_ref[...] = delta.reshape(-1, delta.shape[-1]).astype(jnp.bfloat16)


def deep_kernel(
    batch,
    bands,
    near_ref,
    far_ref,
    last_ref,
    third_w_ref,
    fourth_w_ref,
    fourth_wt_ref,
    head_ref,
    fourth_taps_ref,
    fourth_flat_ref,
    head_grad_ref,
    *refs,
):
    third_grad_ref, second_ref, label_ref, third_taps_ref = refs[:4]
    third_ref, third_slope_ref, third_delta_ref, fourth_delta_ref = refs[4:]
    zero_row(second_ref)
    take_samples((near_ref, far_ref, last_ref), second_ref, label_ref, bands)
    value, logit_grad, delta = deep_layers(
        batch,
        bands,
        third_w_ref,
        fourth_w_ref,
        lambda ref, *_: functools.partial(delta_parts, ref, fourth_wt_ref),
        head_ref,
        fourth_taps_ref,
        second_ref,
        label_ref,
        third_taps_ref,
        third_ref,
        third_slope_ref,
        third_delta_ref,
        fourth_delta_ref,
    )

    head_grad = jnp.sum(value * logit_grad, axis=0, keepdims=True)
    add_to(head_grad_ref, head_grad)
    fourth_flat_ref[...] = delta.astype(jnp.bfloat16)
    delta = third_delta_ref[...]
    delta = delta.reshape(-1, delta.shape[-1]).astype(jnp.bfloat16)
    add_to(third_grad_ref, dot_tn(delta, third_taps_ref[...]).T)


def local_kernel(
    batch,
    bands,
    payload_ref,
    third_w_ref,
    fourth_w_ref,
    head_ref,
    second_w_ref,
    even_ref,
    odd_ref,
    first_ref,
    first_slope_ref,
    second_slope_ref,
    *refs,
):
    keep_ref, pass_ref = refs[:2]
    third_ref, second_ref, first_delta_ref, flat_ref, second_map_ref, label_ref = refs[2:8]
    fourth_taps_ref = refs[8]
    third_delta_ref = refs[12]
    zero_row(second_map_ref)
    put_sample(payload_ref, 0, second_map_ref, label_ref, 0, bands)
    deep_layers(
        batch,
        bands,
        third_w_ref,
        fourth_w_ref,
        lambda ref, *size: functools.partial(
            column_parts, delta_columns(ref, *size), fourth_w_ref
        ),
        head_ref,
        fourth_taps_ref,
        second_map_ref,
        label_ref,
        *refs[9:14],
    )
    sample = lax.axis_index("dp")
    _, rows, phases, _, _ = third_delta_ref.shape
    fill_delta(third_ref, third_delta_ref[...])
    last_row_zero(third_ref)
    last_row_zero(second_ref)
    columns = delta_columns(third_ref, rows, phases)
    for row_parity in range(2):
        for col_parity in range(2):
            part = column_parts(columns, third_w_ref, row_parity, col_parity, rows, phases)
            for row in range(rows):
                for phase in range(phases):
                    at = (slice(None), 2 * row + row_parity, 2 * phase + col_parity)
                    second_ref[at] = rounded(part[:, row, phase] * second_slope_ref[at])
    rows, phases = 2 * rows, 2 * phases
    second_ref[:, :, phases] = shift_block(second_ref[:, :, 0], -1)
    columns = delta_columns(second_ref, rows, phases)
    for row_parity in range(2):
        for col_parity in range(2):
            part = column_parts(columns, second_w_ref, row_parity, col_parity, rows, phases)
            for row in range(rows):
                for phase in range(phases):
                    at = (slice(None), 2 * row + row_parity, 2 * phase + col_parity)
                    first_delta_ref[at] = rounded(part[:, row, phase] * first_slope_ref[at])
    delta = second_ref[:, pl.ds(0, rows), pl.ds(0, phases)]
    delta = delta.reshape(-1, delta.shape[-1]).astype(jnp.bfloat16)
    depth = first_ref.shape[-1]
    for tap in range(9):
        cells = map_tap(first_ref, tap // 3, tap % 3, rows, phases)
        flat_ref[pl.ds((12 + tap) * depth, depth)] = dot_tn(cells, delta)
    delta = first_delta_ref[...]
    delta = delta.reshape(-1, delta.shape[-1]).astype(jnp.bfloat16)
    cells = delta.shape[0]
    row_cells = cells // (2 * rows)
    taps = (odd_ref[pl.ds(0, cells)], even_ref[...], odd_ref[pl.ds(row_cells, cells)])
    for tap in range(3):
        part = dot_tn(delta, taps[tap])
        for piece in range(4):
            flat_ref[pl.ds((4 * tap + piece) * depth, depth)] = part[
                :, piece * 128 : piece * 128 + 128
            ]
    share = keep_ref.shape[1]
    for slot in range(4):
        at = pl.multiple_of(((sample % 4) ^ slot) * share, share)
        ref = pass_ref if slot % 2 else keep_ref
        ref[slot // 2] = flat_ref[pl.ds(at, share)].astype(jnp.bfloat16)


def add_to(ref, value):
    first = pl.program_id(0) == 0
    ref[...] = jnp.where(first, 0.0, ref[...]) + value


def third_grad_kernel(taps_ref, delta_ref, out_hbm, grad_ref, sems):
    depth = grad_ref.shape[1]
    delta = delta_ref[...].T
    copies = []
    for row_tap in range(3):
        part = dot_nn(delta, taps_ref[:, pl.ds(3 * row_tap * depth, 3 * depth)])
        grad_ref[pl.ds(3 * row_tap, 3)] = part.T.reshape(3, depth, part.shape[0])
        rows = pl.ds(3 * row_tap, 3)
        copies.append(
            pltpu.make_async_copy(grad_ref.at[rows], out_hbm.at[rows], sems.at[row_tap])
        )
        copies[-1].start()
    for copy in copies:
        copy.wait()


def fourth_grad_alone_kernel(fourth_taps_ref, fourth_flat_ref, out_hbm, grad_ref, sems):
    depth = grad_ref.shape[1]
    copies = []
    for tap in range(9):
        grad_ref[tap] = dot_tn(
            fourth_taps_ref[:, pl.ds(tap * depth, depth)], fourth_flat_ref[...]
        )
        copy = pltpu.make_async_copy(grad_ref.at[tap], out_hbm.at[tap], sems.at[tap])
        copy.start()
        copies.append(copy)
    for copy in copies:
        copy.wait()


def fourth_grad_kernel(fourth_taps_ref, fourth_flat_ref, out_ref):
    @pl.when(pl.program_id(1) == 0)
    def _():
        out_ref[...] = jnp.zeros(out_ref.shape, jnp.float32)

    out_ref[...] += dot_tn(fourth_taps_ref[...], fourth_flat_ref[...])


def finish_kernel(*refs):
    got_refs = refs[:4]
    temporal_hbm, middle_hbm, temporal_ref, middle_ref, flat_ref, sems = refs[4:]
    me = lax.axis_index("dp") % 4
    share = got_refs[0].shape[0]
    for slot in range(4):
        at = pl.multiple_of((me ^ slot) * share, share)
        flat_ref[pl.ds(at, share)] = got_refs[slot][...].astype(jnp.float32)
    depth = temporal_ref.shape[2]
    middle_ref[...] = flat_ref[pl.ds(12 * depth, 9 * depth)]
    copies = [pltpu.make_async_copy(middle_ref, middle_hbm, sems.at[3])]
    copies[0].start()
    rest = temporal_ref.shape[1] - 128
    for tap in range(3):
        parts = [flat_ref[pl.ds((4 * tap + piece) * depth, depth)].T for piece in range(4)]
        for col_tap in range(3):
            temporal_ref[3 * tap + col_tap, pl.ds(0, 128)] = parts[col_tap]
            temporal_ref[3 * tap + col_tap, pl.ds(128, rest)] = parts[3][
                col_tap * rest : col_tap * rest + rest
            ]
        rows = pl.ds(3 * tap, 3)
        copies.append(
            pltpu.make_async_copy(temporal_ref.at[rows], temporal_hbm.at[rows], sems.at[tap])
        )
        copies[-1].start()
    for copy in copies:
        copy.wait()


def cost(flops, size):
    return pl.CostEstimate(flops=flops, bytes_accessed=size, transcendentals=0)


def swapped(value, axis, bit):
    return lax.ppermute(value, axis, [(i, i ^ bit) for i in range(lax.axis_size(axis))])


def band_pieces(value, bands):
    pieces = [value]
    bit = 1
    while bit < bands:
        whole = pieces[0] if bit == 1 else jnp.concatenate(pieces, axis=0)
        pieces.append(swapped(whole, "space", bit))
        bit *= 2
    return pieces


def put(buffer, part, at):
    return lax.dynamic_update_slice(buffer, part, (at,) + (0,) * (buffer.ndim - 1))


def after(value, *others):
    return lax.optimization_barrier((value, *others))[0]


def gather_and_sum(payload, local_sums, transposed, samples):
    half, quarter = samples // 2, samples // 4
    near = put(jnp.zeros((half,) + payload.shape[1:], payload.dtype), payload, 0)
    got = swapped(payload, "dp", quarter * 2) if quarter > 1 else None
    keep, passed = local_sums()
    core = swapped(passed, "dp", 1)
    mine, theirs = added(keep[0], core[0]), added(keep[1], core[1])
    mine_beside = swapped(theirs, "dp", 2)
    weights = transposed(theirs)
    count, beside_count = 1, 0
    while count < quarter:
        near = put(near, after(got, keep), count)
        count *= 2
        if count < quarter:
            part = near[beside_count:count]
            got = swapped(near[:count], "dp", half // count)
            beside = swapped(after(part, theirs), "dp", 2)
            near = put(near, beside, quarter + beside_count)
            beside_count = count
    total = added(mine, after(mine_beside, weights))
    beside = swapped(after(near[beside_count:quarter], theirs), "dp", 2)
    early = swapped(near[: quarter + beside_count], "dp", 1)
    bit = 4
    while 2 * bit < samples:
        other = swapped(total, "dp", bit)
        beside = after(beside, total)
        total = added(total, after(other, beside))
        bit *= 2
    near = put(near, beside, quarter + beside_count)
    last = swapped(beside, "dp", 1)
    return near, early, last, total, bit, weights


def added(*parts):
    total = parts[0].astype(jnp.float32)
    for part in parts[1:]:
        total = total + part.astype(jnp.float32)
    return total.astype(jnp.bfloat16)


def local(
    occupancy,
    state_labels,
    lift_weight,
    temporal_weight,
    middle_weight,
    deeper_weight,
    deepest_weight,
    head_weight,
):
    bands = lax.axis_size("space")
    samples = lax.axis_size("dp")
    _, frames, band, cols = occupancy.shape
    lift_all = frames * lift_weight.shape[1]
    one, two = middle_weight.shape[2:]
    three, four = deepest_weight.shape[2:]
    f32, bf16 = jnp.float32, jnp.bfloat16
    shaped = jax.ShapeDtypeStruct
    phases = cols // BLOCK
    rows = bands * band
    small = samples * bands <= 32
    vmem = pl.BlockSpec(memory_space=pltpu.VMEM)

    def grant(size):
        return pltpu.CompilerParams(vmem_limit_bytes=(size if small else 60) * MIB)

    lines = band_pieces(occupancy, bands)
    first_w = temporal_weight.reshape(9, lift_all, one)
    second_w = middle_weight.reshape(9, one, two)
    third_w = deeper_weight.reshape(9, two, three)
    fourth_w = deepest_weight.reshape(9, three, four)
    head = head_weight.reshape(1, four)

    sent = rows // 4 * phases // 4 * BLOCK + 16
    hbm = pl.BlockSpec(memory_space=pltpu.HBM)
    even_shape = shaped((rows // 2 * cols // 2, 512), bf16)
    odd_shape = shaped(((rows // 2 + 1) * cols // 2, 512), bf16)
    bits_scratch = pltpu.VMEM((band * 128, cols), bf16)
    own_cells = shaped((band // 2 * cols // 2, 512), bf16)
    own_args = [
        pltpu.with_memory_space_constraint(value, pltpu.HBM)
        for value in (
            occupancy,
            state_labels,
            lift_weight,
            first_w,
            second_w,
            third_w,
            fourth_w,
        )
    ]
    (
        own_even,
        own_odd,
        own_labels,
        lift_all_w,
        first_all,
        second_w2,
        third_w2,
        fourth_w2,
    ) = pl.pallas_call(
        own_kernel,
        out_shape=(
            own_cells,
            own_cells,
            shaped((16, two), bf16),
            shaped((128, 256), bf16),
            shaped((3, 512, one), bf16),
            shaped(second_w.shape, bf16),
            shaped(third_w.shape, bf16),
            shaped(fourth_w.shape, bf16),
        ),
        in_specs=[hbm] * 7,
        out_specs=(vmem,) * 8,
        scratch_shapes=[
            pltpu.VMEM(occupancy.shape, occupancy.dtype),
            pltpu.VMEM(state_labels.shape, state_labels.dtype),
            pltpu.VMEM(lift_weight.shape, bf16),
            pltpu.VMEM(first_w.shape, bf16),
            bits_scratch,
            pltpu.SemaphoreType.DMA((15,)),
        ],
        compiler_params=grant(24),
        cost_estimate=cost(100_000_000, 10_000_000),
        name="own_band",
    )(*own_args)
    pieces = len(lines) - 1
    even, odd, payload, first, first_slope, second_slope = pl.pallas_call(
        functools.partial(early_kernel, pieces, lift_all - 128),
        out_shape=(
            even_shape,
            odd_shape,
            shaped((sent, two), bf16),
            shaped((1, rows // 4 + 1, 2, phases // 4 + 1, 2, BLOCK, one), f32),
            shaped((1, rows // 2, phases // 2, BLOCK, one), f32),
            shaped((1, rows // 4, phases // 4, BLOCK, two), f32),
        ),
        in_specs=[vmem] * (pieces + 5),
        out_specs=(vmem,) * 6,
        scratch_shapes=[bits_scratch],
        compiler_params=grant(24),
        cost_estimate=cost(150_000_000, 4_000_000),
        name="early",
    )(*lines[1:], lift_all_w, first_all, second_w2, own_even, own_odd)

    labels, bit = own_labels, 1
    while bit < bands:
        labels = labels + swapped(labels, "space", bit)
        bit *= 2
    payload = put(payload, labels, sent - 16)[None]
    deep_weights = (third_w2, fourth_w2)

    third_cells = 2 * bands * 2 * BLOCK
    fourth_cells = bands * BLOCK

    def second_scratch(count):
        return pltpu.VMEM((count, 2 * bands + 1, 2, 3, 2, BLOCK, two), f32)

    def third_taps_scratch(count):
        return pltpu.VMEM((count * third_cells, 9 * two), bf16)

    def deep_scratch(count):
        return [
            third_taps_scratch(count),
            pltpu.VMEM((count, bands + 1, 2, 2, 2, BLOCK, three), f32),
            pltpu.VMEM((count, bands, 2, 1, 2, BLOCK, three), f32),
            pltpu.VMEM((count, 2 * bands, 2, BLOCK, three), f32),
            pltpu.VMEM((count, bands + 1, 2, BLOCK, four), f32),
        ]

    share = 21 * one // 4
    local_call = pl.pallas_call(
        functools.partial(local_kernel, samples, bands),
        out_shape=(shaped((2, share, two), bf16),) * 2,
        in_specs=[vmem] * 10,
        out_specs=(vmem,) * 2,
        scratch_shapes=[
            pltpu.VMEM((1, 2 * bands + 1, 3, BLOCK, three), f32),
            pltpu.VMEM((1, 4 * bands + 1, 5, BLOCK, two), f32),
            pltpu.VMEM(first_slope.shape, f32),
            pltpu.VMEM((21 * one, two), f32),
            second_scratch(1),
            pltpu.VMEM((1, bands, BLOCK, two), f32),
            pltpu.VMEM((fourth_cells, 9 * three), bf16),
        ]
        + deep_scratch(1),
        compiler_params=grant(24),
        cost_estimate=cost(300_000_000, 9_000_000),
        name="local",
    )
    maps = (head, second_w2, even, odd, first, first_slope, second_slope)
    transpose_call = pl.pallas_call(
        transpose_kernel,
        out_shape=shaped((9, four, three), bf16),
        in_specs=[vmem],
        out_specs=vmem,
        compiler_params=grant(16),
        cost_estimate=cost(10_000_000, 5_000_000),
        name="transpose",
    )

    near, far, last, total, bit, fourth_wt = gather_and_sum(
        payload,
        lambda: local_call(payload, *deep_weights, *maps),
        lambda keep: transpose_call(after(fourth_w2, keep)),
        samples,
    )
    near = after(near, total)

    chunk = max(1, min(samples, 32 // bands))
    steps = samples // chunk
    full = lambda *shape: pl.BlockSpec(shape, lambda i: (0,) * len(shape))
    grad_shape = shaped((9 * two, three), f32)
    fourth_shapes = (
        shaped((samples * fourth_cells, 9 * three), bf16),
        shaped((samples * fourth_cells, four), bf16),
        shaped((1, four), f32),
    )
    label_scratch = pltpu.VMEM((chunk, bands, BLOCK, two), f32)
    deep_cost = cost(1_300_000_000, 12_000_000)
    if small:
        half = samples // 2
        half_shapes = (
            shaped((half * third_cells, 9 * two), bf16),
            shaped((half, 2 * bands, 2, BLOCK, three), f32),
            shaped((half, 2 * bands, 2, BLOCK, three), f32),
        )
        near_third = pl.pallas_call(
            functools.partial(near_kernel, bands),
            out_shape=half_shapes,
            in_specs=[vmem] * 2,
            out_specs=(vmem,) * 3,
            scratch_shapes=[second_scratch(half)],
            compiler_params=grant(24),
            cost_estimate=cost(300_000_000, 4_000_000),
            name="near",
        )(near, third_w2)
        fourth_taps, fourth_flat, head_grad, *thirds = pl.pallas_call(
            functools.partial(far_kernel, samples, bands),
            out_shape=fourth_shapes
            + (
                shaped((samples * third_cells, 9 * two), bf16),
                shaped((samples * third_cells, three), bf16),
            ),
            in_specs=[vmem] * 10,
            out_specs=(vmem,) * 5,
            scratch_shapes=[second_scratch(half), third_taps_scratch(half), label_scratch]
            + deep_scratch(chunk)[1:],
            compiler_params=grant(40),
            cost_estimate=deep_cost,
            name="deep",
        )(near, far, last, *near_third, *deep_weights, fourth_wt, head)
        deeper_grad = None
    else:
        fourth_taps, fourth_flat, head_grad, deeper_grad = pl.pallas_call(
            functools.partial(deep_kernel, samples, bands),
            grid=(steps,),
            out_shape=fourth_shapes + (grad_shape,),
            in_specs=[
                full(*value.shape) for value in (near, far, last, *deep_weights, fourth_wt, head)
            ],
            out_specs=(
                pl.BlockSpec((chunk * fourth_cells, 9 * three), lambda i: (i, 0)),
                pl.BlockSpec((chunk * fourth_cells, four), lambda i: (i, 0)),
                full(1, four),
                full(9 * two, three),
            ),
            scratch_shapes=[second_scratch(chunk), label_scratch] + deep_scratch(chunk),
            compiler_params=grant(40),
            cost_estimate=deep_cost,
            name="deep",
        )(near, far, last, *deep_weights, fourth_wt, head)

    if bit < samples:
        other, fourth_flat = lax.optimization_barrier((swapped(total, "dp", bit), fourth_flat))
        total = added(total, other)
    beside = swapped(total, "dp", 2)
    core = swapped(total, "dp", 1)
    if small:
        deepest_grad = pl.pallas_call(
            fourth_grad_alone_kernel,
            out_shape=shaped((9, three, four), f32),
            in_specs=[vmem] * 2,
            out_specs=pl.BlockSpec(memory_space=pl.ANY),
            scratch_shapes=[
                pltpu.VMEM((9, three, four), f32),
                pltpu.SemaphoreType.DMA((9,)),
            ],
            compiler_params=grant(16),
            cost_estimate=cost(600_000_000, 6_000_000),
            name="fourth_grad",
        )(fourth_taps, fourth_flat)
    else:
        deepest_grad = pl.pallas_call(
            fourth_grad_kernel,
            grid=(3, steps),
            out_shape=shaped((9 * three, four), f32),
            in_specs=[
                pl.BlockSpec((chunk * fourth_cells, 3 * three), lambda t, i: (i, t)),
                pl.BlockSpec((chunk * fourth_cells, four), lambda t, i: (i, 0)),
            ],
            out_specs=pl.BlockSpec((3 * three, four), lambda t, i: (t, 0)),
            compiler_params=grant(16),
            cost_estimate=cost(600_000_000, 6_000_000),
            name="fourth_grad",
        )(fourth_taps, fourth_flat)
    beside, deepest_grad = lax.optimization_barrier((beside, deepest_grad))
    across = swapped(beside, "dp", 1)
    if small:
        deeper_grad = pl.pallas_call(
            third_grad_kernel,
            out_shape=shaped((9, two, three), f32),
            in_specs=[vmem] * 2,
            out_specs=pl.BlockSpec(memory_space=pl.ANY),
            scratch_shapes=[
                pltpu.VMEM((9, two, three), f32),
                pltpu.SemaphoreType.DMA((3,)),
            ],
            compiler_params=grant(24),
            cost_estimate=cost(600_000_000, 4_000_000),
            name="third_grad",
        )(*thirds)
    across, deeper_grad = lax.optimization_barrier((across, deeper_grad))
    temporal_grad, middle_grad = pl.pallas_call(
        finish_kernel,
        out_shape=(shaped((9, lift_all, one), f32), shaped((9 * one, two), f32)),
        in_specs=[vmem] * 4,
        out_specs=(pl.BlockSpec(memory_space=pl.ANY),) * 2,
        scratch_shapes=[
            pltpu.VMEM((9, lift_all, one), f32),
            pltpu.VMEM((9 * one, two), f32),
            pltpu.VMEM((21 * one, two), f32),
            pltpu.SemaphoreType.DMA((4,)),
        ],
        compiler_params=grant(16),
        cost_estimate=cost(1_000_000, 1_500_000),
        name="finish",
    )(total, core, beside, across)
    return (
        temporal_grad.reshape(temporal_weight.shape),
        middle_grad.reshape(middle_weight.shape),
        deeper_grad.reshape(deeper_weight.shape),
        deepest_grad.reshape(deepest_weight.shape),
        head_grad.reshape(four),
    )


def solution(mesh):
    return jax.shard_map(
        local,
        mesh=mesh,
        in_specs=(
            P("dp", None, "space", None),
            P("dp", "space", None),
            P(),
            P(),
            P(),
            P(),
            P(),
            P(),
        ),
        out_specs=(P(), P(), P(), P(), P()),
        check_vma=False,
    )
```

```python
import functools

import jax
import jax.numpy as jnp
from jax import lax
from jax.experimental import pallas as pl
from jax.experimental.pallas import tpu as pltpu
from jax.sharding import PartitionSpec as P

BLOCK = 8
MIB = 1 << 20


def f32_dot(left, right, contract):
    return lax.dot_general(
        left, right, ((contract[0], contract[1]), ((), ())), preferred_element_type=jnp.float32
    )


def dot_nn(left, right):
    return f32_dot(left, right, ((1,), (0,)))


def dot_nt(left, right):
    return f32_dot(left, right, ((1,), (1,)))


def dot_tn(left, right):
    return f32_dot(left, right, ((0,), (0,)))


def rounded(value):
    return value.astype(jnp.bfloat16).astype(jnp.float32)


def silu_and_slope(pre):
    gate = jax.nn.sigmoid(pre)
    return rounded(pre * gate), gate * (1.0 + pre * (1.0 - gate))


def zero_row(ref):
    ref[:, 0, 0] = jnp.zeros(ref.shape[:1] + ref.shape[3:], ref.dtype)


def last_row_zero(ref):
    ref[:, ref.shape[1] - 1] = jnp.zeros(ref.shape[:1] + ref.shape[2:], ref.dtype)


def shift_block(value, step):
    shape = value.shape
    flat = value.reshape(-1, shape[-1])
    moved = pltpu.roll(flat, step % flat.shape[0], 0)
    index = lax.broadcasted_iota(jnp.int32, flat.shape, 0) % BLOCK
    edge = 0 if step > 0 else BLOCK - 1
    return jnp.where(index == edge, 0.0, moved).reshape(shape)


def fill_map(ref, value, offset):
    n, rows, phases, _, channels = value.shape
    split = value.reshape(n, rows, phases // 2, 2, BLOCK, channels)
    for row in range(rows):
        pair, parity = divmod(row + offset, 2)
        ref[:, pair, parity, pl.ds(0, phases // 2), 1] = split[:, row, :, 0]
        ref[:, pair, parity, pl.ds(1, phases // 2), 0] = split[:, row, :, 1]
        ref[:, pair, parity, 0, 0] = shift_block(split[:, row, phases // 2 - 1, 1], 1)


def map_tap(ref, row_tap, col_tap, out_rows, out_phases):
    cells = ref[
        :,
        pl.ds(row_tap // 2, out_rows),
        row_tap % 2,
        pl.ds(col_tap // 2, out_phases),
        col_tap % 2,
    ]
    return cells.reshape(-1, cells.shape[-1]).astype(jnp.bfloat16)


def fill_delta(ref, value):
    rows, phases = value.shape[1:3]
    ref[:, pl.ds(0, rows), pl.ds(0, phases)] = value
    ref[:, pl.ds(0, rows), phases] = shift_block(value[:, :, 0], -1)


def delta_parts(ref, weight_ref, row_parity, col_parity, rows, phases):
    taps = (((1, 0),), ((2, 0), (0, 1)))
    total = None
    for row_tap, row_step in taps[row_parity]:
        for col_tap, col_step in taps[col_parity]:
            cells = ref[:, pl.ds(row_step, rows), pl.ds(col_step, phases)]
            lead = cells.shape[:-1]
            flat = cells.reshape(-1, cells.shape[-1]).astype(jnp.bfloat16)
            part = dot_nn(flat, weight_ref[3 * row_tap + col_tap])
            total = part if total is None else total + part
    return total.reshape(*lead, total.shape[-1])


def column_order(cols):
    place = lax.broadcasted_iota(jnp.int32, (cols, cols), 0)
    column = lax.broadcasted_iota(jnp.int32, (cols, cols), 1)
    source = (place % BLOCK) * (cols // BLOCK) + place // BLOCK
    return jnp.where(column == source, 1.0, 0.0).astype(jnp.bfloat16)


def band_cells(got_ref, inner, index, order, lift_ref, bits_ref, even_ref, odd_ref, rest):
    _, frames, band, cols = got_ref.shape
    phases, row_cells = cols // BLOCK, cols // 2
    height = lax.broadcasted_iota(jnp.int32, (16, cols), 0)
    for row in range(band):
        for frame in range(frames):
            line = jnp.broadcast_to(got_ref[inner, frame, pl.ds(row, 1)], height.shape)
            bit = jnp.bitwise_and(jnp.right_shift(line, height), 1)
            bits_ref[pl.ds(row * 128 + frame * 16, 16)] = bit.astype(jnp.float32).astype(
                jnp.bfloat16
            )
    spread = dot_nt(order, bits_ref[...]).astype(jnp.bfloat16)
    stacked = jnp.concatenate(
        [spread[:, row * 128 : row * 128 + 128] for row in range(band)], axis=0
    )
    lifted = jnp.maximum(dot_nn(stacked, lift_ref[...]), 0.0)
    lifted = lifted.reshape(band // 2, 2, phases // 2, 2, BLOCK, lifted.shape[-1])
    for parity, ref in ((0, even_ref), (1, odd_ref)):
        here = lifted[:, parity, :, 0]
        right = lifted[:, parity, :, 1]
        left = jnp.concatenate([shift_block(right[:, -1], 1)[:, None], right[:, :-1]], axis=1)
        taps = [part.reshape(-1, part.shape[-1]) for part in (left, here, right)]
        lane = lax.broadcasted_iota(jnp.int32, (taps[0].shape[0], 128), 1)
        tail = jnp.where(lane < rest, taps[0][:, 128:], taps[1][:, 128:])
        tail = jnp.where(lane < 2 * rest, tail, taps[2][:, 128:])
        cells = jnp.concatenate([part[:, :128] for part in taps] + [tail], axis=1)
        if index is None:
            ref[...] = cells.astype(jnp.bfloat16)
        else:
            at = pl.multiple_of((index * (band // 2) + parity) * row_cells, row_cells)
            ref[pl.ds(at, cells.shape[0])] = cells.astype(jnp.bfloat16)


def band_label(label_ref, inner, index, shape):
    lane = lax.broadcasted_iota(jnp.int32, shape, 1)
    row = lax.broadcasted_iota(jnp.int32, (shape[0], BLOCK), 0)
    column = lax.broadcasted_iota(jnp.int32, (shape[0], BLOCK), 1)
    label = jnp.broadcast_to(label_ref[inner].astype(jnp.float32), row.shape)
    label = jnp.sum(jnp.where(row == column, label, 0.0), axis=1, keepdims=True)
    return jnp.where(lane == index, label, 0.0)


def own_kernel(
    got_hbm,
    label_hbm,
    lift_hbm,
    first_w_hbm,
    second_w_hbm,
    third_w_hbm,
    fourth_w_hbm,
    even_ref,
    odd_ref,
    labels_ref,
    lift_all_ref,
    first_all_ref,
    second_w_ref,
    third_w_ref,
    fourth_w_ref,
    got_ref,
    label_ref,
    lift_ref,
    first_w_ref,
    bits_ref,
    sems,
):
    pairs = (
        (got_hbm, got_ref),
        (lift_hbm, lift_ref),
        (label_hbm, label_ref),
        (first_w_hbm, first_w_ref),
        (second_w_hbm, second_w_ref),
        (third_w_hbm, third_w_ref),
        (fourth_w_hbm, fourth_w_ref),
    )
    pairs = pairs[:-1] + tuple(
        (fourth_w_hbm.at[pl.ds(tap, 1)], fourth_w_ref.at[pl.ds(tap, 1)]) for tap in range(9)
    )
    copies = [
        pltpu.make_async_copy(source, target, sems.at[k])
        for k, (source, target) in enumerate(pairs)
    ]
    for copy in copies:
        copy.start()
    me = lax.axis_index("space")
    _, frames, _, cols = got_ref.shape
    heights, width = lift_ref.shape
    rest = first_w_ref.shape[1] - 128
    bits_ref[...] = jnp.zeros(bits_ref.shape, jnp.bfloat16)
    first_all_ref[...] = jnp.zeros(first_all_ref.shape, jnp.bfloat16)
    order = column_order(cols)
    copies[1].wait()
    tall = jnp.concatenate(
        [lift_ref[...].astype(jnp.float32), jnp.zeros((16 - heights, width), jnp.float32)], axis=0
    )
    tall = jnp.concatenate([tall] * (256 // width), axis=1)
    tall = jnp.concatenate([tall] * 8, axis=0)
    frame_of_row = lax.broadcasted_iota(jnp.int32, tall.shape, 0) // 16
    lane = lax.broadcasted_iota(jnp.int32, tall.shape, 1)
    frame_of_lane = jnp.minimum(lane // width, frames - 1)
    keep = (frame_of_row == frame_of_lane) & (lane < 128 + 3 * rest)
    lift_all_ref[...] = jnp.where(keep, tall, 0.0).astype(jnp.bfloat16)
    copies[0].wait()
    band_cells(got_ref, 0, None, order, lift_all_ref, bits_ref, even_ref, odd_ref, rest)
    copies[2].wait()
    labels_ref[...] = band_label(label_ref, 0, me, labels_ref.shape).astype(jnp.bfloat16)
    copies[3].wait()
    for tap in range(9):
        row_tap, col_tap = divmod(tap, 3)
        first_all_ref[row_tap, pl.ds(col_tap * 128, 128)] = first_w_ref[tap, pl.ds(0, 128)]
        first_all_ref[row_tap, pl.ds(384 + col_tap * rest, rest)] = first_w_ref[
            tap, pl.ds(128, rest)
        ]
    for copy in copies[4:]:
        copy.wait()


def early_kernel(pieces, rest, *refs):
    got_refs = refs[:pieces]
    (
        lift_all_ref,
        first_all_ref,
        second_w_ref,
        own_even_ref,
        own_odd_ref,
        even_ref,
        odd_ref,
        send_ref,
        first_ref,
        first_slope_ref,
        second_slope_ref,
        bits_ref,
    ) = refs[pieces:]
    me = lax.axis_index("space")
    bands = 1 << pieces
    _, _, band, cols = got_refs[0].shape
    phases, row_cells = cols // BLOCK, cols // 2
    order = column_order(cols)
    cells = own_even_ref.shape[0]
    at = pl.multiple_of(me * cells, cells)
    even_ref[pl.ds(at, cells)] = own_even_ref[...]
    odd_ref[pl.ds(pl.multiple_of(at + row_cells, row_cells), cells)] = own_odd_ref[...]
    odd_ref[pl.ds(0, row_cells)] = jnp.zeros((row_cells, odd_ref.shape[1]), jnp.bfloat16)
    bits_ref[...] = jnp.zeros(bits_ref.shape, jnp.bfloat16)
    for slot in range(1, bands):
        piece = slot.bit_length() - 1
        inner = slot - (1 << piece)
        band_cells(
            got_refs[piece],
            inner,
            me ^ slot,
            order,
            lift_all_ref,
            bits_ref,
            even_ref,
            odd_ref,
            rest,
        )

    rows, phases = bands * band // 2, phases // 2
    cells = rows * row_cells
    pre = dot_nn(odd_ref[pl.ds(0, cells)], first_all_ref[0])
    pre += dot_nn(even_ref[...], first_all_ref[1])
    pre += dot_nn(odd_ref[pl.ds(row_cells, cells)], first_all_ref[2])
    value, slope = silu_and_slope(pre)
    shape = (1, rows, phases, BLOCK, value.shape[-1])
    zero_row(first_ref)
    fill_map(first_ref, value.reshape(shape), 1)
    first_slope_ref[...] = slope.reshape(shape)

    rows, phases = rows // 2, phases // 2
    pre = None
    for tap in range(9):
        cells = map_tap(first_ref, tap // 3, tap % 3, rows, phases)
        part = dot_nn(cells, second_w_ref[tap])
        pre = part if pre is None else pre + part
    value, slope = silu_and_slope(pre)
    second_slope_ref[...] = slope.reshape(second_slope_ref.shape)
    sent = value.shape[0]
    send_ref[pl.ds(0, sent)] = value.astype(jnp.bfloat16)
    send_ref[pl.ds(sent, 16)] = jnp.zeros((16, send_ref.shape[1]), jnp.bfloat16)


def transpose_kernel(weight_ref, out_ref):
    for tap in range(weight_ref.shape[0]):
        out_ref[tap] = weight_ref[tap].T


def take_samples(slot_refs, second_ref, label_ref, bands):
    count = sum(ref.shape[0] for ref in slot_refs)
    width = count.bit_length() - 1
    chunk = second_ref.shape[0]
    me = lax.axis_index("dp")
    where = [(ref, inner) for ref in slot_refs for inner in range(ref.shape[0])]
    for slot in range(count):
        reverse = sum(((slot >> k) & 1) << (width - 1 - k) for k in range(width))
        sample = me ^ reverse
        ref, inner = where[slot]

        def take(ref=ref, inner=inner, place=sample % chunk):
            put_sample(ref, inner, second_ref, label_ref, place, bands)

        if chunk == count:
            take()
        else:
            pl.when(sample // chunk == pl.program_id(0))(take)


def third_taps(second_ref, taps_ref, rows, phases):
    channels = second_ref.shape[-1]
    for tap in range(9):
        taps_ref[:, pl.ds(tap * channels, channels)] = map_tap(
            second_ref, tap // 3, tap % 3, rows, phases
        )


def delta_columns(ref, rows, phases):
    columns = {}
    for row_step in range(2):
        for col_step in range(2):
            cells = ref[:, pl.ds(row_step, rows), pl.ds(col_step, phases)]
            cells = cells.reshape(-1, cells.shape[-1])
            columns[row_step, col_step] = cells.T.astype(jnp.bfloat16)
    return columns


def column_parts(columns, weight_ref, row_parity, col_parity, rows, phases):
    taps = (((1, 0),), ((2, 0), (0, 1)))
    total = None
    for row_tap, row_step in taps[row_parity]:
        for col_tap, col_step in taps[col_parity]:
            part = dot_nn(weight_ref[3 * row_tap + col_tap], columns[row_step, col_step])
            total = part if total is None else total + part
    return total.T.reshape(-1, rows, phases, BLOCK, total.shape[0])


def put_label(ref, inner, label_ref, place, bands):
    cells = 4 * bands * 4 * BLOCK
    label = ref[inner, pl.ds(cells, 16)].astype(jnp.float32)[:BLOCK]
    for index in range(bands):
        label_ref[place, index] = jnp.broadcast_to(label[:, index : index + 1], label.shape)


def put_sample(ref, inner, second_ref, label_ref, place, bands):
    rows, phases = 4 * bands, 4
    cells = rows * phases * BLOCK
    second = ref[inner, pl.ds(0, cells)].astype(jnp.float32)
    fill_map(
        second_ref.at[pl.ds(place, 1)],
        second.reshape(1, rows, phases, BLOCK, second.shape[-1]),
        1,
    )
    if label_ref is not None:
        put_label(ref, inner, label_ref, place, bands)


def deep_layers(
    batch,
    bands,
    third_w_ref,
    fourth_w_ref,
    fourth_parts,
    head_ref,
    fourth_taps_ref,
    second_ref,
    label_ref,
    third_taps_ref,
    third_ref,
    third_slope_ref,
    third_delta_ref,
    fourth_delta_ref,
):
    value, slope = third_layer(second_ref, third_w_ref, third_taps_ref, bands)
    zero_row(third_ref)
    fill_map(third_ref, value, 1)
    third_slope_ref[...] = slope.reshape(third_slope_ref.shape)
    return deeper_layers(
        batch,
        bands,
        fourth_w_ref,
        fourth_parts,
        head_ref,
        fourth_taps_ref,
        label_ref,
        third_ref,
        third_slope_ref,
        third_delta_ref,
        fourth_delta_ref,
    )


def third_layer(second_ref, third_w_ref, third_taps_ref, bands):
    rows, phases = 2 * bands, 2
    third_taps(second_ref, third_taps_ref, rows, phases)
    weight = third_w_ref[...].reshape(third_taps_ref.shape[1], -1)
    value, slope = silu_and_slope(dot_nn(third_taps_ref[...], weight))
    shape = (second_ref.shape[0], rows, phases, BLOCK, value.shape[-1])
    return value.reshape(shape), slope.reshape(shape)


def deeper_layers(
    batch,
    bands,
    fourth_w_ref,
    fourth_parts,
    head_ref,
    fourth_taps_ref,
    label_ref,
    third_ref,
    third_slope_ref,
    third_delta_ref,
    fourth_delta_ref,
):
    samples, channels = third_ref.shape[0], third_ref.shape[-1]
    rows, phases = bands, 1
    for tap in range(9):
        fourth_taps_ref[:, pl.ds(tap * channels, channels)] = map_tap(
            third_ref, tap // 3, tap % 3, rows, phases
        )
    weight = fourth_w_ref[...].reshape(fourth_taps_ref.shape[1], -1)
    value, slope = silu_and_slope(dot_nn(fourth_taps_ref[...], weight))
    head = head_ref[...].astype(jnp.float32)
    labels = label_ref[...].reshape(-1, label_ref.shape[-1])[:, :1]
    logits = jnp.sum(value * head, axis=1, keepdims=True)
    logit_grad = (jax.nn.sigmoid(logits) - labels) / batch
    delta = rounded(logit_grad * head * slope)
    last_row_zero(fourth_delta_ref)
    fill_delta(fourth_delta_ref, delta.reshape(samples, rows, phases, BLOCK, delta.shape[-1]))
    parts = fourth_parts(fourth_delta_ref, rows, phases)
    for row_parity in range(2):
        for col_parity in range(2):
            part = parts(row_parity, col_parity, rows, phases)
            part = rounded(part * third_slope_ref[:, :, row_parity, :, col_parity])
            for row in range(rows):
                third_delta_ref[:, 2 * row + row_parity, col_parity] = part[:, row, 0]
    return value, logit_grad, delta


def near_kernel(bands, near_ref, third_w_ref, taps_ref, map_ref, slope_ref, second_ref):
    zero_row(second_ref)
    for slot in range(near_ref.shape[0]):
        put_sample(near_ref, slot, second_ref, None, slot, bands)
    value, slope = third_layer(second_ref, third_w_ref, taps_ref, bands)
    map_ref[...] = value
    slope_ref[...] = slope


def far_kernel(
    batch,
    bands,
    near_ref,
    far_ref,
    last_ref,
    near_taps_ref,
    near_map_ref,
    near_slope_ref,
    third_w_ref,
    fourth_w_ref,
    fourth_wt_ref,
    head_ref,
    fourth_taps_ref,
    fourth_flat_ref,
    head_grad_ref,
    third_taps_ref,
    third_flat_ref,
    second_ref,
    far_taps_ref,
    label_ref,
    third_ref,
    third_slope_ref,
    third_delta_ref,
    fourth_delta_ref,
):
    half, early = near_ref.shape[0], far_ref.shape[0]
    zero_row(second_ref)
    for slot in range(half):
        ref, inner = (far_ref, slot) if slot < early else (last_ref, slot - early)
        put_sample(ref, inner, second_ref, None, slot, bands)
    value, slope = third_layer(second_ref, third_w_ref, far_taps_ref, bands)
    cells = far_taps_ref.shape[0] // half
    width = half.bit_length()
    me = lax.axis_index("dp")
    zero_row(third_ref)
    for slot in range(2 * half):
        place = me ^ sum(((slot >> k) & 1) << (width - 1 - k) for k in range(width))
        inner = slot % half
        at = pl.ds(pl.multiple_of(place * cells, cells), cells)
        one = pl.ds(place, 1)
        if slot < half:
            third_taps_ref[at] = near_taps_ref[pl.ds(inner * cells, cells)]
            fill_map(third_ref.at[one], near_map_ref[pl.ds(inner, 1)], 1)
            third_slope_ref[one] = near_slope_ref[pl.ds(inner, 1)].reshape(
                (1,) + third_slope_ref.shape[1:]
            )
            put_label(near_ref, inner, label_ref, place, bands)
        else:
            third_taps_ref[at] = far_taps_ref[pl.ds(inner * cells, cells)]
            fill_map(third_ref.at[one], value[inner : inner + 1], 1)
            third_slope_ref[one] = slope[inner : inner + 1].reshape(
                (1,) + third_slope_ref.shape[1:]
            )
            ref, inner = (far_ref, inner) if inner < early else (last_ref, inner - early)
            put_label(ref, inner, label_ref, place, bands)
    value, logit_grad, delta = deeper_layers(
        batch,
        bands,
        fourth_w_ref,
        lambda ref, *_: functools.partial(delta_parts, ref, fourth_wt_ref),
        head_ref,
        fourth_taps_ref,
        label_ref,
        third_ref,
        third_slope_ref,
        third_delta_ref,
        fourth_delta_ref,
    )
    head_grad_ref[...] = jnp.sum(value * logit_grad, axis=0, keepdims=True)
    fourth_flat_ref[...] = delta.astype(jnp.bfloat16)
    delta = third_delta_ref[...]
    third_flat_ref[...] = delta.reshape(-1, delta.shape[-1]).astype(jnp.bfloat16)


def deep_kernel(
    batch,
    bands,
    near_ref,
    far_ref,
    last_ref,
    third_w_ref,
    fourth_w_ref,
    fourth_wt_ref,
    head_ref,
    fourth_taps_ref,
    fourth_flat_ref,
    head_grad_ref,
    *refs,
):
    third_grad_ref, second_ref, label_ref, third_taps_ref = refs[:4]
    third_ref, third_slope_ref, third_delta_ref, fourth_delta_ref = refs[4:]
    zero_row(second_ref)
    take_samples((near_ref, far_ref, last_ref), second_ref, label_ref, bands)
    value, logit_grad, delta = deep_layers(
        batch,
        bands,
        third_w_ref,
        fourth_w_ref,
        lambda ref, *_: functools.partial(delta_parts, ref, fourth_wt_ref),
        head_ref,
        fourth_taps_ref,
        second_ref,
        label_ref,
        third_taps_ref,
        third_ref,
        third_slope_ref,
        third_delta_ref,
        fourth_delta_ref,
    )

    head_grad = jnp.sum(value * logit_grad, axis=0, keepdims=True)
    add_to(head_grad_ref, head_grad)
    fourth_flat_ref[...] = delta.astype(jnp.bfloat16)
    delta = third_delta_ref[...]
    delta = delta.reshape(-1, delta.shape[-1]).astype(jnp.bfloat16)
    add_to(third_grad_ref, dot_tn(delta, third_taps_ref[...]).T)


def local_kernel(
    batch,
    bands,
    payload_ref,
    third_w_ref,
    fourth_w_ref,
    head_ref,
    second_w_ref,
    even_ref,
    odd_ref,
    first_ref,
    first_slope_ref,
    second_slope_ref,
    *refs,
):
    keep_ref, pass_ref = refs[:2]
    third_ref, second_ref, first_delta_ref, flat_ref, second_map_ref, label_ref = refs[2:8]
    fourth_taps_ref = refs[8]
    third_delta_ref = refs[12]
    zero_row(second_map_ref)
    put_sample(payload_ref, 0, second_map_ref, label_ref, 0, bands)
    deep_layers(
        batch,
        bands,
        third_w_ref,
        fourth_w_ref,
        lambda ref, *size: functools.partial(
            column_parts, delta_columns(ref, *size), fourth_w_ref
        ),
        head_ref,
        fourth_taps_ref,
        second_map_ref,
        label_ref,
        *refs[9:14],
    )
    sample = lax.axis_index("dp")
    _, rows, phases, _, _ = third_delta_ref.shape
    fill_delta(third_ref, third_delta_ref[...])
    last_row_zero(third_ref)
    last_row_zero(second_ref)
    columns = delta_columns(third_ref, rows, phases)
    for row_parity in range(2):
        for col_parity in range(2):
            part = column_parts(columns, third_w_ref, row_parity, col_parity, rows, phases)
            for row in range(rows):
                for phase in range(phases):
                    at = (slice(None), 2 * row + row_parity, 2 * phase + col_parity)
                    second_ref[at] = rounded(part[:, row, phase] * second_slope_ref[at])
    rows, phases = 2 * rows, 2 * phases
    second_ref[:, :, phases] = shift_block(second_ref[:, :, 0], -1)
    columns = delta_columns(second_ref, rows, phases)
    for row_parity in range(2):
        for col_parity in range(2):
            part = column_parts(columns, second_w_ref, row_parity, col_parity, rows, phases)
            for row in range(rows):
                for phase in range(phases):
                    at = (slice(None), 2 * row + row_parity, 2 * phase + col_parity)
                    first_delta_ref[at] = rounded(part[:, row, phase] * first_slope_ref[at])
    delta = second_ref[:, pl.ds(0, rows), pl.ds(0, phases)]
    delta = delta.reshape(-1, delta.shape[-1]).astype(jnp.bfloat16)
    depth = first_ref.shape[-1]
    for tap in range(9):
        cells = map_tap(first_ref, tap // 3, tap % 3, rows, phases)
        flat_ref[pl.ds((12 + tap) * depth, depth)] = dot_tn(cells, delta)
    delta = first_delta_ref[...]
    delta = delta.reshape(-1, delta.shape[-1]).astype(jnp.bfloat16)
    cells = delta.shape[0]
    row_cells = cells // (2 * rows)
    taps = (odd_ref[pl.ds(0, cells)], even_ref[...], odd_ref[pl.ds(row_cells, cells)])
    for tap in range(3):
        part = dot_tn(delta, taps[tap])
        for piece in range(4):
            flat_ref[pl.ds((4 * tap + piece) * depth, depth)] = part[
                :, piece * 128 : piece * 128 + 128
            ]
    share = keep_ref.shape[1]
    for slot in range(4):
        at = pl.multiple_of(((sample % 4) ^ slot) * share, share)
        ref = pass_ref if slot % 2 else keep_ref
        ref[slot // 2] = flat_ref[pl.ds(at, share)].astype(jnp.bfloat16)


def add_to(ref, value):
    first = pl.program_id(0) == 0
    ref[...] = jnp.where(first, 0.0, ref[...]) + value


def third_grad_kernel(taps_ref, delta_ref, out_hbm, grad_ref, sems):
    depth = grad_ref.shape[1]
    delta = delta_ref[...].T
    copies = []
    for row_tap in range(3):
        part = dot_nn(delta, taps_ref[:, pl.ds(3 * row_tap * depth, 3 * depth)])
        grad_ref[pl.ds(3 * row_tap, 3)] = part.T.reshape(3, depth, part.shape[0])
        rows = pl.ds(3 * row_tap, 3)
        copies.append(
            pltpu.make_async_copy(grad_ref.at[rows], out_hbm.at[rows], sems.at[row_tap])
        )
        copies[-1].start()
    for copy in copies:
        copy.wait()


def fourth_grad_alone_kernel(fourth_taps_ref, fourth_flat_ref, out_hbm, grad_ref, sems):
    depth = grad_ref.shape[1]
    copies = []
    for tap in range(9):
        grad_ref[tap] = dot_tn(
            fourth_taps_ref[:, pl.ds(tap * depth, depth)], fourth_flat_ref[...]
        )
        copy = pltpu.make_async_copy(grad_ref.at[tap], out_hbm.at[tap], sems.at[tap])
        copy.start()
        copies.append(copy)
    for copy in copies:
        copy.wait()


def fourth_grad_kernel(fourth_taps_ref, fourth_flat_ref, out_ref):
    @pl.when(pl.program_id(1) == 0)
    def _():
        out_ref[...] = jnp.zeros(out_ref.shape, jnp.float32)

    out_ref[...] += dot_tn(fourth_taps_ref[...], fourth_flat_ref[...])


def finish_kernel(*refs):
    got_refs = refs[:4]
    temporal_hbm, middle_hbm, temporal_ref, middle_ref, flat_ref, sems = refs[4:]
    me = lax.axis_index("dp") % 4
    share = got_refs[0].shape[0]
    for slot in range(4):
        at = pl.multiple_of((me ^ slot) * share, share)
        flat_ref[pl.ds(at, share)] = got_refs[slot][...].astype(jnp.float32)
    depth = temporal_ref.shape[2]
    middle_ref[...] = flat_ref[pl.ds(12 * depth, 9 * depth)]
    copies = [pltpu.make_async_copy(middle_ref, middle_hbm, sems.at[3])]
    copies[0].start()
    rest = temporal_ref.shape[1] - 128
    for tap in range(3):
        parts = [flat_ref[pl.ds((4 * tap + piece) * depth, depth)].T for piece in range(4)]
        for col_tap in range(3):
            temporal_ref[3 * tap + col_tap, pl.ds(0, 128)] = parts[col_tap]
            temporal_ref[3 * tap + col_tap, pl.ds(128, rest)] = parts[3][
                col_tap * rest : col_tap * rest + rest
            ]
        rows = pl.ds(3 * tap, 3)
        copies.append(
            pltpu.make_async_copy(temporal_ref.at[rows], temporal_hbm.at[rows], sems.at[tap])
        )
        copies[-1].start()
    for copy in copies:
        copy.wait()


def cost(flops, size):
    return pl.CostEstimate(flops=flops, bytes_accessed=size, transcendentals=0)


def swapped(value, axis, bit):
    return lax.ppermute(value, axis, [(i, i ^ bit) for i in range(lax.axis_size(axis))])


def band_pieces(value, bands):
    pieces = [value]
    bit = 1
    while bit < bands:
        whole = pieces[0] if bit == 1 else jnp.concatenate(pieces, axis=0)
        pieces.append(swapped(whole, "space", bit))
        bit *= 2
    return pieces


def put(buffer, part, at):
    return lax.dynamic_update_slice(buffer, part, (at,) + (0,) * (buffer.ndim - 1))


def after(value, *others):
    return lax.optimization_barrier((value, *others))[0]


def gather_and_sum(payload, local_sums, transposed, samples):
    half, quarter = samples // 2, samples // 4
    near = put(jnp.zeros((half,) + payload.shape[1:], payload.dtype), payload, 0)
    got = swapped(payload, "dp", quarter * 2) if quarter > 1 else None
    keep, passed = local_sums()
    core = swapped(passed, "dp", 1)
    mine, theirs = added(keep[0], core[0]), added(keep[1], core[1])
    mine_beside = swapped(theirs, "dp", 2)
    weights = transposed(theirs)
    count, beside_count = 1, 0
    while count < quarter:
        near = put(near, after(got, keep), count)
        count *= 2
        if count < quarter:
            part = near[beside_count:count]
            got = swapped(near[:count], "dp", half // count)
            beside = swapped(after(part, theirs), "dp", 2)
            near = put(near, beside, quarter + beside_count)
            beside_count = count
    total = added(mine, after(mine_beside, weights))
    beside = swapped(after(near[beside_count:quarter], theirs), "dp", 2)
    early = swapped(near[: quarter + beside_count], "dp", 1)
    bit = 4
    while 2 * bit < samples:
        other = swapped(total, "dp", bit)
        beside = after(beside, total)
        total = added(total, after(other, beside))
        bit *= 2
    near = put(near, beside, quarter + beside_count)
    last = swapped(beside, "dp", 1)
    return near, early, last, total, bit, weights


def added(*parts):
    total = parts[0].astype(jnp.float32)
    for part in parts[1:]:
        total = total + part.astype(jnp.float32)
    return total.astype(jnp.bfloat16)


def local(
    occupancy,
    state_labels,
    lift_weight,
    temporal_weight,
    middle_weight,
    deeper_weight,
    deepest_weight,
    head_weight,
):
    bands = lax.axis_size("space")
    samples = lax.axis_size("dp")
    _, frames, band, cols = occupancy.shape
    lift_all = frames * lift_weight.shape[1]
    one, two = middle_weight.shape[2:]
    three, four = deepest_weight.shape[2:]
    f32, bf16 = jnp.float32, jnp.bfloat16
    shaped = jax.ShapeDtypeStruct
    phases = cols // BLOCK
    rows = bands * band
    small = samples * bands <= 32
    vmem = pl.BlockSpec(memory_space=pltpu.VMEM)

    def grant(size):
        return pltpu.CompilerParams(vmem_limit_bytes=(size if small else 60) * MIB)

    lines = band_pieces(occupancy, bands)
    first_w = temporal_weight.reshape(9, lift_all, one)
    second_w = middle_weight.reshape(9, one, two)
    third_w = deeper_weight.reshape(9, two, three)
    fourth_w = deepest_weight.reshape(9, three, four)
    head = head_weight.reshape(1, four)

    sent = rows // 4 * phases // 4 * BLOCK + 16
    hbm = pl.BlockSpec(memory_space=pltpu.HBM)
    even_shape = shaped((rows // 2 * cols // 2, 512), bf16)
    odd_shape = shaped(((rows // 2 + 1) * cols // 2, 512), bf16)
    bits_scratch = pltpu.VMEM((band * 128, cols), bf16)
    own_cells = shaped((band // 2 * cols // 2, 512), bf16)
    own_args = [
        pltpu.with_memory_space_constraint(value, pltpu.HBM)
        for value in (
            occupancy,
            state_labels,
            lift_weight,
            first_w,
            second_w,
            third_w,
            fourth_w,
        )
    ]
    (
        own_even,
        own_odd,
        own_labels,
        lift_all_w,
        first_all,
        second_w2,
        third_w2,
        fourth_w2,
    ) = pl.pallas_call(
        own_kernel,
        out_shape=(
            own_cells,
            own_cells,
            shaped((16, two), bf16),
            shaped((128, 256), bf16),
            shaped((3, 512, one), bf16),
            shaped(second_w.shape, bf16),
            shaped(third_w.shape, bf16),
            shaped(fourth_w.shape, bf16),
        ),
        in_specs=[hbm] * 7,
        out_specs=(vmem,) * 8,
        scratch_shapes=[
            pltpu.VMEM(occupancy.shape, occupancy.dtype),
            pltpu.VMEM(state_labels.shape, state_labels.dtype),
            pltpu.VMEM(lift_weight.shape, bf16),
            pltpu.VMEM(first_w.shape, bf16),
            bits_scratch,
            pltpu.SemaphoreType.DMA((15,)),
        ],
        compiler_params=grant(24),
        cost_estimate=cost(100_000_000, 10_000_000),
        name="own_band",
    )(*own_args)
    pieces = len(lines) - 1
    even, odd, payload, first, first_slope, second_slope = pl.pallas_call(
        functools.partial(early_kernel, pieces, lift_all - 128),
        out_shape=(
            even_shape,
            odd_shape,
            shaped((sent, two), bf16),
            shaped((1, rows // 4 + 1, 2, phases // 4 + 1, 2, BLOCK, one), f32),
            shaped((1, rows // 2, phases // 2, BLOCK, one), f32),
            shaped((1, rows // 4, phases // 4, BLOCK, two), f32),
        ),
        in_specs=[vmem] * (pieces + 5),
        out_specs=(vmem,) * 6,
        scratch_shapes=[bits_scratch],
        compiler_params=grant(24),
        cost_estimate=cost(150_000_000, 4_000_000),
        name="early",
    )(*lines[1:], lift_all_w, first_all, second_w2, own_even, own_odd)

    labels, bit = own_labels, 1
    while bit < bands:
        labels = labels + swapped(labels, "space", bit)
        bit *= 2
    payload = put(payload, labels, sent - 16)[None]
    deep_weights = (third_w2, fourth_w2)

    third_cells = 2 * bands * 2 * BLOCK
    fourth_cells = bands * BLOCK

    def second_scratch(count):
        return pltpu.VMEM((count, 2 * bands + 1, 2, 3, 2, BLOCK, two), f32)

    def third_taps_scratch(count):
        return pltpu.VMEM((count * third_cells, 9 * two), bf16)

    def deep_scratch(count):
        return [
            third_taps_scratch(count),
            pltpu.VMEM((count, bands + 1, 2, 2, 2, BLOCK, three), f32),
            pltpu.VMEM((count, bands, 2, 1, 2, BLOCK, three), f32),
            pltpu.VMEM((count, 2 * bands, 2, BLOCK, three), f32),
            pltpu.VMEM((count, bands + 1, 2, BLOCK, four), f32),
        ]

    share = 21 * one // 4
    local_call = pl.pallas_call(
        functools.partial(local_kernel, samples, bands),
        out_shape=(shaped((2, share, two), bf16),) * 2,
        in_specs=[vmem] * 10,
        out_specs=(vmem,) * 2,
        scratch_shapes=[
            pltpu.VMEM((1, 2 * bands + 1, 3, BLOCK, three), f32),
            pltpu.VMEM((1, 4 * bands + 1, 5, BLOCK, two), f32),
            pltpu.VMEM(first_slope.shape, f32),
            pltpu.VMEM((21 * one, two), f32),
            second_scratch(1),
            pltpu.VMEM((1, bands, BLOCK, two), f32),
            pltpu.VMEM((fourth_cells, 9 * three), bf16),
        ]
        + deep_scratch(1),
        compiler_params=grant(24),
        cost_estimate=cost(300_000_000, 9_000_000),
        name="local",
    )
    maps = (head, second_w2, even, odd, first, first_slope, second_slope)
    transpose_call = pl.pallas_call(
        transpose_kernel,
        out_shape=shaped((9, four, three), bf16),
        in_specs=[vmem],
        out_specs=vmem,
        compiler_params=grant(16),
        cost_estimate=cost(10_000_000, 5_000_000),
        name="transpose",
    )

    near, far, last, total, bit, fourth_wt = gather_and_sum(
        payload,
        lambda: local_call(payload, *deep_weights, *maps),
        lambda keep: transpose_call(after(fourth_w2, keep)),
        samples,
    )
    near = after(near, total)

    chunk = max(1, min(samples, 32 // bands))
    steps = samples // chunk
    full = lambda *shape: pl.BlockSpec(shape, lambda i: (0,) * len(shape))
    grad_shape = shaped((9 * two, three), f32)
    fourth_shapes = (
        shaped((samples * fourth_cells, 9 * three), bf16),
        shaped((samples * fourth_cells, four), bf16),
        shaped((1, four), f32),
    )
    label_scratch = pltpu.VMEM((chunk, bands, BLOCK, two), f32)
    deep_cost = cost(1_300_000_000, 12_000_000)
    if small:
        half = samples // 2
        half_shapes = (
            shaped((half * third_cells, 9 * two), bf16),
            shaped((half, 2 * bands, 2, BLOCK, three), f32),
            shaped((half, 2 * bands, 2, BLOCK, three), f32),
        )
        near_third = pl.pallas_call(
            functools.partial(near_kernel, bands),
            out_shape=half_shapes,
            in_specs=[vmem] * 2,
            out_specs=(vmem,) * 3,
            scratch_shapes=[second_scratch(half)],
            compiler_params=grant(24),
            cost_estimate=cost(300_000_000, 4_000_000),
            name="near",
        )(near, third_w2)
        fourth_taps, fourth_flat, head_grad, *thirds = pl.pallas_call(
            functools.partial(far_kernel, samples, bands),
            out_shape=fourth_shapes
            + (
                shaped((samples * third_cells, 9 * two), bf16),
                shaped((samples * third_cells, three), bf16),
            ),
            in_specs=[vmem] * 10,
            out_specs=(vmem,) * 5,
            scratch_shapes=[second_scratch(half), third_taps_scratch(half), label_scratch]
            + deep_scratch(chunk)[1:],
            compiler_params=grant(40),
            cost_estimate=deep_cost,
            name="deep",
        )(near, far, last, *near_third, *deep_weights, fourth_wt, head)
        deeper_grad = None
    else:
        fourth_taps, fourth_flat, head_grad, deeper_grad = pl.pallas_call(
            functools.partial(deep_kernel, samples, bands),
            grid=(steps,),
            out_shape=fourth_shapes + (grad_shape,),
            in_specs=[
                full(*value.shape) for value in (near, far, last, *deep_weights, fourth_wt, head)
            ],
            out_specs=(
                pl.BlockSpec((chunk * fourth_cells, 9 * three), lambda i: (i, 0)),
                pl.BlockSpec((chunk * fourth_cells, four), lambda i: (i, 0)),
                full(1, four),
                full(9 * two, three),
            ),
            scratch_shapes=[second_scratch(chunk), label_scratch] + deep_scratch(chunk),
            compiler_params=grant(40),
            cost_estimate=deep_cost,
            name="deep",
        )(near, far, last, *deep_weights, fourth_wt, head)

    if small:
        deeper_grad = pl.pallas_call(
            third_grad_kernel,
            out_shape=shaped((9, two, three), f32),
            in_specs=[vmem] * 2,
            out_specs=pl.BlockSpec(memory_space=pl.ANY),
            scratch_shapes=[
                pltpu.VMEM((9, two, three), f32),
                pltpu.SemaphoreType.DMA((3,)),
            ],
            compiler_params=grant(24),
            cost_estimate=cost(600_000_000, 4_000_000),
            name="third_grad",
        )(*thirds)
    if bit < samples:
        other, fourth_flat, deeper_grad = lax.optimization_barrier(
            (swapped(total, "dp", bit), fourth_flat, deeper_grad)
        )
        total = added(total, other)
    beside = swapped(total, "dp", 2)
    core = swapped(total, "dp", 1)
    if small:
        deepest_grad = pl.pallas_call(
            fourth_grad_alone_kernel,
            out_shape=shaped((9, three, four), f32),
            in_specs=[vmem] * 2,
            out_specs=pl.BlockSpec(memory_space=pl.ANY),
            scratch_shapes=[
                pltpu.VMEM((9, three, four), f32),
                pltpu.SemaphoreType.DMA((9,)),
            ],
            compiler_params=grant(16),
            cost_estimate=cost(600_000_000, 6_000_000),
            name="fourth_grad",
        )(fourth_taps, fourth_flat)
    else:
        deepest_grad = pl.pallas_call(
            fourth_grad_kernel,
            grid=(3, steps),
            out_shape=shaped((9 * three, four), f32),
            in_specs=[
                pl.BlockSpec((chunk * fourth_cells, 3 * three), lambda t, i: (i, t)),
                pl.BlockSpec((chunk * fourth_cells, four), lambda t, i: (i, 0)),
            ],
            out_specs=pl.BlockSpec((3 * three, four), lambda t, i: (t, 0)),
            compiler_params=grant(16),
            cost_estimate=cost(600_000_000, 6_000_000),
            name="fourth_grad",
        )(fourth_taps, fourth_flat)
    beside, deepest_grad = lax.optimization_barrier((beside, deepest_grad))
    across = swapped(beside, "dp", 1)
    temporal_grad, middle_grad = pl.pallas_call(
        finish_kernel,
        out_shape=(shaped((9, lift_all, one), f32), shaped((9 * one, two), f32)),
        in_specs=[vmem] * 4,
        out_specs=(pl.BlockSpec(memory_space=pl.ANY),) * 2,
        scratch_shapes=[
            pltpu.VMEM((9, lift_all, one), f32),
            pltpu.VMEM((9 * one, two), f32),
            pltpu.VMEM((21 * one, two), f32),
            pltpu.SemaphoreType.DMA((4,)),
        ],
        compiler_params=grant(16),
        cost_estimate=cost(1_000_000, 1_500_000),
        name="finish",
    )(total, core, beside, across)
    return (
        temporal_grad.reshape(temporal_weight.shape),
        middle_grad.reshape(middle_weight.shape),
        deeper_grad.reshape(deeper_weight.shape),
        deepest_grad.reshape(deepest_weight.shape),
        head_grad.reshape(four),
    )


def solution(mesh):
    return jax.shard_map(
        local,
        mesh=mesh,
        in_specs=(
            P("dp", None, "space", None),
            P("dp", "space", None),
            P(),
            P(),
            P(),
            P(),
            P(),
            P(),
        ),
        out_specs=(P(), P(), P(), P(), P()),
        check_vma=False,
    )
```
